32 devices in a mesh: dp: 4 (over x, core), seq: 8 (over z, y).
Axes of the slice: x: 2, y: 2, z: 4, core: 2. Of those that a mesh axis runs over, the one named last changes fastest.
Arguments:
- tokens: bfloat16 [4, 2048, 1536], P('dp', 'seq'), may hold values from -6 to 6
- segments: int32 [4, 2048], P('dp', 'seq'), may hold values from 0 to 6, as said below
- out_grad: bfloat16 [4, 2048, 1536], P('dp', 'seq'), may hold values from -6 to 6
- norm_gain: float32 [2, 1536], replicated, may hold values from 0.5 to 1.5
- in_weight: bfloat16 [2, 1536, 6448], P(None, ('dp', 'seq')), may hold values from -0.15625 to 0.15625
- conv_weight: float32 [2, 4, 3328], replicated, may hold values from -3 to 3
- conv_bias: float32 [2, 3328], replicated, may hold values from -3 to 3
- dt_bias: float32 [2, 48], replicated, may hold values from -11 to -2
- a_log: float32 [2, 48], replicated, may hold values from -1 to 2
- skip: float32 [2, 48], replicated, may hold values from 0.5 to 2
- out_gain: float32 [2, 3072], replicated, may hold values from 0.5 to 1.5
- out_weight: bfloat16 [2, 3072, 1536], P(None, ('dp', 'seq')), may hold values from -0.109375 to 0.109375
Outputs:
- mixed: bfloat16 [4, 2048, 1536], P('dp', 'seq')
- tokens_grad: float32 [4, 2048, 1536], P('dp', 'seq')
- norm_gain_grad: float32 [2, 1536], replicated
- in_weight_grad: float32 [2, 1536, 6448], P(None, ('dp', 'seq'))
- conv_weight_grad: float32 [2, 4, 3328], replicated
- conv_bias_grad: float32 [2, 3328], replicated
- dt_bias_grad: float32 [2, 48], replicated
- a_log_grad: float32 [2, 48], replicated
- skip_grad: float32 [2, 48], replicated
- out_gain_grad: float32 [2, 3072], replicated
- out_weight_grad: float32 [2, 3072, 1536], P(None, ('dp', 'seq'))
The draws below stay inside these ranges and needn't reach their ends.
Inputs may be any that keep to these rules, and one draw needn't show every extreme that they name: `segments`: along each sequence segment numbers never fall and start at 0; exactly three documents begin among positions 1 to 255 and three among positions 1793 to 2047, and no other.
All inputs are finite; a program needn't handle non-finite values.
Results may differ from the reference program's by a relative error of at most 0.013.
Values may be sent and summed in bfloat16 or wider, within the bound.
No kernel may reach another device: no remote copies, remote signals or barrier semaphores. Data moves between devices by JAX's collectives and lax.ppermute only.
A program may use at most 448 MiB of HBM per device.

```python
import jax
import jax.numpy as jnp
from jax import lax

D = 1536
HEADS = 48
HEADDIM = 64
STATE = 128
CONV = 4
GROUP = 256
LAYERS = 2
TOK_DEV = 256
INNER = 3072
CONVDIM = 3328
PROJ = 6448
BATCH = 4
LEN = 2048


def starts_of(row_key):
    first_key, last_key = jax.random.split(row_key)
    head_marks = jax.random.permutation(first_key, TOK_DEV - 1)[:3] + 1
    tail_marks = jax.random.permutation(last_key, TOK_DEV - 1)[:3] + (LEN - TOK_DEV + 1)
    marks = jnp.zeros((LEN,), jnp.int32).at[head_marks].set(1).at[tail_marks].set(1)
    return jnp.cumsum(marks).astype(jnp.int32)


def draw_segments(key, part):
    key = jax.random.fold_in(key, 11)
    return jax.vmap(starts_of)(jax.random.split(key, BATCH))


def steps_of(own_key, shape, pieces, least, largest):
    def one(dim, parts):
        steps = jax.random.uniform(jax.random.fold_in(jax.random.fold_in(own_key, 6), dim), (parts,), jnp.float32, least / len(pieces), largest / len(pieces))
        return jnp.repeat(jnp.exp(steps), shape[dim] // parts).reshape((-1,) + (1,) * (len(shape) - dim - 1))

    gain = one(*pieces[0])
    for cut in pieces[1:]:
        gain = gain * one(*cut)
    return gain


def normal_values(rng, shape, width, limit, shards=(), held_as=jnp.bfloat16):
    drawn = jax.random.normal(rng, shape, jnp.float32) * width
    if len(shards) > 0:
        drawn = steps_of(rng, shape, shards, -0.22, 0.18) * drawn
    return jnp.clip(drawn, min=-limit, max=limit).astype(held_as)


def setup_inputs(seed: int = 0) -> dict:
    key_of = jax.random.split(jax.random.key(seed), 13)
    return {
        "tokens": normal_values(key_of[0], (BATCH, LEN, D), 1.0, 6.0, ((0, 4), (1, 8))),
        "segments": draw_segments(jax.random.fold_in(key_of[12], 71), 0),
        "out_grad": normal_values(key_of[2], (BATCH, LEN, D), 1.0, 6.0, ((0, 4), (1, 8))),
        "norm_gain": jnp.clip(1.0 + 0.1 * jax.random.normal(key_of[3], (LAYERS, D), jnp.float32), 0.5, 1.5),
        "in_weight": normal_values(key_of[4], (LAYERS, D, PROJ), D ** -0.5, 0.15625, ((1, 32),)),
        "conv_weight": normal_values(key_of[5], (LAYERS, CONV, CONVDIM), CONV ** -0.5, 3.0, (), jnp.float32),
        "conv_bias": normal_values(key_of[6], (LAYERS, CONVDIM), 0.5, 3.0, (), jnp.float32),
        "dt_bias": jnp.clip(jax.random.uniform(key_of[7], (LAYERS, HEADS), jnp.float32, -11.0, -2.0), -11.0, -2.0),
        "a_log": jnp.clip(jax.random.uniform(key_of[8], (LAYERS, HEADS), jnp.float32, -1.0, 2.0), -1.0, 2.0),
        "skip": jnp.clip(jax.random.uniform(key_of[9], (LAYERS, HEADS), jnp.float32, 0.5, 2.0), 0.5, 2.0),
        "out_gain": jnp.clip(1.0 + 0.1 * jax.random.normal(key_of[10], (LAYERS, INNER), jnp.float32), 0.5, 1.5),
        "out_weight": normal_values(key_of[11], (LAYERS, INNER, D), INNER ** -0.5, 0.109375, ((1, 32),)),
    }


EPS = 1e-05
HIGHEST = lax.Precision.HIGHEST

@jax.custom_vjp
def low(v):
    return lax.optimization_barrier(v.astype(jnp.bfloat16)).astype(jnp.float32)

@jax.custom_vjp
def low_back(v):
    return v

def low_keep(v):
    return (low(v), None)

def low_pass(kept, grad):
    return (grad,)

def back_keep(v):
    return (v, None)

def back_low(kept, grad):
    return (low(grad),)
low.defvjp(low_keep, low_pass)
low_back.defvjp(back_keep, back_low)

def rms_scale(values):
    return values * lax.rsqrt(lax.optimization_barrier(jnp.mean(values * values, axis=-1, keepdims=True)) + EPS)

def conv_silu(seg_ext, extended, conv_taps, conv_shift):
    length = extended.shape[-2] - CONV + 1
    seg_here = seg_ext[..., CONV - 1:]
    summed = conv_shift
    for offset in range(CONV):
        same_doc = (seg_ext[..., offset:offset + length] == seg_here)[..., None]
        summed = summed + conv_taps[offset] * extended[..., offset:offset + length, :] * same_doc
    return jax.nn.silu(summed)

def group_pass(carry_in, block_in):
    prior_state, prior_seg = carry_in
    heads_x, b_in, c_out, log_step, step_dt, seg_block = block_in
    length = heads_x.shape[0]
    cumulative = jnp.cumsum(log_step, axis=0)
    places = jnp.arange(length)
    same_doc = (seg_block[:, None] == seg_block[None, :]) & (places[:, None] >= places[None, :])
    gap_logs = jnp.where(same_doc[:, :, None], cumulative[:, None, :] - cumulative[None, :, :], 0.0)
    decays = jnp.exp(gap_logs) * same_doc[:, :, None]
    scores = jnp.dot(c_out, b_in.T, precision=HIGHEST)
    mixing = scores[:, :, None] * decays * step_dt[None, :, :]
    inside = jnp.einsum('ijh,jhp->ihp', mixing, heads_x, precision=HIGHEST)
    entering = jnp.exp(cumulative) * (seg_block == prior_seg)[:, None]
    carried = jnp.einsum('in,hpn->ihp', c_out, prior_state, precision=HIGHEST) * entering[:, :, None]
    last_seg = seg_block[-1]
    leaving = jnp.exp(cumulative[-1][None, :] - cumulative) * (seg_block == last_seg)[:, None] * step_dt
    fresh_state = jnp.einsum('jh,jhp,jn->hpn', leaving, heads_x, b_in, precision=HIGHEST)
    new_state = prior_state * entering[-1][:, None, None] + fresh_state
    return ((new_state, last_seg), inside + carried)

def layer_pass(stream, seg_row, norm_scale, in_matrix, conv_taps, conv_shift, dt_offset, decay_log, skip_scale, gate_scale, out_matrix):
    length = stream.shape[0]
    normed = low(rms_scale(stream) * norm_scale)
    projected = low_back(jnp.dot(normed, in_matrix, precision=HIGHEST))
    gate_raw = projected[:, :INNER]
    conv_in = low(projected[:, INNER:INNER + CONVDIM])
    raw_dt = projected[:, INNER + CONVDIM:]
    padded = jnp.pad(conv_in, ((CONV - 1, 0), (0, 0)))
    seg_pad = jnp.pad(seg_row, (CONV - 1, 0))
    conv_act = low(conv_silu(seg_pad, padded, conv_taps, conv_shift))
    heads_x = conv_act[:, :INNER].reshape(length, HEADS, HEADDIM)
    b_in = conv_act[:, INNER:INNER + STATE]
    c_out = conv_act[:, INNER + STATE:]
    step_dt = jax.nn.softplus(raw_dt + dt_offset)
    log_step = -jnp.exp(decay_log) * step_dt
    count = length // GROUP
    blocks = tuple((member.reshape((count, GROUP) + member.shape[1:]) for member in (heads_x, b_in, c_out, log_step, step_dt, seg_row)))
    start = (jnp.zeros((HEADS, HEADDIM, STATE), jnp.float32), seg_row[0])
    _, outputs = lax.scan(jax.checkpoint(group_pass), start, blocks)
    ssd_y = low_back(outputs.reshape(length, HEADS, HEADDIM) + skip_scale[:, None] * heads_x).reshape(length, INNER)
    normed_y = low(rms_scale(ssd_y * jax.nn.silu(gate_raw)) * gate_scale)
    branch = low_back(jnp.dot(normed_y, out_matrix, precision=HIGHEST))
    return stream + branch
layer_checked = jax.checkpoint(layer_pass)

def reference(tokens, segments, out_grad, norm_gain, in_weight, conv_weight, conv_bias, dt_bias, a_log, skip, out_gain, out_weight):
    weights = (norm_gain, in_weight.astype(jnp.float32), conv_weight, conv_bias, dt_bias, a_log, skip, out_gain, out_weight.astype(jnp.float32))

    def per_sequence(totals, item):
        seq_tokens, seq_segments, seq_grad = item

        def forward(stream, params):
            for layer_id in range(LAYERS):
                stream = layer_checked(stream, seq_segments, *[member[layer_id] for member in params])
            return stream
        result, pull = jax.vjp(forward, seq_tokens.astype(jnp.float32), weights)
        grad_tokens, grad_weights = pull(seq_grad.astype(jnp.float32))
        totals = jax.tree.map(jnp.add, totals, grad_weights)
        return (totals, (result.astype(jnp.bfloat16), grad_tokens))
    start = jax.tree.map(jnp.zeros_like, weights)
    totals, (mixed, tokens_grad) = lax.scan(per_sequence, start, (tokens, segments, out_grad))
    return (mixed, tokens_grad, totals[0], totals[1], totals[2], totals[3], totals[4], totals[5], totals[6], totals[7], totals[8])
```

```python
from functools import partial

import jax
import jax.numpy as jnp
from jax import lax
from jax.experimental import pallas as pl
from jax.experimental.pallas import tpu as pltpu
from jax.sharding import Mesh
from jax.sharding import PartitionSpec as P

HEADS = 48
HEADDIM = 64
STATE = 128
CONV = 4
INNER = 3072
CONVDIM = 3328

TEAM = 4
HEADS_Q = HEADS // TEAM
INNER_Q = INNER // TEAM
BC_Q = 2 * STATE // TEAM
CONV_Q = INNER_Q + BC_Q
WIDE = 896

EPS = 1e-05
NEAR = 4
SWAP = [(0, 1), (1, 0)]
BF16 = jnp.bfloat16
F32 = jnp.float32


def shift(block, axis, distance):
    size = lax.axis_size(axis)
    return lax.ppermute(block, axis, [(i, (i + distance) % size) for i in range(size)])


def step_line(block, axis, distance):
    devices = range(lax.axis_size(axis))
    return lax.ppermute(block, axis, [(i, i + distance) for i in devices if i + distance in devices])


def core_swap(block):
    return lax.ppermute(block, "core", SWAP)


def y_swap(block):
    return lax.ppermute(block, "y", SWAP)


def diagonal_swap(block):
    return lax.ppermute(block, ("core", "y"), [(0, 3), (1, 2), (2, 1), (3, 0)])


def xor_sum(values, axis):
    size = lax.axis_size(axis)
    bit = 1
    while bit < size:
        values = tie(values + lax.ppermute(values, axis, [(i, i ^ bit) for i in range(size)]))
        bit *= 2
    return values


def member():
    return lax.axis_index("y") * 2 + lax.axis_index("core")


def in_order(parts):
    q = member()
    return [lax.select_n(q ^ j, *parts) for j in range(TEAM)]


def around_team(blocks):
    return blocks[0], core_swap(blocks[1]), y_swap(blocks[2]), diagonal_swap(blocks[3])


def by_y(own, other):
    first = lax.axis_index("y") == 0
    return jnp.where(first, jnp.concatenate((own, other), 1), jnp.concatenate((other, own), 1))


def team_gather(block):
    pair = jnp.stack((block, core_swap(block)))
    crossed = y_swap(block)
    other = jnp.stack((crossed, core_swap(crossed)))
    return by_y(pair, other)


def team_scatter(values):
    total = values[0] + core_swap(values[1].astype(BF16)).astype(F32)
    half = total.shape[0] // 2
    y = lax.axis_index("y")
    mine = lax.dynamic_slice_in_dim(total, y * half, half, 0)
    theirs = lax.dynamic_slice_in_dim(total, (1 - y) * half, half, 0)
    return mine + y_swap(theirs.astype(BF16)).astype(F32)


def team_sum(values):
    across = core_swap(values) + diagonal_swap(values)
    return (values + y_swap(values)) + across[::-1]


def x_swap(block):
    return lax.ppermute(block, "x", SWAP)


def line_pieces(piece):
    return [piece] + [shift(piece, "z", hop) for hop in range(1, lax.axis_size("z"))]


def fetch(piece):
    line = line_pieces(piece)
    return line, line + [x_swap(p) for p in line]


def far_columns(piece):
    line = lax.all_gather(piece, "z")
    both = jnp.stack((line, x_swap(line)))
    size, (rows, width) = line.shape[0], line.shape[2:]
    both = jnp.moveaxis(both.reshape(2, size, 2, 2, rows, width), 1, 2)
    return both.reshape(-1, width)


def far_rows(rows):
    line = lax.all_gather(rows, "z")
    other = x_swap(line)
    first = lax.axis_index("x") == 0
    out = jnp.where(first, jnp.stack((line, other), 1), jnp.stack((other, line), 1))
    return out.reshape(-1, rows.shape[-1])


def far_out_scatter(grad, size, rows):
    x = lax.axis_index("x")
    whole = grad.reshape(size, 2, rows, -1)
    own = lax.dynamic_index_in_dim(whole, x, 1, False)
    other = lax.dynamic_index_in_dim(whole, 1 - x, 1, False)
    total = own + x_swap(other.astype(BF16)).astype(F32)
    return lax.psum_scatter(total, "z", scatter_dimension=0)


def far_columns_scatter(grad, size, rows):
    width = grad.shape[-1]
    whole = jnp.moveaxis(grad.reshape(2, 2, size, 2, rows, width), 2, 1)
    own, other = whole.reshape(2, size, TEAM, rows, width)
    total = own + x_swap(other.astype(BF16)).astype(F32)
    return lax.psum_scatter(total, "z", scatter_dimension=0)


def send_sums(own, come):
    sums = [o + c.astype(F32) for o, c in zip(own, come)]
    arrived = [shift(v.astype(BF16), "z", hop) for hop, v in enumerate(sums) if hop]
    return arrived, sums[0]


def total_of(own, arrived):
    return sum([v.astype(F32) for v in arrived], own)


TURN = [(0, 0), (1, 2), (2, 1), (3, 3)]


def x_first(values):
    low, high = jnp.split(values, 2, axis=-1)
    first = lax.axis_index("x") == 0
    return jnp.where(first, jnp.concatenate((low, high), -1), jnp.concatenate((high, low), -1))


def rms_scale(values):
    return values * lax.rsqrt(jnp.mean(values * values, axis=-1, keepdims=True) + EPS)


def norm_piece(stream, norm_scale):
    return rms_scale(stream) * norm_scale


def conv_piece(seg_ext, extended, conv_taps, conv_shift):
    length = extended.shape[-2] - CONV + 1
    seg_here = seg_ext[..., CONV - 1 :]
    summed = conv_shift
    for offset in range(CONV):
        same_doc = (seg_ext[..., offset : offset + length] == seg_here)[..., None]
        summed = summed + conv_taps[offset] * extended[..., offset : offset + length, :] * same_doc
    return jax.nn.silu(summed)


CHUNK = 128
LANE = 64
NEVER = -1e30
TILE = INNER_Q // 128


def split_parts(values):
    high = values.astype(BF16)
    rest = values - high.astype(F32)
    middle = rest.astype(BF16)
    return high, middle, (rest - middle.astype(F32)).astype(BF16)


def mm(a, b, over=(1, 0)):
    return lax.dot_general(
        a, b, (((over[0],), (over[1],)), ((), ())), preferred_element_type=F32
    )


def exact_mm(values, ones, over=(1, 0)):
    high, middle, low = split_parts(values)
    return (mm(low, ones, over) + mm(middle, ones, over)) + mm(high, ones, over)


def spread_mm(values, ones, over=(1, 0)):
    high, low = halves(values)
    return mm(low, ones, over) + mm(high, ones, over)


def mm_exact(ones, values):
    high, middle, low = split_parts(values)
    return (mm(ones, low) + mm(ones, middle)) + mm(ones, high)


def halves(values):
    high = values.astype(BF16)
    return high, (values - high.astype(F32)).astype(BF16)


def mm_wide(narrow, values, over=(1, 0)):
    high, low = halves(values)
    return mm(narrow, low, over) + mm(narrow, high, over)


def softplus(values):
    tail = jnp.exp(-jnp.abs(values))
    series = tail * (1.0 - tail * (0.5 - tail * (1.0 / 3.0)))
    return jnp.maximum(values, 0.0) + jnp.where(tail < 0.01, series, jnp.log(1.0 + tail))


def sigmoid(values):
    return 1.0 / (1.0 + jnp.exp(-values))


def grids(shape):
    return lax.broadcasted_iota(jnp.int32, shape, 0), lax.broadcasted_iota(jnp.int32, shape, 1)


def column(row):
    return jnp.broadcast_to(row, (CHUNK, CHUNK)).T


def step_terms(raw_ref, par_ref):
    down, across = grids((CHUNK, CHUNK))
    lower = (down >= across).astype(F32).astype(BF16)
    step = softplus(raw_ref[0] + par_ref[0:1])
    sums = mm_exact(lower, -par_ref[1:2] * step)
    return step, sums, sums[CHUNK - 1 :]


def seg_terms(seg_ref):
    return column(seg_ref[0, 0, 0:1]), seg_ref[0, 0, 0:1], seg_ref[0, 0, 1:2], seg_ref[0, 0, 2:3]


def chunk_decay(total, before, last, spread):
    kept = jnp.exp(total) * (before == last).astype(F32)
    return exact_mm(jnp.broadcast_to(kept, (8, CHUNK)), spread)


def state_kernel(x, bc, raw, seg, par, spread, before_out, reach_out, end_out, total_out, bits_out, state, reach):
    @pl.when(pl.program_id(1) == 0)
    def _():
        state[...] = jnp.zeros_like(state)
        reach[...] = jnp.ones_like(reach)

    step, sums, total = step_terms(raw, par)
    lines, _, before, last = seg_terms(seg)
    before_out[0, 0] = state[...]
    reach_out[0, 0] = reach[...]
    leaving = jnp.where(lines == last, jnp.exp(total - sums), 0.0)
    fed = (x[0].astype(F32) * spread_mm(step, spread[...])).astype(BF16).astype(F32)
    fed = fed * spread_mm(leaving, spread[...])
    decay = chunk_decay(total, before, last, spread[...])
    state[...] = state[...] * decay[0:1] + mm_wide(bc[0, :, :STATE], fed, (0, 0))
    reach[...] = reach[...] * decay
    end_out[0] = state[...]
    total_out[0] = reach[...]
    lines = [v[0:1] for v in split_parts(reach[...])]
    bits_out[0] = jnp.concatenate(lines + [jnp.zeros((13, INNER_Q), BF16)], axis=0)


def inside_kernel(x, bc, raw, seg, par, spread, y_out):
    step, sums, _ = step_terms(raw, par)
    lines, row, _, _ = seg_terms(seg)
    down, across = grids((CHUNK, CHUNK))
    bias = jnp.where((lines == row) & (down >= across), 0.0, NEVER)
    scores = mm(bc[0, :, STATE:], bc[0, :, :STATE], (1, 1))
    turned = sums.T
    fed = (x[0].astype(F32) * spread_mm(step, spread[...])).astype(BF16)
    for pair in range(HEADS_Q // 2):
        lanes = slice(pair * 128, pair * 128 + 128)
        mixing = []
        for head in (LANE + 2 * pair, LANE + 2 * pair + 1):
            gap = jnp.broadcast_to(sums[:, head : head + 1], (CHUNK, CHUNK)) - turned[head : head + 1]
            mixing.append((scores * jnp.exp(gap + bias)).astype(BF16))
        both = mm(jnp.concatenate(mixing, axis=0), fed[:, lanes])
        y_out[0, :, lanes] = jnp.where(across < HEADDIM, both[:CHUNK], both[CHUNK:])


def outer_kernel(
    y_in, x, bc, raw, seg, par, spread, before, reach, start, gate, rows, y_out, gated_out, square_out
):
    _, sums, _ = step_terms(raw, par)
    lines, _, ahead, _ = seg_terms(seg)
    entering = spread_mm(jnp.where(lines == ahead, jnp.exp(sums), 0.0), spread[...])
    state = before[0, 0] + reach[0, 0, 0:1] * start[0]
    y = y_in[0] + entering * mm_wide(bc[0, :, STATE:], state)
    y_out[0] = y
    raw_gate = gate[0]
    gated = (y + rows[0:1] * x[0].astype(F32)) * (raw_gate * sigmoid(raw_gate))
    gated_out[0] = gated
    square = gated * gated
    folded = square[:, :128]
    for tile in range(1, INNER_Q // 128):
        folded = folded + square[:, tile * 128 : tile * 128 + 128]
    square_out[0, 0] = jnp.sum(folded.T, axis=0, keepdims=True)


def along_kernel(grad, gated, rows, scale, along_out, gain_out):
    @pl.when(pl.program_id(1) == 0)
    def _():
        gain_out[...] = jnp.zeros_like(gain_out)

    product = grad[0] * gated[0]
    weighed = product * rows[1:2]
    folded = weighed[:, :128]
    for tile in range(1, INNER_Q // 128):
        folded = folded + weighed[:, tile * 128 : tile * 128 + 128]
    along_out[0, 0] = jnp.sum(folded.T, axis=0, keepdims=True)
    lines = jnp.concatenate([column(scale[0, 0])] * (INNER_Q // 128), axis=1)
    gain_out[0] += jnp.sum((product * lines).reshape(CHUNK // 8, 8, INNER_Q), axis=0)


def gate_back_kernel(
    grad, gated, y, x, gate, bc, raw, seg, par, spread, rows, scale, along,
    grad_out, gate_out, after_out, beyond_out, start_out, state, reach,
):
    @pl.when(pl.program_id(1) == 0)
    def _():
        state[...] = jnp.zeros_like(state)
        reach[...] = jnp.ones_like(reach)

    wide = lambda row: jnp.concatenate([column(row)] * (INNER_Q // 128), axis=1)
    factor = scale[0, 0]
    pull = factor * factor * factor * along[0, 0] * (1.0 / INNER)
    grad_gated = grad[0] * rows[1:2] * wide(factor) - gated[0] * wide(pull)
    raw_gate = gate[0]
    sig = sigmoid(raw_gate)
    grad_y = (grad_gated * (raw_gate * sig)).astype(BF16)
    ssd_y = y[0] + rows[0:1] * x[0].astype(F32)
    gate_out[0] = (grad_gated * ssd_y * (sig * (1.0 + raw_gate * (1.0 - sig)))).astype(BF16)
    grad_out[0] = grad_y

    _, sums, total = step_terms(raw, par)
    lines, _, before, last = seg_terms(seg)
    after_out[0, 0] = state[...]
    beyond_out[0, 0] = reach[...]
    entering = spread_mm(jnp.where(lines == before, jnp.exp(sums), 0.0), spread[...])
    decay = chunk_decay(total, before, last, spread[...])
    fed = grad_y.astype(F32) * entering
    state[...] = state[...] * decay[0:1] + mm_wide(bc[0, :, STATE:], fed, (0, 0))
    reach[...] = reach[...] * decay
    start_out[0] = state[...]


def inside_back_kernel(x, bc, raw, seg, par, spread, grad, fed_out, b_out, c_out):
    step, sums, _ = step_terms(raw, par)
    lines, row, _, _ = seg_terms(seg)
    down, across = grids((CHUNK, CHUNK))
    bias = jnp.where((lines == row) & (across >= down), 0.0, NEVER)
    b_in, c_in = bc[0, :, :STATE], bc[0, :, STATE:]
    scores = mm(b_in, c_in, (1, 1))
    turned = sums.T
    fed = (x[0].astype(F32) * spread_mm(step, spread[...])).astype(BF16)
    grad_scores = jnp.zeros((CHUNK, CHUNK), F32)
    for pair in range(HEADS_Q // 2):
        lanes = slice(pair * 128, pair * 128 + 128)
        fed_pair, grad_pair = fed[:, lanes], grad[0, :, lanes]
        none = jnp.zeros_like(fed_pair)
        apart = jnp.concatenate(
            (jnp.where(across < HEADDIM, fed_pair, none), jnp.where(across < HEADDIM, none, fed_pair)),
            axis=0,
        )
        grad_mixing = mm(apart, grad_pair, (1, 1))
        mixing = []
        for which in range(2):
            head = LANE + 2 * pair + which
            gap = turned[head : head + 1] - jnp.broadcast_to(sums[:, head : head + 1], (CHUNK, CHUNK))
            decays = jnp.exp(gap + bias)
            mixing.append((scores * decays).astype(BF16))
            grad_scores = grad_scores + grad_mixing[which * CHUNK : which * CHUNK + CHUNK] * decays
        both = mm(jnp.concatenate(mixing, axis=0), grad_pair)
        fed_out[0, :, lanes] = jnp.where(across < HEADDIM, both[:CHUNK], both[CHUNK:])
    grad_scores = grad_scores.astype(BF16)
    b_out[0] = mm(grad_scores, c_in)
    c_out[0] = mm(grad_scores, b_in, (0, 0))


def outer_back_kernel(
    fed_in, b_in, c_in, x, bc, raw, seg, par, spread, before, reach, start, after, beyond, grad_end,
    end, total_reach, grad, y, rows,
    x_out, bc_out, raw_out, sums_out, skip_out, carry,
):
    @pl.when(pl.program_id(1) == 0)
    def _():
        sums_out[...] = jnp.zeros_like(sums_out)
        skip_out[...] = jnp.zeros_like(skip_out)
        last_state = end[0] + total_reach[0, 0:1] * start[0]
        meet = jnp.sum((grad_end[0] * last_state).reshape(STATE // 8, 8, INNER_Q), axis=0)
        meet = jnp.sum(spread_mm(meet, spread[...], (1, 1)), axis=0, keepdims=True)
        carry[...] = jnp.broadcast_to(meet, carry.shape)

    step, sums, total = step_terms(raw, par)
    lines, _, ahead, last = seg_terms(seg)
    ones = spread[...]
    state = (before[0, 0] + reach[0, 0, 0:1] * start[0]).astype(BF16)
    grad_state = after[0, 0] + beyond[0, 0, 0:1] * grad_end[0]
    values = x[0].astype(F32)
    grad_y = grad[0].astype(F32)
    wide_step = spread_mm(step, ones)
    leaving = spread_mm(jnp.where(lines == last, jnp.exp(total - sums), 0.0), ones)
    entering = spread_mm(jnp.where(lines == ahead, jnp.exp(sums), 0.0), ones)
    fed = (values * wide_step).astype(BF16).astype(F32)
    grad_fed = fed_in[0] + leaving * mm_wide(bc[0, :, :STATE], grad_state)
    x_out[0] = wide_step * grad_fed + rows[0:1] * grad_y
    bc_out[0, :, :STATE] = b_in[0] + mm((leaving * fed).astype(BF16), grad_state.astype(BF16), (1, 1))
    bc_out[0, :, STATE:] = c_in[0] + mm((entering * grad_y).astype(BF16), state, (1, 1))
    skip_out[0] += jnp.sum((grad_y * values).reshape(CHUNK // 8, 8, INNER_Q), axis=0)

    by_step = spread_mm(values * grad_fed, ones, (1, 1))
    flow = spread_mm(grad_y * y[0] - fed * grad_fed, ones, (1, 1))
    down, across = grids((CHUNK, CHUNK))
    upper = (across >= down).astype(F32).astype(BF16)
    grad_log = mm_exact(upper, flow) + carry[0:1]
    carry[...] = jnp.broadcast_to(grad_log[0:1], carry.shape)
    rate = par[1:2]
    grad_raw = (by_step - rate * grad_log) * sigmoid(raw[0] + par[0:1])
    raw_out[0] = grad_raw
    fold = lambda v: jnp.sum(v.reshape(CHUNK // 8, 8, CHUNK), axis=0)
    sums_out[0, 0:8] += fold(-rate * step * grad_log)
    sums_out[0, 8:16] += fold(grad_raw)


def chunk_spec(width, back=0, column_block=0):
    turn = (lambda c: back - 1 - c) if back else (lambda c: c)
    return pl.BlockSpec((1, CHUNK, width), lambda s, c: (s, turn(c), column_block))


def per_chunk(lines, width, back=0):
    turn = (lambda c: back - 1 - c) if back else (lambda c: c)
    return pl.BlockSpec((1, 1, lines, width), lambda s, c: (s, turn(c), 0, 0))


def per_sequence(lines, width):
    return pl.BlockSpec((1, lines, width), lambda s, c: (s, 0, 0))


def fixed(lines, width):
    return pl.BlockSpec((lines, width), lambda s, c: (0, 0))


def shaped(shape, dtype=F32):
    return jax.ShapeDtypeStruct(shape, dtype)


def call(kernel, name, chunks, ins, outs, operands, scratch=(), flops=0, after=()):
    in_specs = [spec for spec, _ in zip(ins, operands, strict=True)]
    moved = sum(v.size * v.dtype.itemsize for v in operands)
    moved += sum(v.size * v.dtype.itemsize for _, v in outs)
    count, skipped = len(in_specs), len(after)
    in_specs = in_specs + [pl.BlockSpec(memory_space=pl.ANY)] * skipped
    operands = tuple(operands) + tuple(after)
    return pl.pallas_call(
        lambda *refs: kernel(*refs[:count], *refs[count + skipped :]),
        name=name,
        grid=(2, chunks),
        in_specs=in_specs,
        out_specs=[spec for spec, _ in outs],
        out_shape=[shape for _, shape in outs],
        scratch_shapes=list(scratch),
        cost_estimate=pl.CostEstimate(flops=flops, bytes_accessed=moved, transcendentals=0),
        compiler_params=pltpu.CompilerParams(
            dimension_semantics=("arbitrary", "arbitrary"), vmem_limit_bytes=40 * 1024 * 1024
        ),
    )(*operands)


STATE_SCRATCH = (pltpu.VMEM((STATE, INNER_Q), F32), pltpu.VMEM((8, INNER_Q), F32))


def scan_states(x, bc, raw, seg, par, spread, after=()):
    span = x.shape[1]
    n = span // CHUNK
    return call(
        state_kernel, "chunk_states", n,
        [chunk_spec(INNER_Q), chunk_spec(2 * STATE), chunk_spec(128, 0, TILE), per_chunk(8, 128), fixed(8, 128),
         fixed(128, INNER_Q)],
        [(per_chunk(STATE, INNER_Q), shaped((2, n, STATE, INNER_Q))), (per_chunk(8, INNER_Q), shaped((2, n, 8, INNER_Q))),
         (per_sequence(STATE, INNER_Q), shaped((2, STATE, INNER_Q))), (per_sequence(8, INNER_Q), shaped((2, 8, INNER_Q))),
         (per_sequence(16, INNER_Q), shaped((2, 16, INNER_Q), BF16))],
        (x, bc, raw, seg, par, spread), STATE_SCRATCH, 2 * 2 * span * STATE * INNER_Q, after=after,
    )


def scan_inside(x, bc, raw, seg, par, spread, after=()):
    span = x.shape[1]
    n = span // CHUNK
    return call(
        inside_kernel, "inside_chunks", n,
        [chunk_spec(INNER_Q), chunk_spec(2 * STATE), chunk_spec(128, 0, TILE), per_chunk(8, 128), fixed(8, 128),
         fixed(128, INNER_Q)],
        [(chunk_spec(INNER_Q), shaped(x.shape))],
        (x, bc, raw, seg, par, spread), (), 8 * 2 * span * CHUNK * INNER_Q, after=after,
    )[0]


def scan_outer(y, x, bc, raw, seg, par, spread, before, reach, start, gate, rows, after=()):
    span = x.shape[1]
    n = span // CHUNK
    return call(
        outer_kernel, "scan_and_gate", n,
        [chunk_spec(INNER_Q), chunk_spec(INNER_Q), chunk_spec(2 * STATE), chunk_spec(128, 0, TILE), per_chunk(8, 128), fixed(8, 128),
         fixed(128, INNER_Q), per_chunk(STATE, INNER_Q), per_chunk(8, INNER_Q), per_sequence(STATE, INNER_Q),
         chunk_spec(INNER_Q), fixed(8, INNER_Q)],
        [(chunk_spec(INNER_Q), shaped(x.shape)), (chunk_spec(INNER_Q), shaped(x.shape)),
         (per_chunk(1, 128), shaped((2, n, 1, 128)))],
        (y, x, bc, raw, seg, par, spread, before, reach, start, gate, rows), (), 8 * span * STATE * INNER_Q, after=after,
    )


def gate_along(grad, gated, rows, scale, after=()):
    span = gated.shape[1]
    n = span // CHUNK
    return call(
        along_kernel, "gate_along", n,
        [chunk_spec(INNER_Q), chunk_spec(INNER_Q), fixed(8, INNER_Q), per_chunk(1, 128)],
        [(per_chunk(1, 128), shaped((2, n, 1, 128))), (per_sequence(8, INNER_Q), shaped((2, 8, INNER_Q)))],
        (grad, gated, rows, scale), (), 10 * span * INNER_Q, after=after,
    )


def gate_back(grad, gated, y, x, gate, bc, raw, seg, par, spread, rows, scale, along, after=()):
    span = x.shape[1]
    n = span // CHUNK
    return call(
        gate_back_kernel, "gate_back_and_states", n,
        [chunk_spec(INNER_Q, n)] * 5 + [chunk_spec(2 * STATE, n), chunk_spec(128, n, TILE), per_chunk(8, 128, n), fixed(8, 128),
         fixed(128, INNER_Q), fixed(8, INNER_Q), per_chunk(1, 128, n), per_chunk(1, 128, n)],
        [(chunk_spec(INNER_Q, n), shaped(x.shape, BF16)), (chunk_spec(INNER_Q, n), shaped(x.shape, BF16)),
         (per_chunk(STATE, INNER_Q, n), shaped((2, n, STATE, INNER_Q))), (per_chunk(8, INNER_Q, n), shaped((2, n, 8, INNER_Q))),
         (per_sequence(STATE, INNER_Q), shaped((2, STATE, INNER_Q)))],
        (grad, gated, y, x, gate, bc, raw, seg, par, spread, rows, scale, along), STATE_SCRATCH,
        8 * span * STATE * INNER_Q, after=after,
    )


def scan_inside_back(x, bc, raw, seg, par, spread, grad, after=()):
    span = x.shape[1]
    n = span // CHUNK
    return call(
        inside_back_kernel, "inside_chunks_back", n,
        [chunk_spec(INNER_Q), chunk_spec(2 * STATE), chunk_spec(128, 0, TILE), per_chunk(8, 128), fixed(8, 128),
         fixed(128, INNER_Q), chunk_spec(INNER_Q)],
        [(chunk_spec(INNER_Q), shaped(x.shape)), (chunk_spec(STATE), shaped((2, span, STATE))),
         (chunk_spec(STATE), shaped((2, span, STATE)))],
        (x, bc, raw, seg, par, spread, grad), (), 24 * 2 * span * CHUNK * INNER_Q, after=after,
    )


def scan_outer_back(
    fed, b, c, x, bc, raw, seg, par, spread, before, reach, start, later, beyond, grad_end, end, total, grad, y, rows, after=()
):
    span = x.shape[1]
    n = span // CHUNK
    return call(
        outer_back_kernel, "scan_back", n,
        [chunk_spec(INNER_Q, n), chunk_spec(STATE, n), chunk_spec(STATE, n), chunk_spec(INNER_Q, n), chunk_spec(2 * STATE, n),
         chunk_spec(128, n, TILE), per_chunk(8, 128, n), fixed(8, 128), fixed(128, INNER_Q), per_chunk(STATE, INNER_Q, n),
         per_chunk(8, INNER_Q, n), per_sequence(STATE, INNER_Q), per_chunk(STATE, INNER_Q, n), per_chunk(8, INNER_Q, n),
         per_sequence(STATE, INNER_Q), per_sequence(STATE, INNER_Q), per_sequence(8, INNER_Q), chunk_spec(INNER_Q, n),
         chunk_spec(INNER_Q, n), fixed(8, INNER_Q)],
        [(chunk_spec(INNER_Q, n), shaped(x.shape)), (chunk_spec(2 * STATE, n), shaped((2, span, 2 * STATE))),
         (chunk_spec(128, n), shaped((2, span, 128))), (per_sequence(16, 128), shaped((2, 16, 128))),
         (per_sequence(8, INNER_Q), shaped((2, 8, INNER_Q)))],
        (fed, b, c, x, bc, raw, seg, par, spread, before, reach, start, later, beyond, grad_end, end, total, grad, y, rows),
        (pltpu.VMEM((8, 128), F32),), 24 * span * STATE * INNER_Q, after=after,
    )


def seg_table(seg_now, seg_before):
    span = seg_now.shape[1]
    rows = seg_now.reshape(2, span // CHUNK, 1, CHUNK)
    last = rows[..., -1:]
    before = jnp.concatenate((seg_before.reshape(2, 1, 1, 1), last[:, :-1]), axis=1)
    spread = lambda v: jnp.broadcast_to(v, rows.shape)
    return jnp.concatenate((rows, spread(before), spread(last)) + (rows,) * 5, axis=2)


def conv_terms(wide_ref, halo_ref, taps_ref, mask_ref, tail):
    own = wide_ref[0].astype(BF16).astype(F32)
    longer = jnp.concatenate((tail, own), axis=0)
    rows = [own]
    total = taps_ref[CONV : CONV + 1] + taps_ref[CONV - 1 : CONV] * own
    for back in range(1, CONV):
        same = jnp.concatenate([column(mask_ref[0, 0, back : back + 1])] * (own.shape[1] // 128), axis=1)
        earlier = longer[8 - back : 8 - back + CHUNK] * same
        rows.append(earlier)
        total = total + taps_ref[CONV - 1 - back : CONV - back] * earlier
    return own, rows, total


def conv_kernel(wide, halo, taps, mask, out, tail):
    @pl.when(pl.program_id(1) == 0)
    def _():
        tail[...] = halo[0].astype(F32)

    own, _, total = conv_terms(wide, halo, taps, mask, tail[...])
    tail[...] = own[CHUNK - 8 :]
    out[0] = (total * sigmoid(total)).astype(BF16)


def conv_back_kernel(wide, before, halo, taps, mask, grad, returned, out, sums_out, ahead):
    chunk = pl.num_programs(1) - 1 - pl.program_id(1)

    @pl.when(pl.program_id(1) == 0)
    def _():
        sums_out[...] = jnp.zeros_like(sums_out)
        ahead[...] = jnp.zeros_like(ahead)

    tail = jnp.where(chunk == 0, halo[0].astype(F32), before[0].astype(BF16).astype(F32))
    _, rows, total = conv_terms(wide, halo, taps, mask, tail)
    sig = sigmoid(total)
    pull = grad[0] * (sig * (1.0 + total * (1.0 - sig)))
    result = taps[CONV - 1 : CONV] * pull
    fold = lambda v: jnp.sum(v.reshape(CHUNK // 8, 8, v.shape[1]), axis=0)
    for back in range(1, CONV):
        same = jnp.concatenate([column(mask[0, 0, back : back + 1])] * (pull.shape[1] // 128), axis=1)
        masked = pull * same
        longer = jnp.concatenate((masked, ahead[8 * back - 8 : 8 * back]), axis=0)
        result = result + taps[CONV - 1 - back : CONV - back] * longer[back : back + CHUNK]
        ahead[8 * back - 8 : 8 * back] = masked[:8]
    for back in range(CONV):
        place = CONV - 1 - back
        sums_out[0, 8 * place : 8 * place + 8] += fold(pull * rows[back])
    sums_out[0, 8 * CONV : 8 * CONV + 8] += fold(pull)
    late = (pl.program_id(1) == 0).astype(F32) * returned[0].astype(F32)
    late = jnp.concatenate((jnp.zeros((CHUNK - 8, late.shape[1]), F32), late), axis=0)
    out[0] = (result + late).astype(BF16)


def conv_forward(wide, halo, taps, mask, width, at, after=()):
    n = wide.shape[1] // CHUNK
    lines = lambda rows: pl.BlockSpec((1, rows, width), lambda s, c: (s, 0, at))
    return call(
        conv_kernel, "conv", n,
        [chunk_spec(width, 0, at), lines(8), pl.BlockSpec((8, width), lambda s, c: (0, at)), per_chunk(8, 128)],
        [(chunk_spec(width), shaped(wide.shape[:2] + (width,), BF16))],
        (wide, halo, taps, mask), (pltpu.VMEM((8, width), F32),), 30 * wide.shape[1] * width, after=after,
    )[0]


def conv_backward(wide, halo, taps, mask, grad, returned, width, at, after=()):
    n = wide.shape[1] // CHUNK
    lines = lambda rows: pl.BlockSpec((1, rows, width), lambda s, c: (s, 0, at))
    steps = CHUNK // 8
    early = pl.BlockSpec(
        (1, 8, width), lambda s, c: (s, jnp.maximum((n - 1 - c) * steps - 1, 0), at)
    )
    return call(
        conv_back_kernel, "conv_back", n,
        [chunk_spec(width, n, at), early, lines(8), pl.BlockSpec((8, width), lambda s, c: (0, at)),
         per_chunk(8, 128, n), chunk_spec(width, n), lines(8)],
        [(chunk_spec(width, n), shaped(wide.shape[:2] + (width,), BF16)), (per_sequence(8 * CONV + 8, width), shaped((2, 8 * CONV + 8, width)))],
        (wide, wide, halo, taps, mask, grad, returned), (pltpu.VMEM((8 * CONV, width), F32),), 60 * wide.shape[1] * width, after=after,
    )


def mask_table(seg_ext, edge_rows):
    span = seg_ext.shape[1] - edge_rows
    here = seg_ext[:, edge_rows:]
    rows = [here == seg_ext[:, edge_rows - back : edge_rows - back + span] for back in range(CONV)]
    table = jnp.stack(rows + rows, axis=1).astype(F32)
    return jnp.moveaxis(table.reshape(2, 2 * CONV, span // CHUNK, CHUNK), 2, 1)


def tile_picks(owner, rows):
    down, across = grids((2 * STATE, 128))
    bc = (down - BC_Q * owner == across) & (across < BC_Q)
    down, across = grids((HEADS, 128))
    head = across - LANE
    dt = (down - HEADS_Q * owner == head) & (head >= 0) & (head < HEADS_Q)
    return bc.astype(F32), dt.astype(F32)


def cut_weights_kernel(q_ref, weight, *outs):
    for layer in range(weight.shape[0]):
        for k in range(TEAM):
            owner = q_ref[0] ^ k
            start = pl.multiple_of(owner * INNER_Q, 128)
            part = outs[layer * TEAM + k]
            part[:, :INNER_Q] = weight[layer, :, pl.ds(start, INNER_Q)]
            part[:, INNER_Q : 2 * INNER_Q] = weight[layer, :, pl.ds(INNER + start, INNER_Q)]
            bc, dt = tile_picks(owner, None)
            tile = mm(weight[layer, :, 2 * INNER : 2 * INNER + 2 * STATE], bc.astype(BF16))
            tile = tile + mm(weight[layer, :, INNER + CONVDIM :], dt.astype(BF16))
            part[:, 2 * INNER_Q :] = tile.astype(BF16)


def whole_spec(shape):
    return pl.BlockSpec(shape, lambda *_: (0,) * len(shape))


def whole_call(kernel, name, index, operands, outs, after=()):
    count, skipped = 1 + len(operands), len(after)
    return pl.pallas_call(
        lambda *refs: kernel(*refs[:count], *refs[count + skipped :]),
        name=name,
        grid_spec=pltpu.PrefetchScalarGridSpec(
            num_scalar_prefetch=1,
            grid=(1,),
            in_specs=[whole_spec(v.shape) for v in operands]
            + [pl.BlockSpec(memory_space=pl.ANY)] * skipped,
            out_specs=[whole_spec(s.shape) for s in outs],
        ),
        out_shape=list(outs),
        compiler_params=pltpu.CompilerParams(vmem_limit_bytes=40 * 1024 * 1024),
    )(index, *operands, *after)


def tie(value, *after):
    anywhere = pl.BlockSpec(memory_space=pl.ANY)
    return pl.pallas_call(
        lambda *refs: None,
        name="tie",
        in_specs=[anywhere] * (1 + len(after)),
        out_specs=anywhere,
        out_shape=shaped(value.shape, value.dtype),
        input_output_aliases={0: 0},
    )(value, *after)


def norm_kernel(x_ref, stream, gain, out):
    values = stream[...].astype(F32)
    mean = jnp.mean(values * values, axis=-1, keepdims=True)
    normed = (values * lax.rsqrt(mean + EPS) * gain[...]).astype(BF16)
    width = normed.shape[1] // 2
    x = x_ref[0]
    out[:, pl.ds(pl.multiple_of(x * width, 128), width)] = normed[:, :width]
    out[:, pl.ds(pl.multiple_of((1 - x) * width, 128), width)] = normed[:, width:]


def norm_rows(x, stream, gain, after=()):
    return whole_call(norm_kernel, "norm", x, (stream, gain), [shaped(stream.shape, BF16)], after)[0]


def scale_kernel(gated, scale, rows, out):
    lines = jnp.concatenate([column(scale[0, 0])] * (INNER_Q // 128), axis=1)
    out[0] = (gated[0] * lines * rows[1:2]).astype(BF16)


def scale_rows(gated, scale, rows, after=()):
    n = gated.shape[1] // CHUNK
    return call(
        scale_kernel, "scale_rows", n,
        [chunk_spec(INNER_Q), per_chunk(1, 128), fixed(8, INNER_Q)],
        [(chunk_spec(INNER_Q), shaped(gated.shape, BF16))],
        (gated, scale, rows), (), 4 * gated.size, after=after,
    )[0]


def cut_weights(q, weight):
    layers, rows = weight.shape[:2]
    outs = [shaped((rows, INNER_Q + WIDE), BF16)] * (TEAM * layers)
    outs = whole_call(cut_weights_kernel, "cut_weights", q, (weight,), outs)
    return [outs[TEAM * layer : TEAM * layer + TEAM] for layer in range(layers)]


def place_of(owner):
    return (owner % 2) * 2 + owner // 2


def wide_piece_kernel(q_ref, *refs):
    out = refs[-1]
    for k in range(TEAM):
        out[place_of(q_ref[0] ^ k)] = refs[k][:, INNER_Q:]


def gate_piece_kernel(q_ref, *refs):
    out = refs[-1]
    for k in range(TEAM):
        out[place_of(q_ref[0] ^ k)] = refs[k][:, :INNER_Q]


def wide_piece(q, parts, after=()):
    shape = (TEAM, parts[0].shape[0], WIDE)
    return whole_call(wide_piece_kernel, "wide_piece", q, parts, [shaped(shape, BF16)], after)[0]


def gate_piece(q, parts, after=()):
    shape = (TEAM, parts[0].shape[0], INNER_Q)
    return whole_call(gate_piece_kernel, "gate_piece", q, parts, [shaped(shape, BF16)], after)[0]


def whole_wide_kernel(place, *refs):
    out = refs[-1]
    size = out.shape[2]
    for side in range(2):
        for hop in range(size):
            source = lax.rem(place[0] - hop + size, size)
            for block in range(TEAM):
                out[side, block // 2, source, block % 2] = refs[side * size + hop][block]


def whole_out_kernel(place, *refs):
    out = refs[-1]
    size = out.shape[0]
    for side in range(2):
        x = place[1] if side == 0 else 1 - place[1]
        for hop in range(size):
            source = lax.rem(place[0] - hop + size, size)
            out[source, x] = refs[side * size + hop][...]


def whole_columns(place, pieces, after=()):
    size = len(pieces) // 2
    rows, width = pieces[0].shape[1:]
    outs = [shaped((2, 2, size, 2, rows, width), BF16)]
    whole = whole_call(whole_wide_kernel, "whole_columns", place, pieces, outs, after)[0]
    return whole.reshape(-1, width)


def whole_rows(place, pieces):
    size = len(pieces) // 2
    outs = [shaped((size, 2) + pieces[0].shape, BF16)]
    whole = whole_call(whole_out_kernel, "whole_rows", place, pieces, outs)[0]
    return whole.reshape(-1, pieces[0].shape[-1])


def cut_out_kernel(place, grad, far, own):
    size = far.shape[0]
    for hop in range(size):
        target = lax.rem(place[0] + hop, size)
        far[hop] = grad[target, 1 - place[1]].astype(BF16)
        own[hop] = grad[target, place[1]]


def cut_gate_kernel(place, grad, far, own):
    size = far.shape[0]
    for hop in range(size):
        target = lax.rem(place[0] + hop, size)
        for block in range(TEAM):
            far[hop, block] = grad[1, block // 2, target, block % 2].astype(BF16)
            own[hop, block] = grad[0, block // 2, target, block % 2]


def cut_wide_kernel(place, grad, *outs):
    size = len(outs) // 2
    for hop in range(size):
        target = lax.rem(place[0] + hop, size)
        for block in range(TEAM):
            outs[hop][block] = grad[1, block // 2, target, block % 2].astype(BF16)
            outs[size + hop][block] = grad[0, block // 2, target, block % 2]


def cut_out(place, grad, size, rows):
    shape = (size, rows, grad.shape[-1])
    outs = [shaped(shape, BF16), shaped(shape)]
    return whole_call(cut_out_kernel, "cut_out", place, (grad.reshape(size, 2, rows, -1),), outs)


def cut_gate(place, grad, size, rows):
    shape = (size, TEAM, rows, INNER_Q)
    operands = (grad.reshape(2, 2, size, 2, rows, INNER_Q),)
    return whole_call(cut_gate_kernel, "cut_gate", place, operands, [shaped(shape, BF16), shaped(shape)])


def cut_wide(place, grad, size, rows):
    shape = (TEAM, rows, WIDE)
    outs = [shaped(shape, BF16)] * size + [shaped(shape)] * size
    operands = (grad.reshape(2, 2, size, 2, rows, WIDE),)
    outs = whole_call(cut_wide_kernel, "cut_wide", place, operands, outs)
    return outs[:size], outs[size:]


def grad_parts_kernel(q_ref, gate, wide, *refs):
    count = len(refs) - TEAM
    for k in range(TEAM):
        block = place_of(q_ref[0] ^ k)
        total = wide[block]
        for come in refs[:count]:
            total = total + come[block].astype(F32)
        refs[count + k][:, :INNER_Q] = gate[block].astype(BF16)
        refs[count + k][:, INNER_Q:] = total.astype(BF16)


def grad_parts(q, gate, wide, come):
    outs = [shaped((wide.shape[1], INNER_Q + WIDE), BF16)] * TEAM
    return whole_call(grad_parts_kernel, "grad_parts", q, (gate, wide, *come), outs)


def cut_params_kernel(q_ref, conv_weight, conv_bias, dt_bias, a_log, skip, out_gain, spread, taps, par, rows):
    owner = q_ref[0]
    start = pl.multiple_of(owner * INNER_Q, 128)
    bc, dt = tile_picks(owner, None)
    bc, dt = bc.astype(BF16), dt.astype(BF16)
    mine = pl.ds(start, INNER_Q)
    for layer in range(conv_weight.shape[0]):
        one = slice(layer, layer + 1)
        taps[layer, :CONV, :INNER_Q] = conv_weight[layer, :, mine]
        taps[layer, :CONV, INNER_Q:] = exact_mm(conv_weight[layer, :, INNER:], bc)
        taps[layer, CONV : CONV + 1, :INNER_Q] = conv_bias[one, mine]
        taps[layer, CONV : CONV + 1, INNER_Q:] = exact_mm(conv_bias[one, INNER:], bc)
        taps[layer, CONV + 1 :] = jnp.zeros((7 - CONV, WIDE), F32)
        par[layer, 0:1] = exact_mm(dt_bias[one], dt)
        par[layer, 1:2] = exact_mm(jnp.exp(a_log[one]), dt)
        par[layer, 2:] = jnp.zeros((6, 128), F32)
        rows[layer, 0:1] = exact_mm(exact_mm(skip[one], dt), spread[...])
        rows[layer, 1:2] = out_gain[one, mine]
        rows[layer, 2:] = jnp.zeros((6, INNER_Q), F32)


def cut_params(q, params, after):
    layers = params[0].shape[0]
    shapes = [(layers, 8, WIDE), (layers, 8, 128), (layers, 8, INNER_Q)]
    return whole_call(cut_params_kernel, "cut_params", q, params, [shaped(s) for s in shapes], after)


def join_kernel(q_ref, *refs):
    out = refs[-1]
    for layer in range(out.shape[0]):
        shared = 0.0
        for k in range(TEAM):
            owner = q_ref[0] ^ k
            start = pl.multiple_of(owner * INNER_Q, 128)
            part = refs[layer * TEAM + k]
            out[layer, :, pl.ds(start, INNER_Q)] = part[:, :INNER_Q].astype(F32)
            out[layer, :, pl.ds(INNER + start, INNER_Q)] = part[:, INNER_Q : 2 * INNER_Q].astype(F32)
            bc, dt = tile_picks(owner, None)
            both = jnp.concatenate((bc, dt), axis=0).astype(BF16)
            shared = shared + mm(part[:, 2 * INNER_Q :], both, (1, 1))
        out[layer, :, 2 * INNER :] = shared


def join_weights(q, parts):
    flat = [v for layer in parts for v in layer]
    shape = (len(parts), flat[0].shape[0], 2 * INNER + 2 * STATE + HEADS)
    return whole_call(join_kernel, "join_weights", q, flat, [shaped(shape)])[0]


SMALL = (16, WIDE)


def pack_small_kernel(conv_x, conv_tile, heads, skip, gain, norm, spread, out):
    fold = lambda v, rows: jnp.sum(v[:, rows], axis=(0, 1), keepdims=True)[0]
    for line in range(CONV + 1):
        rows = slice(8 * line, 8 * line + 8)
        out[line : line + 1, :INNER_Q] = fold(conv_x[...], rows)
        out[line : line + 1, INNER_Q:] = fold(conv_tile[...], rows)
    line = CONV + 1
    out[line:] = jnp.zeros((SMALL[0] - line, WIDE), F32)
    every = slice(0, 8)
    out[line + 1 : line + 2, :INNER_Q] = fold(gain[...], every)
    out[line + 2 : line + 3, :128] = fold(heads[...], slice(8, 16))
    out[line + 3 : line + 4, :128] = fold(heads[...], every)
    by_head = exact_mm(skip[0] + skip[1], spread[...], (1, 1))
    out[line + 4 : line + 5, :128] = jnp.sum(by_head, axis=0, keepdims=True)
    width = norm.shape[1] // 2
    out[line + 5 : line + 6, :width] = norm[:, :width]
    out[line + 6 : line + 7, :width] = norm[:, width:]


def pack_small(*parts):
    return pl.pallas_call(pack_small_kernel, name="pack_small", out_shape=shaped(SMALL))(*parts)


def lanes_of(values):
    return lax.broadcasted_iota(jnp.int32, values.shape, 1)


def open_small_kernel(q_ref, *refs):
    norm, conv_weight, conv_bias, dt_bias, a_log, skip, gain = refs[-7:]
    layers = norm.shape[0]
    line = CONV + 1
    for layer in range(layers):
        one = slice(layer, layer + 1)
        packs = [ref[layer] for ref in refs[:TEAM]]
        shared, heads = [], 0.0
        for k in range(TEAM):
            owner = q_ref[0] ^ k
            start = pl.multiple_of(owner * INNER_Q, 128)
            mine = pl.ds(start, INNER_Q)
            pack = packs[k]
            conv_weight[layer, :, mine] = pack[:CONV, :INNER_Q]
            conv_bias[one, mine] = pack[CONV:line, :INNER_Q]
            tile = pack[:8, INNER_Q:]
            tile = jnp.where(lanes_of(tile) < BC_Q, tile, 0.0)
            tile = jnp.where(owner % 2 == 0, tile, pltpu.roll(tile, BC_Q, 1))
            shared.append([jnp.where(owner // 2 == side, tile, 0.0) for side in range(2)])
            rows = pack[line + 2 : line + 5, :128]
            in_head = (lanes_of(rows) >= LANE) & (lanes_of(rows) < LANE + HEADS_Q)
            rows = jnp.where(in_head, rows, 0.0)
            placed = 0.0
            for which in range(TEAM):
                turned = pltpu.roll(rows, (HEADS_Q * which - LANE) % 128, 1)
                placed = placed + jnp.where(owner == which, turned, 0.0)
            heads = heads + placed[:, :HEADS]
            gain[one, mine] = pack[line + 1 : line + 2, :INNER_Q]
        shared = jnp.concatenate([sum([s[side] for s in shared]) for side in range(2)], axis=1)
        conv_weight[layer, :, INNER:] = shared[:CONV]
        conv_bias[one, INNER:] = shared[CONV:line]
        dt_bias[one], a_log[one], skip[one] = heads[0:1], heads[1:2], heads[2:3]
        width = norm.shape[1] // 2
        halves_of = lambda n: packs[n][line + 5 : line + 7, :width]
        total = (halves_of(0) + halves_of(1)) + (halves_of(2) + halves_of(3))
        norm[one, :width] = total[0:1]
        norm[one, width:] = total[1:2]


def open_small(q, packs, features):
    layers = packs[0].shape[0]
    flat = list(packs)
    shapes = [
        (layers, features), (layers, CONV, CONVDIM), (layers, CONVDIM), (layers, HEADS), (layers, HEADS),
        (layers, HEADS), (layers, INNER),
    ]
    return pl.pallas_call(
        open_small_kernel,
        name="open_small",
        grid_spec=pltpu.PrefetchScalarGridSpec(
            num_scalar_prefetch=1,
            grid=(1,),
            in_specs=[whole_spec(v.shape) for v in flat],
            out_specs=[whole_spec(s) for s in shapes],
        ),
        out_shape=[shaped(s) for s in shapes],
    )(q, *flat)


def spread_matrix():
    head = jnp.arange(128)[:, None] - LANE
    return (jnp.arange(INNER_Q)[None, :] // HEADDIM == head).astype(BF16)


def gap_decays(spans):
    rows = []
    for start in range(len(spans)):
        row = []
        running = jnp.ones_like(spans[0])
        for stop, span in enumerate(spans):
            if stop <= start:
                row.append(jnp.zeros_like(running))
                continue
            row.append(running)
            running = running * span
        rows.append(jnp.stack(row))
    return jnp.stack(rows)


def mix_states(states, bits=None, weights=None):
    size = lax.axis_size("z")
    z = lax.axis_index("z")
    width = states.shape[1] // size
    decay = lambda rows: jnp.sum(rows[:, :3].astype(F32), axis=1)
    if size > NEAR:
        if weights is None:
            weights = gap_decays([decay(v) for v in lax.all_gather(bits, "z")])
        cuts = jnp.moveaxis(states.reshape(2, size, width, -1), 1, 0).astype(BF16)
        parts = lax.all_to_all(cuts, "z", 0, 0, tiled=True).astype(F32)
        sums = jnp.sum(weights[:, :, :, None] * parts[:, None], axis=0)
        back = lax.all_to_all(sums.astype(BF16), "z", 0, 0, tiled=True).astype(F32)
        return jnp.moveaxis(back, 0, 1).reshape(states.shape), weights
    ring = lambda k: lax.rem(z + k + size, size)

    def cut(k):
        part = lax.dynamic_slice_in_dim(states, k * width, width, 1).astype(BF16)
        return part if weights is not None else jnp.concatenate((part, bits), axis=1)

    parts = [cut(z)] + [shift(cut(ring(hop)), "z", hop) for hop in range(1, size)]
    if weights is None:
        everyone = jnp.stack([decay(p[:, width:]) for p in parts])
        spans = [
            lax.dynamic_index_in_dim(everyone, lax.rem(z - k + size, size), 0, False)
            for k in range(size)
        ]
        weights = gap_decays(spans)
        parts = [p[:, :width] for p in parts]
    results = []
    for away in range(size):
        to = lax.dynamic_index_in_dim(weights, ring(away), 1, False)
        total = 0.0
        for hop in range(size):
            weight = lax.dynamic_index_in_dim(to, ring(-hop), 0, False)
            total = total + weight[:, None] * parts[hop].astype(F32)
        results.append(total)
    back = [results[0]] + [
        shift(results[hop].astype(BF16), "z", hop).astype(F32) for hop in range(1, size)
    ]
    whole = jnp.zeros(states.shape, F32)
    for hop in range(size):
        whole = lax.dynamic_update_slice_in_dim(whole, back[hop], ring(-hop) * width, 1)
    return whole, weights


def local(
    tokens,
    segments,
    out_grad,
    norm_gain,
    in_weight,
    conv_weight,
    conv_bias,
    dt_bias,
    a_log,
    skip,
    out_gain,
    out_weight,
):
    _, length, features = tokens.shape
    edge = CONV - 1
    layer_count, in_rows = in_weight.shape[:2]
    out_rows = out_weight.shape[1]
    layers = range(layer_count)
    q = member()
    owner = q.reshape(1)
    span = 2 * length
    row_count = 2 * span

    near = lax.axis_size("z") <= NEAR
    x_place = lax.axis_index("x").reshape(1)
    cuts = cut_weights(owner, in_weight)
    size = lax.axis_size("z")
    place = jnp.stack((lax.axis_index("z"), lax.axis_index("x")))
    exchanged = [around_team(parts) for parts in cuts]
    moved = [lax.ppermute(out_weight[k], ("x", "y"), TURN) for k in layers]

    def fetch_wide(layer_id, after):
        piece = wide_piece(owner, exchanged[layer_id], after)
        return fetch(piece) if near else ([piece], [piece])

    def fetch_gate(layer_id, after):
        piece = gate_piece(owner, exchanged[layer_id], after)
        return fetch(piece) if near else ([piece], [piece])

    def fetch_out(layer_id, after):
        piece = tie(moved[layer_id], *after)
        return fetch(piece) if near else ([piece], [piece])

    def columns(pieces, after=()):
        return whole_columns(place, pieces, after) if near else far_columns(*pieces)

    wide_line, wide_all = fetch_wide(0, [])
    later_parts = [v for e in exchanged[1:] for v in e[1:]] + moved[1:]

    seg_now = team_gather(segments.astype(F32).reshape(length))
    prev_seg = step_line(seg_now[:, span - edge :], "z", 1)
    seg_ext = jnp.concatenate((prev_seg, seg_now), axis=1)
    seg = seg_table(seg_now, seg_ext[:, edge - 1])
    mask = mask_table(seg_ext, edge)
    spread = spread_matrix()
    all_taps, all_par, all_rows = cut_params(
        owner, (conv_weight, conv_bias, dt_bias, a_log, skip, out_gain, spread), wide_line[:1]
    )

    stream = tokens.astype(F32).reshape(length, features)
    last_grad = team_gather(out_grad.reshape(length, features))
    saved, full = [], []
    for layer_id in layers:
        taps, par, rows = all_taps[layer_id], all_par[layer_id], all_rows[layer_id]
        first, final = layer_id == 0, layer_id == layer_count - 1
        normed = norm_rows(
            x_place,
            tokens.reshape(length, features) if first else stream,
            norm_gain[layer_id : layer_id + 1],
            cuts[0][0] if first else wide_all[1:] + gate_line[1:],
        )
        normed = team_gather(normed).reshape(row_count, features)
        if first:
            gate_line, gate_all = fetch_gate(0, wide_line[1:] + [normed])
        full_wide = columns(wide_all, [last_grad] if first else [])
        dot = partial(jnp.dot, preferred_element_type=F32)
        wide = dot(normed, full_wide).reshape(2, span, WIDE)
        out_line, out_all = fetch_out(layer_id, gate_line[1:] + [wide])
        full_gate = columns(gate_all)
        gate_raw = dot(normed, full_gate).reshape(2, span, INNER_Q)
        full_out = whole_rows(place, out_all) if near else far_rows(*out_all)
        full.append((full_wide, full_gate, full_out))
        halo = step_line(wide[:, span - 8 :].astype(BF16), "z", 1).astype(F32)
        bc_own = conv_forward(
            wide, halo, taps, mask, 128, TILE, later_parts + gate_line[1:] if first else gate_all[len(gate_line) :]
        )[..., :BC_Q]
        bc_same = y_swap(bc_own)
        bc = jnp.concatenate(
            in_order((bc_own, core_swap(bc_own)[::-1], bc_same, core_swap(bc_same)[::-1])), axis=-1
        )
        heads_x = conv_forward(wide, halo, taps, mask, INNER_Q, 0)
        scan_in = (heads_x, bc, wide, seg, par, spread)
        before, reach, end, total_reach, bits = scan_states(
            *scan_in, after=out_line[1:] + gate_all[len(gate_line) :]
        )
        start, weights = mix_states(end, bits)
        inside = scan_inside(*scan_in)
        scan_y, gated, square = scan_outer(
            inside, *scan_in, before, reach, start, gate_raw, rows,
            out_all[len(out_line) :],
        )
        if not final:
            wide_line, wide_all = fetch_wide(layer_id + 1, out_line[1:] + [start])
        scale = lax.rsqrt(team_sum(square) / INNER + EPS)
        normed_y = scale_rows(gated, scale, rows, [] if final else wide_line[1:2])
        normed_y = normed_y.reshape(row_count, INNER_Q)
        branch = dot(normed_y, full_out)
        if not final:
            gate_line, gate_all = fetch_gate(layer_id + 1, wide_line[1:] + [normed_y])
        saved.append(
            (
                stream,
                normed,
                gate_raw,
                halo,
                scan_in,
                (before, reach, start),
                (end, total_reach),
                weights,
                scan_y,
                gated,
                scale,
                normed_y,
                taps,
                rows,
            )
        )
        stream = stream + team_scatter(branch.reshape(2, span, features))
    grad_stream = out_grad.astype(F32).reshape(length, features)
    in_parts = [None] * layer_count
    out_shards = [None] * layer_count
    small = [None] * layer_count
    gate_z, pending = [], None
    for layer_id in reversed(layers):
        (
            stream_in,
            normed,
            gate_raw,
            halo,
            scan_in,
            states_before,
            states_end,
            weights,
            scan_y,
            gated,
            scale,
            normed_y,
            taps,
            rows,
        ) = saved[layer_id]
        heads_x, scan_rest = scan_in[0], scan_in[1:]
        wide = scan_in[2]
        full_wide, full_gate, full_out = full[layer_id]
        last = layer_id == 0
        grad_branch = team_gather(grad_stream.astype(BF16)) if last_grad is None else last_grad
        last_grad = None
        grad_branch = grad_branch.reshape(row_count, features)
        out_full_grad = jnp.einsum("ri,rd->id", normed_y, grad_branch, preferred_element_type=F32)
        back = partial(jnp.einsum, "rp,dp->rd", preferred_element_type=F32)
        grad_normed_y = back(grad_branch, full_out).reshape(2, span, INNER_Q)
        along, grad_gain = gate_along(grad_normed_y, gated, rows, scale)
        along = team_sum(along)
        grad_ssd, grad_gate, after, beyond, grad_start = gate_back(
            grad_normed_y, gated, scan_y, heads_x, gate_raw, *scan_rest, rows, scale, along,
            gate_z + [out_full_grad],
        )
        turn = partial(jnp.einsum, "rd,rp->dp", preferred_element_type=F32)
        grad_gate = grad_gate.reshape(row_count, INNER_Q)
        gate_grad = turn(normed, grad_gate)
        if near:
            out_far, out_own = cut_out(place, out_full_grad, size, out_rows)
            out_x = x_swap(out_far)
            gate_far, gate_own = cut_gate(place, gate_grad, size, in_rows)
            gate_x = x_swap(gate_far)
        grad_end, _ = mix_states(grad_start, None, weights.swapaxes(0, 1))
        if near:
            out_z, out_total = send_sums(out_own, tie(out_x, grad_end))
            out_total = total_of(out_total, out_z)
            if pending is not None:
                late_own, late_x, late_gate, late_layer = pending
                late_z, total = send_sums(late_own, [tie(late_x[0], grad_end)] + late_x[1:])
                parts = grad_parts(owner, late_gate, total, late_z)
                in_parts[late_layer] = around_team(parts)
            else:
                late_z = []
            gate_z, gate_total = send_sums(gate_own, gate_x)
            gate_total = total_of(gate_total, gate_z)
        else:
            gate_z, late_z, out_z = [], [], []
            out_total = far_out_scatter(out_full_grad, size, out_rows)
            gate_total = far_columns_scatter(gate_grad, size, in_rows)
        out_total = out_total.astype(BF16)
        out_shards[layer_id] = lax.ppermute(out_total, ("x", "y"), TURN).astype(F32)
        grad_inside = scan_inside_back(*scan_in, grad_ssd, after=[out_x, gate_far] if near else [])
        grad_x, grad_bc, grad_raw, head_sums, skip_sums = scan_outer_back(
            *grad_inside,
            *scan_in,
            *states_before,
            after,
            beyond,
            grad_end,
            *states_end,
            grad_ssd,
            scan_y,
            rows,
            [gate_x] if near and last else [],
        )
        blocks = [grad_bc[..., BC_Q * k : BC_Q * k + BC_Q].astype(BF16) for k in range(TEAM)]
        turned = lambda k: lax.select_n(q ^ k, *blocks)
        half = lambda k: turned(k).astype(F32) + core_swap(turned(k ^ 1)).astype(F32)[::-1]
        grad_bc_own = half(0) + y_swap(half(2).astype(BF16)).astype(F32)
        grad_tile = jnp.pad(grad_bc_own, ((0, 0), (0, 0), (0, 128 - BC_Q)))

        edge_in = jnp.concatenate(
            (halo[:, 8 - edge :], wide[:, :edge].astype(BF16).astype(F32)), axis=1
        )
        edge_conv = lambda v: conv_piece(seg_ext[:, : 2 * edge], v, taps[:CONV], taps[CONV])
        edge_grad = jnp.concatenate((grad_x[:, :edge], grad_tile[:, :edge]), axis=-1)
        edge_grad = jax.vjp(edge_conv, edge_in)[1](edge_grad)[0][:, :edge].astype(BF16)
        returned = step_line(edge_grad, "z", -1).astype(F32)
        returned = jnp.pad(returned, ((0, 0), (8 - edge, 0), (0, 0)))
        grad_conv_x, conv_sums = conv_backward(
            wide, halo, taps, mask, grad_x, returned, INNER_Q, 0,
            late_z + (gate_z if last else [gate_x] if near else []),
        )
        grad_conv_tile, tile_sums = conv_backward(
            wide, halo, taps, mask, grad_tile, returned, 128, TILE
        )
        grad_wide = jnp.concatenate(
            (grad_conv_x, grad_conv_tile[..., :BC_Q], grad_raw[..., BC_Q:].astype(BF16)), axis=-1
        ).reshape(row_count, WIDE)
        in_grad = turn(normed, grad_wide)
        if near:
            far, own = cut_wide(place, in_grad, size, in_rows)
            wide_x = [x_swap(v) for v in far]
            if last:
                wide_z, total = send_sums(own, wide_x)
                parts = grad_parts(owner, gate_total, total, wide_z)
                in_parts[layer_id] = around_team(parts)
            pending = own, wide_x, gate_total, layer_id
            grad_wide = tie(grad_wide, *far, *(out_z if last else []))
            grad_gate = tie(grad_gate, wide_x[1])
        else:
            total = far_columns_scatter(in_grad, size, in_rows)
            in_parts[layer_id] = around_team(grad_parts(owner, gate_total, total, []))
        full_wide, full_gate, _ = full[layer_id]
        grad_normed = back(grad_wide, full_wide) + back(grad_gate, full_gate)
        grad_normed = team_scatter(grad_normed.reshape(2, span, features))
        if near:
            grad_normed = tie(grad_normed, *wide_x, *(wide_z[:2] if last else out_z))
        grad_normed = x_first(grad_normed)
        _, pull_norm = jax.vjp(norm_piece, stream_in, norm_gain[layer_id])
        grad_inner, norm_grad = pull_norm(grad_normed)
        grad_stream = grad_stream + grad_inner
        small[layer_id] = pack_small(
            conv_sums, tile_sums, head_sums, skip_sums, grad_gain, norm_grad.reshape(1, features),
            spread,
        )
    mixed = stream.reshape(1, length, features).astype(BF16)
    pack = xor_sum(xor_sum(jnp.stack(small), "x"), "z")
    across = y_swap(pack)
    packs = (pack, core_swap(pack), across, core_swap(across))
    norm_sum, taps_sum, bias_sum, dt_sum, decay_sum, skip_sum, gain_sum = open_small(
        owner, packs, features
    )
    return (
        mixed,
        grad_stream.reshape(1, length, features),
        norm_sum,
        join_weights(owner, in_parts),
        taps_sum,
        bias_sum,
        dt_sum,
        decay_sum,
        skip_sum,
        gain_sum,
        jnp.stack(out_shards),
    )


def solution(mesh):
    rows, spans = mesh.devices.shape
    split = Mesh(mesh.devices.reshape(rows // 2, 2, spans // 2, 2), ("x", "core", "z", "y"))
    tokens = P(("x", "core"), ("z", "y"), None)
    weight = P(None, ("x", "core", "z", "y"), None)
    return jax.shard_map(
        local,
        mesh=split,
        in_specs=(
            tokens,
            P(("x", "core"), ("z", "y")),
            tokens,
            P(),
            weight,
            P(),
            P(),
            P(),
            P(),
            P(),
            P(),
            weight,
        ),
        out_specs=(tokens, tokens, P(), weight, P(), P(), P(), P(), P(), P(), weight),
        check_vma=False,
    )
```

```python
from functools import partial

import jax
import jax.numpy as jnp
from jax import lax
from jax.experimental import pallas as pl
from jax.experimental.pallas import tpu as pltpu
from jax.sharding import Mesh
from jax.sharding import PartitionSpec as P

HEADS = 48
HEADDIM = 64
STATE = 128
CONV = 4
INNER = 3072
CONVDIM = 3328

TEAM = 4
HEADS_Q = HEADS // TEAM
INNER_Q = INNER // TEAM
BC_Q = 2 * STATE // TEAM
CONV_Q = INNER_Q + BC_Q
WIDE = 896

EPS = 1e-05
VMEM_BYTES = 40 * 1024 * 1024
STEP_BYTES = 20 * 1024 * 1024
NEAR = 4
SWAP = [(0, 1), (1, 0)]
BF16 = jnp.bfloat16
F32 = jnp.float32


def shift(block, axis, distance):
    size = lax.axis_size(axis)
    return lax.ppermute(block, axis, [(i, (i + distance) % size) for i in range(size)])


def step_line(block, axis, distance):
    devices = range(lax.axis_size(axis))
    return lax.ppermute(block, axis, [(i, i + distance) for i in devices if i + distance in devices])


def core_swap(block):
    return lax.ppermute(block, "core", SWAP)


def y_swap(block):
    return lax.ppermute(block, "y", SWAP)


def diagonal_swap(block):
    return lax.ppermute(block, ("core", "y"), [(0, 3), (1, 2), (2, 1), (3, 0)])


def xor_sum(values, axis):
    size = lax.axis_size(axis)
    bit = 1
    while bit < size:
        values = tie(values + lax.ppermute(values, axis, [(i, i ^ bit) for i in range(size)]))
        bit *= 2
    return values


def member():
    return lax.axis_index("y") * 2 + lax.axis_index("core")


def in_order(parts):
    q = member()
    return [lax.select_n(q ^ j, *parts) for j in range(TEAM)]


def around_team(blocks):
    return blocks[0], core_swap(blocks[1]), y_swap(blocks[2]), diagonal_swap(blocks[3])


def by_y(own, other):
    first = lax.axis_index("y") == 0
    return jnp.where(first, jnp.concatenate((own, other), 1), jnp.concatenate((other, own), 1))


def team_gather(block):
    pair = jnp.stack((block, core_swap(block)))
    crossed = y_swap(block)
    other = jnp.stack((crossed, core_swap(crossed)))
    return by_y(pair, other)


def team_scatter(own, other):
    total = own + core_swap(other.astype(BF16)).astype(F32)
    half = total.shape[0] // 2
    y = lax.axis_index("y")
    mine = lax.dynamic_slice_in_dim(total, y * half, half, 0)
    theirs = lax.dynamic_slice_in_dim(total, (1 - y) * half, half, 0)
    return mine + y_swap(theirs.astype(BF16)).astype(F32)


def team_sum(values):
    across = core_swap(values) + diagonal_swap(values)
    return (values + y_swap(values)) + across[::-1]


def x_swap(block):
    return lax.ppermute(block, "x", SWAP)


def line_pieces(piece):
    return [piece] + [shift(piece, "z", hop) for hop in range(1, lax.axis_size("z"))]


def fetch(piece):
    line = line_pieces(piece)
    return line, line + [x_swap(p) for p in line]


def sum_to_owner(blocks):
    flat = blocks.reshape((-1,) + blocks.shape[2:])
    return lax.psum_scatter(flat, ("x", "z"), scatter_dimension=0)


def send_sums(own, come):
    sums = [o + c.astype(F32) for o, c in zip(own, come)]
    arrived = [shift(v.astype(BF16), "z", hop) for hop, v in enumerate(sums) if hop]
    return arrived, sums[0]


TURN = [(0, 0), (1, 2), (2, 1), (3, 3)]


def x_first(values):
    low, high = jnp.split(values, 2, axis=-1)
    first = lax.axis_index("x") == 0
    return jnp.where(first, jnp.concatenate((low, high), -1), jnp.concatenate((high, low), -1))


def rms_scale(values):
    return values * lax.rsqrt(jnp.mean(values * values, axis=-1, keepdims=True) + EPS)


def norm_piece(stream, norm_scale):
    return rms_scale(stream) * norm_scale


def conv_piece(seg_ext, extended, conv_taps, conv_shift):
    length = extended.shape[-2] - CONV + 1
    seg_here = seg_ext[..., CONV - 1 :]
    summed = conv_shift
    for offset in range(CONV):
        same_doc = (seg_ext[..., offset : offset + length] == seg_here)[..., None]
        summed = summed + conv_taps[offset] * extended[..., offset : offset + length, :] * same_doc
    return jax.nn.silu(summed)


CHUNK = 128
LANE = 64
NEVER = -1e30
TILE = INNER_Q // 128


def split_parts(values):
    high = values.astype(BF16)
    rest = values - high.astype(F32)
    middle = rest.astype(BF16)
    return high, middle, (rest - middle.astype(F32)).astype(BF16)


def mm(a, b, over=(1, 0)):
    return lax.dot_general(
        a, b, (((over[0],), (over[1],)), ((), ())), preferred_element_type=F32
    )


def exact_mm(values, ones, over=(1, 0)):
    high, middle, low = split_parts(values)
    return (mm(low, ones, over) + mm(middle, ones, over)) + mm(high, ones, over)


def spread_mm(values, ones, over=(1, 0)):
    high, low = halves(values)
    return mm(low, ones, over) + mm(high, ones, over)


def mm_exact(ones, values):
    high, middle, low = split_parts(values)
    return (mm(ones, low) + mm(ones, middle)) + mm(ones, high)


def halves(values):
    high = values.astype(BF16)
    return high, (values - high.astype(F32)).astype(BF16)


def mm_wide(narrow, values, over=(1, 0)):
    high, low = halves(values)
    return mm(narrow, low, over) + mm(narrow, high, over)


def softplus(values):
    tail = jnp.exp(-jnp.abs(values))
    series = tail * (1.0 - tail * (0.5 - tail * (1.0 / 3.0)))
    return jnp.maximum(values, 0.0) + jnp.where(tail < 0.01, series, jnp.log(1.0 + tail))


def sigmoid(values):
    return 1.0 / (1.0 + jnp.exp(-values))


def grids(shape):
    return lax.broadcasted_iota(jnp.int32, shape, 0), lax.broadcasted_iota(jnp.int32, shape, 1)


def column(row):
    return jnp.broadcast_to(row, (CHUNK, CHUNK)).T


def step_terms(raw_ref, par_ref):
    down, across = grids((CHUNK, CHUNK))
    lower = (down >= across).astype(F32).astype(BF16)
    step = softplus(raw_ref[0] + par_ref[0:1])
    sums = mm_exact(lower, -par_ref[1:2] * step)
    return step, sums, sums[CHUNK - 1 :]


def seg_terms(seg_ref):
    return column(seg_ref[0, 0, 0:1]), seg_ref[0, 0, 0:1], seg_ref[0, 0, 1:2], seg_ref[0, 0, 2:3]


def chunk_decay(total, before, last, spread):
    kept = jnp.exp(total) * (before == last).astype(F32)
    return exact_mm(jnp.broadcast_to(kept, (8, CHUNK)), spread)


def state_kernel(x, bc, raw, seg, par, spread, before_out, reach_out, end_out, total_out, bits_out, state, reach):
    @pl.when(pl.program_id(1) == 0)
    def _():
        state[...] = jnp.zeros_like(state)
        reach[...] = jnp.ones_like(reach)

    step, sums, total = step_terms(raw, par)
    lines, _, before, last = seg_terms(seg)
    before_out[0, 0] = state[...]
    reach_out[0, 0] = reach[...]
    leaving = jnp.where(lines == last, jnp.exp(total - sums), 0.0)
    fed = (x[0].astype(F32) * spread_mm(step, spread[...])).astype(BF16).astype(F32)
    fed = fed * spread_mm(leaving, spread[...])
    decay = chunk_decay(total, before, last, spread[...])
    state[...] = state[...] * decay[0:1] + mm_wide(bc[0, :, :STATE], fed, (0, 0))
    reach[...] = reach[...] * decay
    end_out[0] = state[...]
    total_out[0] = reach[...]
    lines = [v[0:1] for v in split_parts(reach[...])]
    bits_out[0] = jnp.concatenate(lines + [jnp.zeros((13, INNER_Q), BF16)], axis=0)


def inside_kernel(x, bc, raw, seg, par, spread, y_out):
    step, sums, _ = step_terms(raw, par)
    lines, row, _, _ = seg_terms(seg)
    down, across = grids((CHUNK, CHUNK))
    bias = jnp.where((lines == row) & (down >= across), 0.0, NEVER)
    scores = mm(bc[0, :, STATE:], bc[0, :, :STATE], (1, 1))
    turned = sums.T
    fed = (x[0].astype(F32) * spread_mm(step, spread[...])).astype(BF16)
    for pair in range(HEADS_Q // 2):
        lanes = slice(pair * 128, pair * 128 + 128)
        mixing = []
        for head in (LANE + 2 * pair, LANE + 2 * pair + 1):
            gap = jnp.broadcast_to(sums[:, head : head + 1], (CHUNK, CHUNK)) - turned[head : head + 1]
            mixing.append((scores * jnp.exp(gap + bias)).astype(BF16))
        both = mm(jnp.concatenate(mixing, axis=0), fed[:, lanes])
        y_out[0, :, lanes] = jnp.where(across < HEADDIM, both[:CHUNK], both[CHUNK:])


def outer_kernel(
    y_in, x, bc, raw, seg, par, spread, before, reach, start, gate, rows, y_out, gated_out, square_out
):
    _, sums, _ = step_terms(raw, par)
    lines, _, ahead, _ = seg_terms(seg)
    entering = spread_mm(jnp.where(lines == ahead, jnp.exp(sums), 0.0), spread[...])
    state = before[0, 0] + reach[0, 0, 0:1] * start[0]
    y = y_in[0] + entering * mm_wide(bc[0, :, STATE:], state)
    y_out[0] = y
    raw_gate = gate[0]
    gated = (y + rows[0:1] * x[0].astype(F32)) * (raw_gate * sigmoid(raw_gate))
    gated_out[0] = gated
    square = gated * gated
    folded = square[:, :128]
    for tile in range(1, INNER_Q // 128):
        folded = folded + square[:, tile * 128 : tile * 128 + 128]
    square_out[0, 0] = jnp.sum(folded.T, axis=0, keepdims=True)


def along_kernel(grad, gated, rows, scale, along_out, gain_out):
    @pl.when(pl.program_id(1) == 0)
    def _():
        gain_out[...] = jnp.zeros_like(gain_out)

    product = grad[0] * gated[0]
    weighed = product * rows[1:2]
    folded = weighed[:, :128]
    for tile in range(1, INNER_Q // 128):
        folded = folded + weighed[:, tile * 128 : tile * 128 + 128]
    along_out[0, 0] = jnp.sum(folded.T, axis=0, keepdims=True)
    lines = jnp.concatenate([column(scale[0, 0])] * (INNER_Q // 128), axis=1)
    gain_out[0] += jnp.sum((product * lines).reshape(CHUNK // 8, 8, INNER_Q), axis=0)


def gate_back_kernel(
    grad, gated, y, x, gate, bc, raw, seg, par, spread, rows, scale, along,
    grad_out, gate_out, after_out, beyond_out, start_out, state, reach,
):
    @pl.when(pl.program_id(1) == 0)
    def _():
        state[...] = jnp.zeros_like(state)
        reach[...] = jnp.ones_like(reach)

    wide = lambda row: jnp.concatenate([column(row)] * (INNER_Q // 128), axis=1)
    factor = scale[0, 0]
    pull = factor * factor * factor * along[0, 0] * (1.0 / INNER)
    grad_gated = grad[0] * rows[1:2] * wide(factor) - gated[0] * wide(pull)
    raw_gate = gate[0]
    sig = sigmoid(raw_gate)
    grad_y = (grad_gated * (raw_gate * sig)).astype(BF16)
    ssd_y = y[0] + rows[0:1] * x[0].astype(F32)
    gate_out[0] = (grad_gated * ssd_y * (sig * (1.0 + raw_gate * (1.0 - sig)))).astype(BF16)
    grad_out[0] = grad_y

    _, sums, total = step_terms(raw, par)
    lines, _, before, last = seg_terms(seg)
    after_out[0, 0] = state[...]
    beyond_out[0, 0] = reach[...]
    entering = spread_mm(jnp.where(lines == before, jnp.exp(sums), 0.0), spread[...])
    decay = chunk_decay(total, before, last, spread[...])
    fed = grad_y.astype(F32) * entering
    state[...] = state[...] * decay[0:1] + mm_wide(bc[0, :, STATE:], fed, (0, 0))
    reach[...] = reach[...] * decay
    start_out[0] = state[...]


def inside_back_kernel(x, bc, raw, seg, par, spread, grad, fed_out, b_out, c_out):
    step, sums, _ = step_terms(raw, par)
    lines, row, _, _ = seg_terms(seg)
    down, across = grids((CHUNK, CHUNK))
    bias = jnp.where((lines == row) & (across >= down), 0.0, NEVER)
    b_in, c_in = bc[0, :, :STATE], bc[0, :, STATE:]
    scores = mm(b_in, c_in, (1, 1))
    turned = sums.T
    fed = (x[0].astype(F32) * spread_mm(step, spread[...])).astype(BF16)
    grad_scores = jnp.zeros((CHUNK, CHUNK), F32)
    for pair in range(HEADS_Q // 2):
        lanes = slice(pair * 128, pair * 128 + 128)
        fed_pair, grad_pair = fed[:, lanes], grad[0, :, lanes]
        none = jnp.zeros_like(fed_pair)
        apart = jnp.concatenate(
            (jnp.where(across < HEADDIM, fed_pair, none), jnp.where(across < HEADDIM, none, fed_pair)),
            axis=0,
        )
        grad_mixing = mm(apart, grad_pair, (1, 1))
        mixing = []
        for which in range(2):
            head = LANE + 2 * pair + which
            gap = turned[head : head + 1] - jnp.broadcast_to(sums[:, head : head + 1], (CHUNK, CHUNK))
            decays = jnp.exp(gap + bias)
            mixing.append((scores * decays).astype(BF16))
            grad_scores = grad_scores + grad_mixing[which * CHUNK : which * CHUNK + CHUNK] * decays
        both = mm(jnp.concatenate(mixing, axis=0), grad_pair)
        fed_out[0, :, lanes] = jnp.where(across < HEADDIM, both[:CHUNK], both[CHUNK:])
    grad_scores = grad_scores.astype(BF16)
    b_out[0] = mm(grad_scores, c_in)
    c_out[0] = mm(grad_scores, b_in, (0, 0))


def outer_back_kernel(
    fed_in, b_in, c_in, x, bc, raw, seg, par, spread, before, reach, start, after, beyond, grad_end,
    end, total_reach, grad, y, rows,
    x_out, bc_out, raw_out, sums_out, skip_out, carry,
):
    @pl.when(pl.program_id(1) == 0)
    def _():
        sums_out[...] = jnp.zeros_like(sums_out)
        skip_out[...] = jnp.zeros_like(skip_out)
        last_state = end[0] + total_reach[0, 0:1] * start[0]
        meet = jnp.sum((grad_end[0] * last_state).reshape(STATE // 8, 8, INNER_Q), axis=0)
        meet = jnp.sum(spread_mm(meet, spread[...], (1, 1)), axis=0, keepdims=True)
        carry[...] = jnp.broadcast_to(meet, carry.shape)

    step, sums, total = step_terms(raw, par)
    lines, _, ahead, last = seg_terms(seg)
    ones = spread[...]
    state = (before[0, 0] + reach[0, 0, 0:1] * start[0]).astype(BF16)
    grad_state = after[0, 0] + beyond[0, 0, 0:1] * grad_end[0]
    values = x[0].astype(F32)
    grad_y = grad[0].astype(F32)
    wide_step = spread_mm(step, ones)
    leaving = spread_mm(jnp.where(lines == last, jnp.exp(total - sums), 0.0), ones)
    entering = spread_mm(jnp.where(lines == ahead, jnp.exp(sums), 0.0), ones)
    fed = (values * wide_step).astype(BF16).astype(F32)
    grad_fed = fed_in[0] + leaving * mm_wide(bc[0, :, :STATE], grad_state)
    x_out[0] = wide_step * grad_fed + rows[0:1] * grad_y
    bc_out[0, :, :STATE] = b_in[0] + mm((leaving * fed).astype(BF16), grad_state.astype(BF16), (1, 1))
    bc_out[0, :, STATE:] = c_in[0] + mm((entering * grad_y).astype(BF16), state, (1, 1))
    skip_out[0] += jnp.sum((grad_y * values).reshape(CHUNK // 8, 8, INNER_Q), axis=0)

    by_step = spread_mm(values * grad_fed, ones, (1, 1))
    flow = spread_mm(grad_y * y[0] - fed * grad_fed, ones, (1, 1))
    down, across = grids((CHUNK, CHUNK))
    upper = (across >= down).astype(F32).astype(BF16)
    grad_log = mm_exact(upper, flow) + carry[0:1]
    carry[...] = jnp.broadcast_to(grad_log[0:1], carry.shape)
    rate = par[1:2]
    grad_raw = (by_step - rate * grad_log) * sigmoid(raw[0] + par[0:1])
    raw_out[0] = grad_raw
    fold = lambda v: jnp.sum(v.reshape(CHUNK // 8, 8, CHUNK), axis=0)
    sums_out[0, 0:8] += fold(-rate * step * grad_log)
    sums_out[0, 8:16] += fold(grad_raw)


def chunk_spec(width, back=0, column_block=0):
    turn = (lambda c: back - 1 - c) if back else (lambda c: c)
    return pl.BlockSpec((1, CHUNK, width), lambda s, c: (s, turn(c), column_block))


def per_chunk(lines, width, back=0):
    turn = (lambda c: back - 1 - c) if back else (lambda c: c)
    return pl.BlockSpec((1, 1, lines, width), lambda s, c: (s, turn(c), 0, 0))


def per_sequence(lines, width):
    return pl.BlockSpec((1, lines, width), lambda s, c: (s, 0, 0))


def fixed(lines, width):
    return pl.BlockSpec((lines, width), lambda s, c: (0, 0))


def shaped(shape, dtype=F32):
    return jax.ShapeDtypeStruct(shape, dtype)


def call(kernel, name, chunks, ins, outs, operands, scratch=(), flops=0, after=()):
    in_specs = [spec for spec, _ in zip(ins, operands, strict=True)]
    moved = sum(v.size * v.dtype.itemsize for v in operands)
    moved += sum(v.size * v.dtype.itemsize for _, v in outs)
    count, skipped = len(in_specs), len(after)
    in_specs = in_specs + [pl.BlockSpec(memory_space=pl.ANY)] * skipped
    operands = tuple(operands) + tuple(after)
    return pl.pallas_call(
        lambda *refs: kernel(*refs[:count], *refs[count + skipped :]),
        name=name,
        grid=(2, chunks),
        in_specs=in_specs,
        out_specs=[spec for spec, _ in outs],
        out_shape=[shape for _, shape in outs],
        scratch_shapes=list(scratch),
        cost_estimate=pl.CostEstimate(flops=flops, bytes_accessed=moved, transcendentals=0),
        compiler_params=pltpu.CompilerParams(
            dimension_semantics=("arbitrary", "arbitrary"), vmem_limit_bytes=STEP_BYTES
        ),
    )(*operands)


STATE_SCRATCH = (pltpu.VMEM((STATE, INNER_Q), F32), pltpu.VMEM((8, INNER_Q), F32))


def scan_states(x, bc, raw, seg, par, spread, after=()):
    span = x.shape[1]
    n = span // CHUNK
    return call(
        state_kernel, "chunk_states", n,
        [chunk_spec(INNER_Q), chunk_spec(2 * STATE), chunk_spec(128, 0, TILE), per_chunk(8, 128), fixed(8, 128),
         fixed(128, INNER_Q)],
        [(per_chunk(STATE, INNER_Q), shaped((2, n, STATE, INNER_Q))), (per_chunk(8, INNER_Q), shaped((2, n, 8, INNER_Q))),
         (per_sequence(STATE, INNER_Q), shaped((2, STATE, INNER_Q))), (per_sequence(8, INNER_Q), shaped((2, 8, INNER_Q))),
         (per_sequence(16, INNER_Q), shaped((2, 16, INNER_Q), BF16))],
        (x, bc, raw, seg, par, spread), STATE_SCRATCH, 2 * 2 * span * STATE * INNER_Q, after=after,
    )


def scan_inside(x, bc, raw, seg, par, spread, after=()):
    span = x.shape[1]
    n = span // CHUNK
    return call(
        inside_kernel, "inside_chunks", n,
        [chunk_spec(INNER_Q), chunk_spec(2 * STATE), chunk_spec(128, 0, TILE), per_chunk(8, 128), fixed(8, 128),
         fixed(128, INNER_Q)],
        [(chunk_spec(INNER_Q), shaped(x.shape))],
        (x, bc, raw, seg, par, spread), (), 8 * 2 * span * CHUNK * INNER_Q, after=after,
    )[0]


def scan_outer(y, x, bc, raw, seg, par, spread, before, reach, start, gate, rows, after=()):
    span = x.shape[1]
    n = span // CHUNK
    return call(
        outer_kernel, "scan_and_gate", n,
        [chunk_spec(INNER_Q), chunk_spec(INNER_Q), chunk_spec(2 * STATE), chunk_spec(128, 0, TILE), per_chunk(8, 128), fixed(8, 128),
         fixed(128, INNER_Q), per_chunk(STATE, INNER_Q), per_chunk(8, INNER_Q), per_sequence(STATE, INNER_Q),
         chunk_spec(INNER_Q), fixed(8, INNER_Q)],
        [(chunk_spec(INNER_Q), shaped(x.shape)), (chunk_spec(INNER_Q), shaped(x.shape)),
         (per_chunk(1, 128), shaped((2, n, 1, 128)))],
        (y, x, bc, raw, seg, par, spread, before, reach, start, gate, rows), (), 8 * span * STATE * INNER_Q, after=after,
    )


def gate_along(grad, gated, rows, scale, after=()):
    span = gated.shape[1]
    n = span // CHUNK
    return call(
        along_kernel, "gate_along", n,
        [chunk_spec(INNER_Q), chunk_spec(INNER_Q), fixed(8, INNER_Q), per_chunk(1, 128)],
        [(per_chunk(1, 128), shaped((2, n, 1, 128))), (per_sequence(8, INNER_Q), shaped((2, 8, INNER_Q)))],
        (grad, gated, rows, scale), (), 10 * span * INNER_Q, after=after,
    )


def gate_back(grad, gated, y, x, gate, bc, raw, seg, par, spread, rows, scale, along, after=()):
    span = x.shape[1]
    n = span // CHUNK
    return call(
        gate_back_kernel, "gate_back_and_states", n,
        [chunk_spec(INNER_Q, n)] * 5 + [chunk_spec(2 * STATE, n), chunk_spec(128, n, TILE), per_chunk(8, 128, n), fixed(8, 128),
         fixed(128, INNER_Q), fixed(8, INNER_Q), per_chunk(1, 128, n), per_chunk(1, 128, n)],
        [(chunk_spec(INNER_Q, n), shaped(x.shape, BF16)), (chunk_spec(INNER_Q, n), shaped(x.shape, BF16)),
         (per_chunk(STATE, INNER_Q, n), shaped((2, n, STATE, INNER_Q))), (per_chunk(8, INNER_Q, n), shaped((2, n, 8, INNER_Q))),
         (per_sequence(STATE, INNER_Q), shaped((2, STATE, INNER_Q)))],
        (grad, gated, y, x, gate, bc, raw, seg, par, spread, rows, scale, along), STATE_SCRATCH,
        8 * span * STATE * INNER_Q, after=after,
    )


def scan_inside_back(x, bc, raw, seg, par, spread, grad, after=()):
    span = x.shape[1]
    n = span // CHUNK
    return call(
        inside_back_kernel, "inside_chunks_back", n,
        [chunk_spec(INNER_Q), chunk_spec(2 * STATE), chunk_spec(128, 0, TILE), per_chunk(8, 128), fixed(8, 128),
         fixed(128, INNER_Q), chunk_spec(INNER_Q)],
        [(chunk_spec(INNER_Q), shaped(x.shape)), (chunk_spec(STATE), shaped((2, span, STATE))),
         (chunk_spec(STATE), shaped((2, span, STATE)))],
        (x, bc, raw, seg, par, spread, grad), (), 24 * 2 * span * CHUNK * INNER_Q, after=after,
    )


def scan_outer_back(
    fed, b, c, x, bc, raw, seg, par, spread, before, reach, start, later, beyond, grad_end, end, total, grad, y, rows, after=()
):
    span = x.shape[1]
    n = span // CHUNK
    return call(
        outer_back_kernel, "scan_back", n,
        [chunk_spec(INNER_Q, n), chunk_spec(STATE, n), chunk_spec(STATE, n), chunk_spec(INNER_Q, n), chunk_spec(2 * STATE, n),
         chunk_spec(128, n, TILE), per_chunk(8, 128, n), fixed(8, 128), fixed(128, INNER_Q), per_chunk(STATE, INNER_Q, n),
         per_chunk(8, INNER_Q, n), per_sequence(STATE, INNER_Q), per_chunk(STATE, INNER_Q, n), per_chunk(8, INNER_Q, n),
         per_sequence(STATE, INNER_Q), per_sequence(STATE, INNER_Q), per_sequence(8, INNER_Q), chunk_spec(INNER_Q, n),
         chunk_spec(INNER_Q, n), fixed(8, INNER_Q)],
        [(chunk_spec(INNER_Q, n), shaped(x.shape)), (chunk_spec(2 * STATE, n), shaped((2, span, 2 * STATE))),
         (chunk_spec(128, n), shaped((2, span, 128))), (per_sequence(16, 128), shaped((2, 16, 128))),
         (per_sequence(8, INNER_Q), shaped((2, 8, INNER_Q)))],
        (fed, b, c, x, bc, raw, seg, par, spread, before, reach, start, later, beyond, grad_end, end, total, grad, y, rows),
        (pltpu.VMEM((8, 128), F32),), 24 * span * STATE * INNER_Q, after=after,
    )


def seg_table(seg_now, seg_before):
    span = seg_now.shape[1]
    rows = seg_now.reshape(2, span // CHUNK, 1, CHUNK)
    last = rows[..., -1:]
    before = jnp.concatenate((seg_before.reshape(2, 1, 1, 1), last[:, :-1]), axis=1)
    spread = lambda v: jnp.broadcast_to(v, rows.shape)
    return jnp.concatenate((rows, spread(before), spread(last)) + (rows,) * 5, axis=2)


def conv_terms(wide_ref, halo_ref, taps_ref, mask_ref, tail):
    own = wide_ref[0].astype(BF16).astype(F32)
    longer = jnp.concatenate((tail, own), axis=0)
    rows = [own]
    total = taps_ref[CONV : CONV + 1] + taps_ref[CONV - 1 : CONV] * own
    for back in range(1, CONV):
        same = jnp.concatenate([column(mask_ref[0, 0, back : back + 1])] * (own.shape[1] // 128), axis=1)
        earlier = longer[8 - back : 8 - back + CHUNK] * same
        rows.append(earlier)
        total = total + taps_ref[CONV - 1 - back : CONV - back] * earlier
    return own, rows, total


def conv_kernel(wide, halo, taps, mask, out, tail):
    @pl.when(pl.program_id(1) == 0)
    def _():
        tail[...] = halo[0].astype(F32)

    own, _, total = conv_terms(wide, halo, taps, mask, tail[...])
    tail[...] = own[CHUNK - 8 :]
    out[0] = (total * sigmoid(total)).astype(BF16)


def conv_back_kernel(wide, before, halo, taps, mask, grad, returned, out, sums_out, ahead):
    chunk = pl.num_programs(1) - 1 - pl.program_id(1)

    @pl.when(pl.program_id(1) == 0)
    def _():
        sums_out[...] = jnp.zeros_like(sums_out)
        ahead[...] = jnp.zeros_like(ahead)

    tail = jnp.where(chunk == 0, halo[0].astype(F32), before[0].astype(BF16).astype(F32))
    _, rows, total = conv_terms(wide, halo, taps, mask, tail)
    sig = sigmoid(total)
    pull = grad[0] * (sig * (1.0 + total * (1.0 - sig)))
    result = taps[CONV - 1 : CONV] * pull
    fold = lambda v: jnp.sum(v.reshape(CHUNK // 8, 8, v.shape[1]), axis=0)
    for back in range(1, CONV):
        same = jnp.concatenate([column(mask[0, 0, back : back + 1])] * (pull.shape[1] // 128), axis=1)
        masked = pull * same
        longer = jnp.concatenate((masked, ahead[8 * back - 8 : 8 * back]), axis=0)
        result = result + taps[CONV - 1 - back : CONV - back] * longer[back : back + CHUNK]
        ahead[8 * back - 8 : 8 * back] = masked[:8]
    for back in range(CONV):
        place = CONV - 1 - back
        sums_out[0, 8 * place : 8 * place + 8] += fold(pull * rows[back])
    sums_out[0, 8 * CONV : 8 * CONV + 8] += fold(pull)
    late = (pl.program_id(1) == 0).astype(F32) * returned[0].astype(F32)
    late = jnp.concatenate((jnp.zeros((CHUNK - 8, late.shape[1]), F32), late), axis=0)
    out[0] = (result + late).astype(BF16)


def conv_forward(wide, halo, taps, mask, width, at, after=()):
    n = wide.shape[1] // CHUNK
    lines = lambda rows: pl.BlockSpec((1, rows, width), lambda s, c: (s, 0, at))
    return call(
        conv_kernel, "conv", n,
        [chunk_spec(width, 0, at), lines(8), pl.BlockSpec((8, width), lambda s, c: (0, at)), per_chunk(8, 128)],
        [(chunk_spec(width), shaped(wide.shape[:2] + (width,), BF16))],
        (wide, halo, taps, mask), (pltpu.VMEM((8, width), F32),), 30 * wide.shape[1] * width, after=after,
    )[0]


def conv_backward(wide, halo, taps, mask, grad, returned, width, at, after=()):
    n = wide.shape[1] // CHUNK
    lines = lambda rows: pl.BlockSpec((1, rows, width), lambda s, c: (s, 0, at))
    steps = CHUNK // 8
    early = pl.BlockSpec(
        (1, 8, width), lambda s, c: (s, jnp.maximum((n - 1 - c) * steps - 1, 0), at)
    )
    return call(
        conv_back_kernel, "conv_back", n,
        [chunk_spec(width, n, at), early, lines(8), pl.BlockSpec((8, width), lambda s, c: (0, at)),
         per_chunk(8, 128, n), chunk_spec(width, n), lines(8)],
        [(chunk_spec(width, n), shaped(wide.shape[:2] + (width,), BF16)), (per_sequence(8 * CONV + 8, width), shaped((2, 8 * CONV + 8, width)))],
        (wide, wide, halo, taps, mask, grad, returned), (pltpu.VMEM((8 * CONV, width), F32),), 60 * wide.shape[1] * width, after=after,
    )


def mask_table(seg_ext, edge_rows):
    span = seg_ext.shape[1] - edge_rows
    here = seg_ext[:, edge_rows:]
    rows = [here == seg_ext[:, edge_rows - back : edge_rows - back + span] for back in range(CONV)]
    table = jnp.stack(rows + rows, axis=1).astype(F32)
    return jnp.moveaxis(table.reshape(2, 2 * CONV, span // CHUNK, CHUNK), 2, 1)


def tile_picks(owner, rows):
    down, across = grids((2 * STATE, 128))
    bc = (down - BC_Q * owner == across) & (across < BC_Q)
    down, across = grids((HEADS, 128))
    head = across - LANE
    dt = (down - HEADS_Q * owner == head) & (head >= 0) & (head < HEADS_Q)
    return bc.astype(F32), dt.astype(F32)


def cut_weights_kernel(q_ref, weight, *outs):
    for layer in range(weight.shape[0]):
        for k in range(TEAM):
            owner = q_ref[0] ^ k
            start = pl.multiple_of(owner * INNER_Q, 128)
            part = outs[layer * TEAM + k]
            part[:, :INNER_Q] = weight[layer, :, pl.ds(start, INNER_Q)]
            part[:, INNER_Q : 2 * INNER_Q] = weight[layer, :, pl.ds(INNER + start, INNER_Q)]
            bc, dt = tile_picks(owner, None)
            tile = mm(weight[layer, :, 2 * INNER : 2 * INNER + 2 * STATE], bc.astype(BF16))
            tile = tile + mm(weight[layer, :, INNER + CONVDIM :], dt.astype(BF16))
            part[:, 2 * INNER_Q :] = tile.astype(BF16)


def whole_spec(shape):
    return pl.BlockSpec(shape, lambda *_: (0,) * len(shape))


def whole_call(kernel, name, index, operands, outs, after=()):
    count, skipped = 1 + len(operands), len(after)
    return pl.pallas_call(
        lambda *refs: kernel(*refs[:count], *refs[count + skipped :]),
        name=name,
        grid_spec=pltpu.PrefetchScalarGridSpec(
            num_scalar_prefetch=1,
            grid=(1,),
            in_specs=[whole_spec(v.shape) for v in operands]
            + [pl.BlockSpec(memory_space=pl.ANY)] * skipped,
            out_specs=[whole_spec(s.shape) for s in outs],
        ),
        out_shape=list(outs),
        compiler_params=pltpu.CompilerParams(vmem_limit_bytes=VMEM_BYTES),
    )(index, *operands, *after)


def tie(value, *after):
    anywhere = pl.BlockSpec(memory_space=pl.ANY)
    return pl.pallas_call(
        lambda *refs: None,
        name="tie",
        in_specs=[anywhere] * (1 + len(after)),
        out_specs=anywhere,
        out_shape=shaped(value.shape, value.dtype),
        input_output_aliases={0: 0},
    )(value, *after)


def norm_kernel(x_ref, stream, gain, out):
    values = stream[...].astype(F32)
    mean = jnp.mean(values * values, axis=-1, keepdims=True)
    normed = (values * lax.rsqrt(mean + EPS) * gain[...]).astype(BF16)
    width = normed.shape[1] // 2
    x = x_ref[0]
    out[:, pl.ds(pl.multiple_of(x * width, 128), width)] = normed[:, :width]
    out[:, pl.ds(pl.multiple_of((1 - x) * width, 128), width)] = normed[:, width:]


def norm_rows(x, stream, gain, after=()):
    return whole_call(norm_kernel, "norm", x, (stream, gain), [shaped(stream.shape, BF16)], after)[0]


def scale_kernel(gated, scale, rows, out):
    lines = jnp.concatenate([column(scale[0, 0])] * (INNER_Q // 128), axis=1)
    out[0] = (gated[0] * lines * rows[1:2]).astype(BF16)


def scale_rows(gated, scale, rows, after=()):
    n = gated.shape[1] // CHUNK
    return call(
        scale_kernel, "scale_rows", n,
        [chunk_spec(INNER_Q), per_chunk(1, 128), fixed(8, INNER_Q)],
        [(chunk_spec(INNER_Q), shaped(gated.shape, BF16))],
        (gated, scale, rows), (), 4 * gated.size, after=after,
    )[0]


def cut_weights(q, weight):
    layers, rows = weight.shape[:2]
    outs = [shaped((rows, INNER_Q + WIDE), BF16)] * (TEAM * layers)
    outs = whole_call(cut_weights_kernel, "cut_weights", q, (weight,), outs)
    return [outs[TEAM * layer : TEAM * layer + TEAM] for layer in range(layers)]


def place_of(owner):
    return (owner % 2) * 2 + owner // 2


def wide_piece_kernel(q_ref, *refs):
    out = refs[-1]
    for k in range(TEAM):
        out[place_of(q_ref[0] ^ k)] = refs[k][:, INNER_Q:]


def gate_piece_kernel(q_ref, *refs):
    rows, out = refs[TEAM], refs[-1]
    for k in range(TEAM):
        out[place_of(q_ref[0] ^ k)] = refs[k][:, :INNER_Q]
    for block in range(TEAM):
        half = block % 2 * INNER_Q
        out[TEAM + block] = rows[block // 2, :, half : half + INNER_Q]


def all_piece_kernel(q_ref, *refs):
    out = refs[-1]
    for k in range(TEAM):
        out[place_of(q_ref[0] ^ k)] = refs[k][...]


def all_piece(q, parts, after=()):
    shape = (TEAM,) + parts[0].shape
    return whole_call(all_piece_kernel, "all_piece", q, parts, [shaped(shape, BF16)], after)[0]


def arrange_kernel(_, gathered, gate, wide):
    for x in range(2):
        for z in range(gate.shape[2]):
            for block in range(TEAM):
                rows = gathered[x, z, block]
                gate[x, block // 2, z, block % 2] = rows[:, :INNER_Q]
                wide[x, block // 2, z, block % 2] = rows[:, INNER_Q:]


def arrange(index, gathered):
    size, rows = gathered.shape[1], gathered.shape[3]
    outs = [shaped((2, 2, size, 2, rows, width), BF16) for width in (INNER_Q, WIDE)]
    gate, wide = whole_call(arrange_kernel, "arrange", index, (gathered,), outs)
    return wide.reshape(-1, WIDE), gate.reshape(-1, INNER_Q)


def by_owner_kernel(x_ref, grad, out):
    for side in range(2):
        x = x_ref[0] if side == 0 else 1 - x_ref[0]
        for z in range(out.shape[1]):
            for block in range(TEAM):
                out[x, z, block] = grad[side, block // 2, z, block % 2].astype(BF16)


def both_by_owner_kernel(x_ref, gate, out_grad, out):
    for side in range(2):
        x = x_ref[0] if side == 0 else 1 - x_ref[0]
        for z in range(out.shape[1]):
            for block in range(TEAM):
                upper, lower = block // 2, block % 2
                half = slice(lower * INNER_Q, lower * INNER_Q + INNER_Q)
                out[x, z, block] = gate[side, upper, z, lower].astype(BF16)
                out[side, z, TEAM + block] = out_grad[z, side, upper, :, half].astype(BF16)


def both_by_owner(x_first_of, gate, out_grad, size, rows):
    operands = (
        gate.reshape(2, 2, size, 2, rows, INNER_Q),
        out_grad.reshape(size, 2, 2, rows, 2 * INNER_Q),
    )
    outs = [shaped((2, size, 2 * TEAM, rows, INNER_Q), BF16)]
    return whole_call(both_by_owner_kernel, "both_by_owner", x_first_of, operands, outs)[0]


def by_owner(x_first_of, grad, size, rows):
    width = grad.shape[-1]
    operands = (grad.reshape(2, 2, size, 2, rows, width),)
    outs = [shaped((2, size, TEAM, rows, width), BF16)]
    return whole_call(by_owner_kernel, "by_owner", x_first_of, operands, outs)[0]


def wide_piece(q, parts, after=()):
    shape = (TEAM, parts[0].shape[0], WIDE)
    return whole_call(wide_piece_kernel, "wide_piece", q, parts, [shaped(shape, BF16)], after)[0]


def gate_piece(q, parts, rows, after=()):
    count = parts[0].shape[0]
    operands = tuple(parts) + (rows.reshape(2, count, -1),)
    outs = [shaped((2 * TEAM, count, INNER_Q), BF16)]
    return whole_call(gate_piece_kernel, "gate_piece", q, operands, outs, after)[0]


def arrange_both_kernel(x_ref, gathered, gate, out):
    for side in range(2):
        x = x_ref[0] if side == 0 else 1 - x_ref[0]
        for z in range(gate.shape[2]):
            for block in range(TEAM):
                upper, lower = block // 2, block % 2
                gate[side, upper, z, lower] = gathered[x, z, block]
                half = slice(lower * INNER_Q, lower * INNER_Q + INNER_Q)
                out[z, side, upper, :, half] = gathered[side, z, TEAM + block]


def arrange_both(x_first_of, gathered):
    size, rows = gathered.shape[1], gathered.shape[3]
    outs = [
        shaped((2, 2, size, 2, rows, INNER_Q), BF16),
        shaped((size, 2, 2, rows, 2 * INNER_Q), BF16),
    ]
    gate, out = whole_call(arrange_both_kernel, "arrange_both", x_first_of, (gathered,), outs)
    return gate.reshape(-1, INNER_Q), out.reshape(-1, 2 * INNER_Q)


def whole_wide_kernel(place, *refs):
    out = refs[-1]
    size = out.shape[2]
    for side in range(2):
        for hop in range(size):
            source = lax.rem(place[0] - hop + size, size)
            for block in range(TEAM):
                out[side, block // 2, source, block % 2] = refs[side * size + hop][block]


def whole_columns(place, pieces, after=()):
    size = len(pieces) // 2
    rows, width = pieces[0].shape[1:]
    outs = [shaped((2, 2, size, 2, rows, width), BF16)]
    whole = whole_call(whole_wide_kernel, "whole_columns", place, pieces, outs, after)[0]
    return whole.reshape(-1, width)


def cut_wide_kernel(place, grad, *outs):
    size = len(outs) // 2
    for hop in range(size):
        target = lax.rem(place[0] + hop, size)
        for block in range(TEAM):
            outs[hop][block] = grad[1, block // 2, target, block % 2].astype(BF16)
            outs[size + hop][block] = grad[0, block // 2, target, block % 2]


def cut_wide(place, grad, size, rows):
    shape = (TEAM, rows, WIDE)
    outs = [shaped(shape, BF16)] * size + [shaped(shape)] * size
    operands = (grad.reshape(2, 2, size, 2, rows, WIDE),)
    outs = whole_call(cut_wide_kernel, "cut_wide", place, operands, outs)
    return outs[:size], outs[size:]


def grad_parts_kernel(q_ref, gate, wide, *refs):
    count = len(refs) - TEAM
    for k in range(TEAM):
        block = place_of(q_ref[0] ^ k)
        total = wide[block]
        for come in refs[:count]:
            total = total + come[block].astype(F32)
        refs[count + k][:, :INNER_Q] = gate[block].astype(BF16)
        refs[count + k][:, INNER_Q:] = total.astype(BF16)


def grad_parts(q, gate, wide, come):
    outs = [shaped((wide.shape[1], INNER_Q + WIDE), BF16)] * TEAM
    return whole_call(grad_parts_kernel, "grad_parts", q, (gate, wide, *come), outs)


def cut_params_kernel(q_ref, conv_weight, conv_bias, dt_bias, a_log, skip, out_gain, spread, taps, par, rows):
    owner = q_ref[0]
    start = pl.multiple_of(owner * INNER_Q, 128)
    bc, dt = tile_picks(owner, None)
    bc, dt = bc.astype(BF16), dt.astype(BF16)
    mine = pl.ds(start, INNER_Q)
    for layer in range(conv_weight.shape[0]):
        one = slice(layer, layer + 1)
        taps[layer, :CONV, :INNER_Q] = conv_weight[layer, :, mine]
        taps[layer, :CONV, INNER_Q:] = exact_mm(conv_weight[layer, :, INNER:], bc)
        taps[layer, CONV : CONV + 1, :INNER_Q] = conv_bias[one, mine]
        taps[layer, CONV : CONV + 1, INNER_Q:] = exact_mm(conv_bias[one, INNER:], bc)
        taps[layer, CONV + 1 :] = jnp.zeros((7 - CONV, WIDE), F32)
        par[layer, 0:1] = exact_mm(dt_bias[one], dt)
        par[layer, 1:2] = exact_mm(jnp.exp(a_log[one]), dt)
        par[layer, 2:] = jnp.zeros((6, 128), F32)
        rows[layer, 0:1] = exact_mm(exact_mm(skip[one], dt), spread[...])
        rows[layer, 1:2] = out_gain[one, mine]
        rows[layer, 2:] = jnp.zeros((6, INNER_Q), F32)


def cut_params(q, params, after):
    layers = params[0].shape[0]
    shapes = [(layers, 8, WIDE), (layers, 8, 128), (layers, 8, INNER_Q)]
    return whole_call(cut_params_kernel, "cut_params", q, params, [shaped(s) for s in shapes], after)


def join_kernel(q_ref, *refs):
    out = refs[-1]
    for layer in range(out.shape[0]):
        shared = 0.0
        for k in range(TEAM):
            owner = q_ref[0] ^ k
            start = pl.multiple_of(owner * INNER_Q, 128)
            part = refs[layer * TEAM + k]
            out[layer, :, pl.ds(start, INNER_Q)] = part[:, :INNER_Q].astype(F32)
            out[layer, :, pl.ds(INNER + start, INNER_Q)] = part[:, INNER_Q : 2 * INNER_Q].astype(F32)
            bc, dt = tile_picks(owner, None)
            both = jnp.concatenate((bc, dt), axis=0).astype(BF16)
            shared = shared + mm(part[:, 2 * INNER_Q :], both, (1, 1))
        out[layer, :, 2 * INNER :] = shared


def join_weights(q, parts):
    flat = [v for layer in parts for v in layer]
    shape = (len(parts), flat[0].shape[0], 2 * INNER + 2 * STATE + HEADS)
    return whole_call(join_kernel, "join_weights", q, flat, [shaped(shape)])[0]


SMALL = (16, WIDE)


def pack_small_kernel(conv_x, conv_tile, heads, skip, gain, norm, spread, out):
    fold = lambda v, rows: jnp.sum(v[:, rows], axis=(0, 1), keepdims=True)[0]
    for line in range(CONV + 1):
        rows = slice(8 * line, 8 * line + 8)
        out[line : line + 1, :INNER_Q] = fold(conv_x[...], rows)
        out[line : line + 1, INNER_Q:] = fold(conv_tile[...], rows)
    line = CONV + 1
    out[line:] = jnp.zeros((SMALL[0] - line, WIDE), F32)
    every = slice(0, 8)
    out[line + 1 : line + 2, :INNER_Q] = fold(gain[...], every)
    out[line + 2 : line + 3, :128] = fold(heads[...], slice(8, 16))
    out[line + 3 : line + 4, :128] = fold(heads[...], every)
    by_head = exact_mm(skip[0] + skip[1], spread[...], (1, 1))
    out[line + 4 : line + 5, :128] = jnp.sum(by_head, axis=0, keepdims=True)
    width = norm.shape[1] // 2
    out[line + 5 : line + 6, :width] = norm[:, :width]
    out[line + 6 : line + 7, :width] = norm[:, width:]


def pack_small(*parts):
    return pl.pallas_call(pack_small_kernel, name="pack_small", out_shape=shaped(SMALL))(*parts)


def lanes_of(values):
    return lax.broadcasted_iota(jnp.int32, values.shape, 1)


def open_small_kernel(q_ref, *refs):
    norm, conv_weight, conv_bias, dt_bias, a_log, skip, gain = refs[-7:]
    layers = norm.shape[0]
    line = CONV + 1
    for layer in range(layers):
        one = slice(layer, layer + 1)
        packs = [ref[layer] for ref in refs[:TEAM]]
        shared, heads = [], 0.0
        for k in range(TEAM):
            owner = q_ref[0] ^ k
            start = pl.multiple_of(owner * INNER_Q, 128)
            mine = pl.ds(start, INNER_Q)
            pack = packs[k]
            conv_weight[layer, :, mine] = pack[:CONV, :INNER_Q]
            conv_bias[one, mine] = pack[CONV:line, :INNER_Q]
            tile = pack[:8, INNER_Q:]
            tile = jnp.where(lanes_of(tile) < BC_Q, tile, 0.0)
            tile = jnp.where(owner % 2 == 0, tile, pltpu.roll(tile, BC_Q, 1))
            shared.append([jnp.where(owner // 2 == side, tile, 0.0) for side in range(2)])
            rows = pack[line + 2 : line + 5, :128]
            in_head = (lanes_of(rows) >= LANE) & (lanes_of(rows) < LANE + HEADS_Q)
            rows = jnp.where(in_head, rows, 0.0)
            placed = 0.0
            for which in range(TEAM):
                turned = pltpu.roll(rows, (HEADS_Q * which - LANE) % 128, 1)
                placed = placed + jnp.where(owner == which, turned, 0.0)
            heads = heads + placed[:, :HEADS]
            gain[one, mine] = pack[line + 1 : line + 2, :INNER_Q]
        shared = jnp.concatenate([sum([s[side] for s in shared]) for side in range(2)], axis=1)
        conv_weight[layer, :, INNER:] = shared[:CONV]
        conv_bias[one, INNER:] = shared[CONV:line]
        dt_bias[one], a_log[one], skip[one] = heads[0:1], heads[1:2], heads[2:3]
        width = norm.shape[1] // 2
        halves_of = lambda n: packs[n][line + 5 : line + 7, :width]
        total = (halves_of(0) + halves_of(1)) + (halves_of(2) + halves_of(3))
        norm[one, :width] = total[0:1]
        norm[one, width:] = total[1:2]


def open_small(q, packs, features):
    layers = packs[0].shape[0]
    flat = list(packs)
    shapes = [
        (layers, features), (layers, CONV, CONVDIM), (layers, CONVDIM), (layers, HEADS), (layers, HEADS),
        (layers, HEADS), (layers, INNER),
    ]
    return pl.pallas_call(
        open_small_kernel,
        name="open_small",
        grid_spec=pltpu.PrefetchScalarGridSpec(
            num_scalar_prefetch=1,
            grid=(1,),
            in_specs=[whole_spec(v.shape) for v in flat],
            out_specs=[whole_spec(s) for s in shapes],
        ),
        out_shape=[shaped(s) for s in shapes],
    )(q, *flat)


def spread_matrix():
    head = jnp.arange(128)[:, None] - LANE
    return (jnp.arange(INNER_Q)[None, :] // HEADDIM == head).astype(BF16)


def gap_decays(spans):
    rows = []
    for start in range(len(spans)):
        row = []
        running = jnp.ones_like(spans[0])
        for stop, span in enumerate(spans):
            if stop <= start:
                row.append(jnp.zeros_like(running))
                continue
            row.append(running)
            running = running * span
        rows.append(jnp.stack(row))
    return jnp.stack(rows)


def mix_states(states, bits=None, weights=None):
    size = lax.axis_size("z")
    z = lax.axis_index("z")
    width = states.shape[1] // size
    decay = lambda rows: jnp.sum(rows[:, :3].astype(F32), axis=1)
    if size > NEAR:
        if weights is None:
            weights = gap_decays([decay(v) for v in lax.all_gather(bits, "z")])
        cuts = jnp.moveaxis(states.reshape(2, size, width, -1), 1, 0).astype(BF16)
        parts = lax.all_to_all(cuts, "z", 0, 0, tiled=True).astype(F32)
        sums = jnp.sum(weights[:, :, :, None] * parts[:, None], axis=0)
        back = lax.all_to_all(sums.astype(BF16), "z", 0, 0, tiled=True).astype(F32)
        return jnp.moveaxis(back, 0, 1).reshape(states.shape), weights
    ring = lambda k: lax.rem(z + k + size, size)

    def cut(k):
        part = lax.dynamic_slice_in_dim(states, k * width, width, 1).astype(BF16)
        return part if weights is not None else jnp.concatenate((part, bits), axis=1)

    parts = [cut(z)] + [shift(cut(ring(hop)), "z", hop) for hop in range(1, size)]
    if weights is None:
        everyone = jnp.stack([decay(p[:, width:]) for p in parts])
        spans = [
            lax.dynamic_index_in_dim(everyone, lax.rem(z - k + size, size), 0, False)
            for k in range(size)
        ]
        weights = gap_decays(spans)
        parts = [p[:, :width] for p in parts]
    results = []
    for away in range(size):
        to = lax.dynamic_index_in_dim(weights, ring(away), 1, False)
        total = 0.0
        for hop in range(size):
            weight = lax.dynamic_index_in_dim(to, ring(-hop), 0, False)
            total = total + weight[:, None] * parts[hop].astype(F32)
        results.append(total)
    back = [results[0]] + [
        shift(results[hop].astype(BF16), "z", hop).astype(F32) for hop in range(1, size)
    ]
    whole = jnp.zeros(states.shape, F32)
    for hop in range(size):
        whole = lax.dynamic_update_slice_in_dim(whole, back[hop], ring(-hop) * width, 1)
    return whole, weights


def local(
    tokens,
    segments,
    out_grad,
    norm_gain,
    in_weight,
    conv_weight,
    conv_bias,
    dt_bias,
    a_log,
    skip,
    out_gain,
    out_weight,
):
    _, length, features = tokens.shape
    edge = CONV - 1
    layer_count, in_rows = in_weight.shape[:2]
    out_rows = out_weight.shape[1]
    layers = range(layer_count)
    q = member()
    owner = q.reshape(1)
    span = 2 * length
    row_count = 2 * span

    near = lax.axis_size("z") <= NEAR
    x_place = lax.axis_index("x").reshape(1)
    cuts = cut_weights(owner, in_weight)
    size = lax.axis_size("z")
    place = jnp.stack((lax.axis_index("z"), lax.axis_index("x")))
    exchanged = [around_team(parts) for parts in cuts]
    moved = [lax.ppermute(out_weight[k], ("x", "y"), TURN) for k in layers]
    nowhere = jnp.zeros((1,), jnp.int32)

    def fetch_rows(rows):
        return lax.all_gather(rows, ("z", "x"), axis=0, tiled=True)

    def fetch_columns(layer_id, after):
        gathered = lax.all_gather(all_piece(owner, exchanged[layer_id], after), ("x", "z"))
        return arrange(nowhere, gathered.reshape((2, size) + gathered.shape[1:]))

    if near:
        wide_line, wide_all = fetch(wide_piece(owner, exchanged[0]))

    seg_now = team_gather(segments.astype(F32).reshape(length))
    prev_seg = step_line(seg_now[:, span - edge :], "z", 1)
    seg_ext = jnp.concatenate((prev_seg, seg_now), axis=1)
    seg = seg_table(seg_now, seg_ext[:, edge - 1])
    mask = mask_table(seg_ext, edge)
    spread = spread_matrix()
    all_taps, all_par, all_rows = cut_params(
        owner, (conv_weight, conv_bias, dt_bias, a_log, skip, out_gain, spread), exchanged[0][1:]
    )

    stream = tokens.astype(F32).reshape(length, features)
    saved, full = [], []
    for layer_id in layers:
        taps, par, rows = all_taps[layer_id], all_par[layer_id], all_rows[layer_id]
        first, final = layer_id == 0, layer_id == layer_count - 1
        fast = near and first
        x_order = x_place if fast else nowhere
        normed = norm_rows(
            x_order,
            tokens.reshape(length, features) if first else stream,
            norm_gain[layer_id : layer_id + 1],
            wide_line[1:2] if fast else [],
        )
        normed = team_gather(normed)
        earlier = step_line(normed[:, span - 16 :], "z", 1).reshape(32, features)
        normed = normed.reshape(row_count, features)
        if first:
            last_grad = team_gather(tie(out_grad.reshape(length, features), normed))
        dot = partial(jnp.dot, preferred_element_type=F32)
        if fast:
            piece = gate_piece(
                owner, exchanged[0], moved[0], wide_line[1:] + [normed, seg, mask, all_taps]
            )
            gathered = lax.all_gather(piece, ("x", "z")).reshape((2, size) + piece.shape)
            full_gate, full_out = arrange_both(x_place, gathered)
            full_wide = whole_columns(place, wide_all, [earlier])
        elif first:
            full_wide, full_gate = fetch_columns(0, [])
        else:
            full_wide, full_gate = next_columns
        wide = dot(normed, full_wide).reshape(2, span, WIDE)
        if not fast:
            full_out = fetch_rows(moved[0]) if first else next_rows
        gate_raw = dot(normed, full_gate).reshape(2, span, INNER_Q)
        full.append((full_wide, full_gate, full_out))
        halo = dot(earlier, full_wide).reshape(2, 16, WIDE)[:, 8:].astype(BF16).astype(F32)
        bc_own = conv_forward(
            wide, halo, taps, mask, 128, TILE
        )[..., :BC_Q]
        bc_same = y_swap(bc_own)
        bc = jnp.concatenate(
            in_order((bc_own, core_swap(bc_own)[::-1], bc_same, core_swap(bc_same)[::-1])), axis=-1
        )
        heads_x = conv_forward(wide, halo, taps, mask, INNER_Q, 0)
        scan_in = (heads_x, bc, wide, seg, par, spread)
        before, reach, end, total_reach, bits = scan_states(
            *scan_in, after=[last_grad] if first else []
        )
        start, weights = mix_states(end, bits)
        if not final:
            next_columns = fetch_columns(layer_id + 1, [start])
            next_rows = fetch_rows(tie(moved[layer_id + 1], start))
        inside = scan_inside(*scan_in)
        scan_y, gated, square = scan_outer(
            inside, *scan_in, before, reach, start, gate_raw, rows,
        )
        scale = lax.rsqrt(team_sum(square) / INNER + EPS)
        normed_y = scale_rows(gated, scale, rows)
        normed_y = normed_y.reshape(row_count, INNER_Q)
        sequence = lambda v, k: lax.slice_in_dim(v, k * span, (k + 1) * span, axis=0)
        branch_far = dot(sequence(normed_y, 1), full_out)
        branch = dot(sequence(normed_y, 0), full_out)
        saved.append(
            (
                stream,
                normed,
                gate_raw,
                halo,
                scan_in,
                (before, reach, start),
                (end, total_reach),
                weights,
                scan_y,
                gated,
                scale,
                normed_y,
                taps,
                rows,
            )
        )
        stream = stream + team_scatter(branch, branch_far)
    grad_stream = out_grad.astype(F32).reshape(length, features)
    in_parts = [None] * layer_count
    out_shards = [None] * layer_count
    small = [None] * layer_count
    for layer_id in reversed(layers):
        (
            stream_in,
            normed,
            gate_raw,
            halo,
            scan_in,
            states_before,
            states_end,
            weights,
            scan_y,
            gated,
            scale,
            normed_y,
            taps,
            rows,
        ) = saved[layer_id]
        heads_x, scan_rest = scan_in[0], scan_in[1:]
        wide = scan_in[2]
        full_wide, full_gate, full_out = full[layer_id]
        last = layer_id == 0
        grad_branch = team_gather(grad_stream.astype(BF16)) if last_grad is None else last_grad
        last_grad = None
        grad_branch = grad_branch.reshape(row_count, features)
        out_full_grad = jnp.einsum("ri,rd->id", normed_y, grad_branch, preferred_element_type=F32)
        back = partial(jnp.einsum, "rp,dp->rd", preferred_element_type=F32)
        grad_normed_y = back(grad_branch, full_out).reshape(2, span, INNER_Q)
        along, grad_gain = gate_along(grad_normed_y, gated, rows, scale)
        along = team_sum(along)
        grad_ssd, grad_gate, after, beyond, grad_start = gate_back(
            grad_normed_y, gated, scan_y, heads_x, gate_raw, *scan_rest, rows, scale, along,
            [out_full_grad],
        )
        turn = partial(jnp.einsum, "rd,rp->dp", preferred_element_type=F32)
        grad_gate = grad_gate.reshape(row_count, INNER_Q)
        gate_grad = turn(normed, grad_gate)
        fast = near and last
        x_order = x_place if fast else nowhere
        both = both_by_owner(x_order, gate_grad, out_full_grad, size, in_rows)
        both_total = sum_to_owner(both)
        gate_total = both_total[:TEAM]
        out_total = both_total[TEAM:].reshape(2, 2, in_rows, INNER_Q).swapaxes(1, 2)
        out_total = out_total.reshape(out_rows, features)
        out_shards[layer_id] = lax.ppermute(out_total, ("x", "y"), TURN).astype(F32)
        grad_end, _ = mix_states(grad_start, None, weights.swapaxes(0, 1))
        grad_inside = scan_inside_back(*scan_in, grad_ssd, after=[both])
        grad_x, grad_bc, grad_raw, head_sums, skip_sums = scan_outer_back(
            *grad_inside,
            *scan_in,
            *states_before,
            after,
            beyond,
            grad_end,
            *states_end,
            grad_ssd,
            scan_y,
            rows,
        )
        blocks = [grad_bc[..., BC_Q * k : BC_Q * k + BC_Q].astype(BF16) for k in range(TEAM)]
        turned = lambda k: lax.select_n(q ^ k, *blocks)
        half = lambda k: turned(k).astype(F32) + core_swap(turned(k ^ 1)).astype(F32)[::-1]
        grad_bc_own = half(0) + y_swap(half(2).astype(BF16)).astype(F32)
        grad_tile = jnp.pad(grad_bc_own, ((0, 0), (0, 0), (0, 128 - BC_Q)))

        edge_in = jnp.concatenate(
            (halo[:, 8 - edge :], wide[:, :edge].astype(BF16).astype(F32)), axis=1
        )
        edge_conv = lambda v: conv_piece(seg_ext[:, : 2 * edge], v, taps[:CONV], taps[CONV])
        edge_grad = jnp.concatenate((grad_x[:, :edge], grad_tile[:, :edge]), axis=-1)
        edge_grad = jax.vjp(edge_conv, edge_in)[1](edge_grad)[0][:, :edge].astype(BF16)
        returned = step_line(edge_grad, "z", -1).astype(F32)
        returned = jnp.pad(returned, ((0, 0), (8 - edge, 0), (0, 0)))
        grad_conv_x, conv_sums = conv_backward(
            wide, halo, taps, mask, grad_x, returned, INNER_Q, 0
        )
        grad_conv_tile, tile_sums = conv_backward(
            wide, halo, taps, mask, grad_tile, returned, 128, TILE
        )
        grad_wide = jnp.concatenate(
            (grad_conv_x, grad_conv_tile[..., :BC_Q], grad_raw[..., BC_Q:].astype(BF16)), axis=-1
        ).reshape(row_count, WIDE)
        in_grad = turn(normed, grad_wide)
        if fast:
            far, own = cut_wide(place, in_grad, size, in_rows)
            wide_x = [x_swap(v) for v in far]
            wide_z, total = send_sums(own, wide_x)
            grad_wide = tie(grad_wide, *far)
        else:
            wide_z, total = [], sum_to_owner(by_owner(x_order, in_grad, size, in_rows)).astype(F32)
        in_parts[layer_id] = around_team(grad_parts(owner, gate_total, total, wide_z))
        full_wide, full_gate, _ = full[layer_id]
        sequence = lambda v, k: lax.slice_in_dim(v, k * span, (k + 1) * span, axis=0)
        both_back = lambda k: back(sequence(grad_wide, k), full_wide) + back(
            sequence(grad_gate, k), full_gate
        )
        grad_far, grad_normed = both_back(1), both_back(0)
        norm_grad = jnp.sum(in_grad * full_wide.astype(F32), axis=1)
        norm_grad = norm_grad + jnp.sum(gate_grad * full_gate.astype(F32), axis=1)
        if fast:
            norm_grad = x_first(norm_grad)
            grad_normed = tie(grad_normed, wide_x[1])
        norm_grad = norm_grad / norm_gain[layer_id]
        grad_normed = team_scatter(grad_normed, grad_far)
        if fast:
            grad_normed = x_first(grad_normed)
        else:
            grad_normed = tie(grad_normed, both_total)
        _, pull_norm = jax.vjp(lambda v: norm_piece(v, norm_gain[layer_id]), stream_in)
        (grad_inner,) = pull_norm(grad_normed)
        grad_stream = grad_stream + grad_inner
        small[layer_id] = pack_small(
            conv_sums, tile_sums, head_sums, skip_sums, grad_gain, norm_grad.reshape(1, features),
            spread,
        )
    mixed = stream.reshape(1, length, features).astype(BF16)
    pack = xor_sum(jnp.stack(small), "x")
    if near:
        pack = tie(pack, *wide_x)
    pack = xor_sum(pack, "z")
    if near:
        pack = tie(pack, *wide_z)
    across = y_swap(pack)
    packs = (pack, core_swap(pack), across, core_swap(across))
    norm_sum, taps_sum, bias_sum, dt_sum, decay_sum, skip_sum, gain_sum = open_small(
        owner, packs, features
    )
    return (
        mixed,
        grad_stream.reshape(1, length, features),
        norm_sum,
        join_weights(owner, in_parts),
        taps_sum,
        bias_sum,
        dt_sum,
        decay_sum,
        skip_sum,
        gain_sum,
        jnp.stack(out_shards),
    )


def solution(mesh):
    rows, spans = mesh.devices.shape
    split = Mesh(mesh.devices.reshape(rows // 2, 2, spans // 2, 2), ("x", "core", "z", "y"))
    tokens = P(("x", "core"), ("z", "y"), None)
    weight = P(None, ("x", "core", "z", "y"), None)
    return jax.shard_map(
        local,
        mesh=split,
        in_specs=(
            tokens,
            P(("x", "core"), ("z", "y")),
            tokens,
            P(),
            weight,
            P(),
            P(),
            P(),
            P(),
            P(),
            P(),
            weight,
        ),
        out_specs=(tokens, tokens, P(), weight, P(), P(), P(), P(), P(), P(), weight),
        check_vma=False,
    )
```

```python
from functools import partial

import jax
import jax.numpy as jnp
from jax import lax
from jax.experimental import pallas as pl
from jax.experimental.pallas import tpu as pltpu
from jax.sharding import Mesh
from jax.sharding import PartitionSpec as P

HEADS = 48
HEADDIM = 64
STATE = 128
CONV = 4
INNER = 3072
CONVDIM = 3328

TEAM = 4
HEADS_Q = HEADS // TEAM
INNER_Q = INNER // TEAM
BC_Q = 2 * STATE // TEAM
CONV_Q = INNER_Q + BC_Q
WIDE = 896

EPS = 1e-05
VMEM_BYTES = 40 * 1024 * 1024
STEP_BYTES = 20 * 1024 * 1024
NEAR = 4
SWAP = [(0, 1), (1, 0)]
BF16 = jnp.bfloat16
F32 = jnp.float32


def shift(block, axis, distance):
    size = lax.axis_size(axis)
    return lax.ppermute(block, axis, [(i, (i + distance) % size) for i in range(size)])


def step_line(block, axis, distance):
    devices = range(lax.axis_size(axis))
    return lax.ppermute(block, axis, [(i, i + distance) for i in devices if i + distance in devices])


def core_swap(block):
    return lax.ppermute(block, "core", SWAP)


def y_swap(block):
    return lax.ppermute(block, "y", SWAP)


def diagonal_swap(block):
    return lax.ppermute(block, ("core", "y"), [(0, 3), (1, 2), (2, 1), (3, 0)])


def xor_sum(values, axis):
    size = lax.axis_size(axis)
    bit = 1
    while bit < size:
        values = tie(values + lax.ppermute(values, axis, [(i, i ^ bit) for i in range(size)]))
        bit *= 2
    return values


def member():
    return lax.axis_index("y") * 2 + lax.axis_index("core")


def in_order(parts):
    q = member()
    return [lax.select_n(q ^ j, *parts) for j in range(TEAM)]


def around_team(blocks):
    return blocks[0], core_swap(blocks[1]), y_swap(blocks[2]), diagonal_swap(blocks[3])


def by_y(own, other):
    first = lax.axis_index("y") == 0
    return jnp.where(first, jnp.concatenate((own, other), 1), jnp.concatenate((other, own), 1))


def team_gather(block):
    pair = jnp.stack((block, core_swap(block)))
    crossed = y_swap(block)
    other = jnp.stack((crossed, core_swap(crossed)))
    return by_y(pair, other)


def team_scatter(own, other):
    total = own + core_swap(other.astype(BF16)).astype(F32)
    half = total.shape[0] // 2
    y = lax.axis_index("y")
    mine = lax.dynamic_slice_in_dim(total, y * half, half, 0)
    theirs = lax.dynamic_slice_in_dim(total, (1 - y) * half, half, 0)
    return mine + y_swap(theirs.astype(BF16)).astype(F32)


def team_sum(values):
    across = core_swap(values) + diagonal_swap(values)
    return (values + y_swap(values)) + across[::-1]


def x_swap(block):
    return lax.ppermute(block, "x", SWAP)


def line_pieces(piece):
    return [piece] + [shift(piece, "z", hop) for hop in range(1, lax.axis_size("z"))]


def fetch(piece):
    line = line_pieces(piece)
    return line, line + [x_swap(p) for p in line]


def sum_to_owner(blocks):
    flat = blocks.reshape((-1,) + blocks.shape[2:])
    return lax.psum_scatter(flat, ("x", "z"), scatter_dimension=0)


TURN = [(0, 0), (1, 2), (2, 1), (3, 3)]


def x_first(values):
    low, high = jnp.split(values, 2, axis=-1)
    first = lax.axis_index("x") == 0
    return jnp.where(first, jnp.concatenate((low, high), -1), jnp.concatenate((high, low), -1))


def rms_scale(values):
    return values * lax.rsqrt(jnp.mean(values * values, axis=-1, keepdims=True) + EPS)


def norm_piece(stream, norm_scale):
    return rms_scale(stream) * norm_scale


def conv_piece(seg_ext, extended, conv_taps, conv_shift):
    length = extended.shape[-2] - CONV + 1
    seg_here = seg_ext[..., CONV - 1 :]
    summed = conv_shift
    for offset in range(CONV):
        same_doc = (seg_ext[..., offset : offset + length] == seg_here)[..., None]
        summed = summed + conv_taps[offset] * extended[..., offset : offset + length, :] * same_doc
    return jax.nn.silu(summed)


CHUNK = 128
LANE = 64
NEVER = -1e30
TILE = INNER_Q // 128


def split_parts(values):
    high = values.astype(BF16)
    rest = values - high.astype(F32)
    middle = rest.astype(BF16)
    return high, middle, (rest - middle.astype(F32)).astype(BF16)


def mm(a, b, over=(1, 0)):
    return lax.dot_general(
        a, b, (((over[0],), (over[1],)), ((), ())), preferred_element_type=F32
    )


def exact_mm(values, ones, over=(1, 0)):
    high, middle, low = split_parts(values)
    return (mm(low, ones, over) + mm(middle, ones, over)) + mm(high, ones, over)


def spread_mm(values, ones, over=(1, 0)):
    high, low = halves(values)
    return mm(low, ones, over) + mm(high, ones, over)


def mm_exact(ones, values):
    high, middle, low = split_parts(values)
    return (mm(ones, low) + mm(ones, middle)) + mm(ones, high)


def halves(values):
    high = values.astype(BF16)
    return high, (values - high.astype(F32)).astype(BF16)


def mm_wide(narrow, values, over=(1, 0)):
    high, low = halves(values)
    return mm(narrow, low, over) + mm(narrow, high, over)


def softplus(values):
    tail = jnp.exp(-jnp.abs(values))
    series = tail * (1.0 - tail * (0.5 - tail * (1.0 / 3.0)))
    return jnp.maximum(values, 0.0) + jnp.where(tail < 0.01, series, jnp.log(1.0 + tail))


def sigmoid(values):
    return 1.0 / (1.0 + jnp.exp(-values))


def grids(shape):
    return lax.broadcasted_iota(jnp.int32, shape, 0), lax.broadcasted_iota(jnp.int32, shape, 1)


def column(row):
    return jnp.broadcast_to(row, (CHUNK, CHUNK)).T


def step_terms(raw_ref, par_ref):
    down, across = grids((CHUNK, CHUNK))
    lower = (down >= across).astype(F32).astype(BF16)
    step = softplus(raw_ref[0] + par_ref[0:1])
    sums = mm_exact(lower, -par_ref[1:2] * step)
    return step, sums, sums[CHUNK - 1 :]


def seg_terms(seg_ref):
    return column(seg_ref[0, 0, 0:1]), seg_ref[0, 0, 0:1], seg_ref[0, 0, 1:2], seg_ref[0, 0, 2:3]


def chunk_decay(total, before, last, spread):
    kept = jnp.exp(total) * (before == last).astype(F32)
    return exact_mm(jnp.broadcast_to(kept, (8, CHUNK)), spread)


def state_kernel(x, bc, raw, seg, par, spread, before_out, reach_out, end_out, total_out, bits_out, state, reach):
    @pl.when(pl.program_id(1) == 0)
    def _():
        state[...] = jnp.zeros_like(state)
        reach[...] = jnp.ones_like(reach)

    step, sums, total = step_terms(raw, par)
    lines, _, before, last = seg_terms(seg)
    before_out[0, 0] = state[...]
    reach_out[0, 0] = reach[...]
    leaving = jnp.where(lines == last, jnp.exp(total - sums), 0.0)
    fed = (x[0].astype(F32) * spread_mm(step, spread[...])).astype(BF16).astype(F32)
    fed = fed * spread_mm(leaving, spread[...])
    decay = chunk_decay(total, before, last, spread[...])
    state[...] = state[...] * decay[0:1] + mm_wide(bc[0, :, :STATE], fed, (0, 0))
    reach[...] = reach[...] * decay
    end_out[0] = state[...]
    total_out[0] = reach[...]
    lines = [v[0:1] for v in split_parts(reach[...])]
    bits_out[0] = jnp.concatenate(lines + [jnp.zeros((13, INNER_Q), BF16)], axis=0)


def inside_kernel(x, bc, raw, seg, par, spread, y_out):
    step, sums, _ = step_terms(raw, par)
    lines, row, _, _ = seg_terms(seg)
    down, across = grids((CHUNK, CHUNK))
    bias = jnp.where((lines == row) & (down >= across), 0.0, NEVER)
    scores = mm(bc[0, :, STATE:], bc[0, :, :STATE], (1, 1))
    turned = sums.T
    fed = (x[0].astype(F32) * spread_mm(step, spread[...])).astype(BF16)
    for pair in range(HEADS_Q // 2):
        lanes = slice(pair * 128, pair * 128 + 128)
        mixing = []
        for head in (LANE + 2 * pair, LANE + 2 * pair + 1):
            gap = jnp.broadcast_to(sums[:, head : head + 1], (CHUNK, CHUNK)) - turned[head : head + 1]
            mixing.append((scores * jnp.exp(gap + bias)).astype(BF16))
        both = mm(jnp.concatenate(mixing, axis=0), fed[:, lanes])
        y_out[0, :, lanes] = jnp.where(across < HEADDIM, both[:CHUNK], both[CHUNK:])


def outer_kernel(
    y_in, x, bc, raw, seg, par, spread, before, reach, start, gate, rows, y_out, gated_out, square_out
):
    _, sums, _ = step_terms(raw, par)
    lines, _, ahead, _ = seg_terms(seg)
    entering = spread_mm(jnp.where(lines == ahead, jnp.exp(sums), 0.0), spread[...])
    state = before[0, 0] + reach[0, 0, 0:1] * start[0]
    y = y_in[0] + entering * mm_wide(bc[0, :, STATE:], state)
    y_out[0] = y
    raw_gate = gate[0]
    gated = (y + rows[0:1] * x[0].astype(F32)) * (raw_gate * sigmoid(raw_gate))
    gated_out[0] = gated
    square = gated * gated
    folded = square[:, :128]
    for tile in range(1, INNER_Q // 128):
        folded = folded + square[:, tile * 128 : tile * 128 + 128]
    square_out[0, 0] = jnp.sum(folded.T, axis=0, keepdims=True)


def along_kernel(grad, gated, rows, scale, along_out, gain_out):
    @pl.when(pl.program_id(1) == 0)
    def _():
        gain_out[...] = jnp.zeros_like(gain_out)

    product = grad[0] * gated[0]
    weighed = product * rows[1:2]
    folded = weighed[:, :128]
    for tile in range(1, INNER_Q // 128):
        folded = folded + weighed[:, tile * 128 : tile * 128 + 128]
    along_out[0, 0] = jnp.sum(folded.T, axis=0, keepdims=True)
    lines = jnp.concatenate([column(scale[0, 0])] * (INNER_Q // 128), axis=1)
    gain_out[0] += jnp.sum((product * lines).reshape(CHUNK // 8, 8, INNER_Q), axis=0)


def gate_back_kernel(
    grad, gated, y, x, gate, bc, raw, seg, par, spread, rows, scale, along,
    grad_out, gate_out, after_out, beyond_out, start_out, state, reach,
):
    @pl.when(pl.program_id(1) == 0)
    def _():
        state[...] = jnp.zeros_like(state)
        reach[...] = jnp.ones_like(reach)

    wide = lambda row: jnp.concatenate([column(row)] * (INNER_Q // 128), axis=1)
    factor = scale[0, 0]
    pull = factor * factor * factor * along[0, 0] * (1.0 / INNER)
    grad_gated = grad[0] * rows[1:2] * wide(factor) - gated[0] * wide(pull)
    raw_gate = gate[0]
    sig = sigmoid(raw_gate)
    grad_y = (grad_gated * (raw_gate * sig)).astype(BF16)
    ssd_y = y[0] + rows[0:1] * x[0].astype(F32)
    gate_out[0] = (grad_gated * ssd_y * (sig * (1.0 + raw_gate * (1.0 - sig)))).astype(BF16)
    grad_out[0] = grad_y

    _, sums, total = step_terms(raw, par)
    lines, _, before, last = seg_terms(seg)
    after_out[0, 0] = state[...]
    beyond_out[0, 0] = reach[...]
    entering = spread_mm(jnp.where(lines == before, jnp.exp(sums), 0.0), spread[...])
    decay = chunk_decay(total, before, last, spread[...])
    fed = grad_y.astype(F32) * entering
    state[...] = state[...] * decay[0:1] + mm_wide(bc[0, :, STATE:], fed, (0, 0))
    reach[...] = reach[...] * decay
    start_out[0] = state[...]


def inside_back_kernel(x, bc, raw, seg, par, spread, grad, fed_out, b_out, c_out):
    step, sums, _ = step_terms(raw, par)
    lines, row, _, _ = seg_terms(seg)
    down, across = grids((CHUNK, CHUNK))
    bias = jnp.where((lines == row) & (across >= down), 0.0, NEVER)
    b_in, c_in = bc[0, :, :STATE], bc[0, :, STATE:]
    scores = mm(b_in, c_in, (1, 1))
    turned = sums.T
    fed = (x[0].astype(F32) * spread_mm(step, spread[...])).astype(BF16)
    grad_scores = jnp.zeros((CHUNK, CHUNK), F32)
    for pair in range(HEADS_Q // 2):
        lanes = slice(pair * 128, pair * 128 + 128)
        fed_pair, grad_pair = fed[:, lanes], grad[0, :, lanes]
        none = jnp.zeros_like(fed_pair)
        apart = jnp.concatenate(
            (jnp.where(across < HEADDIM, fed_pair, none), jnp.where(across < HEADDIM, none, fed_pair)),
            axis=0,
        )
        grad_mixing = mm(apart, grad_pair, (1, 1))
        mixing = []
        for which in range(2):
            head = LANE + 2 * pair + which
            gap = turned[head : head + 1] - jnp.broadcast_to(sums[:, head : head + 1], (CHUNK, CHUNK))
            decays = jnp.exp(gap + bias)
            mixing.append((scores * decays).astype(BF16))
            grad_scores = grad_scores + grad_mixing[which * CHUNK : which * CHUNK + CHUNK] * decays
        both = mm(jnp.concatenate(mixing, axis=0), grad_pair)
        fed_out[0, :, lanes] = jnp.where(across < HEADDIM, both[:CHUNK], both[CHUNK:])
    grad_scores = grad_scores.astype(BF16)
    b_out[0] = mm(grad_scores, c_in)
    c_out[0] = mm(grad_scores, b_in, (0, 0))


def outer_back_kernel(
    fed_in, b_in, c_in, x, bc, raw, seg, par, spread, before, reach, start, after, beyond, grad_end,
    end, total_reach, grad, y, rows,
    x_out, bc_out, raw_out, sums_out, skip_out, carry,
):
    @pl.when(pl.program_id(1) == 0)
    def _():
        sums_out[...] = jnp.zeros_like(sums_out)
        skip_out[...] = jnp.zeros_like(skip_out)
        last_state = end[0] + total_reach[0, 0:1] * start[0]
        meet = jnp.sum((grad_end[0] * last_state).reshape(STATE // 8, 8, INNER_Q), axis=0)
        meet = jnp.sum(spread_mm(meet, spread[...], (1, 1)), axis=0, keepdims=True)
        carry[...] = jnp.broadcast_to(meet, carry.shape)

    step, sums, total = step_terms(raw, par)
    lines, _, ahead, last = seg_terms(seg)
    ones = spread[...]
    state = (before[0, 0] + reach[0, 0, 0:1] * start[0]).astype(BF16)
    grad_state = after[0, 0] + beyond[0, 0, 0:1] * grad_end[0]
    values = x[0].astype(F32)
    grad_y = grad[0].astype(F32)
    wide_step = spread_mm(step, ones)
    leaving = spread_mm(jnp.where(lines == last, jnp.exp(total - sums), 0.0), ones)
    entering = spread_mm(jnp.where(lines == ahead, jnp.exp(sums), 0.0), ones)
    fed = (values * wide_step).astype(BF16).astype(F32)
    grad_fed = fed_in[0] + leaving * mm_wide(bc[0, :, :STATE], grad_state)
    x_out[0] = wide_step * grad_fed + rows[0:1] * grad_y
    bc_out[0, :, :STATE] = b_in[0] + mm((leaving * fed).astype(BF16), grad_state.astype(BF16), (1, 1))
    bc_out[0, :, STATE:] = c_in[0] + mm((entering * grad_y).astype(BF16), state, (1, 1))
    skip_out[0] += jnp.sum((grad_y * values).reshape(CHUNK // 8, 8, INNER_Q), axis=0)

    by_step = spread_mm(values * grad_fed, ones, (1, 1))
    flow = spread_mm(grad_y * y[0] - fed * grad_fed, ones, (1, 1))
    down, across = grids((CHUNK, CHUNK))
    upper = (across >= down).astype(F32).astype(BF16)
    grad_log = mm_exact(upper, flow) + carry[0:1]
    carry[...] = jnp.broadcast_to(grad_log[0:1], carry.shape)
    rate = par[1:2]
    grad_raw = (by_step - rate * grad_log) * sigmoid(raw[0] + par[0:1])
    raw_out[0] = grad_raw
    fold = lambda v: jnp.sum(v.reshape(CHUNK // 8, 8, CHUNK), axis=0)
    sums_out[0, 0:8] += fold(-rate * step * grad_log)
    sums_out[0, 8:16] += fold(grad_raw)


def chunk_spec(width, back=0, column_block=0):
    turn = (lambda c: back - 1 - c) if back else (lambda c: c)
    return pl.BlockSpec((1, CHUNK, width), lambda s, c: (s, turn(c), column_block))


def per_chunk(lines, width, back=0):
    turn = (lambda c: back - 1 - c) if back else (lambda c: c)
    return pl.BlockSpec((1, 1, lines, width), lambda s, c: (s, turn(c), 0, 0))


def per_sequence(lines, width):
    return pl.BlockSpec((1, lines, width), lambda s, c: (s, 0, 0))


def fixed(lines, width):
    return pl.BlockSpec((lines, width), lambda s, c: (0, 0))


def shaped(shape, dtype=F32):
    return jax.ShapeDtypeStruct(shape, dtype)


def call(kernel, name, chunks, ins, outs, operands, scratch=(), flops=0, after=()):
    in_specs = [spec for spec, _ in zip(ins, operands, strict=True)]
    moved = sum(v.size * v.dtype.itemsize for v in operands)
    moved += sum(v.size * v.dtype.itemsize for _, v in outs)
    count, skipped = len(in_specs), len(after)
    in_specs = in_specs + [pl.BlockSpec(memory_space=pl.ANY)] * skipped
    operands = tuple(operands) + tuple(after)
    return pl.pallas_call(
        lambda *refs: kernel(*refs[:count], *refs[count + skipped :]),
        name=name,
        grid=(2, chunks),
        in_specs=in_specs,
        out_specs=[spec for spec, _ in outs],
        out_shape=[shape for _, shape in outs],
        scratch_shapes=list(scratch),
        cost_estimate=pl.CostEstimate(flops=flops, bytes_accessed=moved, transcendentals=0),
        compiler_params=pltpu.CompilerParams(
            dimension_semantics=("arbitrary", "arbitrary"), vmem_limit_bytes=STEP_BYTES
        ),
    )(*operands)


STATE_SCRATCH = (pltpu.VMEM((STATE, INNER_Q), F32), pltpu.VMEM((8, INNER_Q), F32))


def scan_states(x, bc, raw, seg, par, spread, after=()):
    span = x.shape[1]
    n = span // CHUNK
    return call(
        state_kernel, "chunk_states", n,
        [chunk_spec(INNER_Q), chunk_spec(2 * STATE), chunk_spec(128, 0, TILE), per_chunk(8, 128), fixed(8, 128),
         fixed(128, INNER_Q)],
        [(per_chunk(STATE, INNER_Q), shaped((2, n, STATE, INNER_Q))), (per_chunk(8, INNER_Q), shaped((2, n, 8, INNER_Q))),
         (per_sequence(STATE, INNER_Q), shaped((2, STATE, INNER_Q))), (per_sequence(8, INNER_Q), shaped((2, 8, INNER_Q))),
         (per_sequence(16, INNER_Q), shaped((2, 16, INNER_Q), BF16))],
        (x, bc, raw, seg, par, spread), STATE_SCRATCH, 2 * 2 * span * STATE * INNER_Q, after=after,
    )


def scan_inside(x, bc, raw, seg, par, spread, after=()):
    span = x.shape[1]
    n = span // CHUNK
    return call(
        inside_kernel, "inside_chunks", n,
        [chunk_spec(INNER_Q), chunk_spec(2 * STATE), chunk_spec(128, 0, TILE), per_chunk(8, 128), fixed(8, 128),
         fixed(128, INNER_Q)],
        [(chunk_spec(INNER_Q), shaped(x.shape))],
        (x, bc, raw, seg, par, spread), (), 8 * 2 * span * CHUNK * INNER_Q, after=after,
    )[0]


def scan_outer(y, x, bc, raw, seg, par, spread, before, reach, start, gate, rows, after=()):
    span = x.shape[1]
    n = span // CHUNK
    return call(
        outer_kernel, "scan_and_gate", n,
        [chunk_spec(INNER_Q), chunk_spec(INNER_Q), chunk_spec(2 * STATE), chunk_spec(128, 0, TILE), per_chunk(8, 128), fixed(8, 128),
         fixed(128, INNER_Q), per_chunk(STATE, INNER_Q), per_chunk(8, INNER_Q), per_sequence(STATE, INNER_Q),
         chunk_spec(INNER_Q), fixed(8, INNER_Q)],
        [(chunk_spec(INNER_Q), shaped(x.shape)), (chunk_spec(INNER_Q), shaped(x.shape)),
         (per_chunk(1, 128), shaped((2, n, 1, 128)))],
        (y, x, bc, raw, seg, par, spread, before, reach, start, gate, rows), (), 8 * span * STATE * INNER_Q, after=after,
    )


def gate_along(grad, gated, rows, scale, after=()):
    span = gated.shape[1]
    n = span // CHUNK
    return call(
        along_kernel, "gate_along", n,
        [chunk_spec(INNER_Q), chunk_spec(INNER_Q), fixed(8, INNER_Q), per_chunk(1, 128)],
        [(per_chunk(1, 128), shaped((2, n, 1, 128))), (per_sequence(8, INNER_Q), shaped((2, 8, INNER_Q)))],
        (grad, gated, rows, scale), (), 10 * span * INNER_Q, after=after,
    )


def gate_back(grad, gated, y, x, gate, bc, raw, seg, par, spread, rows, scale, along, after=()):
    span = x.shape[1]
    n = span // CHUNK
    return call(
        gate_back_kernel, "gate_back_and_states", n,
        [chunk_spec(INNER_Q, n)] * 5 + [chunk_spec(2 * STATE, n), chunk_spec(128, n, TILE), per_chunk(8, 128, n), fixed(8, 128),
         fixed(128, INNER_Q), fixed(8, INNER_Q), per_chunk(1, 128, n), per_chunk(1, 128, n)],
        [(chunk_spec(INNER_Q, n), shaped(x.shape, BF16)), (chunk_spec(INNER_Q, n), shaped(x.shape, BF16)),
         (per_chunk(STATE, INNER_Q, n), shaped((2, n, STATE, INNER_Q))), (per_chunk(8, INNER_Q, n), shaped((2, n, 8, INNER_Q))),
         (per_sequence(STATE, INNER_Q), shaped((2, STATE, INNER_Q)))],
        (grad, gated, y, x, gate, bc, raw, seg, par, spread, rows, scale, along), STATE_SCRATCH,
        8 * span * STATE * INNER_Q, after=after,
    )


def scan_inside_back(x, bc, raw, seg, par, spread, grad, after=()):
    span = x.shape[1]
    n = span // CHUNK
    return call(
        inside_back_kernel, "inside_chunks_back", n,
        [chunk_spec(INNER_Q), chunk_spec(2 * STATE), chunk_spec(128, 0, TILE), per_chunk(8, 128), fixed(8, 128),
         fixed(128, INNER_Q), chunk_spec(INNER_Q)],
        [(chunk_spec(INNER_Q), shaped(x.shape)), (chunk_spec(STATE), shaped((2, span, STATE))),
         (chunk_spec(STATE), shaped((2, span, STATE)))],
        (x, bc, raw, seg, par, spread, grad), (), 24 * 2 * span * CHUNK * INNER_Q, after=after,
    )


def scan_outer_back(
    fed, b, c, x, bc, raw, seg, par, spread, before, reach, start, later, beyond, grad_end, end, total, grad, y, rows, after=()
):
    span = x.shape[1]
    n = span // CHUNK
    return call(
        outer_back_kernel, "scan_back", n,
        [chunk_spec(INNER_Q, n), chunk_spec(STATE, n), chunk_spec(STATE, n), chunk_spec(INNER_Q, n), chunk_spec(2 * STATE, n),
         chunk_spec(128, n, TILE), per_chunk(8, 128, n), fixed(8, 128), fixed(128, INNER_Q), per_chunk(STATE, INNER_Q, n),
         per_chunk(8, INNER_Q, n), per_sequence(STATE, INNER_Q), per_chunk(STATE, INNER_Q, n), per_chunk(8, INNER_Q, n),
         per_sequence(STATE, INNER_Q), per_sequence(STATE, INNER_Q), per_sequence(8, INNER_Q), chunk_spec(INNER_Q, n),
         chunk_spec(INNER_Q, n), fixed(8, INNER_Q)],
        [(chunk_spec(INNER_Q, n), shaped(x.shape)), (chunk_spec(2 * STATE, n), shaped((2, span, 2 * STATE))),
         (chunk_spec(128, n), shaped((2, span, 128))), (per_sequence(16, 128), shaped((2, 16, 128))),
         (per_sequence(8, INNER_Q), shaped((2, 8, INNER_Q)))],
        (fed, b, c, x, bc, raw, seg, par, spread, before, reach, start, later, beyond, grad_end, end, total, grad, y, rows),
        (pltpu.VMEM((8, 128), F32),), 24 * span * STATE * INNER_Q, after=after,
    )


def seg_table(seg_now, seg_before):
    span = seg_now.shape[1]
    rows = seg_now.reshape(2, span // CHUNK, 1, CHUNK)
    last = rows[..., -1:]
    before = jnp.concatenate((seg_before.reshape(2, 1, 1, 1), last[:, :-1]), axis=1)
    spread = lambda v: jnp.broadcast_to(v, rows.shape)
    return jnp.concatenate((rows, spread(before), spread(last)) + (rows,) * 5, axis=2)


def conv_terms(wide_ref, halo_ref, taps_ref, mask_ref, tail):
    own = wide_ref[0].astype(BF16).astype(F32)
    longer = jnp.concatenate((tail, own), axis=0)
    rows = [own]
    total = taps_ref[CONV : CONV + 1] + taps_ref[CONV - 1 : CONV] * own
    for back in range(1, CONV):
        same = jnp.concatenate([column(mask_ref[0, 0, back : back + 1])] * (own.shape[1] // 128), axis=1)
        earlier = longer[8 - back : 8 - back + CHUNK] * same
        rows.append(earlier)
        total = total + taps_ref[CONV - 1 - back : CONV - back] * earlier
    return own, rows, total


def conv_kernel(wide, halo, taps, mask, out, tail):
    @pl.when(pl.program_id(1) == 0)
    def _():
        tail[...] = halo[0].astype(F32)

    own, _, total = conv_terms(wide, halo, taps, mask, tail[...])
    tail[...] = own[CHUNK - 8 :]
    out[0] = (total * sigmoid(total)).astype(BF16)


def conv_back_kernel(wide, before, halo, taps, mask, grad, returned, out, sums_out, ahead):
    chunk = pl.num_programs(1) - 1 - pl.program_id(1)

    @pl.when(pl.program_id(1) == 0)
    def _():
        sums_out[...] = jnp.zeros_like(sums_out)
        ahead[...] = jnp.zeros_like(ahead)

    tail = jnp.where(chunk == 0, halo[0].astype(F32), before[0].astype(BF16).astype(F32))
    _, rows, total = conv_terms(wide, halo, taps, mask, tail)
    sig = sigmoid(total)
    pull = grad[0] * (sig * (1.0 + total * (1.0 - sig)))
    result = taps[CONV - 1 : CONV] * pull
    fold = lambda v: jnp.sum(v.reshape(CHUNK // 8, 8, v.shape[1]), axis=0)
    for back in range(1, CONV):
        same = jnp.concatenate([column(mask[0, 0, back : back + 1])] * (pull.shape[1] // 128), axis=1)
        masked = pull * same
        longer = jnp.concatenate((masked, ahead[8 * back - 8 : 8 * back]), axis=0)
        result = result + taps[CONV - 1 - back : CONV - back] * longer[back : back + CHUNK]
        ahead[8 * back - 8 : 8 * back] = masked[:8]
    for back in range(CONV):
        place = CONV - 1 - back
        sums_out[0, 8 * place : 8 * place + 8] += fold(pull * rows[back])
    sums_out[0, 8 * CONV : 8 * CONV + 8] += fold(pull)
    late = (pl.program_id(1) == 0).astype(F32) * returned[0].astype(F32)
    late = jnp.concatenate((jnp.zeros((CHUNK - 8, late.shape[1]), F32), late), axis=0)
    out[0] = (result + late).astype(BF16)


def conv_forward(wide, halo, taps, mask, width, at, after=()):
    n = wide.shape[1] // CHUNK
    lines = lambda rows: pl.BlockSpec((1, rows, width), lambda s, c: (s, 0, at))
    return call(
        conv_kernel, "conv", n,
        [chunk_spec(width, 0, at), lines(8), pl.BlockSpec((8, width), lambda s, c: (0, at)), per_chunk(8, 128)],
        [(chunk_spec(width), shaped(wide.shape[:2] + (width,), BF16))],
        (wide, halo, taps, mask), (pltpu.VMEM((8, width), F32),), 30 * wide.shape[1] * width, after=after,
    )[0]


def conv_backward(wide, halo, taps, mask, grad, returned, width, at, after=()):
    n = wide.shape[1] // CHUNK
    lines = lambda rows: pl.BlockSpec((1, rows, width), lambda s, c: (s, 0, at))
    steps = CHUNK // 8
    early = pl.BlockSpec(
        (1, 8, width), lambda s, c: (s, jnp.maximum((n - 1 - c) * steps - 1, 0), at)
    )
    return call(
        conv_back_kernel, "conv_back", n,
        [chunk_spec(width, n, at), early, lines(8), pl.BlockSpec((8, width), lambda s, c: (0, at)),
         per_chunk(8, 128, n), chunk_spec(width, n), lines(8)],
        [(chunk_spec(width, n), shaped(wide.shape[:2] + (width,), BF16)), (per_sequence(8 * CONV + 8, width), shaped((2, 8 * CONV + 8, width)))],
        (wide, wide, halo, taps, mask, grad, returned), (pltpu.VMEM((8 * CONV, width), F32),), 60 * wide.shape[1] * width, after=after,
    )


def mask_table(seg_ext, edge_rows):
    span = seg_ext.shape[1] - edge_rows
    here = seg_ext[:, edge_rows:]
    rows = [here == seg_ext[:, edge_rows - back : edge_rows - back + span] for back in range(CONV)]
    table = jnp.stack(rows + rows, axis=1).astype(F32)
    return jnp.moveaxis(table.reshape(2, 2 * CONV, span // CHUNK, CHUNK), 2, 1)


def tile_picks(owner, rows):
    down, across = grids((2 * STATE, 128))
    bc = (down - BC_Q * owner == across) & (across < BC_Q)
    down, across = grids((HEADS, 128))
    head = across - LANE
    dt = (down - HEADS_Q * owner == head) & (head >= 0) & (head < HEADS_Q)
    return bc.astype(F32), dt.astype(F32)


def cut_weights_kernel(q_ref, weight, *outs):
    for layer in range(weight.shape[0]):
        for k in range(TEAM):
            owner = q_ref[0] ^ k
            start = pl.multiple_of(owner * INNER_Q, 128)
            part = outs[layer * TEAM + k]
            part[:, :INNER_Q] = weight[layer, :, pl.ds(start, INNER_Q)]
            part[:, INNER_Q : 2 * INNER_Q] = weight[layer, :, pl.ds(INNER + start, INNER_Q)]
            bc, dt = tile_picks(owner, None)
            tile = mm(weight[layer, :, 2 * INNER : 2 * INNER + 2 * STATE], bc.astype(BF16))
            tile = tile + mm(weight[layer, :, INNER + CONVDIM :], dt.astype(BF16))
            part[:, 2 * INNER_Q :] = tile.astype(BF16)


def whole_spec(shape):
    return pl.BlockSpec(shape, lambda *_: (0,) * len(shape))


def whole_call(kernel, name, index, operands, outs, after=()):
    count, skipped = 1 + len(operands), len(after)
    return pl.pallas_call(
        lambda *refs: kernel(*refs[:count], *refs[count + skipped :]),
        name=name,
        grid_spec=pltpu.PrefetchScalarGridSpec(
            num_scalar_prefetch=1,
            grid=(1,),
            in_specs=[whole_spec(v.shape) for v in operands]
            + [pl.BlockSpec(memory_space=pl.ANY)] * skipped,
            out_specs=[whole_spec(s.shape) for s in outs],
        ),
        out_shape=list(outs),
        compiler_params=pltpu.CompilerParams(vmem_limit_bytes=VMEM_BYTES),
    )(index, *operands, *after)


def tie(value, *after):
    anywhere = pl.BlockSpec(memory_space=pl.ANY)
    return pl.pallas_call(
        lambda *refs: None,
        name="tie",
        in_specs=[anywhere] * (1 + len(after)),
        out_specs=anywhere,
        out_shape=shaped(value.shape, value.dtype),
        input_output_aliases={0: 0},
    )(value, *after)


def norm_kernel(x_ref, stream, gain, out):
    values = stream[...].astype(F32)
    mean = jnp.mean(values * values, axis=-1, keepdims=True)
    normed = (values * lax.rsqrt(mean + EPS) * gain[...]).astype(BF16)
    width = normed.shape[1] // 2
    x = x_ref[0]
    out[:, pl.ds(pl.multiple_of(x * width, 128), width)] = normed[:, :width]
    out[:, pl.ds(pl.multiple_of((1 - x) * width, 128), width)] = normed[:, width:]


def norm_rows(x, stream, gain, after=()):
    return whole_call(norm_kernel, "norm", x, (stream, gain), [shaped(stream.shape, BF16)], after)[0]


def scale_kernel(gated, scale, rows, out):
    lines = jnp.concatenate([column(scale[0, 0])] * (INNER_Q // 128), axis=1)
    out[0] = (gated[0] * lines * rows[1:2]).astype(BF16)


def scale_rows(gated, scale, rows, after=()):
    n = gated.shape[1] // CHUNK
    return call(
        scale_kernel, "scale_rows", n,
        [chunk_spec(INNER_Q), per_chunk(1, 128), fixed(8, INNER_Q)],
        [(chunk_spec(INNER_Q), shaped(gated.shape, BF16))],
        (gated, scale, rows), (), 4 * gated.size, after=after,
    )[0]


def cut_weights(q, weight):
    layers, rows = weight.shape[:2]
    outs = [shaped((rows, INNER_Q + WIDE), BF16)] * (TEAM * layers)
    outs = whole_call(cut_weights_kernel, "cut_weights", q, (weight,), outs)
    return [outs[TEAM * layer : TEAM * layer + TEAM] for layer in range(layers)]


def place_of(owner):
    return (owner % 2) * 2 + owner // 2


def wide_piece_kernel(q_ref, *refs):
    out = refs[-1]
    for k in range(TEAM):
        out[place_of(q_ref[0] ^ k)] = refs[k][:, INNER_Q:]


def gate_piece_kernel(q_ref, *refs):
    rows, out = refs[TEAM], refs[-1]
    for k in range(TEAM):
        out[place_of(q_ref[0] ^ k)] = refs[k][:, :INNER_Q]
    for block in range(TEAM):
        half = block % 2 * INNER_Q
        out[TEAM + block] = rows[block // 2, :, half : half + INNER_Q]


def all_piece_kernel(q_ref, *refs):
    out = refs[-1]
    for k in range(TEAM):
        out[place_of(q_ref[0] ^ k)] = refs[k][...]


def all_piece(q, parts, after=()):
    shape = (TEAM,) + parts[0].shape
    return whole_call(all_piece_kernel, "all_piece", q, parts, [shaped(shape, BF16)], after)[0]


def arrange_kernel(_, gathered, gate, wide):
    for x in range(2):
        for z in range(gate.shape[2]):
            for block in range(TEAM):
                rows = gathered[x, z, block]
                gate[x, block // 2, z, block % 2] = rows[:, :INNER_Q]
                wide[x, block // 2, z, block % 2] = rows[:, INNER_Q:]


def arrange(index, gathered):
    size, rows = gathered.shape[1], gathered.shape[3]
    outs = [shaped((2, 2, size, 2, rows, width), BF16) for width in (INNER_Q, WIDE)]
    gate, wide = whole_call(arrange_kernel, "arrange", index, (gathered,), outs)
    return wide.reshape(-1, WIDE), gate.reshape(-1, INNER_Q)


def by_owner_kernel(x_ref, grad, out):
    for side in range(2):
        x = x_ref[0] if side == 0 else 1 - x_ref[0]
        for z in range(out.shape[1]):
            for block in range(TEAM):
                out[x, z, block] = grad[side, block // 2, z, block % 2].astype(BF16)


def both_by_owner_kernel(x_ref, gate, out_grad, out):
    for side in range(2):
        x = x_ref[0] if side == 0 else 1 - x_ref[0]
        for z in range(out.shape[1]):
            for block in range(TEAM):
                upper, lower = block // 2, block % 2
                half = slice(lower * INNER_Q, lower * INNER_Q + INNER_Q)
                out[x, z, block] = gate[side, upper, z, lower].astype(BF16)
                out[side, z, TEAM + block] = out_grad[z, side, upper, :, half].astype(BF16)


def both_by_owner(x_first_of, gate, out_grad, size, rows):
    operands = (
        gate.reshape(2, 2, size, 2, rows, INNER_Q),
        out_grad.reshape(size, 2, 2, rows, 2 * INNER_Q),
    )
    outs = [shaped((2, size, 2 * TEAM, rows, INNER_Q), BF16)]
    return whole_call(both_by_owner_kernel, "both_by_owner", x_first_of, operands, outs)[0]


def by_owner(x_first_of, grad, size, rows):
    width = grad.shape[-1]
    operands = (grad.reshape(2, 2, size, 2, rows, width),)
    outs = [shaped((2, size, TEAM, rows, width), BF16)]
    return whole_call(by_owner_kernel, "by_owner", x_first_of, operands, outs)[0]


def wide_piece(q, parts, after=()):
    shape = (TEAM, parts[0].shape[0], WIDE)
    return whole_call(wide_piece_kernel, "wide_piece", q, parts, [shaped(shape, BF16)], after)[0]


def gate_piece(q, parts, rows, after=()):
    count = parts[0].shape[0]
    operands = tuple(parts) + (rows.reshape(2, count, -1),)
    outs = [shaped((2 * TEAM, count, INNER_Q), BF16)]
    return whole_call(gate_piece_kernel, "gate_piece", q, operands, outs, after)[0]


def arrange_both_kernel(x_ref, gathered, gate, out):
    for side in range(2):
        x = x_ref[0] if side == 0 else 1 - x_ref[0]
        for z in range(gate.shape[2]):
            for block in range(TEAM):
                upper, lower = block // 2, block % 2
                gate[side, upper, z, lower] = gathered[x, z, block]
                half = slice(lower * INNER_Q, lower * INNER_Q + INNER_Q)
                out[z, side, upper, :, half] = gathered[side, z, TEAM + block]


def arrange_both(x_first_of, gathered):
    size, rows = gathered.shape[1], gathered.shape[3]
    outs = [
        shaped((2, 2, size, 2, rows, INNER_Q), BF16),
        shaped((size, 2, 2, rows, 2 * INNER_Q), BF16),
    ]
    gate, out = whole_call(arrange_both_kernel, "arrange_both", x_first_of, (gathered,), outs)
    return gate.reshape(-1, INNER_Q), out.reshape(-1, 2 * INNER_Q)


def whole_wide_kernel(place, *refs):
    out = refs[-1]
    size = out.shape[2]
    for side in range(2):
        for hop in range(size):
            source = lax.rem(place[0] - hop + size, size)
            for block in range(TEAM):
                out[side, block // 2, source, block % 2] = refs[side * size + hop][block]


def whole_columns(place, pieces, after=()):
    size = len(pieces) // 2
    rows, width = pieces[0].shape[1:]
    outs = [shaped((2, 2, size, 2, rows, width), BF16)]
    whole = whole_call(whole_wide_kernel, "whole_columns", place, pieces, outs, after)[0]
    return whole.reshape(-1, width)


def grad_parts_kernel(q_ref, gate, wide, *outs):
    for k in range(TEAM):
        block = place_of(q_ref[0] ^ k)
        outs[k][:, :INNER_Q] = gate[block]
        outs[k][:, INNER_Q:] = wide[block]


def grad_parts(q, gate, wide):
    outs = [shaped((wide.shape[1], INNER_Q + WIDE), BF16)] * TEAM
    return whole_call(grad_parts_kernel, "grad_parts", q, (gate, wide), outs)


def cut_params_kernel(q_ref, conv_weight, conv_bias, dt_bias, a_log, skip, out_gain, spread, taps, par, rows):
    owner = q_ref[0]
    start = pl.multiple_of(owner * INNER_Q, 128)
    bc, dt = tile_picks(owner, None)
    bc, dt = bc.astype(BF16), dt.astype(BF16)
    mine = pl.ds(start, INNER_Q)
    for layer in range(conv_weight.shape[0]):
        one = slice(layer, layer + 1)
        taps[layer, :CONV, :INNER_Q] = conv_weight[layer, :, mine]
        taps[layer, :CONV, INNER_Q:] = exact_mm(conv_weight[layer, :, INNER:], bc)
        taps[layer, CONV : CONV + 1, :INNER_Q] = conv_bias[one, mine]
        taps[layer, CONV : CONV + 1, INNER_Q:] = exact_mm(conv_bias[one, INNER:], bc)
        taps[layer, CONV + 1 :] = jnp.zeros((7 - CONV, WIDE), F32)
        par[layer, 0:1] = exact_mm(dt_bias[one], dt)
        par[layer, 1:2] = exact_mm(jnp.exp(a_log[one]), dt)
        par[layer, 2:] = jnp.zeros((6, 128), F32)
        rows[layer, 0:1] = exact_mm(exact_mm(skip[one], dt), spread[...])
        rows[layer, 1:2] = out_gain[one, mine]
        rows[layer, 2:] = jnp.zeros((6, INNER_Q), F32)


def cut_params(q, params, after):
    layers = params[0].shape[0]
    shapes = [(layers, 8, WIDE), (layers, 8, 128), (layers, 8, INNER_Q)]
    return whole_call(cut_params_kernel, "cut_params", q, params, [shaped(s) for s in shapes], after)


def join_kernel(q_ref, *refs):
    out = refs[-1]
    for layer in range(out.shape[0]):
        shared = 0.0
        for k in range(TEAM):
            owner = q_ref[0] ^ k
            start = pl.multiple_of(owner * INNER_Q, 128)
            part = refs[layer * TEAM + k]
            out[layer, :, pl.ds(start, INNER_Q)] = part[:, :INNER_Q].astype(F32)
            out[layer, :, pl.ds(INNER + start, INNER_Q)] = part[:, INNER_Q : 2 * INNER_Q].astype(F32)
            bc, dt = tile_picks(owner, None)
            both = jnp.concatenate((bc, dt), axis=0).astype(BF16)
            shared = shared + mm(part[:, 2 * INNER_Q :], both, (1, 1))
        out[layer, :, 2 * INNER :] = shared


def join_weights(q, parts):
    flat = [v for layer in parts for v in layer]
    shape = (len(parts), flat[0].shape[0], 2 * INNER + 2 * STATE + HEADS)
    return whole_call(join_kernel, "join_weights", q, flat, [shaped(shape)])[0]


SMALL = (16, WIDE)


def pack_small_kernel(conv_x, conv_tile, heads, skip, gain, norm, spread, out):
    fold = lambda v, rows: jnp.sum(v[:, rows], axis=(0, 1), keepdims=True)[0]
    for line in range(CONV + 1):
        rows = slice(8 * line, 8 * line + 8)
        out[line : line + 1, :INNER_Q] = fold(conv_x[...], rows)
        out[line : line + 1, INNER_Q:] = fold(conv_tile[...], rows)
    line = CONV + 1
    out[line:] = jnp.zeros((SMALL[0] - line, WIDE), F32)
    every = slice(0, 8)
    out[line + 1 : line + 2, :INNER_Q] = fold(gain[...], every)
    out[line + 2 : line + 3, :128] = fold(heads[...], slice(8, 16))
    out[line + 3 : line + 4, :128] = fold(heads[...], every)
    by_head = exact_mm(skip[0] + skip[1], spread[...], (1, 1))
    out[line + 4 : line + 5, :128] = jnp.sum(by_head, axis=0, keepdims=True)
    width = norm.shape[1] // 2
    out[line + 5 : line + 6, :width] = norm[:, :width]
    out[line + 6 : line + 7, :width] = norm[:, width:]


def pack_small(*parts):
    return pl.pallas_call(pack_small_kernel, name="pack_small", out_shape=shaped(SMALL))(*parts)


def lanes_of(values):
    return lax.broadcasted_iota(jnp.int32, values.shape, 1)


def open_small_kernel(q_ref, *refs):
    norm, conv_weight, conv_bias, dt_bias, a_log, skip, gain = refs[-7:]
    layers = norm.shape[0]
    line = CONV + 1
    for layer in range(layers):
        one = slice(layer, layer + 1)
        packs = [ref[layer] for ref in refs[:TEAM]]
        shared, heads = [], 0.0
        for k in range(TEAM):
            owner = q_ref[0] ^ k
            start = pl.multiple_of(owner * INNER_Q, 128)
            mine = pl.ds(start, INNER_Q)
            pack = packs[k]
            conv_weight[layer, :, mine] = pack[:CONV, :INNER_Q]
            conv_bias[one, mine] = pack[CONV:line, :INNER_Q]
            tile = pack[:8, INNER_Q:]
            tile = jnp.where(lanes_of(tile) < BC_Q, tile, 0.0)
            tile = jnp.where(owner % 2 == 0, tile, pltpu.roll(tile, BC_Q, 1))
            shared.append([jnp.where(owner // 2 == side, tile, 0.0) for side in range(2)])
            rows = pack[line + 2 : line + 5, :128]
            in_head = (lanes_of(rows) >= LANE) & (lanes_of(rows) < LANE + HEADS_Q)
            rows = jnp.where(in_head, rows, 0.0)
            placed = 0.0
            for which in range(TEAM):
                turned = pltpu.roll(rows, (HEADS_Q * which - LANE) % 128, 1)
                placed = placed + jnp.where(owner == which, turned, 0.0)
            heads = heads + placed[:, :HEADS]
            gain[one, mine] = pack[line + 1 : line + 2, :INNER_Q]
        shared = jnp.concatenate([sum([s[side] for s in shared]) for side in range(2)], axis=1)
        conv_weight[layer, :, INNER:] = shared[:CONV]
        conv_bias[one, INNER:] = shared[CONV:line]
        dt_bias[one], a_log[one], skip[one] = heads[0:1], heads[1:2], heads[2:3]
        width = norm.shape[1] // 2
        halves_of = lambda n: packs[n][line + 5 : line + 7, :width]
        total = (halves_of(0) + halves_of(1)) + (halves_of(2) + halves_of(3))
        norm[one, :width] = total[0:1]
        norm[one, width:] = total[1:2]


def open_small(q, packs, features):
    layers = packs[0].shape[0]
    flat = list(packs)
    shapes = [
        (layers, features), (layers, CONV, CONVDIM), (layers, CONVDIM), (layers, HEADS), (layers, HEADS),
        (layers, HEADS), (layers, INNER),
    ]
    return pl.pallas_call(
        open_small_kernel,
        name="open_small",
        grid_spec=pltpu.PrefetchScalarGridSpec(
            num_scalar_prefetch=1,
            grid=(1,),
            in_specs=[whole_spec(v.shape) for v in flat],
            out_specs=[whole_spec(s) for s in shapes],
        ),
        out_shape=[shaped(s) for s in shapes],
    )(q, *flat)


def spread_matrix():
    head = jnp.arange(128)[:, None] - LANE
    return (jnp.arange(INNER_Q)[None, :] // HEADDIM == head).astype(BF16)


def gap_decays(spans):
    rows = []
    for start in range(len(spans)):
        row = []
        running = jnp.ones_like(spans[0])
        for stop, span in enumerate(spans):
            if stop <= start:
                row.append(jnp.zeros_like(running))
                continue
            row.append(running)
            running = running * span
        rows.append(jnp.stack(row))
    return jnp.stack(rows)


def mix_states(states, bits=None, weights=None):
    size = lax.axis_size("z")
    z = lax.axis_index("z")
    width = states.shape[1] // size
    decay = lambda rows: jnp.sum(rows[:, :3].astype(F32), axis=1)
    if size > NEAR:
        if weights is None:
            weights = gap_decays([decay(v) for v in lax.all_gather(bits, "z")])
        cuts = jnp.moveaxis(states.reshape(2, size, width, -1), 1, 0).astype(BF16)
        parts = lax.all_to_all(cuts, "z", 0, 0, tiled=True).astype(F32)
        sums = jnp.sum(weights[:, :, :, None] * parts[:, None], axis=0)
        back = lax.all_to_all(sums.astype(BF16), "z", 0, 0, tiled=True).astype(F32)
        return jnp.moveaxis(back, 0, 1).reshape(states.shape), weights
    ring = lambda k: lax.rem(z + k + size, size)

    def cut(k):
        part = lax.dynamic_slice_in_dim(states, k * width, width, 1).astype(BF16)
        return part if weights is not None else jnp.concatenate((part, bits), axis=1)

    parts = [cut(z)] + [shift(cut(ring(hop)), "z", hop) for hop in range(1, size)]
    if weights is None:
        everyone = jnp.stack([decay(p[:, width:]) for p in parts])
        spans = [
            lax.dynamic_index_in_dim(everyone, lax.rem(z - k + size, size), 0, False)
            for k in range(size)
        ]
        weights = gap_decays(spans)
        parts = [p[:, :width] for p in parts]
    results = []
    for away in range(size):
        to = lax.dynamic_index_in_dim(weights, ring(away), 1, False)
        total = 0.0
        for hop in range(size):
            weight = lax.dynamic_index_in_dim(to, ring(-hop), 0, False)
            total = total + weight[:, None] * parts[hop].astype(F32)
        results.append(total)
    back = [results[0]] + [
        shift(results[hop].astype(BF16), "z", hop).astype(F32) for hop in range(1, size)
    ]
    whole = jnp.zeros(states.shape, F32)
    for hop in range(size):
        whole = lax.dynamic_update_slice_in_dim(whole, back[hop], ring(-hop) * width, 1)
    return whole, weights


def local(
    tokens,
    segments,
    out_grad,
    norm_gain,
    in_weight,
    conv_weight,
    conv_bias,
    dt_bias,
    a_log,
    skip,
    out_gain,
    out_weight,
):
    _, length, features = tokens.shape
    edge = CONV - 1
    layer_count, in_rows = in_weight.shape[:2]
    out_rows = out_weight.shape[1]
    layers = range(layer_count)
    q = member()
    owner = q.reshape(1)
    span = 2 * length
    row_count = 2 * span

    near = lax.axis_size("z") <= NEAR
    x_place = lax.axis_index("x").reshape(1)
    cuts = cut_weights(owner, in_weight)
    size = lax.axis_size("z")
    place = jnp.stack((lax.axis_index("z"), lax.axis_index("x")))
    exchanged = [around_team(parts) for parts in cuts]
    moved = [lax.ppermute(out_weight[k], ("x", "y"), TURN) for k in layers]
    nowhere = jnp.zeros((1,), jnp.int32)

    def fetch_rows(rows):
        return lax.all_gather(rows, ("z", "x"), axis=0, tiled=True)

    def fetch_columns(layer_id, after):
        gathered = lax.all_gather(all_piece(owner, exchanged[layer_id], after), ("x", "z"))
        return arrange(nowhere, gathered.reshape((2, size) + gathered.shape[1:]))

    if near:
        wide_line, wide_all = fetch(wide_piece(owner, exchanged[0]))

    seg_now = team_gather(segments.astype(F32).reshape(length))
    prev_seg = step_line(seg_now[:, span - edge :], "z", 1)
    seg_ext = jnp.concatenate((prev_seg, seg_now), axis=1)
    seg = seg_table(seg_now, seg_ext[:, edge - 1])
    mask = mask_table(seg_ext, edge)
    spread = spread_matrix()
    all_taps, all_par, all_rows = cut_params(
        owner, (conv_weight, conv_bias, dt_bias, a_log, skip, out_gain, spread), exchanged[0][1:]
    )

    stream = tokens.astype(F32).reshape(length, features)
    saved, full = [], []
    for layer_id in layers:
        taps, par, rows = all_taps[layer_id], all_par[layer_id], all_rows[layer_id]
        first, final = layer_id == 0, layer_id == layer_count - 1
        fast = near and first
        x_order = x_place if fast else nowhere
        normed = norm_rows(
            x_order,
            tokens.reshape(length, features) if first else stream,
            norm_gain[layer_id : layer_id + 1],
            wide_line[1:2] if fast else [],
        )
        normed = team_gather(normed)
        earlier = step_line(normed[:, span - 16 :], "z", 1).reshape(32, features)
        normed = normed.reshape(row_count, features)
        if first:
            last_grad = team_gather(tie(out_grad.reshape(length, features), normed))
        dot = partial(jnp.dot, preferred_element_type=F32)
        if fast:
            piece = gate_piece(
                owner, exchanged[0], moved[0], wide_line[1:] + [normed, seg, mask, all_taps]
            )
            gathered = lax.all_gather(piece, ("x", "z")).reshape((2, size) + piece.shape)
            full_gate, full_out = arrange_both(x_place, gathered)
            full_wide = whole_columns(place, wide_all, [earlier])
        elif first:
            full_wide, full_gate = fetch_columns(0, [])
        else:
            full_wide, full_gate = next_columns
        wide = dot(normed, full_wide).reshape(2, span, WIDE)
        if not fast:
            full_out = fetch_rows(moved[0]) if first else next_rows
        gate_raw = dot(normed, full_gate).reshape(2, span, INNER_Q)
        full.append((full_wide, full_gate, full_out))
        halo = dot(earlier, full_wide).reshape(2, 16, WIDE)[:, 8:].astype(BF16).astype(F32)
        bc_own = conv_forward(
            wide, halo, taps, mask, 128, TILE, [v for e in exchanged[1:] for v in e[1:]] if first else []
        )[..., :BC_Q]
        bc_same = y_swap(bc_own)
        bc = jnp.concatenate(
            in_order((bc_own, core_swap(bc_own)[::-1], bc_same, core_swap(bc_same)[::-1])), axis=-1
        )
        heads_x = conv_forward(wide, halo, taps, mask, INNER_Q, 0)
        scan_in = (heads_x, bc, wide, seg, par, spread)
        before, reach, end, total_reach, bits = scan_states(
            *scan_in, after=[last_grad] if first else []
        )
        start, weights = mix_states(end, bits)
        inside = scan_inside(*scan_in, after=[] if first else [full_out])
        if not final:
            next_columns = fetch_columns(layer_id + 1, [start, inside])
            next_rows = fetch_rows(tie(moved[layer_id + 1], start))
        scan_y, gated, square = scan_outer(
            inside, *scan_in, before, reach, start, gate_raw, rows,
        )
        scale = lax.rsqrt(team_sum(square) / INNER + EPS)
        normed_y = scale_rows(gated, scale, rows)
        normed_y = normed_y.reshape(row_count, INNER_Q)
        sequence = lambda v, k: lax.slice_in_dim(v, k * span, (k + 1) * span, axis=0)
        branch_far = dot(sequence(normed_y, 1), full_out)
        branch = dot(sequence(normed_y, 0), full_out)
        saved.append(
            (
                stream,
                normed,
                gate_raw,
                halo,
                scan_in,
                (before, reach, start),
                (end, total_reach),
                weights,
                scan_y,
                gated,
                scale,
                normed_y,
                taps,
                rows,
            )
        )
        stream = stream + team_scatter(branch, branch_far)
    grad_stream = out_grad.astype(F32).reshape(length, features)
    in_parts = [None] * layer_count
    out_shards = [None] * layer_count
    small = [None] * layer_count
    for layer_id in reversed(layers):
        (
            stream_in,
            normed,
            gate_raw,
            halo,
            scan_in,
            states_before,
            states_end,
            weights,
            scan_y,
            gated,
            scale,
            normed_y,
            taps,
            rows,
        ) = saved[layer_id]
        heads_x, scan_rest = scan_in[0], scan_in[1:]
        wide = scan_in[2]
        full_wide, full_gate, full_out = full[layer_id]
        last = layer_id == 0
        grad_branch = team_gather(grad_stream.astype(BF16)) if last_grad is None else last_grad
        last_grad = None
        grad_branch = grad_branch.reshape(row_count, features)
        out_full_grad = jnp.einsum("ri,rd->id", normed_y, grad_branch, preferred_element_type=F32)
        back = partial(jnp.einsum, "rp,dp->rd", preferred_element_type=F32)
        grad_normed_y = back(grad_branch, full_out).reshape(2, span, INNER_Q)
        along, grad_gain = gate_along(grad_normed_y, gated, rows, scale)
        along = team_sum(along)
        grad_ssd, grad_gate, after, beyond, grad_start = gate_back(
            grad_normed_y, gated, scan_y, heads_x, gate_raw, *scan_rest, rows, scale, along,
            [out_full_grad],
        )
        turn = partial(jnp.einsum, "rd,rp->dp", preferred_element_type=F32)
        grad_gate = grad_gate.reshape(row_count, INNER_Q)
        gate_grad = turn(normed, grad_gate)
        fast = near and last
        x_order = x_place if fast else nowhere
        both = both_by_owner(x_order, gate_grad, out_full_grad, size, in_rows)
        both_total = sum_to_owner(both)
        gate_total = both_total[:TEAM]
        out_total = both_total[TEAM:].reshape(2, 2, in_rows, INNER_Q).swapaxes(1, 2)
        out_total = out_total.reshape(out_rows, features)
        out_shards[layer_id] = lax.ppermute(out_total, ("x", "y"), TURN).astype(F32)
        grad_end, _ = mix_states(grad_start, None, weights.swapaxes(0, 1))
        grad_inside = scan_inside_back(*scan_in, grad_ssd, after=[both])
        grad_x, grad_bc, grad_raw, head_sums, skip_sums = scan_outer_back(
            *grad_inside,
            *scan_in,
            *states_before,
            after,
            beyond,
            grad_end,
            *states_end,
            grad_ssd,
            scan_y,
            rows,
        )
        blocks = [grad_bc[..., BC_Q * k : BC_Q * k + BC_Q].astype(BF16) for k in range(TEAM)]
        turned = lambda k: lax.select_n(q ^ k, *blocks)
        half = lambda k: turned(k).astype(F32) + core_swap(turned(k ^ 1)).astype(F32)[::-1]
        grad_bc_own = half(0) + y_swap(half(2).astype(BF16)).astype(F32)
        grad_tile = jnp.pad(grad_bc_own, ((0, 0), (0, 0), (0, 128 - BC_Q)))

        edge_in = jnp.concatenate(
            (halo[:, 8 - edge :], wide[:, :edge].astype(BF16).astype(F32)), axis=1
        )
        edge_conv = lambda v: conv_piece(seg_ext[:, : 2 * edge], v, taps[:CONV], taps[CONV])
        edge_grad = jnp.concatenate((grad_x[:, :edge], grad_tile[:, :edge]), axis=-1)
        edge_grad = jax.vjp(edge_conv, edge_in)[1](edge_grad)[0][:, :edge].astype(BF16)
        returned = step_line(edge_grad, "z", -1).astype(F32)
        returned = jnp.pad(returned, ((0, 0), (8 - edge, 0), (0, 0)))
        grad_conv_x, conv_sums = conv_backward(
            wide, halo, taps, mask, grad_x, returned, INNER_Q, 0
        )
        grad_conv_tile, tile_sums = conv_backward(
            wide, halo, taps, mask, grad_tile, returned, 128, TILE
        )
        grad_wide = jnp.concatenate(
            (grad_conv_x, grad_conv_tile[..., :BC_Q], grad_raw[..., BC_Q:].astype(BF16)), axis=-1
        ).reshape(row_count, WIDE)
        in_grad = turn(normed, grad_wide)
        total = sum_to_owner(by_owner(x_order, in_grad, size, in_rows))
        in_parts[layer_id] = around_team(grad_parts(owner, gate_total, total))
        full_wide, full_gate, _ = full[layer_id]
        sequence = lambda v, k: lax.slice_in_dim(v, k * span, (k + 1) * span, axis=0)
        both_back = lambda k: back(sequence(grad_wide, k), full_wide) + back(
            sequence(grad_gate, k), full_gate
        )
        grad_far, grad_normed = both_back(1), both_back(0)
        norm_grad = jnp.sum(in_grad * full_wide.astype(F32), axis=1)
        norm_grad = norm_grad + jnp.sum(gate_grad * full_gate.astype(F32), axis=1)
        if fast:
            norm_grad = x_first(norm_grad)
        norm_grad = norm_grad / norm_gain[layer_id]
        grad_normed = team_scatter(grad_normed, grad_far)
        if fast:
            grad_normed = x_first(grad_normed)
        else:
            grad_normed = tie(grad_normed, both_total)
        _, pull_norm = jax.vjp(lambda v: norm_piece(v, norm_gain[layer_id]), stream_in)
        (grad_inner,) = pull_norm(grad_normed)
        grad_stream = grad_stream + grad_inner
        small[layer_id] = pack_small(
            conv_sums, tile_sums, head_sums, skip_sums, grad_gain, norm_grad.reshape(1, features),
            spread,
        )
    mixed = stream.reshape(1, length, features).astype(BF16)
    pack = xor_sum(xor_sum(jnp.stack(small), "x"), "z")
    across = y_swap(pack)
    packs = (pack, core_swap(pack), across, core_swap(across))
    norm_sum, taps_sum, bias_sum, dt_sum, decay_sum, skip_sum, gain_sum = open_small(
        owner, packs, features
    )
    return (
        mixed,
        grad_stream.reshape(1, length, features),
        norm_sum,
        join_weights(owner, in_parts),
        taps_sum,
        bias_sum,
        dt_sum,
        decay_sum,
        skip_sum,
        gain_sum,
        jnp.stack(out_shards),
    )


def solution(mesh):
    rows, spans = mesh.devices.shape
    split = Mesh(mesh.devices.reshape(rows // 2, 2, spans // 2, 2), ("x", "core", "z", "y"))
    tokens = P(("x", "core"), ("z", "y"), None)
    weight = P(None, ("x", "core", "z", "y"), None)
    return jax.shard_map(
        local,
        mesh=split,
        in_specs=(
            tokens,
            P(("x", "core"), ("z", "y")),
            tokens,
            P(),
            weight,
            P(),
            P(),
            P(),
            P(),
            P(),
            P(),
            weight,
        ),
        out_specs=(tokens, tokens, P(), weight, P(), P(), P(), P(), P(), P(), weight),
        check_vma=False,
    )
```

```python
from functools import partial

import jax
import jax.numpy as jnp
from jax import lax
from jax.experimental import pallas as pl
from jax.experimental.pallas import tpu as pltpu
from jax.sharding import Mesh
from jax.sharding import PartitionSpec as P

HEADS = 48
HEADDIM = 64
STATE = 128
CONV = 4
INNER = 3072
CONVDIM = 3328

TEAM = 4
HEADS_Q = HEADS // TEAM
INNER_Q = INNER // TEAM
BC_Q = 2 * STATE // TEAM
CONV_Q = INNER_Q + BC_Q
WIDE = 896

EPS = 1e-05
VMEM_BYTES = 40 * 1024 * 1024
STEP_BYTES = 20 * 1024 * 1024
NEAR = 4
SWAP = [(0, 1), (1, 0)]
BF16 = jnp.bfloat16
F32 = jnp.float32


def shift(block, axis, distance):
    size = lax.axis_size(axis)
    return lax.ppermute(block, axis, [(i, (i + distance) % size) for i in range(size)])


def step_line(block, axis, distance):
    devices = range(lax.axis_size(axis))
    return lax.ppermute(block, axis, [(i, i + distance) for i in devices if i + distance in devices])


def core_swap(block):
    return lax.ppermute(block, "core", SWAP)


def y_swap(block):
    return lax.ppermute(block, "y", SWAP)


def diagonal_swap(block):
    return lax.ppermute(block, ("core", "y"), [(0, 3), (1, 2), (2, 1), (3, 0)])


def xor_sum(values, axis):
    size = lax.axis_size(axis)
    bit = 1
    while bit < size:
        values = tie(values + lax.ppermute(values, axis, [(i, i ^ bit) for i in range(size)]))
        bit *= 2
    return values


def member():
    return lax.axis_index("y") * 2 + lax.axis_index("core")


def in_order(parts):
    q = member()
    return [lax.select_n(q ^ j, *parts) for j in range(TEAM)]


def around_team(blocks):
    return blocks[0], core_swap(blocks[1]), y_swap(blocks[2]), diagonal_swap(blocks[3])


def by_y(own, other):
    first = lax.axis_index("y") == 0
    return jnp.where(first, jnp.concatenate((own, other), 1), jnp.concatenate((other, own), 1))


def team_gather(block):
    pair = jnp.stack((block, core_swap(block)))
    crossed = y_swap(block)
    other = jnp.stack((crossed, core_swap(crossed)))
    return by_y(pair, other)


def team_scatter(own, other):
    total = own + core_swap(other.astype(BF16)).astype(F32)
    half = total.shape[0] // 2
    y = lax.axis_index("y")
    mine = lax.dynamic_slice_in_dim(total, y * half, half, 0)
    theirs = lax.dynamic_slice_in_dim(total, (1 - y) * half, half, 0)
    return mine + y_swap(theirs.astype(BF16)).astype(F32)


def team_sum(values):
    across = core_swap(values) + diagonal_swap(values)
    return (values + y_swap(values)) + across[::-1]


def x_swap(block):
    return lax.ppermute(block, "x", SWAP)


def line_pieces(piece):
    return [piece] + [shift(piece, "z", hop) for hop in range(1, lax.axis_size("z"))]


def fetch(piece):
    line = line_pieces(piece)
    return line, line + [x_swap(p) for p in line]


def sum_to_owner(blocks):
    flat = blocks.reshape((-1,) + blocks.shape[2:])
    return lax.psum_scatter(flat, ("x", "z"), scatter_dimension=0)


TURN = [(0, 0), (1, 2), (2, 1), (3, 3)]


def x_first(values):
    low, high = jnp.split(values, 2, axis=-1)
    first = lax.axis_index("x") == 0
    return jnp.where(first, jnp.concatenate((low, high), -1), jnp.concatenate((high, low), -1))


def rms_scale(values):
    return values * lax.rsqrt(jnp.mean(values * values, axis=-1, keepdims=True) + EPS)


def norm_piece(stream, norm_scale):
    return rms_scale(stream) * norm_scale


def conv_piece(seg_ext, extended, conv_taps, conv_shift):
    length = extended.shape[-2] - CONV + 1
    seg_here = seg_ext[..., CONV - 1 :]
    summed = conv_shift
    for offset in range(CONV):
        same_doc = (seg_ext[..., offset : offset + length] == seg_here)[..., None]
        summed = summed + conv_taps[offset] * extended[..., offset : offset + length, :] * same_doc
    return jax.nn.silu(summed)


CHUNK = 128
LANE = 64
NEVER = -1e30
TILE = INNER_Q // 128


def split_parts(values):
    high = values.astype(BF16)
    rest = values - high.astype(F32)
    middle = rest.astype(BF16)
    return high, middle, (rest - middle.astype(F32)).astype(BF16)


def mm(a, b, over=(1, 0)):
    return lax.dot_general(
        a, b, (((over[0],), (over[1],)), ((), ())), preferred_element_type=F32
    )


def exact_mm(values, ones, over=(1, 0)):
    high, middle, low = split_parts(values)
    return (mm(low, ones, over) + mm(middle, ones, over)) + mm(high, ones, over)


def spread_mm(values, ones, over=(1, 0)):
    high, low = halves(values)
    return mm(low, ones, over) + mm(high, ones, over)


def mm_exact(ones, values):
    high, middle, low = split_parts(values)
    return (mm(ones, low) + mm(ones, middle)) + mm(ones, high)


def halves(values):
    high = values.astype(BF16)
    return high, (values - high.astype(F32)).astype(BF16)


def mm_wide(narrow, values, over=(1, 0)):
    high, low = halves(values)
    return mm(narrow, low, over) + mm(narrow, high, over)


def softplus(values):
    tail = jnp.exp(-jnp.abs(values))
    series = tail * (1.0 - tail * (0.5 - tail * (1.0 / 3.0)))
    return jnp.maximum(values, 0.0) + jnp.where(tail < 0.01, series, jnp.log(1.0 + tail))


def sigmoid(values):
    return 1.0 / (1.0 + jnp.exp(-values))


def grids(shape):
    return lax.broadcasted_iota(jnp.int32, shape, 0), lax.broadcasted_iota(jnp.int32, shape, 1)


def column(row):
    return jnp.broadcast_to(row, (CHUNK, CHUNK)).T


def step_terms(raw_ref, par_ref):
    down, across = grids((CHUNK, CHUNK))
    lower = (down >= across).astype(F32).astype(BF16)
    step = softplus(raw_ref[0] + par_ref[0:1])
    sums = mm_exact(lower, -par_ref[1:2] * step)
    return step, sums, sums[CHUNK - 1 :]


def seg_terms(seg_ref):
    return column(seg_ref[0, 0, 0:1]), seg_ref[0, 0, 0:1], seg_ref[0, 0, 1:2], seg_ref[0, 0, 2:3]


def chunk_decay(total, before, last, spread):
    kept = jnp.exp(total) * (before == last).astype(F32)
    return exact_mm(jnp.broadcast_to(kept, (8, CHUNK)), spread)


def state_kernel(x, bc, raw, seg, par, spread, before_out, reach_out, end_out, total_out, bits_out, state, reach):
    @pl.when(pl.program_id(1) == 0)
    def _():
        state[...] = jnp.zeros_like(state)
        reach[...] = jnp.ones_like(reach)

    step, sums, total = step_terms(raw, par)
    lines, _, before, last = seg_terms(seg)
    before_out[0, 0] = state[...]
    reach_out[0, 0] = reach[...]
    leaving = jnp.where(lines == last, jnp.exp(total - sums), 0.0)
    fed = (x[0].astype(F32) * spread_mm(step, spread[...])).astype(BF16).astype(F32)
    fed = fed * spread_mm(leaving, spread[...])
    decay = chunk_decay(total, before, last, spread[...])
    state[...] = state[...] * decay[0:1] + mm_wide(bc[0, :, :STATE], fed, (0, 0))
    reach[...] = reach[...] * decay
    end_out[0] = state[...]
    total_out[0] = reach[...]
    lines = [v[0:1] for v in split_parts(reach[...])]
    bits_out[0] = jnp.concatenate(lines + [jnp.zeros((13, INNER_Q), BF16)], axis=0)


def inside_kernel(x, bc, raw, seg, par, spread, y_out):
    step, sums, _ = step_terms(raw, par)
    lines, row, _, _ = seg_terms(seg)
    down, across = grids((CHUNK, CHUNK))
    bias = jnp.where((lines == row) & (down >= across), 0.0, NEVER)
    scores = mm(bc[0, :, STATE:], bc[0, :, :STATE], (1, 1))
    turned = sums.T
    fed = (x[0].astype(F32) * spread_mm(step, spread[...])).astype(BF16)
    for pair in range(HEADS_Q // 2):
        lanes = slice(pair * 128, pair * 128 + 128)
        mixing = []
        for head in (LANE + 2 * pair, LANE + 2 * pair + 1):
            gap = jnp.broadcast_to(sums[:, head : head + 1], (CHUNK, CHUNK)) - turned[head : head + 1]
            mixing.append((scores * jnp.exp(gap + bias)).astype(BF16))
        both = mm(jnp.concatenate(mixing, axis=0), fed[:, lanes])
        y_out[0, :, lanes] = jnp.where(across < HEADDIM, both[:CHUNK], both[CHUNK:])


def outer_kernel(
    y_in, x, bc, raw, seg, par, spread, before, reach, start, gate, rows, y_out, gated_out, square_out
):
    _, sums, _ = step_terms(raw, par)
    lines, _, ahead, _ = seg_terms(seg)
    entering = spread_mm(jnp.where(lines == ahead, jnp.exp(sums), 0.0), spread[...])
    state = before[0, 0] + reach[0, 0, 0:1] * start[0]
    y = y_in[0] + entering * mm_wide(bc[0, :, STATE:], state)
    y_out[0] = y
    raw_gate = gate[0]
    gated = (y + rows[0:1] * x[0].astype(F32)) * (raw_gate * sigmoid(raw_gate))
    gated_out[0] = gated
    square = gated * gated
    folded = square[:, :128]
    for tile in range(1, INNER_Q // 128):
        folded = folded + square[:, tile * 128 : tile * 128 + 128]
    square_out[0, 0] = jnp.sum(folded.T, axis=0, keepdims=True)


def along_kernel(grad, gated, rows, scale, along_out, gain_out):
    @pl.when(pl.program_id(1) == 0)
    def _():
        gain_out[...] = jnp.zeros_like(gain_out)

    product = grad[0] * gated[0]
    weighed = product * rows[1:2]
    folded = weighed[:, :128]
    for tile in range(1, INNER_Q // 128):
        folded = folded + weighed[:, tile * 128 : tile * 128 + 128]
    along_out[0, 0] = jnp.sum(folded.T, axis=0, keepdims=True)
    lines = jnp.concatenate([column(scale[0, 0])] * (INNER_Q // 128), axis=1)
    gain_out[0] += jnp.sum((product * lines).reshape(CHUNK // 8, 8, INNER_Q), axis=0)


def gate_back_kernel(
    grad, gated, y, x, gate, bc, raw, seg, par, spread, rows, scale, along,
    grad_out, gate_out, after_out, beyond_out, start_out, state, reach,
):
    @pl.when(pl.program_id(1) == 0)
    def _():
        state[...] = jnp.zeros_like(state)
        reach[...] = jnp.ones_like(reach)

    wide = lambda row: jnp.concatenate([column(row)] * (INNER_Q // 128), axis=1)
    factor = scale[0, 0]
    pull = factor * factor * factor * along[0, 0] * (1.0 / INNER)
    grad_gated = grad[0] * rows[1:2] * wide(factor) - gated[0] * wide(pull)
    raw_gate = gate[0]
    sig = sigmoid(raw_gate)
    grad_y = (grad_gated * (raw_gate * sig)).astype(BF16)
    ssd_y = y[0] + rows[0:1] * x[0].astype(F32)
    gate_out[0] = (grad_gated * ssd_y * (sig * (1.0 + raw_gate * (1.0 - sig)))).astype(BF16)
    grad_out[0] = grad_y

    _, sums, total = step_terms(raw, par)
    lines, _, before, last = seg_terms(seg)
    after_out[0, 0] = state[...]
    beyond_out[0, 0] = reach[...]
    entering = spread_mm(jnp.where(lines == before, jnp.exp(sums), 0.0), spread[...])
    decay = chunk_decay(total, before, last, spread[...])
    fed = grad_y.astype(F32) * entering
    state[...] = state[...] * decay[0:1] + mm_wide(bc[0, :, STATE:], fed, (0, 0))
    reach[...] = reach[...] * decay
    start_out[0] = state[...]


def inside_back_kernel(x, bc, raw, seg, par, spread, grad, fed_out, b_out, c_out):
    step, sums, _ = step_terms(raw, par)
    lines, row, _, _ = seg_terms(seg)
    down, across = grids((CHUNK, CHUNK))
    bias = jnp.where((lines == row) & (across >= down), 0.0, NEVER)
    b_in, c_in = bc[0, :, :STATE], bc[0, :, STATE:]
    scores = mm(b_in, c_in, (1, 1))
    turned = sums.T
    fed = (x[0].astype(F32) * spread_mm(step, spread[...])).astype(BF16)
    grad_scores = jnp.zeros((CHUNK, CHUNK), F32)
    for pair in range(HEADS_Q // 2):
        lanes = slice(pair * 128, pair * 128 + 128)
        fed_pair, grad_pair = fed[:, lanes], grad[0, :, lanes]
        none = jnp.zeros_like(fed_pair)
        apart = jnp.concatenate(
            (jnp.where(across < HEADDIM, fed_pair, none), jnp.where(across < HEADDIM, none, fed_pair)),
            axis=0,
        )
        grad_mixing = mm(apart, grad_pair, (1, 1))
        mixing = []
        for which in range(2):
            head = LANE + 2 * pair + which
            gap = turned[head : head + 1] - jnp.broadcast_to(sums[:, head : head + 1], (CHUNK, CHUNK))
            decays = jnp.exp(gap + bias)
            mixing.append((scores * decays).astype(BF16))
            grad_scores = grad_scores + grad_mixing[which * CHUNK : which * CHUNK + CHUNK] * decays
        both = mm(jnp.concatenate(mixing, axis=0), grad_pair)
        fed_out[0, :, lanes] = jnp.where(across < HEADDIM, both[:CHUNK], both[CHUNK:])
    grad_scores = grad_scores.astype(BF16)
    b_out[0] = mm(grad_scores, c_in)
    c_out[0] = mm(grad_scores, b_in, (0, 0))


def outer_back_kernel(
    fed_in, b_in, c_in, x, bc, raw, seg, par, spread, before, reach, start, after, beyond, grad_end,
    end, total_reach, grad, y, rows,
    x_out, bc_out, raw_out, sums_out, skip_out, carry,
):
    @pl.when(pl.program_id(1) == 0)
    def _():
        sums_out[...] = jnp.zeros_like(sums_out)
        skip_out[...] = jnp.zeros_like(skip_out)
        last_state = end[0] + total_reach[0, 0:1] * start[0]
        meet = jnp.sum((grad_end[0] * last_state).reshape(STATE // 8, 8, INNER_Q), axis=0)
        meet = jnp.sum(spread_mm(meet, spread[...], (1, 1)), axis=0, keepdims=True)
        carry[...] = jnp.broadcast_to(meet, carry.shape)

    step, sums, total = step_terms(raw, par)
    lines, _, ahead, last = seg_terms(seg)
    ones = spread[...]
    state = (before[0, 0] + reach[0, 0, 0:1] * start[0]).astype(BF16)
    grad_state = after[0, 0] + beyond[0, 0, 0:1] * grad_end[0]
    values = x[0].astype(F32)
    grad_y = grad[0].astype(F32)
    wide_step = spread_mm(step, ones)
    leaving = spread_mm(jnp.where(lines == last, jnp.exp(total - sums), 0.0), ones)
    entering = spread_mm(jnp.where(lines == ahead, jnp.exp(sums), 0.0), ones)
    fed = (values * wide_step).astype(BF16).astype(F32)
    grad_fed = fed_in[0] + leaving * mm_wide(bc[0, :, :STATE], grad_state)
    x_out[0] = wide_step * grad_fed + rows[0:1] * grad_y
    bc_out[0, :, :STATE] = b_in[0] + mm((leaving * fed).astype(BF16), grad_state.astype(BF16), (1, 1))
    bc_out[0, :, STATE:] = c_in[0] + mm((entering * grad_y).astype(BF16), state, (1, 1))
    skip_out[0] += jnp.sum((grad_y * values).reshape(CHUNK // 8, 8, INNER_Q), axis=0)

    by_step = spread_mm(values * grad_fed, ones, (1, 1))
    flow = spread_mm(grad_y * y[0] - fed * grad_fed, ones, (1, 1))
    down, across = grids((CHUNK, CHUNK))
    upper = (across >= down).astype(F32).astype(BF16)
    grad_log = mm_exact(upper, flow) + carry[0:1]
    carry[...] = jnp.broadcast_to(grad_log[0:1], carry.shape)
    rate = par[1:2]
    grad_raw = (by_step - rate * grad_log) * sigmoid(raw[0] + par[0:1])
    raw_out[0] = grad_raw
    fold = lambda v: jnp.sum(v.reshape(CHUNK // 8, 8, CHUNK), axis=0)
    sums_out[0, 0:8] += fold(-rate * step * grad_log)
    sums_out[0, 8:16] += fold(grad_raw)


def chunk_spec(width, back=0, column_block=0):
    turn = (lambda c: back - 1 - c) if back else (lambda c: c)
    return pl.BlockSpec((1, CHUNK, width), lambda s, c: (s, turn(c), column_block))


def per_chunk(lines, width, back=0):
    turn = (lambda c: back - 1 - c) if back else (lambda c: c)
    return pl.BlockSpec((1, 1, lines, width), lambda s, c: (s, turn(c), 0, 0))


def per_sequence(lines, width):
    return pl.BlockSpec((1, lines, width), lambda s, c: (s, 0, 0))


def fixed(lines, width):
    return pl.BlockSpec((lines, width), lambda s, c: (0, 0))


def shaped(shape, dtype=F32):
    return jax.ShapeDtypeStruct(shape, dtype)


def call(kernel, name, chunks, ins, outs, operands, scratch=(), flops=0, after=()):
    in_specs = [spec for spec, _ in zip(ins, operands, strict=True)]
    moved = sum(v.size * v.dtype.itemsize for v in operands)
    moved += sum(v.size * v.dtype.itemsize for _, v in outs)
    count, skipped = len(in_specs), len(after)
    in_specs = in_specs + [pl.BlockSpec(memory_space=pl.ANY)] * skipped
    operands = tuple(operands) + tuple(after)
    return pl.pallas_call(
        lambda *refs: kernel(*refs[:count], *refs[count + skipped :]),
        name=name,
        grid=(2, chunks),
        in_specs=in_specs,
        out_specs=[spec for spec, _ in outs],
        out_shape=[shape for _, shape in outs],
        scratch_shapes=list(scratch),
        cost_estimate=pl.CostEstimate(flops=flops, bytes_accessed=moved, transcendentals=0),
        compiler_params=pltpu.CompilerParams(
            dimension_semantics=("arbitrary", "arbitrary"), vmem_limit_bytes=STEP_BYTES
        ),
    )(*operands)


STATE_SCRATCH = (pltpu.VMEM((STATE, INNER_Q), F32), pltpu.VMEM((8, INNER_Q), F32))


def scan_states(x, bc, raw, seg, par, spread, after=()):
    span = x.shape[1]
    n = span // CHUNK
    return call(
        state_kernel, "chunk_states", n,
        [chunk_spec(INNER_Q), chunk_spec(2 * STATE), chunk_spec(128, 0, TILE), per_chunk(8, 128), fixed(8, 128),
         fixed(128, INNER_Q)],
        [(per_chunk(STATE, INNER_Q), shaped((2, n, STATE, INNER_Q))), (per_chunk(8, INNER_Q), shaped((2, n, 8, INNER_Q))),
         (per_sequence(STATE, INNER_Q), shaped((2, STATE, INNER_Q))), (per_sequence(8, INNER_Q), shaped((2, 8, INNER_Q))),
         (per_sequence(16, INNER_Q), shaped((2, 16, INNER_Q), BF16))],
        (x, bc, raw, seg, par, spread), STATE_SCRATCH, 2 * 2 * span * STATE * INNER_Q, after=after,
    )


def scan_inside(x, bc, raw, seg, par, spread, after=()):
    span = x.shape[1]
    n = span // CHUNK
    return call(
        inside_kernel, "inside_chunks", n,
        [chunk_spec(INNER_Q), chunk_spec(2 * STATE), chunk_spec(128, 0, TILE), per_chunk(8, 128), fixed(8, 128),
         fixed(128, INNER_Q)],
        [(chunk_spec(INNER_Q), shaped(x.shape))],
        (x, bc, raw, seg, par, spread), (), 8 * 2 * span * CHUNK * INNER_Q, after=after,
    )[0]


def scan_outer(y, x, bc, raw, seg, par, spread, before, reach, start, gate, rows, after=()):
    span = x.shape[1]
    n = span // CHUNK
    return call(
        outer_kernel, "scan_and_gate", n,
        [chunk_spec(INNER_Q), chunk_spec(INNER_Q), chunk_spec(2 * STATE), chunk_spec(128, 0, TILE), per_chunk(8, 128), fixed(8, 128),
         fixed(128, INNER_Q), per_chunk(STATE, INNER_Q), per_chunk(8, INNER_Q), per_sequence(STATE, INNER_Q),
         chunk_spec(INNER_Q), fixed(8, INNER_Q)],
        [(chunk_spec(INNER_Q), shaped(x.shape)), (chunk_spec(INNER_Q), shaped(x.shape)),
         (per_chunk(1, 128), shaped((2, n, 1, 128)))],
        (y, x, bc, raw, seg, par, spread, before, reach, start, gate, rows), (), 8 * span * STATE * INNER_Q, after=after,
    )


def gate_along(grad, gated, rows, scale, after=()):
    span = gated.shape[1]
    n = span // CHUNK
    return call(
        along_kernel, "gate_along", n,
        [chunk_spec(INNER_Q), chunk_spec(INNER_Q), fixed(8, INNER_Q), per_chunk(1, 128)],
        [(per_chunk(1, 128), shaped((2, n, 1, 128))), (per_sequence(8, INNER_Q), shaped((2, 8, INNER_Q)))],
        (grad, gated, rows, scale), (), 10 * span * INNER_Q, after=after,
    )


def gate_back(grad, gated, y, x, gate, bc, raw, seg, par, spread, rows, scale, along, after=()):
    span = x.shape[1]
    n = span // CHUNK
    return call(
        gate_back_kernel, "gate_back_and_states", n,
        [chunk_spec(INNER_Q, n)] * 5 + [chunk_spec(2 * STATE, n), chunk_spec(128, n, TILE), per_chunk(8, 128, n), fixed(8, 128),
         fixed(128, INNER_Q), fixed(8, INNER_Q), per_chunk(1, 128, n), per_chunk(1, 128, n)],
        [(chunk_spec(INNER_Q, n), shaped(x.shape, BF16)), (chunk_spec(INNER_Q, n), shaped(x.shape, BF16)),
         (per_chunk(STATE, INNER_Q, n), shaped((2, n, STATE, INNER_Q))), (per_chunk(8, INNER_Q, n), shaped((2, n, 8, INNER_Q))),
         (per_sequence(STATE, INNER_Q), shaped((2, STATE, INNER_Q)))],
        (grad, gated, y, x, gate, bc, raw, seg, par, spread, rows, scale, along), STATE_SCRATCH,
        8 * span * STATE * INNER_Q, after=after,
    )


def scan_inside_back(x, bc, raw, seg, par, spread, grad, after=()):
    span = x.shape[1]
    n = span // CHUNK
    return call(
        inside_back_kernel, "inside_chunks_back", n,
        [chunk_spec(INNER_Q), chunk_spec(2 * STATE), chunk_spec(128, 0, TILE), per_chunk(8, 128), fixed(8, 128),
         fixed(128, INNER_Q), chunk_spec(INNER_Q)],
        [(chunk_spec(INNER_Q), shaped(x.shape)), (chunk_spec(STATE), shaped((2, span, STATE))),
         (chunk_spec(STATE), shaped((2, span, STATE)))],
        (x, bc, raw, seg, par, spread, grad), (), 24 * 2 * span * CHUNK * INNER_Q, after=after,
    )


def scan_outer_back(
    fed, b, c, x, bc, raw, seg, par, spread, before, reach, start, later, beyond, grad_end, end, total, grad, y, rows, after=()
):
    span = x.shape[1]
    n = span // CHUNK
    return call(
        outer_back_kernel, "scan_back", n,
        [chunk_spec(INNER_Q, n), chunk_spec(STATE, n), chunk_spec(STATE, n), chunk_spec(INNER_Q, n), chunk_spec(2 * STATE, n),
         chunk_spec(128, n, TILE), per_chunk(8, 128, n), fixed(8, 128), fixed(128, INNER_Q), per_chunk(STATE, INNER_Q, n),
         per_chunk(8, INNER_Q, n), per_sequence(STATE, INNER_Q), per_chunk(STATE, INNER_Q, n), per_chunk(8, INNER_Q, n),
         per_sequence(STATE, INNER_Q), per_sequence(STATE, INNER_Q), per_sequence(8, INNER_Q), chunk_spec(INNER_Q, n),
         chunk_spec(INNER_Q, n), fixed(8, INNER_Q)],
        [(chunk_spec(INNER_Q, n), shaped(x.shape)), (chunk_spec(2 * STATE, n), shaped((2, span, 2 * STATE))),
         (chunk_spec(128, n), shaped((2, span, 128))), (per_sequence(16, 128), shaped((2, 16, 128))),
         (per_sequence(8, INNER_Q), shaped((2, 8, INNER_Q)))],
        (fed, b, c, x, bc, raw, seg, par, spread, before, reach, start, later, beyond, grad_end, end, total, grad, y, rows),
        (pltpu.VMEM((8, 128), F32),), 24 * span * STATE * INNER_Q, after=after,
    )


def seg_table(seg_now, seg_before):
    span = seg_now.shape[1]
    rows = seg_now.reshape(2, span // CHUNK, 1, CHUNK)
    last = rows[..., -1:]
    before = jnp.concatenate((seg_before.reshape(2, 1, 1, 1), last[:, :-1]), axis=1)
    spread = lambda v: jnp.broadcast_to(v, rows.shape)
    return jnp.concatenate((rows, spread(before), spread(last)) + (rows,) * 5, axis=2)


def conv_terms(wide_ref, halo_ref, taps_ref, mask_ref, tail):
    own = wide_ref[0].astype(BF16).astype(F32)
    longer = jnp.concatenate((tail, own), axis=0)
    rows = [own]
    total = taps_ref[CONV : CONV + 1] + taps_ref[CONV - 1 : CONV] * own
    for back in range(1, CONV):
        same = jnp.concatenate([column(mask_ref[0, 0, back : back + 1])] * (own.shape[1] // 128), axis=1)
        earlier = longer[8 - back : 8 - back + CHUNK] * same
        rows.append(earlier)
        total = total + taps_ref[CONV - 1 - back : CONV - back] * earlier
    return own, rows, total


def conv_kernel(wide, halo, taps, mask, out, tail):
    @pl.when(pl.program_id(1) == 0)
    def _():
        tail[...] = halo[0].astype(F32)

    own, _, total = conv_terms(wide, halo, taps, mask, tail[...])
    tail[...] = own[CHUNK - 8 :]
    out[0] = (total * sigmoid(total)).astype(BF16)


def conv_back_kernel(wide, before, halo, taps, mask, grad, returned, out, sums_out, ahead):
    chunk = pl.num_programs(1) - 1 - pl.program_id(1)

    @pl.when(pl.program_id(1) == 0)
    def _():
        sums_out[...] = jnp.zeros_like(sums_out)
        ahead[...] = jnp.zeros_like(ahead)

    tail = jnp.where(chunk == 0, halo[0].astype(F32), before[0].astype(BF16).astype(F32))
    _, rows, total = conv_terms(wide, halo, taps, mask, tail)
    sig = sigmoid(total)
    pull = grad[0] * (sig * (1.0 + total * (1.0 - sig)))
    result = taps[CONV - 1 : CONV] * pull
    fold = lambda v: jnp.sum(v.reshape(CHUNK // 8, 8, v.shape[1]), axis=0)
    for back in range(1, CONV):
        same = jnp.concatenate([column(mask[0, 0, back : back + 1])] * (pull.shape[1] // 128), axis=1)
        masked = pull * same
        longer = jnp.concatenate((masked, ahead[8 * back - 8 : 8 * back]), axis=0)
        result = result + taps[CONV - 1 - back : CONV - back] * longer[back : back + CHUNK]
        ahead[8 * back - 8 : 8 * back] = masked[:8]
    for back in range(CONV):
        place = CONV - 1 - back
        sums_out[0, 8 * place : 8 * place + 8] += fold(pull * rows[back])
    sums_out[0, 8 * CONV : 8 * CONV + 8] += fold(pull)
    late = (pl.program_id(1) == 0).astype(F32) * returned[0].astype(F32)
    late = jnp.concatenate((jnp.zeros((CHUNK - 8, late.shape[1]), F32), late), axis=0)
    out[0] = (result + late).astype(BF16)


def conv_forward(wide, halo, taps, mask, width, at, after=()):
    n = wide.shape[1] // CHUNK
    lines = lambda rows: pl.BlockSpec((1, rows, width), lambda s, c: (s, 0, at))
    return call(
        conv_kernel, "conv", n,
        [chunk_spec(width, 0, at), lines(8), pl.BlockSpec((8, width), lambda s, c: (0, at)), per_chunk(8, 128)],
        [(chunk_spec(width), shaped(wide.shape[:2] + (width,), BF16))],
        (wide, halo, taps, mask), (pltpu.VMEM((8, width), F32),), 30 * wide.shape[1] * width, after=after,
    )[0]


def conv_backward(wide, halo, taps, mask, grad, returned, width, at, after=()):
    n = wide.shape[1] // CHUNK
    lines = lambda rows: pl.BlockSpec((1, rows, width), lambda s, c: (s, 0, at))
    steps = CHUNK // 8
    early = pl.BlockSpec(
        (1, 8, width), lambda s, c: (s, jnp.maximum((n - 1 - c) * steps - 1, 0), at)
    )
    return call(
        conv_back_kernel, "conv_back", n,
        [chunk_spec(width, n, at), early, lines(8), pl.BlockSpec((8, width), lambda s, c: (0, at)),
         per_chunk(8, 128, n), chunk_spec(width, n), lines(8)],
        [(chunk_spec(width, n), shaped(wide.shape[:2] + (width,), BF16)), (per_sequence(8 * CONV + 8, width), shaped((2, 8 * CONV + 8, width)))],
        (wide, wide, halo, taps, mask, grad, returned), (pltpu.VMEM((8 * CONV, width), F32),), 60 * wide.shape[1] * width, after=after,
    )


def mask_table(seg_ext, edge_rows):
    span = seg_ext.shape[1] - edge_rows
    here = seg_ext[:, edge_rows:]
    rows = [here == seg_ext[:, edge_rows - back : edge_rows - back + span] for back in range(CONV)]
    table = jnp.stack(rows + rows, axis=1).astype(F32)
    return jnp.moveaxis(table.reshape(2, 2 * CONV, span // CHUNK, CHUNK), 2, 1)


def tile_picks(owner, rows):
    down, across = grids((2 * STATE, 128))
    bc = (down - BC_Q * owner == across) & (across < BC_Q)
    down, across = grids((HEADS, 128))
    head = across - LANE
    dt = (down - HEADS_Q * owner == head) & (head >= 0) & (head < HEADS_Q)
    return bc.astype(F32), dt.astype(F32)


def cut_weights_kernel(q_ref, weight, *outs):
    for layer in range(weight.shape[0]):
        for k in range(TEAM):
            owner = q_ref[0] ^ k
            start = pl.multiple_of(owner * INNER_Q, 128)
            part = outs[layer * TEAM + k]
            part[:, :INNER_Q] = weight[layer, :, pl.ds(start, INNER_Q)]
            part[:, INNER_Q : 2 * INNER_Q] = weight[layer, :, pl.ds(INNER + start, INNER_Q)]
            bc, dt = tile_picks(owner, None)
            tile = mm(weight[layer, :, 2 * INNER : 2 * INNER + 2 * STATE], bc.astype(BF16))
            tile = tile + mm(weight[layer, :, INNER + CONVDIM :], dt.astype(BF16))
            part[:, 2 * INNER_Q :] = tile.astype(BF16)


def whole_spec(shape):
    return pl.BlockSpec(shape, lambda *_: (0,) * len(shape))


def whole_call(kernel, name, index, operands, outs, after=()):
    count, skipped = 1 + len(operands), len(after)
    return pl.pallas_call(
        lambda *refs: kernel(*refs[:count], *refs[count + skipped :]),
        name=name,
        grid_spec=pltpu.PrefetchScalarGridSpec(
            num_scalar_prefetch=1,
            grid=(1,),
            in_specs=[whole_spec(v.shape) for v in operands]
            + [pl.BlockSpec(memory_space=pl.ANY)] * skipped,
            out_specs=[whole_spec(s.shape) for s in outs],
        ),
        out_shape=list(outs),
        compiler_params=pltpu.CompilerParams(vmem_limit_bytes=VMEM_BYTES),
    )(index, *operands, *after)


def tie(value, *after):
    anywhere = pl.BlockSpec(memory_space=pl.ANY)
    return pl.pallas_call(
        lambda *refs: None,
        name="tie",
        in_specs=[anywhere] * (1 + len(after)),
        out_specs=anywhere,
        out_shape=shaped(value.shape, value.dtype),
        input_output_aliases={0: 0},
    )(value, *after)


def norm_kernel(x_ref, stream, gain, out):
    values = stream[...].astype(F32)
    mean = jnp.mean(values * values, axis=-1, keepdims=True)
    normed = (values * lax.rsqrt(mean + EPS) * gain[...]).astype(BF16)
    width = normed.shape[1] // 2
    x = x_ref[0]
    out[:, pl.ds(pl.multiple_of(x * width, 128), width)] = normed[:, :width]
    out[:, pl.ds(pl.multiple_of((1 - x) * width, 128), width)] = normed[:, width:]


def norm_rows(x, stream, gain, after=()):
    return whole_call(norm_kernel, "norm", x, (stream, gain), [shaped(stream.shape, BF16)], after)[0]


def scale_kernel(gated, scale, rows, out):
    lines = jnp.concatenate([column(scale[0, 0])] * (INNER_Q // 128), axis=1)
    out[0] = (gated[0] * lines * rows[1:2]).astype(BF16)


def scale_rows(gated, scale, rows, after=()):
    n = gated.shape[1] // CHUNK
    return call(
        scale_kernel, "scale_rows", n,
        [chunk_spec(INNER_Q), per_chunk(1, 128), fixed(8, INNER_Q)],
        [(chunk_spec(INNER_Q), shaped(gated.shape, BF16))],
        (gated, scale, rows), (), 4 * gated.size, after=after,
    )[0]


def cut_weights(q, weight):
    layers, rows = weight.shape[:2]
    outs = [shaped((rows, INNER_Q + WIDE), BF16)] * (TEAM * layers)
    outs = whole_call(cut_weights_kernel, "cut_weights", q, (weight,), outs)
    return [outs[TEAM * layer : TEAM * layer + TEAM] for layer in range(layers)]


def place_of(owner):
    return (owner % 2) * 2 + owner // 2


def wide_piece_kernel(q_ref, *refs):
    out = refs[-1]
    for k in range(TEAM):
        out[place_of(q_ref[0] ^ k)] = refs[k][:, INNER_Q:]


def gate_piece_kernel(q_ref, *refs):
    rows, out = refs[TEAM], refs[-1]
    for k in range(TEAM):
        out[place_of(q_ref[0] ^ k)] = refs[k][:, :INNER_Q]
    for block in range(TEAM):
        half = block % 2 * INNER_Q
        out[TEAM + block] = rows[block // 2, :, half : half + INNER_Q]


def all_piece_kernel(q_ref, *refs):
    out = refs[-1]
    for k in range(TEAM):
        out[place_of(q_ref[0] ^ k)] = refs[k][...]


def all_piece(q, parts, after=()):
    shape = (TEAM,) + parts[0].shape
    return whole_call(all_piece_kernel, "all_piece", q, parts, [shaped(shape, BF16)], after)[0]


def arrange_kernel(_, gathered, gate, wide):
    for x in range(2):
        for z in range(gate.shape[2]):
            for block in range(TEAM):
                rows = gathered[x, z, block]
                gate[x, block // 2, z, block % 2] = rows[:, :INNER_Q]
                wide[x, block // 2, z, block % 2] = rows[:, INNER_Q:]


def arrange(index, gathered):
    size, rows = gathered.shape[1], gathered.shape[3]
    outs = [shaped((2, 2, size, 2, rows, width), BF16) for width in (INNER_Q, WIDE)]
    gate, wide = whole_call(arrange_kernel, "arrange", index, (gathered,), outs)
    return wide.reshape(-1, WIDE), gate.reshape(-1, INNER_Q)


def by_owner_kernel(x_ref, grad, out):
    for side in range(2):
        x = x_ref[0] if side == 0 else 1 - x_ref[0]
        for z in range(out.shape[1]):
            for block in range(TEAM):
                out[x, z, block] = grad[side, block // 2, z, block % 2].astype(BF16)


def both_by_owner_kernel(x_ref, gate, out_grad, out):
    for side in range(2):
        x = x_ref[0] if side == 0 else 1 - x_ref[0]
        for z in range(out.shape[1]):
            for block in range(TEAM):
                upper, lower = block // 2, block % 2
                half = slice(lower * INNER_Q, lower * INNER_Q + INNER_Q)
                out[x, z, block] = gate[side, upper, z, lower].astype(BF16)
                out[side, z, TEAM + block] = out_grad[z, side, upper, :, half].astype(BF16)


def both_by_owner(x_first_of, gate, out_grad, size, rows):
    operands = (
        gate.reshape(2, 2, size, 2, rows, INNER_Q),
        out_grad.reshape(size, 2, 2, rows, 2 * INNER_Q),
    )
    outs = [shaped((2, size, 2 * TEAM, rows, INNER_Q), BF16)]
    return whole_call(both_by_owner_kernel, "both_by_owner", x_first_of, operands, outs)[0]


def by_owner(x_first_of, grad, size, rows):
    width = grad.shape[-1]
    operands = (grad.reshape(2, 2, size, 2, rows, width),)
    outs = [shaped((2, size, TEAM, rows, width), BF16)]
    return whole_call(by_owner_kernel, "by_owner", x_first_of, operands, outs)[0]


def wide_piece(q, parts, after=()):
    shape = (TEAM, parts[0].shape[0], WIDE)
    return whole_call(wide_piece_kernel, "wide_piece", q, parts, [shaped(shape, BF16)], after)[0]


def gate_piece(q, parts, rows, after=()):
    count = parts[0].shape[0]
    operands = tuple(parts) + (rows.reshape(2, count, -1),)
    outs = [shaped((2 * TEAM, count, INNER_Q), BF16)]
    return whole_call(gate_piece_kernel, "gate_piece", q, operands, outs, after)[0]


def arrange_both_kernel(x_ref, gathered, gate, out):
    for side in range(2):
        x = x_ref[0] if side == 0 else 1 - x_ref[0]
        for z in range(gate.shape[2]):
            for block in range(TEAM):
                upper, lower = block // 2, block % 2
                gate[side, upper, z, lower] = gathered[x, z, block]
                half = slice(lower * INNER_Q, lower * INNER_Q + INNER_Q)
                out[z, side, upper, :, half] = gathered[side, z, TEAM + block]


def arrange_both(x_first_of, gathered):
    size, rows = gathered.shape[1], gathered.shape[3]
    outs = [
        shaped((2, 2, size, 2, rows, INNER_Q), BF16),
        shaped((size, 2, 2, rows, 2 * INNER_Q), BF16),
    ]
    gate, out = whole_call(arrange_both_kernel, "arrange_both", x_first_of, (gathered,), outs)
    return gate.reshape(-1, INNER_Q), out.reshape(-1, 2 * INNER_Q)


def whole_wide_kernel(place, *refs):
    out = refs[-1]
    size = out.shape[2]
    for side in range(2):
        for hop in range(size):
            source = lax.rem(place[0] - hop + size, size)
            for block in range(TEAM):
                out[side, block // 2, source, block % 2] = refs[side * size + hop][block]


def whole_columns(place, pieces, after=()):
    size = len(pieces) // 2
    rows, width = pieces[0].shape[1:]
    outs = [shaped((2, 2, size, 2, rows, width), BF16)]
    whole = whole_call(whole_wide_kernel, "whole_columns", place, pieces, outs, after)[0]
    return whole.reshape(-1, width)


def grad_parts_kernel(q_ref, gate, wide, *outs):
    for k in range(TEAM):
        block = place_of(q_ref[0] ^ k)
        outs[k][:, :INNER_Q] = gate[block]
        outs[k][:, INNER_Q:] = wide[block]


def grad_parts(q, gate, wide):
    outs = [shaped((wide.shape[1], INNER_Q + WIDE), BF16)] * TEAM
    return whole_call(grad_parts_kernel, "grad_parts", q, (gate, wide), outs)


def cut_params_kernel(q_ref, conv_weight, conv_bias, dt_bias, a_log, skip, out_gain, spread, taps, par, rows):
    owner = q_ref[0]
    start = pl.multiple_of(owner * INNER_Q, 128)
    bc, dt = tile_picks(owner, None)
    bc, dt = bc.astype(BF16), dt.astype(BF16)
    mine = pl.ds(start, INNER_Q)
    for layer in range(conv_weight.shape[0]):
        one = slice(layer, layer + 1)
        taps[layer, :CONV, :INNER_Q] = conv_weight[layer, :, mine]
        taps[layer, :CONV, INNER_Q:] = exact_mm(conv_weight[layer, :, INNER:], bc)
        taps[layer, CONV : CONV + 1, :INNER_Q] = conv_bias[one, mine]
        taps[layer, CONV : CONV + 1, INNER_Q:] = exact_mm(conv_bias[one, INNER:], bc)
        taps[layer, CONV + 1 :] = jnp.zeros((7 - CONV, WIDE), F32)
        par[layer, 0:1] = exact_mm(dt_bias[one], dt)
        par[layer, 1:2] = exact_mm(jnp.exp(a_log[one]), dt)
        par[layer, 2:] = jnp.zeros((6, 128), F32)
        rows[layer, 0:1] = exact_mm(exact_mm(skip[one], dt), spread[...])
        rows[layer, 1:2] = out_gain[one, mine]
        rows[layer, 2:] = jnp.zeros((6, INNER_Q), F32)


def cut_params(q, params, after):
    layers = params[0].shape[0]
    shapes = [(layers, 8, WIDE), (layers, 8, 128), (layers, 8, INNER_Q)]
    return whole_call(cut_params_kernel, "cut_params", q, params, [shaped(s) for s in shapes], after)


def join_kernel(q_ref, *refs):
    out = refs[-1]
    for layer in range(out.shape[0]):
        shared = 0.0
        for k in range(TEAM):
            owner = q_ref[0] ^ k
            start = pl.multiple_of(owner * INNER_Q, 128)
            part = refs[layer * TEAM + k]
            out[layer, :, pl.ds(start, INNER_Q)] = part[:, :INNER_Q].astype(F32)
            out[layer, :, pl.ds(INNER + start, INNER_Q)] = part[:, INNER_Q : 2 * INNER_Q].astype(F32)
            bc, dt = tile_picks(owner, None)
            both = jnp.concatenate((bc, dt), axis=0).astype(BF16)
            shared = shared + mm(part[:, 2 * INNER_Q :], both, (1, 1))
        out[layer, :, 2 * INNER :] = shared


def join_weights(q, parts):
    flat = [v for layer in parts for v in layer]
    shape = (len(parts), flat[0].shape[0], 2 * INNER + 2 * STATE + HEADS)
    return whole_call(join_kernel, "join_weights", q, flat, [shaped(shape)])[0]


SMALL = (16, WIDE)


def pack_small_kernel(conv_x, conv_tile, heads, skip, gain, norm, spread, out):
    fold = lambda v, rows: jnp.sum(v[:, rows], axis=(0, 1), keepdims=True)[0]
    for line in range(CONV + 1):
        rows = slice(8 * line, 8 * line + 8)
        out[line : line + 1, :INNER_Q] = fold(conv_x[...], rows)
        out[line : line + 1, INNER_Q:] = fold(conv_tile[...], rows)
    line = CONV + 1
    out[line:] = jnp.zeros((SMALL[0] - line, WIDE), F32)
    every = slice(0, 8)
    out[line + 1 : line + 2, :INNER_Q] = fold(gain[...], every)
    out[line + 2 : line + 3, :128] = fold(heads[...], slice(8, 16))
    out[line + 3 : line + 4, :128] = fold(heads[...], every)
    by_head = exact_mm(skip[0] + skip[1], spread[...], (1, 1))
    out[line + 4 : line + 5, :128] = jnp.sum(by_head, axis=0, keepdims=True)
    width = norm.shape[1] // 2
    out[line + 5 : line + 6, :width] = norm[:, :width]
    out[line + 6 : line + 7, :width] = norm[:, width:]


def pack_small(*parts):
    return pl.pallas_call(pack_small_kernel, name="pack_small", out_shape=shaped(SMALL))(*parts)


def lanes_of(values):
    return lax.broadcasted_iota(jnp.int32, values.shape, 1)


def open_small_kernel(q_ref, *refs):
    norm, conv_weight, conv_bias, dt_bias, a_log, skip, gain = refs[-7:]
    layers = norm.shape[0]
    line = CONV + 1
    for layer in range(layers):
        one = slice(layer, layer + 1)
        packs = [ref[layer] for ref in refs[:TEAM]]
        shared, heads = [], 0.0
        for k in range(TEAM):
            owner = q_ref[0] ^ k
            start = pl.multiple_of(owner * INNER_Q, 128)
            mine = pl.ds(start, INNER_Q)
            pack = packs[k]
            conv_weight[layer, :, mine] = pack[:CONV, :INNER_Q]
            conv_bias[one, mine] = pack[CONV:line, :INNER_Q]
            tile = pack[:8, INNER_Q:]
            tile = jnp.where(lanes_of(tile) < BC_Q, tile, 0.0)
            tile = jnp.where(owner % 2 == 0, tile, pltpu.roll(tile, BC_Q, 1))
            shared.append([jnp.where(owner // 2 == side, tile, 0.0) for side in range(2)])
            rows = pack[line + 2 : line + 5, :128]
            in_head = (lanes_of(rows) >= LANE) & (lanes_of(rows) < LANE + HEADS_Q)
            rows = jnp.where(in_head, rows, 0.0)
            placed = 0.0
            for which in range(TEAM):
                turned = pltpu.roll(rows, (HEADS_Q * which - LANE) % 128, 1)
                placed = placed + jnp.where(owner == which, turned, 0.0)
            heads = heads + placed[:, :HEADS]
            gain[one, mine] = pack[line + 1 : line + 2, :INNER_Q]
        shared = jnp.concatenate([sum([s[side] for s in shared]) for side in range(2)], axis=1)
        conv_weight[layer, :, INNER:] = shared[:CONV]
        conv_bias[one, INNER:] = shared[CONV:line]
        dt_bias[one], a_log[one], skip[one] = heads[0:1], heads[1:2], heads[2:3]
        width = norm.shape[1] // 2
        halves_of = lambda n: packs[n][line + 5 : line + 7, :width]
        total = (halves_of(0) + halves_of(1)) + (halves_of(2) + halves_of(3))
        norm[one, :width] = total[0:1]
        norm[one, width:] = total[1:2]


def open_small(q, packs, features):
    layers = packs[0].shape[0]
    flat = list(packs)
    shapes = [
        (layers, features), (layers, CONV, CONVDIM), (layers, CONVDIM), (layers, HEADS), (layers, HEADS),
        (layers, HEADS), (layers, INNER),
    ]
    return pl.pallas_call(
        open_small_kernel,
        name="open_small",
        grid_spec=pltpu.PrefetchScalarGridSpec(
            num_scalar_prefetch=1,
            grid=(1,),
            in_specs=[whole_spec(v.shape) for v in flat],
            out_specs=[whole_spec(s) for s in shapes],
        ),
        out_shape=[shaped(s) for s in shapes],
    )(q, *flat)


def spread_matrix():
    head = jnp.arange(128)[:, None] - LANE
    return (jnp.arange(INNER_Q)[None, :] // HEADDIM == head).astype(BF16)


def gap_decays(spans):
    rows = []
    for start in range(len(spans)):
        row = []
        running = jnp.ones_like(spans[0])
        for stop, span in enumerate(spans):
            if stop <= start:
                row.append(jnp.zeros_like(running))
                continue
            row.append(running)
            running = running * span
        rows.append(jnp.stack(row))
    return jnp.stack(rows)


def mix_states(states, bits=None, weights=None):
    size = lax.axis_size("z")
    z = lax.axis_index("z")
    width = states.shape[1] // size
    decay = lambda rows: jnp.sum(rows[:, :3].astype(F32), axis=1)
    if size > NEAR:
        if weights is None:
            weights = gap_decays([decay(v) for v in lax.all_gather(bits, "z")])
        cuts = jnp.moveaxis(states.reshape(2, size, width, -1), 1, 0).astype(BF16)
        parts = lax.all_to_all(cuts, "z", 0, 0, tiled=True).astype(F32)
        sums = jnp.sum(weights[:, :, :, None] * parts[:, None], axis=0)
        back = lax.all_to_all(sums.astype(BF16), "z", 0, 0, tiled=True).astype(F32)
        return jnp.moveaxis(back, 0, 1).reshape(states.shape), weights
    ring = lambda k: lax.rem(z + k + size, size)

    def cut(k):
        part = lax.dynamic_slice_in_dim(states, k * width, width, 1).astype(BF16)
        return part if weights is not None else jnp.concatenate((part, bits), axis=1)

    parts = [cut(z)] + [shift(cut(ring(hop)), "z", hop) for hop in range(1, size)]
    if weights is None:
        everyone = jnp.stack([decay(p[:, width:]) for p in parts])
        spans = [
            lax.dynamic_index_in_dim(everyone, lax.rem(z - k + size, size), 0, False)
            for k in range(size)
        ]
        weights = gap_decays(spans)
        parts = [p[:, :width] for p in parts]
    results = []
    for away in range(size):
        to = lax.dynamic_index_in_dim(weights, ring(away), 1, False)
        total = 0.0
        for hop in range(size):
            weight = lax.dynamic_index_in_dim(to, ring(-hop), 0, False)
            total = total + weight[:, None] * parts[hop].astype(F32)
        results.append(total)
    back = [results[0]] + [
        shift(results[hop].astype(BF16), "z", hop).astype(F32) for hop in range(1, size)
    ]
    whole = jnp.zeros(states.shape, F32)
    for hop in range(size):
        whole = lax.dynamic_update_slice_in_dim(whole, back[hop], ring(-hop) * width, 1)
    return whole, weights


def local(
    tokens,
    segments,
    out_grad,
    norm_gain,
    in_weight,
    conv_weight,
    conv_bias,
    dt_bias,
    a_log,
    skip,
    out_gain,
    out_weight,
):
    _, length, features = tokens.shape
    edge = CONV - 1
    layer_count, in_rows = in_weight.shape[:2]
    out_rows = out_weight.shape[1]
    layers = range(layer_count)
    q = member()
    owner = q.reshape(1)
    span = 2 * length
    row_count = 2 * span

    near = lax.axis_size("z") <= NEAR
    x_place = lax.axis_index("x").reshape(1)
    cuts = cut_weights(owner, in_weight)
    size = lax.axis_size("z")
    place = jnp.stack((lax.axis_index("z"), lax.axis_index("x")))
    exchanged = [around_team(parts) for parts in cuts]
    moved = [lax.ppermute(out_weight[k], ("x", "y"), TURN) for k in layers]
    nowhere = jnp.zeros((1,), jnp.int32)

    def fetch_rows(rows):
        return lax.all_gather(rows, ("z", "x"), axis=0, tiled=True)

    def fetch_columns(layer_id, after):
        gathered = lax.all_gather(all_piece(owner, exchanged[layer_id], after), ("x", "z"))
        return arrange(nowhere, gathered.reshape((2, size) + gathered.shape[1:]))

    if near:
        wide_line, wide_all = fetch(wide_piece(owner, exchanged[0]))

    seg_now = team_gather(segments.astype(F32).reshape(length))
    prev_seg = step_line(seg_now[:, span - edge :], "z", 1)
    seg_ext = jnp.concatenate((prev_seg, seg_now), axis=1)
    seg = seg_table(seg_now, seg_ext[:, edge - 1])
    mask = mask_table(seg_ext, edge)
    spread = spread_matrix()
    all_taps, all_par, all_rows = cut_params(
        owner, (conv_weight, conv_bias, dt_bias, a_log, skip, out_gain, spread), exchanged[0][1:]
    )

    stream = tokens.astype(F32).reshape(length, features)
    last_grad = team_gather(tie(out_grad.reshape(length, features), exchanged[0][1]))
    saved, full = [], []
    for layer_id in layers:
        taps, par, rows = all_taps[layer_id], all_par[layer_id], all_rows[layer_id]
        first, final = layer_id == 0, layer_id == layer_count - 1
        fast = near and first
        x_order = x_place if fast else nowhere
        normed = norm_rows(
            x_order,
            tokens.reshape(length, features) if first else stream,
            norm_gain[layer_id : layer_id + 1],
            (wide_all[1:] if fast else []) + ([last_grad] if first else []),
        )
        normed = team_gather(normed)
        earlier = step_line(normed[:, span - 16 :], "z", 1).reshape(32, features)
        normed = normed.reshape(row_count, features)
        dot = partial(jnp.dot, preferred_element_type=F32)
        if fast:
            piece = gate_piece(
                owner, exchanged[0], moved[0], wide_all[1:] + [seg, mask, all_taps]
            )
            gathered = lax.all_gather(piece, ("x", "z")).reshape((2, size) + piece.shape)
            full_gate, full_out = arrange_both(x_place, gathered)
            full_wide = whole_columns(place, wide_all)
        elif first:
            full_wide, full_gate = fetch_columns(0, [])
        else:
            full_wide, full_gate = next_columns
        wide = dot(normed, full_wide).reshape(2, span, WIDE)
        if not fast:
            full_out = fetch_rows(moved[0]) if first else next_rows
        gate_raw = dot(normed, full_gate).reshape(2, span, INNER_Q)
        full.append((full_wide, full_gate, full_out))
        halo = dot(earlier, full_wide).reshape(2, 16, WIDE)[:, 8:].astype(BF16).astype(F32)
        bc_own = conv_forward(
            wide, halo, taps, mask, 128, TILE, [v for e in exchanged[1:] for v in e[1:]] if first else []
        )[..., :BC_Q]
        bc_same = y_swap(bc_own)
        bc = jnp.concatenate(
            in_order((bc_own, core_swap(bc_own)[::-1], bc_same, core_swap(bc_same)[::-1])), axis=-1
        )
        heads_x = conv_forward(wide, halo, taps, mask, INNER_Q, 0)
        scan_in = (heads_x, bc, wide, seg, par, spread)
        before, reach, end, total_reach, bits = scan_states(
            *scan_in
        )
        start, weights = mix_states(end, bits)
        inside = scan_inside(*scan_in, after=[] if first else [full_out])
        if not final:
            next_columns = fetch_columns(layer_id + 1, [start, inside])
            next_rows = fetch_rows(tie(moved[layer_id + 1], start))
        scan_y, gated, square = scan_outer(
            inside, *scan_in, before, reach, start, gate_raw, rows,
        )
        scale = lax.rsqrt(team_sum(square) / INNER + EPS)
        normed_y = scale_rows(gated, scale, rows)
        normed_y = normed_y.reshape(row_count, INNER_Q)
        sequence = lambda v, k: lax.slice_in_dim(v, k * span, (k + 1) * span, axis=0)
        branch_far = dot(sequence(normed_y, 1), full_out)
        branch = dot(sequence(normed_y, 0), full_out)
        saved.append(
            (
                stream,
                normed,
                gate_raw,
                halo,
                scan_in,
                (before, reach, start),
                (end, total_reach),
                weights,
                scan_y,
                gated,
                scale,
                normed_y,
                taps,
                rows,
            )
        )
        stream = stream + team_scatter(branch, branch_far)
    grad_stream = out_grad.astype(F32).reshape(length, features)
    in_parts = [None] * layer_count
    out_shards = [None] * layer_count
    small = [None] * layer_count
    for layer_id in reversed(layers):
        (
            stream_in,
            normed,
            gate_raw,
            halo,
            scan_in,
            states_before,
            states_end,
            weights,
            scan_y,
            gated,
            scale,
            normed_y,
            taps,
            rows,
        ) = saved[layer_id]
        heads_x, scan_rest = scan_in[0], scan_in[1:]
        wide = scan_in[2]
        full_wide, full_gate, full_out = full[layer_id]
        last = layer_id == 0
        grad_branch = team_gather(grad_stream.astype(BF16)) if last_grad is None else last_grad
        last_grad = None
        grad_branch = grad_branch.reshape(row_count, features)
        out_full_grad = jnp.einsum("ri,rd->id", normed_y, grad_branch, preferred_element_type=F32)
        back = partial(jnp.einsum, "rp,dp->rd", preferred_element_type=F32)
        grad_normed_y = back(grad_branch, full_out).reshape(2, span, INNER_Q)
        along, grad_gain = gate_along(grad_normed_y, gated, rows, scale)
        along = team_sum(along)
        grad_ssd, grad_gate, after, beyond, grad_start = gate_back(
            grad_normed_y, gated, scan_y, heads_x, gate_raw, *scan_rest, rows, scale, along,
            [out_full_grad],
        )
        turn = partial(jnp.einsum, "rd,rp->dp", preferred_element_type=F32)
        grad_gate = grad_gate.reshape(row_count, INNER_Q)
        gate_grad = turn(normed, grad_gate)
        fast = near and last
        x_order = x_place if fast else nowhere
        both = both_by_owner(x_order, gate_grad, out_full_grad, size, in_rows)
        both_total = sum_to_owner(both)
        gate_total = both_total[:TEAM]
        out_total = both_total[TEAM:].reshape(2, 2, in_rows, INNER_Q).swapaxes(1, 2)
        out_total = out_total.reshape(out_rows, features)
        out_shards[layer_id] = lax.ppermute(out_total, ("x", "y"), TURN).astype(F32)
        grad_end, _ = mix_states(grad_start, None, weights.swapaxes(0, 1))
        grad_inside = scan_inside_back(*scan_in, grad_ssd, after=[both])
        grad_x, grad_bc, grad_raw, head_sums, skip_sums = scan_outer_back(
            *grad_inside,
            *scan_in,
            *states_before,
            after,
            beyond,
            grad_end,
            *states_end,
            grad_ssd,
            scan_y,
            rows,
        )
        blocks = [grad_bc[..., BC_Q * k : BC_Q * k + BC_Q].astype(BF16) for k in range(TEAM)]
        turned = lambda k: lax.select_n(q ^ k, *blocks)
        half = lambda k: turned(k).astype(F32) + core_swap(turned(k ^ 1)).astype(F32)[::-1]
        grad_bc_own = half(0) + y_swap(half(2).astype(BF16)).astype(F32)
        grad_tile = jnp.pad(grad_bc_own, ((0, 0), (0, 0), (0, 128 - BC_Q)))

        edge_in = jnp.concatenate(
            (halo[:, 8 - edge :], wide[:, :edge].astype(BF16).astype(F32)), axis=1
        )
        edge_conv = lambda v: conv_piece(seg_ext[:, : 2 * edge], v, taps[:CONV], taps[CONV])
        edge_grad = jnp.concatenate((grad_x[:, :edge], grad_tile[:, :edge]), axis=-1)
        edge_grad = jax.vjp(edge_conv, edge_in)[1](edge_grad)[0][:, :edge].astype(BF16)
        returned = step_line(edge_grad, "z", -1).astype(F32)
        returned = jnp.pad(returned, ((0, 0), (8 - edge, 0), (0, 0)))
        grad_conv_x, conv_sums = conv_backward(
            wide, halo, taps, mask, grad_x, returned, INNER_Q, 0
        )
        grad_conv_tile, tile_sums = conv_backward(
            wide, halo, taps, mask, grad_tile, returned, 128, TILE
        )
        grad_wide = jnp.concatenate(
            (grad_conv_x, grad_conv_tile[..., :BC_Q], grad_raw[..., BC_Q:].astype(BF16)), axis=-1
        ).reshape(row_count, WIDE)
        in_grad = turn(normed, grad_wide)
        total = sum_to_owner(by_owner(x_order, in_grad, size, in_rows))
        in_parts[layer_id] = around_team(grad_parts(owner, gate_total, total))
        full_wide, full_gate, _ = full[layer_id]
        sequence = lambda v, k: lax.slice_in_dim(v, k * span, (k + 1) * span, axis=0)
        both_back = lambda k: back(sequence(grad_wide, k), full_wide) + back(
            sequence(grad_gate, k), full_gate
        )
        grad_far, grad_normed = both_back(1), both_back(0)
        norm_grad = jnp.sum(in_grad * full_wide.astype(F32), axis=1)
        norm_grad = norm_grad + jnp.sum(gate_grad * full_gate.astype(F32), axis=1)
        if fast:
            norm_grad = x_first(norm_grad)
        norm_grad = norm_grad / norm_gain[layer_id]
        grad_normed = team_scatter(grad_normed, grad_far)
        if fast:
            grad_normed = x_first(grad_normed)
        else:
            grad_normed = tie(grad_normed, both_total)
        _, pull_norm = jax.vjp(lambda v: norm_piece(v, norm_gain[layer_id]), stream_in)
        (grad_inner,) = pull_norm(grad_normed)
        grad_stream = grad_stream + grad_inner
        small[layer_id] = pack_small(
            conv_sums, tile_sums, head_sums, skip_sums, grad_gain, norm_grad.reshape(1, features),
            spread,
        )
    mixed = stream.reshape(1, length, features).astype(BF16)
    pack = xor_sum(xor_sum(jnp.stack(small), "x"), "z")
    across = y_swap(pack)
    packs = (pack, core_swap(pack), across, core_swap(across))
    norm_sum, taps_sum, bias_sum, dt_sum, decay_sum, skip_sum, gain_sum = open_small(
        owner, packs, features
    )
    return (
        mixed,
        grad_stream.reshape(1, length, features),
        norm_sum,
        join_weights(owner, in_parts),
        taps_sum,
        bias_sum,
        dt_sum,
        decay_sum,
        skip_sum,
        gain_sum,
        jnp.stack(out_shards),
    )


def solution(mesh):
    rows, spans = mesh.devices.shape
    split = Mesh(mesh.devices.reshape(rows // 2, 2, spans // 2, 2), ("x", "core", "z", "y"))
    tokens = P(("x", "core"), ("z", "y"), None)
    weight = P(None, ("x", "core", "z", "y"), None)
    return jax.shard_map(
        local,
        mesh=split,
        in_specs=(
            tokens,
            P(("x", "core"), ("z", "y")),
            tokens,
            P(),
            weight,
            P(),
            P(),
            P(),
            P(),
            P(),
            P(),
            weight,
        ),
        out_specs=(tokens, tokens, P(), weight, P(), P(), P(), P(), P(), P(), weight),
        check_vma=False,
    )
```

```python
from functools import partial

import jax
import jax.numpy as jnp
from jax import lax
from jax.experimental import pallas as pl
from jax.experimental.pallas import tpu as pltpu
from jax.sharding import Mesh
from jax.sharding import PartitionSpec as P

HEADS = 48
HEADDIM = 64
STATE = 128
CONV = 4
INNER = 3072
CONVDIM = 3328

TEAM = 4
HEADS_Q = HEADS // TEAM
INNER_Q = INNER // TEAM
BC_Q = 2 * STATE // TEAM
CONV_Q = INNER_Q + BC_Q
WIDE = 896

EPS = 1e-05
VMEM_BYTES = 40 * 1024 * 1024
STEP_BYTES = 20 * 1024 * 1024
NEAR = 4
SWAP = [(0, 1), (1, 0)]
BF16 = jnp.bfloat16
F32 = jnp.float32


def shift(block, axis, distance):
    size = lax.axis_size(axis)
    return lax.ppermute(block, axis, [(i, (i + distance) % size) for i in range(size)])


def step_line(block, axis, distance):
    devices = range(lax.axis_size(axis))
    return lax.ppermute(block, axis, [(i, i + distance) for i in devices if i + distance in devices])


def core_swap(block):
    return lax.ppermute(block, "core", SWAP)


def y_swap(block):
    return lax.ppermute(block, "y", SWAP)


def diagonal_swap(block):
    return lax.ppermute(block, ("core", "y"), [(0, 3), (1, 2), (2, 1), (3, 0)])


def xor_sum(values, axis):
    size = lax.axis_size(axis)
    bit = 1
    while bit < size:
        values = tie(values + lax.ppermute(values, axis, [(i, i ^ bit) for i in range(size)]))
        bit *= 2
    return values


def member():
    return lax.axis_index("y") * 2 + lax.axis_index("core")


def in_order(parts):
    q = member()
    return [lax.select_n(q ^ j, *parts) for j in range(TEAM)]


def around_team(blocks):
    return blocks[0], core_swap(blocks[1]), y_swap(blocks[2]), diagonal_swap(blocks[3])


def by_y(own, other):
    first = lax.axis_index("y") == 0
    return jnp.where(first, jnp.concatenate((own, other), 1), jnp.concatenate((other, own), 1))


def team_gather(block):
    pair = jnp.stack((block, core_swap(block)))
    crossed = y_swap(block)
    other = jnp.stack((crossed, core_swap(crossed)))
    return by_y(pair, other)


def team_scatter(own, other):
    total = own + core_swap(other.astype(BF16)).astype(F32)
    half = total.shape[0] // 2
    y = lax.axis_index("y")
    mine = lax.dynamic_slice_in_dim(total, y * half, half, 0)
    theirs = lax.dynamic_slice_in_dim(total, (1 - y) * half, half, 0)
    return mine + y_swap(theirs.astype(BF16)).astype(F32)


def team_sum(values):
    across = core_swap(values) + diagonal_swap(values)
    return (values + y_swap(values)) + across[::-1]


def x_swap(block):
    return lax.ppermute(block, "x", SWAP)


def line_pieces(piece):
    return [piece] + [shift(piece, "z", hop) for hop in range(1, lax.axis_size("z"))]


def fetch(piece):
    line = line_pieces(piece)
    return line, line + [x_swap(p) for p in line]


def sum_to_owner(blocks):
    flat = blocks.reshape((-1,) + blocks.shape[2:])
    return lax.psum_scatter(flat, ("x", "z"), scatter_dimension=0)


TURN = [(0, 0), (1, 2), (2, 1), (3, 3)]


def x_first(values):
    low, high = jnp.split(values, 2, axis=-1)
    first = lax.axis_index("x") == 0
    return jnp.where(first, jnp.concatenate((low, high), -1), jnp.concatenate((high, low), -1))


def rms_scale(values):
    return values * lax.rsqrt(jnp.mean(values * values, axis=-1, keepdims=True) + EPS)


def norm_piece(stream, norm_scale):
    return rms_scale(stream) * norm_scale


def conv_piece(seg_ext, extended, conv_taps, conv_shift):
    length = extended.shape[-2] - CONV + 1
    seg_here = seg_ext[..., CONV - 1 :]
    summed = conv_shift
    for offset in range(CONV):
        same_doc = (seg_ext[..., offset : offset + length] == seg_here)[..., None]
        summed = summed + conv_taps[offset] * extended[..., offset : offset + length, :] * same_doc
    return jax.nn.silu(summed)


CHUNK = 128
LANE = 64
NEVER = -1e30
TILE = INNER_Q // 128


def split_parts(values):
    high = values.astype(BF16)
    rest = values - high.astype(F32)
    middle = rest.astype(BF16)
    return high, middle, (rest - middle.astype(F32)).astype(BF16)


def mm(a, b, over=(1, 0)):
    return lax.dot_general(
        a, b, (((over[0],), (over[1],)), ((), ())), preferred_element_type=F32
    )


def exact_mm(values, ones, over=(1, 0)):
    high, middle, low = split_parts(values)
    return (mm(low, ones, over) + mm(middle, ones, over)) + mm(high, ones, over)


def spread_mm(values, ones, over=(1, 0)):
    high, low = halves(values)
    return mm(low, ones, over) + mm(high, ones, over)


def mm_exact(ones, values):
    high, middle, low = split_parts(values)
    return (mm(ones, low) + mm(ones, middle)) + mm(ones, high)


def halves(values):
    high = values.astype(BF16)
    return high, (values - high.astype(F32)).astype(BF16)


def mm_wide(narrow, values, over=(1, 0)):
    high, low = halves(values)
    return mm(narrow, low, over) + mm(narrow, high, over)


def softplus(values):
    tail = jnp.exp(-jnp.abs(values))
    series = tail * (1.0 - tail * (0.5 - tail * (1.0 / 3.0)))
    return jnp.maximum(values, 0.0) + jnp.where(tail < 0.01, series, jnp.log(1.0 + tail))


def sigmoid(values):
    return 1.0 / (1.0 + jnp.exp(-values))


def grids(shape):
    return lax.broadcasted_iota(jnp.int32, shape, 0), lax.broadcasted_iota(jnp.int32, shape, 1)


def column(row):
    return jnp.broadcast_to(row, (CHUNK, CHUNK)).T


def step_terms(raw_ref, par_ref):
    down, across = grids((CHUNK, CHUNK))
    lower = (down >= across).astype(F32).astype(BF16)
    step = softplus(raw_ref[0] + par_ref[0:1])
    sums = mm_exact(lower, -par_ref[1:2] * step)
    return step, sums, sums[CHUNK - 1 :]


def seg_terms(seg_ref):
    return column(seg_ref[0, 0, 0:1]), seg_ref[0, 0, 0:1], seg_ref[0, 0, 1:2], seg_ref[0, 0, 2:3]


def chunk_decay(total, before, last, spread):
    kept = jnp.exp(total) * (before == last).astype(F32)
    return exact_mm(jnp.broadcast_to(kept, (8, CHUNK)), spread)


def state_kernel(x, bc, raw, seg, par, spread, before_out, reach_out, end_out, total_out, bits_out, state, reach):
    @pl.when(pl.program_id(1) == 0)
    def _():
        state[...] = jnp.zeros_like(state)
        reach[...] = jnp.ones_like(reach)

    step, sums, total = step_terms(raw, par)
    lines, _, before, last = seg_terms(seg)
    before_out[0, 0] = state[...]
    reach_out[0, 0] = reach[...]
    leaving = jnp.where(lines == last, jnp.exp(total - sums), 0.0)
    fed = (x[0].astype(F32) * spread_mm(step, spread[...])).astype(BF16).astype(F32)
    fed = fed * spread_mm(leaving, spread[...])
    decay = chunk_decay(total, before, last, spread[...])
    state[...] = state[...] * decay[0:1] + mm_wide(bc[0, :, :STATE], fed, (0, 0))
    reach[...] = reach[...] * decay
    end_out[0] = state[...]
    total_out[0] = reach[...]
    lines = [v[0:1] for v in split_parts(reach[...])]
    bits_out[0] = jnp.concatenate(lines + [jnp.zeros((13, INNER_Q), BF16)], axis=0)


def inside_kernel(x, bc, raw, seg, par, spread, y_out):
    step, sums, _ = step_terms(raw, par)
    lines, row, _, _ = seg_terms(seg)
    down, across = grids((CHUNK, CHUNK))
    bias = jnp.where((lines == row) & (down >= across), 0.0, NEVER)
    scores = mm(bc[0, :, STATE:], bc[0, :, :STATE], (1, 1))
    turned = sums.T
    fed = (x[0].astype(F32) * spread_mm(step, spread[...])).astype(BF16)
    for pair in range(HEADS_Q // 2):
        lanes = slice(pair * 128, pair * 128 + 128)
        mixing = []
        for head in (LANE + 2 * pair, LANE + 2 * pair + 1):
            gap = jnp.broadcast_to(sums[:, head : head + 1], (CHUNK, CHUNK)) - turned[head : head + 1]
            mixing.append((scores * jnp.exp(gap + bias)).astype(BF16))
        both = mm(jnp.concatenate(mixing, axis=0), fed[:, lanes])
        y_out[0, :, lanes] = jnp.where(across < HEADDIM, both[:CHUNK], both[CHUNK:])


def outer_kernel(
    y_in, x, bc, raw, seg, par, spread, before, reach, start, gate, rows, y_out, gated_out, square_out
):
    _, sums, _ = step_terms(raw, par)
    lines, _, ahead, _ = seg_terms(seg)
    entering = spread_mm(jnp.where(lines == ahead, jnp.exp(sums), 0.0), spread[...])
    state = before[0, 0] + reach[0, 0, 0:1] * start[0]
    y = y_in[0] + entering * mm_wide(bc[0, :, STATE:], state)
    y_out[0] = y
    raw_gate = gate[0]
    gated = (y + rows[0:1] * x[0].astype(F32)) * (raw_gate * sigmoid(raw_gate))
    gated_out[0] = gated
    square = gated * gated
    folded = square[:, :128]
    for tile in range(1, INNER_Q // 128):
        folded = folded + square[:, tile * 128 : tile * 128 + 128]
    square_out[0, 0] = jnp.sum(folded.T, axis=0, keepdims=True)


def along_kernel(grad, gated, rows, scale, along_out, gain_out):
    @pl.when(pl.program_id(1) == 0)
    def _():
        gain_out[...] = jnp.zeros_like(gain_out)

    product = grad[0] * gated[0]
    weighed = product * rows[1:2]
    folded = weighed[:, :128]
    for tile in range(1, INNER_Q // 128):
        folded = folded + weighed[:, tile * 128 : tile * 128 + 128]
    along_out[0, 0] = jnp.sum(folded.T, axis=0, keepdims=True)
    lines = jnp.concatenate([column(scale[0, 0])] * (INNER_Q // 128), axis=1)
    gain_out[0] += jnp.sum((product * lines).reshape(CHUNK // 8, 8, INNER_Q), axis=0)


def gate_back_kernel(
    grad, gated, y, x, gate, bc, raw, seg, par, spread, rows, scale, along,
    grad_out, gate_out, after_out, beyond_out, start_out, state, reach,
):
    @pl.when(pl.program_id(1) == 0)
    def _():
        state[...] = jnp.zeros_like(state)
        reach[...] = jnp.ones_like(reach)

    wide = lambda row: jnp.concatenate([column(row)] * (INNER_Q // 128), axis=1)
    factor = scale[0, 0]
    pull = factor * factor * factor * along[0, 0] * (1.0 / INNER)
    grad_gated = grad[0] * rows[1:2] * wide(factor) - gated[0] * wide(pull)
    raw_gate = gate[0]
    sig = sigmoid(raw_gate)
    grad_y = (grad_gated * (raw_gate * sig)).astype(BF16)
    ssd_y = y[0] + rows[0:1] * x[0].astype(F32)
    gate_out[0] = (grad_gated * ssd_y * (sig * (1.0 + raw_gate * (1.0 - sig)))).astype(BF16)
    grad_out[0] = grad_y

    _, sums, total = step_terms(raw, par)
    lines, _, before, last = seg_terms(seg)
    after_out[0, 0] = state[...]
    beyond_out[0, 0] = reach[...]
    entering = spread_mm(jnp.where(lines == before, jnp.exp(sums), 0.0), spread[...])
    decay = chunk_decay(total, before, last, spread[...])
    fed = grad_y.astype(F32) * entering
    state[...] = state[...] * decay[0:1] + mm_wide(bc[0, :, STATE:], fed, (0, 0))
    reach[...] = reach[...] * decay
    start_out[0] = state[...]


def inside_back_kernel(x, bc, raw, seg, par, spread, grad, fed_out, b_out, c_out):
    step, sums, _ = step_terms(raw, par)
    lines, row, _, _ = seg_terms(seg)
    down, across = grids((CHUNK, CHUNK))
    bias = jnp.where((lines == row) & (across >= down), 0.0, NEVER)
    b_in, c_in = bc[0, :, :STATE], bc[0, :, STATE:]
    scores = mm(b_in, c_in, (1, 1))
    turned = sums.T
    fed = (x[0].astype(F32) * spread_mm(step, spread[...])).astype(BF16)
    grad_scores = jnp.zeros((CHUNK, CHUNK), F32)
    for pair in range(HEADS_Q // 2):
        lanes = slice(pair * 128, pair * 128 + 128)
        fed_pair, grad_pair = fed[:, lanes], grad[0, :, lanes]
        none = jnp.zeros_like(fed_pair)
        apart = jnp.concatenate(
            (jnp.where(across < HEADDIM, fed_pair, none), jnp.where(across < HEADDIM, none, fed_pair)),
            axis=0,
        )
        grad_mixing = mm(apart, grad_pair, (1, 1))
        mixing = []
        for which in range(2):
            head = LANE + 2 * pair + which
            gap = turned[head : head + 1] - jnp.broadcast_to(sums[:, head : head + 1], (CHUNK, CHUNK))
            decays = jnp.exp(gap + bias)
            mixing.append((scores * decays).astype(BF16))
            grad_scores = grad_scores + grad_mixing[which * CHUNK : which * CHUNK + CHUNK] * decays
        both = mm(jnp.concatenate(mixing, axis=0), grad_pair)
        fed_out[0, :, lanes] = jnp.where(across < HEADDIM, both[:CHUNK], both[CHUNK:])
    grad_scores = grad_scores.astype(BF16)
    b_out[0] = mm(grad_scores, c_in)
    c_out[0] = mm(grad_scores, b_in, (0, 0))


def outer_back_kernel(
    fed_in, b_in, c_in, x, bc, raw, seg, par, spread, before, reach, start, after, beyond, grad_end,
    end, total_reach, grad, y, rows,
    x_out, bc_out, raw_out, sums_out, skip_out, carry,
):
    @pl.when(pl.program_id(1) == 0)
    def _():
        sums_out[...] = jnp.zeros_like(sums_out)
        skip_out[...] = jnp.zeros_like(skip_out)
        last_state = end[0] + total_reach[0, 0:1] * start[0]
        meet = jnp.sum((grad_end[0] * last_state).reshape(STATE // 8, 8, INNER_Q), axis=0)
        meet = jnp.sum(spread_mm(meet, spread[...], (1, 1)), axis=0, keepdims=True)
        carry[...] = jnp.broadcast_to(meet, carry.shape)

    step, sums, total = step_terms(raw, par)
    lines, _, ahead, last = seg_terms(seg)
    ones = spread[...]
    state = (before[0, 0] + reach[0, 0, 0:1] * start[0]).astype(BF16)
    grad_state = after[0, 0] + beyond[0, 0, 0:1] * grad_end[0]
    values = x[0].astype(F32)
    grad_y = grad[0].astype(F32)
    wide_step = spread_mm(step, ones)
    leaving = spread_mm(jnp.where(lines == last, jnp.exp(total - sums), 0.0), ones)
    entering = spread_mm(jnp.where(lines == ahead, jnp.exp(sums), 0.0), ones)
    fed = (values * wide_step).astype(BF16).astype(F32)
    grad_fed = fed_in[0] + leaving * mm_wide(bc[0, :, :STATE], grad_state)
    x_out[0] = wide_step * grad_fed + rows[0:1] * grad_y
    bc_out[0, :, :STATE] = b_in[0] + mm((leaving * fed).astype(BF16), grad_state.astype(BF16), (1, 1))
    bc_out[0, :, STATE:] = c_in[0] + mm((entering * grad_y).astype(BF16), state, (1, 1))
    skip_out[0] += jnp.sum((grad_y * values).reshape(CHUNK // 8, 8, INNER_Q), axis=0)

    by_step = spread_mm(values * grad_fed, ones, (1, 1))
    flow = spread_mm(grad_y * y[0] - fed * grad_fed, ones, (1, 1))
    down, across = grids((CHUNK, CHUNK))
    upper = (across >= down).astype(F32).astype(BF16)
    grad_log = mm_exact(upper, flow) + carry[0:1]
    carry[...] = jnp.broadcast_to(grad_log[0:1], carry.shape)
    rate = par[1:2]
    grad_raw = (by_step - rate * grad_log) * sigmoid(raw[0] + par[0:1])
    raw_out[0] = grad_raw
    fold = lambda v: jnp.sum(v.reshape(CHUNK // 8, 8, CHUNK), axis=0)
    sums_out[0, 0:8] += fold(-rate * step * grad_log)
    sums_out[0, 8:16] += fold(grad_raw)


def chunk_spec(width, back=0, column_block=0):
    turn = (lambda c: back - 1 - c) if back else (lambda c: c)
    return pl.BlockSpec((1, CHUNK, width), lambda s, c: (s, turn(c), column_block))


def per_chunk(lines, width, back=0):
    turn = (lambda c: back - 1 - c) if back else (lambda c: c)
    return pl.BlockSpec((1, 1, lines, width), lambda s, c: (s, turn(c), 0, 0))


def per_sequence(lines, width):
    return pl.BlockSpec((1, lines, width), lambda s, c: (s, 0, 0))


def fixed(lines, width):
    return pl.BlockSpec((lines, width), lambda s, c: (0, 0))


def shaped(shape, dtype=F32):
    return jax.ShapeDtypeStruct(shape, dtype)


def call(kernel, name, chunks, ins, outs, operands, scratch=(), flops=0, after=()):
    in_specs = [spec for spec, _ in zip(ins, operands, strict=True)]
    moved = sum(v.size * v.dtype.itemsize for v in operands)
    moved += sum(v.size * v.dtype.itemsize for _, v in outs)
    count, skipped = len(in_specs), len(after)
    in_specs = in_specs + [pl.BlockSpec(memory_space=pl.ANY)] * skipped
    operands = tuple(operands) + tuple(after)
    return pl.pallas_call(
        lambda *refs: kernel(*refs[:count], *refs[count + skipped :]),
        name=name,
        grid=(2, chunks),
        in_specs=in_specs,
        out_specs=[spec for spec, _ in outs],
        out_shape=[shape for _, shape in outs],
        scratch_shapes=list(scratch),
        cost_estimate=pl.CostEstimate(flops=flops, bytes_accessed=moved, transcendentals=0),
        compiler_params=pltpu.CompilerParams(
            dimension_semantics=("arbitrary", "arbitrary"), vmem_limit_bytes=STEP_BYTES
        ),
    )(*operands)


STATE_SCRATCH = (pltpu.VMEM((STATE, INNER_Q), F32), pltpu.VMEM((8, INNER_Q), F32))


def scan_states(x, bc, raw, seg, par, spread, after=()):
    span = x.shape[1]
    n = span // CHUNK
    return call(
        state_kernel, "chunk_states", n,
        [chunk_spec(INNER_Q), chunk_spec(2 * STATE), chunk_spec(128, 0, TILE), per_chunk(8, 128), fixed(8, 128),
         fixed(128, INNER_Q)],
        [(per_chunk(STATE, INNER_Q), shaped((2, n, STATE, INNER_Q))), (per_chunk(8, INNER_Q), shaped((2, n, 8, INNER_Q))),
         (per_sequence(STATE, INNER_Q), shaped((2, STATE, INNER_Q))), (per_sequence(8, INNER_Q), shaped((2, 8, INNER_Q))),
         (per_sequence(16, INNER_Q), shaped((2, 16, INNER_Q), BF16))],
        (x, bc, raw, seg, par, spread), STATE_SCRATCH, 2 * 2 * span * STATE * INNER_Q, after=after,
    )


def scan_inside(x, bc, raw, seg, par, spread, after=()):
    span = x.shape[1]
    n = span // CHUNK
    return call(
        inside_kernel, "inside_chunks", n,
        [chunk_spec(INNER_Q), chunk_spec(2 * STATE), chunk_spec(128, 0, TILE), per_chunk(8, 128), fixed(8, 128),
         fixed(128, INNER_Q)],
        [(chunk_spec(INNER_Q), shaped(x.shape))],
        (x, bc, raw, seg, par, spread), (), 8 * 2 * span * CHUNK * INNER_Q, after=after,
    )[0]


def scan_outer(y, x, bc, raw, seg, par, spread, before, reach, start, gate, rows, after=()):
    span = x.shape[1]
    n = span // CHUNK
    return call(
        outer_kernel, "scan_and_gate", n,
        [chunk_spec(INNER_Q), chunk_spec(INNER_Q), chunk_spec(2 * STATE), chunk_spec(128, 0, TILE), per_chunk(8, 128), fixed(8, 128),
         fixed(128, INNER_Q), per_chunk(STATE, INNER_Q), per_chunk(8, INNER_Q), per_sequence(STATE, INNER_Q),
         chunk_spec(INNER_Q), fixed(8, INNER_Q)],
        [(chunk_spec(INNER_Q), shaped(x.shape)), (chunk_spec(INNER_Q), shaped(x.shape)),
         (per_chunk(1, 128), shaped((2, n, 1, 128)))],
        (y, x, bc, raw, seg, par, spread, before, reach, start, gate, rows), (), 8 * span * STATE * INNER_Q, after=after,
    )


def gate_along(grad, gated, rows, scale, after=()):
    span = gated.shape[1]
    n = span // CHUNK
    return call(
        along_kernel, "gate_along", n,
        [chunk_spec(INNER_Q), chunk_spec(INNER_Q), fixed(8, INNER_Q), per_chunk(1, 128)],
        [(per_chunk(1, 128), shaped((2, n, 1, 128))), (per_sequence(8, INNER_Q), shaped((2, 8, INNER_Q)))],
        (grad, gated, rows, scale), (), 10 * span * INNER_Q, after=after,
    )


def gate_back(grad, gated, y, x, gate, bc, raw, seg, par, spread, rows, scale, along, after=()):
    span = x.shape[1]
    n = span // CHUNK
    return call(
        gate_back_kernel, "gate_back_and_states", n,
        [chunk_spec(INNER_Q, n)] * 5 + [chunk_spec(2 * STATE, n), chunk_spec(128, n, TILE), per_chunk(8, 128, n), fixed(8, 128),
         fixed(128, INNER_Q), fixed(8, INNER_Q), per_chunk(1, 128, n), per_chunk(1, 128, n)],
        [(chunk_spec(INNER_Q, n), shaped(x.shape, BF16)), (chunk_spec(INNER_Q, n), shaped(x.shape, BF16)),
         (per_chunk(STATE, INNER_Q, n), shaped((2, n, STATE, INNER_Q))), (per_chunk(8, INNER_Q, n), shaped((2, n, 8, INNER_Q))),
         (per_sequence(STATE, INNER_Q), shaped((2, STATE, INNER_Q)))],
        (grad, gated, y, x, gate, bc, raw, seg, par, spread, rows, scale, along), STATE_SCRATCH,
        8 * span * STATE * INNER_Q, after=after,
    )


def scan_inside_back(x, bc, raw, seg, par, spread, grad, after=()):
    span = x.shape[1]
    n = span // CHUNK
    return call(
        inside_back_kernel, "inside_chunks_back", n,
        [chunk_spec(INNER_Q), chunk_spec(2 * STATE), chunk_spec(128, 0, TILE), per_chunk(8, 128), fixed(8, 128),
         fixed(128, INNER_Q), chunk_spec(INNER_Q)],
        [(chunk_spec(INNER_Q), shaped(x.shape)), (chunk_spec(STATE), shaped((2, span, STATE))),
         (chunk_spec(STATE), shaped((2, span, STATE)))],
        (x, bc, raw, seg, par, spread, grad), (), 24 * 2 * span * CHUNK * INNER_Q, after=after,
    )


def scan_outer_back(
    fed, b, c, x, bc, raw, seg, par, spread, before, reach, start, later, beyond, grad_end, end, total, grad, y, rows, after=()
):
    span = x.shape[1]
    n = span // CHUNK
    return call(
        outer_back_kernel, "scan_back", n,
        [chunk_spec(INNER_Q, n), chunk_spec(STATE, n), chunk_spec(STATE, n), chunk_spec(INNER_Q, n), chunk_spec(2 * STATE, n),
         chunk_spec(128, n, TILE), per_chunk(8, 128, n), fixed(8, 128), fixed(128, INNER_Q), per_chunk(STATE, INNER_Q, n),
         per_chunk(8, INNER_Q, n), per_sequence(STATE, INNER_Q), per_chunk(STATE, INNER_Q, n), per_chunk(8, INNER_Q, n),
         per_sequence(STATE, INNER_Q), per_sequence(STATE, INNER_Q), per_sequence(8, INNER_Q), chunk_spec(INNER_Q, n),
         chunk_spec(INNER_Q, n), fixed(8, INNER_Q)],
        [(chunk_spec(INNER_Q, n), shaped(x.shape)), (chunk_spec(2 * STATE, n), shaped((2, span, 2 * STATE))),
         (chunk_spec(128, n), shaped((2, span, 128))), (per_sequence(16, 128), shaped((2, 16, 128))),
         (per_sequence(8, INNER_Q), shaped((2, 8, INNER_Q)))],
        (fed, b, c, x, bc, raw, seg, par, spread, before, reach, start, later, beyond, grad_end, end, total, grad, y, rows),
        (pltpu.VMEM((8, 128), F32),), 24 * span * STATE * INNER_Q, after=after,
    )


def seg_table(seg_now, seg_before):
    span = seg_now.shape[1]
    rows = seg_now.reshape(2, span // CHUNK, 1, CHUNK)
    last = rows[..., -1:]
    before = jnp.concatenate((seg_before.reshape(2, 1, 1, 1), last[:, :-1]), axis=1)
    spread = lambda v: jnp.broadcast_to(v, rows.shape)
    return jnp.concatenate((rows, spread(before), spread(last)) + (rows,) * 5, axis=2)


def conv_terms(wide_ref, halo_ref, taps_ref, mask_ref, tail):
    own = wide_ref[0].astype(BF16).astype(F32)
    longer = jnp.concatenate((tail, own), axis=0)
    rows = [own]
    total = taps_ref[CONV : CONV + 1] + taps_ref[CONV - 1 : CONV] * own
    for back in range(1, CONV):
        same = jnp.concatenate([column(mask_ref[0, 0, back : back + 1])] * (own.shape[1] // 128), axis=1)
        earlier = longer[8 - back : 8 - back + CHUNK] * same
        rows.append(earlier)
        total = total + taps_ref[CONV - 1 - back : CONV - back] * earlier
    return own, rows, total


def conv_kernel(wide, halo, taps, mask, out, tail):
    @pl.when(pl.program_id(1) == 0)
    def _():
        tail[...] = halo[0].astype(F32)

    own, _, total = conv_terms(wide, halo, taps, mask, tail[...])
    tail[...] = own[CHUNK - 8 :]
    out[0] = (total * sigmoid(total)).astype(BF16)


def conv_back_kernel(wide, before, halo, taps, mask, grad, returned, out, sums_out, ahead):
    chunk = pl.num_programs(1) - 1 - pl.program_id(1)

    @pl.when(pl.program_id(1) == 0)
    def _():
        sums_out[...] = jnp.zeros_like(sums_out)
        ahead[...] = jnp.zeros_like(ahead)

    tail = jnp.where(chunk == 0, halo[0].astype(F32), before[0].astype(BF16).astype(F32))
    _, rows, total = conv_terms(wide, halo, taps, mask, tail)
    sig = sigmoid(total)
    pull = grad[0] * (sig * (1.0 + total * (1.0 - sig)))
    result = taps[CONV - 1 : CONV] * pull
    fold = lambda v: jnp.sum(v.reshape(CHUNK // 8, 8, v.shape[1]), axis=0)
    for back in range(1, CONV):
        same = jnp.concatenate([column(mask[0, 0, back : back + 1])] * (pull.shape[1] // 128), axis=1)
        masked = pull * same
        longer = jnp.concatenate((masked, ahead[8 * back - 8 : 8 * back]), axis=0)
        result = result + taps[CONV - 1 - back : CONV - back] * longer[back : back + CHUNK]
        ahead[8 * back - 8 : 8 * back] = masked[:8]
    for back in range(CONV):
        place = CONV - 1 - back
        sums_out[0, 8 * place : 8 * place + 8] += fold(pull * rows[back])
    sums_out[0, 8 * CONV : 8 * CONV + 8] += fold(pull)
    late = (pl.program_id(1) == 0).astype(F32) * returned[0].astype(F32)
    late = jnp.concatenate((jnp.zeros((CHUNK - 8, late.shape[1]), F32), late), axis=0)
    out[0] = (result + late).astype(BF16)


def conv_forward(wide, halo, taps, mask, width, at, after=()):
    n = wide.shape[1] // CHUNK
    lines = lambda rows: pl.BlockSpec((1, rows, width), lambda s, c: (s, 0, at))
    return call(
        conv_kernel, "conv", n,
        [chunk_spec(width, 0, at), lines(8), pl.BlockSpec((8, width), lambda s, c: (0, at)), per_chunk(8, 128)],
        [(chunk_spec(width), shaped(wide.shape[:2] + (width,), BF16))],
        (wide, halo, taps, mask), (pltpu.VMEM((8, width), F32),), 30 * wide.shape[1] * width, after=after,
    )[0]


def conv_backward(wide, halo, taps, mask, grad, returned, width, at, after=()):
    n = wide.shape[1] // CHUNK
    lines = lambda rows: pl.BlockSpec((1, rows, width), lambda s, c: (s, 0, at))
    steps = CHUNK // 8
    early = pl.BlockSpec(
        (1, 8, width), lambda s, c: (s, jnp.maximum((n - 1 - c) * steps - 1, 0), at)
    )
    return call(
        conv_back_kernel, "conv_back", n,
        [chunk_spec(width, n, at), early, lines(8), pl.BlockSpec((8, width), lambda s, c: (0, at)),
         per_chunk(8, 128, n), chunk_spec(width, n), lines(8)],
        [(chunk_spec(width, n), shaped(wide.shape[:2] + (width,), BF16)), (per_sequence(8 * CONV + 8, width), shaped((2, 8 * CONV + 8, width)))],
        (wide, wide, halo, taps, mask, grad, returned), (pltpu.VMEM((8 * CONV, width), F32),), 60 * wide.shape[1] * width, after=after,
    )


def mask_table(seg_ext, edge_rows):
    span = seg_ext.shape[1] - edge_rows
    here = seg_ext[:, edge_rows:]
    rows = [here == seg_ext[:, edge_rows - back : edge_rows - back + span] for back in range(CONV)]
    table = jnp.stack(rows + rows, axis=1).astype(F32)
    return jnp.moveaxis(table.reshape(2, 2 * CONV, span // CHUNK, CHUNK), 2, 1)


def tile_picks(owner, rows):
    down, across = grids((2 * STATE, 128))
    bc = (down - BC_Q * owner == across) & (across < BC_Q)
    down, across = grids((HEADS, 128))
    head = across - LANE
    dt = (down - HEADS_Q * owner == head) & (head >= 0) & (head < HEADS_Q)
    return bc.astype(F32), dt.astype(F32)


def cut_weights_kernel(q_ref, weight, *outs):
    for layer in range(weight.shape[0]):
        for k in range(TEAM):
            owner = q_ref[0] ^ k
            start = pl.multiple_of(owner * INNER_Q, 128)
            part = outs[layer * TEAM + k]
            part[:, :INNER_Q] = weight[layer, :, pl.ds(start, INNER_Q)]
            part[:, INNER_Q : 2 * INNER_Q] = weight[layer, :, pl.ds(INNER + start, INNER_Q)]
            bc, dt = tile_picks(owner, None)
            tile = mm(weight[layer, :, 2 * INNER : 2 * INNER + 2 * STATE], bc.astype(BF16))
            tile = tile + mm(weight[layer, :, INNER + CONVDIM :], dt.astype(BF16))
            part[:, 2 * INNER_Q :] = tile.astype(BF16)


def whole_spec(shape):
    return pl.BlockSpec(shape, lambda *_: (0,) * len(shape))


def whole_call(kernel, name, index, operands, outs, after=()):
    count, skipped = 1 + len(operands), len(after)
    return pl.pallas_call(
        lambda *refs: kernel(*refs[:count], *refs[count + skipped :]),
        name=name,
        grid_spec=pltpu.PrefetchScalarGridSpec(
            num_scalar_prefetch=1,
            grid=(1,),
            in_specs=[whole_spec(v.shape) for v in operands]
            + [pl.BlockSpec(memory_space=pl.ANY)] * skipped,
            out_specs=[whole_spec(s.shape) for s in outs],
        ),
        out_shape=list(outs),
        compiler_params=pltpu.CompilerParams(vmem_limit_bytes=VMEM_BYTES),
    )(index, *operands, *after)


def tie(value, *after):
    anywhere = pl.BlockSpec(memory_space=pl.ANY)
    return pl.pallas_call(
        lambda *refs: None,
        name="tie",
        in_specs=[anywhere] * (1 + len(after)),
        out_specs=anywhere,
        out_shape=shaped(value.shape, value.dtype),
        input_output_aliases={0: 0},
    )(value, *after)


def norm_kernel(x_ref, stream, gain, out):
    values = stream[...].astype(F32)
    mean = jnp.mean(values * values, axis=-1, keepdims=True)
    normed = (values * lax.rsqrt(mean + EPS) * gain[...]).astype(BF16)
    width = normed.shape[1] // 2
    x = x_ref[0]
    out[:, pl.ds(pl.multiple_of(x * width, 128), width)] = normed[:, :width]
    out[:, pl.ds(pl.multiple_of((1 - x) * width, 128), width)] = normed[:, width:]


def norm_rows(x, stream, gain, after=()):
    return whole_call(norm_kernel, "norm", x, (stream, gain), [shaped(stream.shape, BF16)], after)[0]


def scale_kernel(gated, scale, rows, out):
    lines = jnp.concatenate([column(scale[0, 0])] * (INNER_Q // 128), axis=1)
    out[0] = (gated[0] * lines * rows[1:2]).astype(BF16)


def scale_rows(gated, scale, rows, after=()):
    n = gated.shape[1] // CHUNK
    return call(
        scale_kernel, "scale_rows", n,
        [chunk_spec(INNER_Q), per_chunk(1, 128), fixed(8, INNER_Q)],
        [(chunk_spec(INNER_Q), shaped(gated.shape, BF16))],
        (gated, scale, rows), (), 4 * gated.size, after=after,
    )[0]


def cut_weights(q, weight):
    layers, rows = weight.shape[:2]
    outs = [shaped((rows, INNER_Q + WIDE), BF16)] * (TEAM * layers)
    outs = whole_call(cut_weights_kernel, "cut_weights", q, (weight,), outs)
    return [outs[TEAM * layer : TEAM * layer + TEAM] for layer in range(layers)]


def place_of(owner):
    return (owner % 2) * 2 + owner // 2


def wide_piece_kernel(q_ref, *refs):
    out = refs[-1]
    for k in range(TEAM):
        out[place_of(q_ref[0] ^ k)] = refs[k][:, INNER_Q:]


def gate_piece_kernel(q_ref, *refs):
    rows, out = refs[TEAM], refs[-1]
    for k in range(TEAM):
        out[place_of(q_ref[0] ^ k)] = refs[k][:, :INNER_Q]
    for block in range(TEAM):
        half = block % 2 * INNER_Q
        out[TEAM + block] = rows[block // 2, :, half : half + INNER_Q]


def all_piece_kernel(q_ref, *refs):
    out = refs[-1]
    for k in range(TEAM):
        out[place_of(q_ref[0] ^ k)] = refs[k][...]


def all_piece(q, parts, after=()):
    shape = (TEAM,) + parts[0].shape
    return whole_call(all_piece_kernel, "all_piece", q, parts, [shaped(shape, BF16)], after)[0]


def arrange_kernel(_, gathered, gate, wide):
    for x in range(2):
        for z in range(gate.shape[2]):
            for block in range(TEAM):
                rows = gathered[x, z, block]
                gate[x, block // 2, z, block % 2] = rows[:, :INNER_Q]
                wide[x, block // 2, z, block % 2] = rows[:, INNER_Q:]


def arrange(index, gathered):
    size, rows = gathered.shape[1], gathered.shape[3]
    outs = [shaped((2, 2, size, 2, rows, width), BF16) for width in (INNER_Q, WIDE)]
    gate, wide = whole_call(arrange_kernel, "arrange", index, (gathered,), outs)
    return wide.reshape(-1, WIDE), gate.reshape(-1, INNER_Q)


def by_owner_kernel(x_ref, grad, out):
    for side in range(2):
        x = x_ref[0] if side == 0 else 1 - x_ref[0]
        for z in range(out.shape[1]):
            for block in range(TEAM):
                out[x, z, block] = grad[side, block // 2, z, block % 2].astype(BF16)


def both_by_owner_kernel(x_ref, gate, out_grad, out):
    for side in range(2):
        x = x_ref[0] if side == 0 else 1 - x_ref[0]
        for z in range(out.shape[1]):
            for block in range(TEAM):
                upper, lower = block // 2, block % 2
                half = slice(lower * INNER_Q, lower * INNER_Q + INNER_Q)
                out[x, z, block] = gate[side, upper, z, lower].astype(BF16)
                out[side, z, TEAM + block] = out_grad[z, side, upper, :, half].astype(BF16)


def both_by_owner(x_first_of, gate, out_grad, size, rows):
    operands = (
        gate.reshape(2, 2, size, 2, rows, INNER_Q),
        out_grad.reshape(size, 2, 2, rows, 2 * INNER_Q),
    )
    outs = [shaped((2, size, 2 * TEAM, rows, INNER_Q), BF16)]
    return whole_call(both_by_owner_kernel, "both_by_owner", x_first_of, operands, outs)[0]


def by_owner(x_first_of, grad, size, rows):
    width = grad.shape[-1]
    operands = (grad.reshape(2, 2, size, 2, rows, width),)
    outs = [shaped((2, size, TEAM, rows, width), BF16)]
    return whole_call(by_owner_kernel, "by_owner", x_first_of, operands, outs)[0]


def wide_piece(q, parts, after=()):
    shape = (TEAM, parts[0].shape[0], WIDE)
    return whole_call(wide_piece_kernel, "wide_piece", q, parts, [shaped(shape, BF16)], after)[0]


def gate_piece(q, parts, rows, after=()):
    count = parts[0].shape[0]
    operands = tuple(parts) + (rows.reshape(2, count, -1),)
    outs = [shaped((2 * TEAM, count, INNER_Q), BF16)]
    return whole_call(gate_piece_kernel, "gate_piece", q, operands, outs, after)[0]


def arrange_both_kernel(x_ref, gathered, gate, out):
    for side in range(2):
        x = x_ref[0] if side == 0 else 1 - x_ref[0]
        for z in range(gate.shape[2]):
            for block in range(TEAM):
                upper, lower = block // 2, block % 2
                gate[side, upper, z, lower] = gathered[x, z, block]
                half = slice(lower * INNER_Q, lower * INNER_Q + INNER_Q)
                out[z, side, upper, :, half] = gathered[side, z, TEAM + block]


def arrange_both(x_first_of, gathered):
    size, rows = gathered.shape[1], gathered.shape[3]
    outs = [
        shaped((2, 2, size, 2, rows, INNER_Q), BF16),
        shaped((size, 2, 2, rows, 2 * INNER_Q), BF16),
    ]
    gate, out = whole_call(arrange_both_kernel, "arrange_both", x_first_of, (gathered,), outs)
    return gate.reshape(-1, INNER_Q), out.reshape(-1, 2 * INNER_Q)


def whole_wide_kernel(place, *refs):
    out = refs[-1]
    size = out.shape[2]
    for side in range(2):
        for hop in range(size):
            source = lax.rem(place[0] - hop + size, size)
            for block in range(TEAM):
                out[side, block // 2, source, block % 2] = refs[side * size + hop][block]


def whole_columns(place, pieces, after=()):
    size = len(pieces) // 2
    rows, width = pieces[0].shape[1:]
    outs = [shaped((2, 2, size, 2, rows, width), BF16)]
    whole = whole_call(whole_wide_kernel, "whole_columns", place, pieces, outs, after)[0]
    return whole.reshape(-1, width)


def grad_parts_kernel(q_ref, gate, wide, *outs):
    for k in range(TEAM):
        block = place_of(q_ref[0] ^ k)
        outs[k][:, :INNER_Q] = gate[block]
        outs[k][:, INNER_Q:] = wide[block]


def grad_parts(q, gate, wide):
    outs = [shaped((wide.shape[1], INNER_Q + WIDE), BF16)] * TEAM
    return whole_call(grad_parts_kernel, "grad_parts", q, (gate, wide), outs)


def cut_params_kernel(q_ref, conv_weight, conv_bias, dt_bias, a_log, skip, out_gain, spread, taps, par, rows):
    owner = q_ref[0]
    start = pl.multiple_of(owner * INNER_Q, 128)
    bc, dt = tile_picks(owner, None)
    bc, dt = bc.astype(BF16), dt.astype(BF16)
    mine = pl.ds(start, INNER_Q)
    for layer in range(conv_weight.shape[0]):
        one = slice(layer, layer + 1)
        taps[layer, :CONV, :INNER_Q] = conv_weight[layer, :, mine]
        taps[layer, :CONV, INNER_Q:] = exact_mm(conv_weight[layer, :, INNER:], bc)
        taps[layer, CONV : CONV + 1, :INNER_Q] = conv_bias[one, mine]
        taps[layer, CONV : CONV + 1, INNER_Q:] = exact_mm(conv_bias[one, INNER:], bc)
        taps[layer, CONV + 1 :] = jnp.zeros((7 - CONV, WIDE), F32)
        par[layer, 0:1] = exact_mm(dt_bias[one], dt)
        par[layer, 1:2] = exact_mm(jnp.exp(a_log[one]), dt)
        par[layer, 2:] = jnp.zeros((6, 128), F32)
        rows[layer, 0:1] = exact_mm(exact_mm(skip[one], dt), spread[...])
        rows[layer, 1:2] = out_gain[one, mine]
        rows[layer, 2:] = jnp.zeros((6, INNER_Q), F32)


def cut_params(q, params, after):
    layers = params[0].shape[0]
    shapes = [(layers, 8, WIDE), (layers, 8, 128), (layers, 8, INNER_Q)]
    return whole_call(cut_params_kernel, "cut_params", q, params, [shaped(s) for s in shapes], after)


def join_kernel(q_ref, *refs):
    out = refs[-1]
    for layer in range(out.shape[0]):
        shared = 0.0
        for k in range(TEAM):
            owner = q_ref[0] ^ k
            start = pl.multiple_of(owner * INNER_Q, 128)
            part = refs[layer * TEAM + k]
            out[layer, :, pl.ds(start, INNER_Q)] = part[:, :INNER_Q].astype(F32)
            out[layer, :, pl.ds(INNER + start, INNER_Q)] = part[:, INNER_Q : 2 * INNER_Q].astype(F32)
            bc, dt = tile_picks(owner, None)
            both = jnp.concatenate((bc, dt), axis=0).astype(BF16)
            shared = shared + mm(part[:, 2 * INNER_Q :], both, (1, 1))
        out[layer, :, 2 * INNER :] = shared


def join_weights(q, parts):
    flat = [v for layer in parts for v in layer]
    shape = (len(parts), flat[0].shape[0], 2 * INNER + 2 * STATE + HEADS)
    return whole_call(join_kernel, "join_weights", q, flat, [shaped(shape)])[0]


SMALL = (16, WIDE)


def pack_small_kernel(conv_x, conv_tile, heads, skip, gain, norm, spread, out):
    fold = lambda v, rows: jnp.sum(v[:, rows], axis=(0, 1), keepdims=True)[0]
    for line in range(CONV + 1):
        rows = slice(8 * line, 8 * line + 8)
        out[line : line + 1, :INNER_Q] = fold(conv_x[...], rows)
        out[line : line + 1, INNER_Q:] = fold(conv_tile[...], rows)
    line = CONV + 1
    out[line:] = jnp.zeros((SMALL[0] - line, WIDE), F32)
    every = slice(0, 8)
    out[line + 1 : line + 2, :INNER_Q] = fold(gain[...], every)
    out[line + 2 : line + 3, :128] = fold(heads[...], slice(8, 16))
    out[line + 3 : line + 4, :128] = fold(heads[...], every)
    by_head = exact_mm(skip[0] + skip[1], spread[...], (1, 1))
    out[line + 4 : line + 5, :128] = jnp.sum(by_head, axis=0, keepdims=True)
    width = norm.shape[1] // 2
    out[line + 5 : line + 6, :width] = norm[:, :width]
    out[line + 6 : line + 7, :width] = norm[:, width:]


def pack_small(*parts):
    return pl.pallas_call(pack_small_kernel, name="pack_small", out_shape=shaped(SMALL))(*parts)


def lanes_of(values):
    return lax.broadcasted_iota(jnp.int32, values.shape, 1)


def open_small_kernel(q_ref, *refs):
    norm, conv_weight, conv_bias, dt_bias, a_log, skip, gain = refs[-7:]
    layers = norm.shape[0]
    line = CONV + 1
    for layer in range(layers):
        one = slice(layer, layer + 1)
        packs = [ref[layer] for ref in refs[:TEAM]]
        shared, heads = [], 0.0
        for k in range(TEAM):
            owner = q_ref[0] ^ k
            start = pl.multiple_of(owner * INNER_Q, 128)
            mine = pl.ds(start, INNER_Q)
            pack = packs[k]
            conv_weight[layer, :, mine] = pack[:CONV, :INNER_Q]
            conv_bias[one, mine] = pack[CONV:line, :INNER_Q]
            tile = pack[:8, INNER_Q:]
            tile = jnp.where(lanes_of(tile) < BC_Q, tile, 0.0)
            tile = jnp.where(owner % 2 == 0, tile, pltpu.roll(tile, BC_Q, 1))
            shared.append([jnp.where(owner // 2 == side, tile, 0.0) for side in range(2)])
            rows = pack[line + 2 : line + 5, :128]
            in_head = (lanes_of(rows) >= LANE) & (lanes_of(rows) < LANE + HEADS_Q)
            rows = jnp.where(in_head, rows, 0.0)
            placed = 0.0
            for which in range(TEAM):
                turned = pltpu.roll(rows, (HEADS_Q * which - LANE) % 128, 1)
                placed = placed + jnp.where(owner == which, turned, 0.0)
            heads = heads + placed[:, :HEADS]
            gain[one, mine] = pack[line + 1 : line + 2, :INNER_Q]
        shared = jnp.concatenate([sum([s[side] for s in shared]) for side in range(2)], axis=1)
        conv_weight[layer, :, INNER:] = shared[:CONV]
        conv_bias[one, INNER:] = shared[CONV:line]
        dt_bias[one], a_log[one], skip[one] = heads[0:1], heads[1:2], heads[2:3]
        width = norm.shape[1] // 2
        halves_of = lambda n: packs[n][line + 5 : line + 7, :width]
        total = (halves_of(0) + halves_of(1)) + (halves_of(2) + halves_of(3))
        norm[one, :width] = total[0:1]
        norm[one, width:] = total[1:2]


def open_small(q, packs, features):
    layers = packs[0].shape[0]
    flat = list(packs)
    shapes = [
        (layers, features), (layers, CONV, CONVDIM), (layers, CONVDIM), (layers, HEADS), (layers, HEADS),
        (layers, HEADS), (layers, INNER),
    ]
    return pl.pallas_call(
        open_small_kernel,
        name="open_small",
        grid_spec=pltpu.PrefetchScalarGridSpec(
            num_scalar_prefetch=1,
            grid=(1,),
            in_specs=[whole_spec(v.shape) for v in flat],
            out_specs=[whole_spec(s) for s in shapes],
        ),
        out_shape=[shaped(s) for s in shapes],
    )(q, *flat)


def spread_matrix():
    head = jnp.arange(128)[:, None] - LANE
    return (jnp.arange(INNER_Q)[None, :] // HEADDIM == head).astype(BF16)


def gap_decays(spans):
    rows = []
    for start in range(len(spans)):
        row = []
        running = jnp.ones_like(spans[0])
        for stop, span in enumerate(spans):
            if stop <= start:
                row.append(jnp.zeros_like(running))
                continue
            row.append(running)
            running = running * span
        rows.append(jnp.stack(row))
    return jnp.stack(rows)


def mix_states(states, bits=None, weights=None):
    size = lax.axis_size("z")
    z = lax.axis_index("z")
    width = states.shape[1] // size
    decay = lambda rows: jnp.sum(rows[:, :3].astype(F32), axis=1)
    if size > NEAR:
        if weights is None:
            weights = gap_decays([decay(v) for v in lax.all_gather(bits, "z")])
        cuts = jnp.moveaxis(states.reshape(2, size, width, -1), 1, 0).astype(BF16)
        parts = lax.all_to_all(cuts, "z", 0, 0, tiled=True).astype(F32)
        sums = jnp.sum(weights[:, :, :, None] * parts[:, None], axis=0)
        back = lax.all_to_all(sums.astype(BF16), "z", 0, 0, tiled=True).astype(F32)
        return jnp.moveaxis(back, 0, 1).reshape(states.shape), weights
    ring = lambda k: lax.rem(z + k + size, size)

    def cut(k):
        part = lax.dynamic_slice_in_dim(states, k * width, width, 1).astype(BF16)
        return part if weights is not None else jnp.concatenate((part, bits), axis=1)

    parts = [cut(z)] + [shift(cut(ring(hop)), "z", hop) for hop in range(1, size)]
    if weights is None:
        everyone = jnp.stack([decay(p[:, width:]) for p in parts])
        spans = [
            lax.dynamic_index_in_dim(everyone, lax.rem(z - k + size, size), 0, False)
            for k in range(size)
        ]
        weights = gap_decays(spans)
        parts = [p[:, :width] for p in parts]
    results = []
    for away in range(size):
        to = lax.dynamic_index_in_dim(weights, ring(away), 1, False)
        total = 0.0
        for hop in range(size):
            weight = lax.dynamic_index_in_dim(to, ring(-hop), 0, False)
            total = total + weight[:, None] * parts[hop].astype(F32)
        results.append(total)
    back = [results[0]] + [
        shift(results[hop].astype(BF16), "z", hop).astype(F32) for hop in range(1, size)
    ]
    whole = jnp.zeros(states.shape, F32)
    for hop in range(size):
        whole = lax.dynamic_update_slice_in_dim(whole, back[hop], ring(-hop) * width, 1)
    return whole, weights


def local(
    tokens,
    segments,
    out_grad,
    norm_gain,
    in_weight,
    conv_weight,
    conv_bias,
    dt_bias,
    a_log,
    skip,
    out_gain,
    out_weight,
):
    _, length, features = tokens.shape
    edge = CONV - 1
    layer_count, in_rows = in_weight.shape[:2]
    out_rows = out_weight.shape[1]
    layers = range(layer_count)
    q = member()
    owner = q.reshape(1)
    span = 2 * length
    row_count = 2 * span

    near = lax.axis_size("z") <= NEAR
    x_place = lax.axis_index("x").reshape(1)
    cuts = cut_weights(owner, in_weight)
    size = lax.axis_size("z")
    place = jnp.stack((lax.axis_index("z"), lax.axis_index("x")))
    exchanged = [around_team(parts) for parts in cuts]
    moved = [lax.ppermute(out_weight[k], ("x", "y"), TURN) for k in layers]
    nowhere = jnp.zeros((1,), jnp.int32)

    def fetch_rows(rows):
        return lax.all_gather(rows, ("z", "x"), axis=0, tiled=True)

    def fetch_columns(layer_id, after):
        gathered = lax.all_gather(all_piece(owner, exchanged[layer_id], after), ("x", "z"))
        return arrange(nowhere, gathered.reshape((2, size) + gathered.shape[1:]))

    if near:
        wide_line, wide_all = fetch(wide_piece(owner, exchanged[0]))

    seg_now = team_gather(segments.astype(F32).reshape(length))
    prev_seg = step_line(seg_now[:, span - edge :], "z", 1)
    seg_ext = jnp.concatenate((prev_seg, seg_now), axis=1)
    seg = seg_table(seg_now, seg_ext[:, edge - 1])
    mask = mask_table(seg_ext, edge)
    spread = spread_matrix()
    all_taps, all_par, all_rows = cut_params(
        owner, (conv_weight, conv_bias, dt_bias, a_log, skip, out_gain, spread), exchanged[0][1:]
    )

    stream = tokens.astype(F32).reshape(length, features)
    last_grad = tie(out_grad.reshape(length, features), wide_line[1] if near else exchanged[0][1])
    last_grad = team_gather(last_grad)
    saved, full = [], []
    for layer_id in layers:
        taps, par, rows = all_taps[layer_id], all_par[layer_id], all_rows[layer_id]
        first, final = layer_id == 0, layer_id == layer_count - 1
        fast = near and first
        x_order = x_place if fast else nowhere
        normed = norm_rows(
            x_order,
            tokens.reshape(length, features) if first else stream,
            norm_gain[layer_id : layer_id + 1],
            (wide_all[1:] if fast else []) + ([last_grad] if first else []),
        )
        normed = team_gather(normed)
        earlier = step_line(normed[:, span - 16 :], "z", 1).reshape(32, features)
        normed = normed.reshape(row_count, features)
        dot = partial(jnp.dot, preferred_element_type=F32)
        if fast:
            piece = gate_piece(
                owner, exchanged[0], moved[0], wide_all[1:] + [seg, mask, all_taps]
            )
            gathered = lax.all_gather(piece, ("x", "z")).reshape((2, size) + piece.shape)
            full_gate, full_out = arrange_both(x_place, gathered)
            full_wide = whole_columns(place, wide_all)
        elif first:
            full_wide, full_gate = fetch_columns(0, [])
        else:
            full_wide, full_gate = next_columns
        wide = dot(normed, full_wide).reshape(2, span, WIDE)
        if not fast:
            full_out = fetch_rows(moved[0]) if first else next_rows
        gate_raw = dot(normed, full_gate).reshape(2, span, INNER_Q)
        full.append((full_wide, full_gate, full_out))
        halo = dot(earlier, full_wide).reshape(2, 16, WIDE)[:, 8:].astype(BF16).astype(F32)
        bc_own = conv_forward(
            wide, halo, taps, mask, 128, TILE, [v for e in exchanged[1:] for v in e[1:]] if first else []
        )[..., :BC_Q]
        bc_same = y_swap(bc_own)
        bc = jnp.concatenate(
            in_order((bc_own, core_swap(bc_own)[::-1], bc_same, core_swap(bc_same)[::-1])), axis=-1
        )
        heads_x = conv_forward(wide, halo, taps, mask, INNER_Q, 0)
        scan_in = (heads_x, bc, wide, seg, par, spread)
        before, reach, end, total_reach, bits = scan_states(
            *scan_in
        )
        start, weights = mix_states(end, bits)
        inside = scan_inside(*scan_in, after=[] if first else [full_out])
        if not final:
            next_columns = fetch_columns(layer_id + 1, [start, inside])
            next_rows = fetch_rows(tie(moved[layer_id + 1], start))
        scan_y, gated, square = scan_outer(
            inside, *scan_in, before, reach, start, gate_raw, rows,
        )
        scale = lax.rsqrt(team_sum(square) / INNER + EPS)
        normed_y = scale_rows(gated, scale, rows)
        normed_y = normed_y.reshape(row_count, INNER_Q)
        sequence = lambda v, k: lax.slice_in_dim(v, k * span, (k + 1) * span, axis=0)
        branch_far = dot(sequence(normed_y, 1), full_out)
        branch = dot(sequence(normed_y, 0), full_out)
        saved.append(
            (
                stream,
                normed,
                gate_raw,
                halo,
                scan_in,
                (before, reach, start),
                (end, total_reach),
                weights,
                scan_y,
                gated,
                scale,
                normed_y,
                taps,
                rows,
            )
        )
        stream = stream + team_scatter(branch, branch_far)
    grad_stream = out_grad.astype(F32).reshape(length, features)
    in_parts = [None] * layer_count
    out_shards = [None] * layer_count
    small = [None] * layer_count
    for layer_id in reversed(layers):
        (
            stream_in,
            normed,
            gate_raw,
            halo,
            scan_in,
            states_before,
            states_end,
            weights,
            scan_y,
            gated,
            scale,
            normed_y,
            taps,
            rows,
        ) = saved[layer_id]
        heads_x, scan_rest = scan_in[0], scan_in[1:]
        wide = scan_in[2]
        full_wide, full_gate, full_out = full[layer_id]
        last = layer_id == 0
        grad_branch = team_gather(grad_stream.astype(BF16)) if last_grad is None else last_grad
        last_grad = None
        grad_branch = grad_branch.reshape(row_count, features)
        out_full_grad = jnp.einsum("ri,rd->id", normed_y, grad_branch, preferred_element_type=F32)
        back = partial(jnp.einsum, "rp,dp->rd", preferred_element_type=F32)
        grad_normed_y = back(grad_branch, full_out).reshape(2, span, INNER_Q)
        along, grad_gain = gate_along(grad_normed_y, gated, rows, scale)
        along = team_sum(along)
        grad_ssd, grad_gate, after, beyond, grad_start = gate_back(
            grad_normed_y, gated, scan_y, heads_x, gate_raw, *scan_rest, rows, scale, along,
            [out_full_grad],
        )
        turn = partial(jnp.einsum, "rd,rp->dp", preferred_element_type=F32)
        grad_gate = grad_gate.reshape(row_count, INNER_Q)
        gate_grad = turn(normed, grad_gate)
        fast = near and last
        x_order = x_place if fast else nowhere
        both = both_by_owner(x_order, gate_grad, out_full_grad, size, in_rows)
        both_total = sum_to_owner(both)
        gate_total = both_total[:TEAM]
        out_total = both_total[TEAM:].reshape(2, 2, in_rows, INNER_Q).swapaxes(1, 2)
        out_total = out_total.reshape(out_rows, features)
        out_shards[layer_id] = lax.ppermute(out_total, ("x", "y"), TURN).astype(F32)
        grad_end, _ = mix_states(grad_start, None, weights.swapaxes(0, 1))
        grad_inside = scan_inside_back(*scan_in, grad_ssd, after=[both])
        grad_x, grad_bc, grad_raw, head_sums, skip_sums = scan_outer_back(
            *grad_inside,
            *scan_in,
            *states_before,
            after,
            beyond,
            grad_end,
            *states_end,
            grad_ssd,
            scan_y,
            rows,
        )
        blocks = [grad_bc[..., BC_Q * k : BC_Q * k + BC_Q].astype(BF16) for k in range(TEAM)]
        turned = lambda k: lax.select_n(q ^ k, *blocks)
        half = lambda k: turned(k).astype(F32) + core_swap(turned(k ^ 1)).astype(F32)[::-1]
        grad_bc_own = half(0) + y_swap(half(2).astype(BF16)).astype(F32)
        grad_tile = jnp.pad(grad_bc_own, ((0, 0), (0, 0), (0, 128 - BC_Q)))

        edge_in = jnp.concatenate(
            (halo[:, 8 - edge :], wide[:, :edge].astype(BF16).astype(F32)), axis=1
        )
        edge_conv = lambda v: conv_piece(seg_ext[:, : 2 * edge], v, taps[:CONV], taps[CONV])
        edge_grad = jnp.concatenate((grad_x[:, :edge], grad_tile[:, :edge]), axis=-1)
        edge_grad = jax.vjp(edge_conv, edge_in)[1](edge_grad)[0][:, :edge].astype(BF16)
        returned = step_line(edge_grad, "z", -1).astype(F32)
        returned = jnp.pad(returned, ((0, 0), (8 - edge, 0), (0, 0)))
        grad_conv_x, conv_sums = conv_backward(
            wide, halo, taps, mask, grad_x, returned, INNER_Q, 0
        )
        grad_conv_tile, tile_sums = conv_backward(
            wide, halo, taps, mask, grad_tile, returned, 128, TILE
        )
        grad_wide = jnp.concatenate(
            (grad_conv_x, grad_conv_tile[..., :BC_Q], grad_raw[..., BC_Q:].astype(BF16)), axis=-1
        ).reshape(row_count, WIDE)
        in_grad = turn(normed, grad_wide)
        total = sum_to_owner(by_owner(x_order, in_grad, size, in_rows))
        in_parts[layer_id] = around_team(grad_parts(owner, gate_total, total))
        full_wide, full_gate, _ = full[layer_id]
        sequence = lambda v, k: lax.slice_in_dim(v, k * span, (k + 1) * span, axis=0)
        both_back = lambda k: back(sequence(grad_wide, k), full_wide) + back(
            sequence(grad_gate, k), full_gate
        )
        grad_far, grad_normed = both_back(1), both_back(0)
        norm_grad = jnp.sum(in_grad * full_wide.astype(F32), axis=1)
        norm_grad = norm_grad + jnp.sum(gate_grad * full_gate.astype(F32), axis=1)
        if fast:
            norm_grad = x_first(norm_grad)
        norm_grad = norm_grad / norm_gain[layer_id]
        grad_normed = team_scatter(grad_normed, grad_far)
        if fast:
            grad_normed = x_first(grad_normed)
        else:
            grad_normed = tie(grad_normed, both_total)
        _, pull_norm = jax.vjp(lambda v: norm_piece(v, norm_gain[layer_id]), stream_in)
        (grad_inner,) = pull_norm(grad_normed)
        grad_stream = grad_stream + grad_inner
        small[layer_id] = pack_small(
            conv_sums, tile_sums, head_sums, skip_sums, grad_gain, norm_grad.reshape(1, features),
            spread,
        )
    mixed = stream.reshape(1, length, features).astype(BF16)
    pack = xor_sum(xor_sum(jnp.stack(small), "x"), "z")
    across = y_swap(pack)
    packs = (pack, core_swap(pack), across, core_swap(across))
    norm_sum, taps_sum, bias_sum, dt_sum, decay_sum, skip_sum, gain_sum = open_small(
        owner, packs, features
    )
    return (
        mixed,
        grad_stream.reshape(1, length, features),
        norm_sum,
        join_weights(owner, in_parts),
        taps_sum,
        bias_sum,
        dt_sum,
        decay_sum,
        skip_sum,
        gain_sum,
        jnp.stack(out_shards),
    )


def solution(mesh):
    rows, spans = mesh.devices.shape
    split = Mesh(mesh.devices.reshape(rows // 2, 2, spans // 2, 2), ("x", "core", "z", "y"))
    tokens = P(("x", "core"), ("z", "y"), None)
    weight = P(None, ("x", "core", "z", "y"), None)
    return jax.shard_map(
        local,
        mesh=split,
        in_specs=(
            tokens,
            P(("x", "core"), ("z", "y")),
            tokens,
            P(),
            weight,
            P(),
            P(),
            P(),
            P(),
            P(),
            P(),
            weight,
        ),
        out_specs=(tokens, tokens, P(), weight, P(), P(), P(), P(), P(), P(), weight),
        check_vma=False,
    )
```

```python
from functools import partial

import jax
import jax.numpy as jnp
from jax import lax
from jax.experimental import pallas as pl
from jax.experimental.pallas import tpu as pltpu
from jax.sharding import Mesh
from jax.sharding import PartitionSpec as P

HEADS = 48
HEADDIM = 64
STATE = 128
CONV = 4
INNER = 3072
CONVDIM = 3328

TEAM = 4
HEADS_Q = HEADS // TEAM
INNER_Q = INNER // TEAM
BC_Q = 2 * STATE // TEAM
CONV_Q = INNER_Q + BC_Q
WIDE = 896

EPS = 1e-05
VMEM_BYTES = 40 * 1024 * 1024
STEP_BYTES = 20 * 1024 * 1024
NEAR = 4
SWAP = [(0, 1), (1, 0)]
BF16 = jnp.bfloat16
F32 = jnp.float32


def shift(block, axis, distance):
    size = lax.axis_size(axis)
    return lax.ppermute(block, axis, [(i, (i + distance) % size) for i in range(size)])


def step_line(block, axis, distance):
    devices = range(lax.axis_size(axis))
    return lax.ppermute(block, axis, [(i, i + distance) for i in devices if i + distance in devices])


def core_swap(block):
    return lax.ppermute(block, "core", SWAP)


def y_swap(block):
    return lax.ppermute(block, "y", SWAP)


def diagonal_swap(block):
    return lax.ppermute(block, ("core", "y"), [(0, 3), (1, 2), (2, 1), (3, 0)])


def xor_sum(values, axis):
    size = lax.axis_size(axis)
    bit = 1
    while bit < size:
        values = tie(values + lax.ppermute(values, axis, [(i, i ^ bit) for i in range(size)]))
        bit *= 2
    return values


def member():
    return lax.axis_index("y") * 2 + lax.axis_index("core")


def in_order(parts):
    q = member()
    return [lax.select_n(q ^ j, *parts) for j in range(TEAM)]


def around_team(blocks):
    return blocks[0], core_swap(blocks[1]), y_swap(blocks[2]), diagonal_swap(blocks[3])


def by_y(own, other):
    first = lax.axis_index("y") == 0
    return jnp.where(first, jnp.concatenate((own, other), 1), jnp.concatenate((other, own), 1))


def team_gather(block):
    pair = jnp.stack((block, core_swap(block)))
    crossed = y_swap(block)
    other = jnp.stack((crossed, core_swap(crossed)))
    return by_y(pair, other)


def team_scatter(own, other):
    total = own + core_swap(other.astype(BF16)).astype(F32)
    half = total.shape[0] // 2
    y = lax.axis_index("y")
    mine = lax.dynamic_slice_in_dim(total, y * half, half, 0)
    theirs = lax.dynamic_slice_in_dim(total, (1 - y) * half, half, 0)
    return mine + y_swap(theirs.astype(BF16)).astype(F32)


def team_sum(values):
    across = core_swap(values) + diagonal_swap(values)
    return (values + y_swap(values)) + across[::-1]


def x_swap(block):
    return lax.ppermute(block, "x", SWAP)


def line_pieces(piece):
    return [piece] + [shift(piece, "z", hop) for hop in range(1, lax.axis_size("z"))]


def fetch(piece):
    line = line_pieces(piece)
    return line, line + [x_swap(p) for p in line]


def sum_to_owner(blocks):
    flat = blocks.reshape((-1,) + blocks.shape[2:])
    return lax.psum_scatter(flat, ("x", "z"), scatter_dimension=0)


TURN = [(0, 0), (1, 2), (2, 1), (3, 3)]


def x_first(values):
    low, high = jnp.split(values, 2, axis=-1)
    first = lax.axis_index("x") == 0
    return jnp.where(first, jnp.concatenate((low, high), -1), jnp.concatenate((high, low), -1))


def rms_scale(values):
    return values * lax.rsqrt(jnp.mean(values * values, axis=-1, keepdims=True) + EPS)


def norm_piece(stream, norm_scale):
    return rms_scale(stream) * norm_scale


def conv_piece(seg_ext, extended, conv_taps, conv_shift):
    length = extended.shape[-2] - CONV + 1
    seg_here = seg_ext[..., CONV - 1 :]
    summed = conv_shift
    for offset in range(CONV):
        same_doc = (seg_ext[..., offset : offset + length] == seg_here)[..., None]
        summed = summed + conv_taps[offset] * extended[..., offset : offset + length, :] * same_doc
    return jax.nn.silu(summed)


CHUNK = 128
LANE = 64
NEVER = -1e30
TILE = INNER_Q // 128


def split_parts(values):
    high = values.astype(BF16)
    rest = values - high.astype(F32)
    middle = rest.astype(BF16)
    return high, middle, (rest - middle.astype(F32)).astype(BF16)


def mm(a, b, over=(1, 0)):
    return lax.dot_general(
        a, b, (((over[0],), (over[1],)), ((), ())), preferred_element_type=F32
    )


def exact_mm(values, ones, over=(1, 0)):
    high, middle, low = split_parts(values)
    return (mm(low, ones, over) + mm(middle, ones, over)) + mm(high, ones, over)


def spread_mm(values, ones, over=(1, 0)):
    high, low = halves(values)
    return mm(low, ones, over) + mm(high, ones, over)


def mm_exact(ones, values):
    high, middle, low = split_parts(values)
    return (mm(ones, low) + mm(ones, middle)) + mm(ones, high)


def halves(values):
    high = values.astype(BF16)
    return high, (values - high.astype(F32)).astype(BF16)


def mm_wide(narrow, values, over=(1, 0)):
    high, low = halves(values)
    return mm(narrow, low, over) + mm(narrow, high, over)


def softplus(values):
    tail = jnp.exp(-jnp.abs(values))
    series = tail * (1.0 - tail * (0.5 - tail * (1.0 / 3.0)))
    return jnp.maximum(values, 0.0) + jnp.where(tail < 0.01, series, jnp.log(1.0 + tail))


def sigmoid(values):
    return 1.0 / (1.0 + jnp.exp(-values))


def grids(shape):
    return lax.broadcasted_iota(jnp.int32, shape, 0), lax.broadcasted_iota(jnp.int32, shape, 1)


def column(row):
    return jnp.broadcast_to(row, (CHUNK, CHUNK)).T


def step_terms(raw_ref, par_ref):
    down, across = grids((CHUNK, CHUNK))
    lower = (down >= across).astype(F32).astype(BF16)
    step = softplus(raw_ref[0] + par_ref[0:1])
    sums = mm_exact(lower, -par_ref[1:2] * step)
    return step, sums, sums[CHUNK - 1 :]


def seg_terms(seg_ref):
    return column(seg_ref[0, 0, 0:1]), seg_ref[0, 0, 0:1], seg_ref[0, 0, 1:2], seg_ref[0, 0, 2:3]


def chunk_decay(total, before, last, spread):
    kept = jnp.exp(total) * (before == last).astype(F32)
    return exact_mm(jnp.broadcast_to(kept, (8, CHUNK)), spread)


def state_kernel(x, bc, raw, seg, par, spread, before_out, reach_out, end_out, total_out, bits_out, state, reach):
    @pl.when(pl.program_id(1) == 0)
    def _():
        state[...] = jnp.zeros_like(state)
        reach[...] = jnp.ones_like(reach)

    step, sums, total = step_terms(raw, par)
    lines, _, before, last = seg_terms(seg)
    before_out[0, 0] = state[...]
    reach_out[0, 0] = reach[...]
    leaving = jnp.where(lines == last, jnp.exp(total - sums), 0.0)
    fed = (x[0].astype(F32) * spread_mm(step, spread[...])).astype(BF16).astype(F32)
    fed = fed * spread_mm(leaving, spread[...])
    decay = chunk_decay(total, before, last, spread[...])
    state[...] = state[...] * decay[0:1] + mm_wide(bc[0, :, :STATE], fed, (0, 0))
    reach[...] = reach[...] * decay
    end_out[0] = state[...]
    total_out[0] = reach[...]
    lines = [v[0:1] for v in split_parts(reach[...])]
    bits_out[0] = jnp.concatenate(lines + [jnp.zeros((13, INNER_Q), BF16)], axis=0)


def inside_kernel(x, bc, raw, seg, par, spread, y_out):
    step, sums, _ = step_terms(raw, par)
    lines, row, _, _ = seg_terms(seg)
    down, across = grids((CHUNK, CHUNK))
    bias = jnp.where((lines == row) & (down >= across), 0.0, NEVER)
    scores = mm(bc[0, :, STATE:], bc[0, :, :STATE], (1, 1))
    turned = sums.T
    fed = (x[0].astype(F32) * spread_mm(step, spread[...])).astype(BF16)
    for pair in range(HEADS_Q // 2):
        lanes = slice(pair * 128, pair * 128 + 128)
        mixing = []
        for head in (LANE + 2 * pair, LANE + 2 * pair + 1):
            gap = jnp.broadcast_to(sums[:, head : head + 1], (CHUNK, CHUNK)) - turned[head : head + 1]
            mixing.append((scores * jnp.exp(gap + bias)).astype(BF16))
        both = mm(jnp.concatenate(mixing, axis=0), fed[:, lanes])
        y_out[0, :, lanes] = jnp.where(across < HEADDIM, both[:CHUNK], both[CHUNK:])


def outer_kernel(
    y_in, x, bc, raw, seg, par, spread, before, reach, start, gate, rows, y_out, gated_out, square_out
):
    _, sums, _ = step_terms(raw, par)
    lines, _, ahead, _ = seg_terms(seg)
    entering = spread_mm(jnp.where(lines == ahead, jnp.exp(sums), 0.0), spread[...])
    state = before[0, 0] + reach[0, 0, 0:1] * start[0]
    y = y_in[0] + entering * mm_wide(bc[0, :, STATE:], state)
    y_out[0] = y
    raw_gate = gate[0]
    gated = (y + rows[0:1] * x[0].astype(F32)) * (raw_gate * sigmoid(raw_gate))
    gated_out[0] = gated
    square = gated * gated
    folded = square[:, :128]
    for tile in range(1, INNER_Q // 128):
        folded = folded + square[:, tile * 128 : tile * 128 + 128]
    square_out[0, 0] = jnp.sum(folded.T, axis=0, keepdims=True)


def along_kernel(grad, gated, rows, scale, along_out, gain_out):
    @pl.when(pl.program_id(1) == 0)
    def _():
        gain_out[...] = jnp.zeros_like(gain_out)

    product = grad[0] * gated[0]
    weighed = product * rows[1:2]
    folded = weighed[:, :128]
    for tile in range(1, INNER_Q // 128):
        folded = folded + weighed[:, tile * 128 : tile * 128 + 128]
    along_out[0, 0] = jnp.sum(folded.T, axis=0, keepdims=True)
    lines = jnp.concatenate([column(scale[0, 0])] * (INNER_Q // 128), axis=1)
    gain_out[0] += jnp.sum((product * lines).reshape(CHUNK // 8, 8, INNER_Q), axis=0)


def gate_back_kernel(
    grad, gated, y, x, gate, bc, raw, seg, par, spread, rows, scale, along,
    grad_out, gate_out, after_out, beyond_out, start_out, state, reach,
):
    @pl.when(pl.program_id(1) == 0)
    def _():
        state[...] = jnp.zeros_like(state)
        reach[...] = jnp.ones_like(reach)

    wide = lambda row: jnp.concatenate([column(row)] * (INNER_Q // 128), axis=1)
    factor = scale[0, 0]
    pull = factor * factor * factor * along[0, 0] * (1.0 / INNER)
    grad_gated = grad[0] * rows[1:2] * wide(factor) - gated[0] * wide(pull)
    raw_gate = gate[0]
    sig = sigmoid(raw_gate)
    grad_y = (grad_gated * (raw_gate * sig)).astype(BF16)
    ssd_y = y[0] + rows[0:1] * x[0].astype(F32)
    gate_out[0] = (grad_gated * ssd_y * (sig * (1.0 + raw_gate * (1.0 - sig)))).astype(BF16)
    grad_out[0] = grad_y

    _, sums, total = step_terms(raw, par)
    lines, _, before, last = seg_terms(seg)
    after_out[0, 0] = state[...]
    beyond_out[0, 0] = reach[...]
    entering = spread_mm(jnp.where(lines == before, jnp.exp(sums), 0.0), spread[...])
    decay = chunk_decay(total, before, last, spread[...])
    fed = grad_y.astype(F32) * entering
    state[...] = state[...] * decay[0:1] + mm_wide(bc[0, :, STATE:], fed, (0, 0))
    reach[...] = reach[...] * decay
    start_out[0] = state[...]


def inside_back_kernel(x, bc, raw, seg, par, spread, grad, fed_out, b_out, c_out):
    step, sums, _ = step_terms(raw, par)
    lines, row, _, _ = seg_terms(seg)
    down, across = grids((CHUNK, CHUNK))
    bias = jnp.where((lines == row) & (across >= down), 0.0, NEVER)
    b_in, c_in = bc[0, :, :STATE], bc[0, :, STATE:]
    scores = mm(b_in, c_in, (1, 1))
    turned = sums.T
    fed = (x[0].astype(F32) * spread_mm(step, spread[...])).astype(BF16)
    grad_scores = jnp.zeros((CHUNK, CHUNK), F32)
    for pair in range(HEADS_Q // 2):
        lanes = slice(pair * 128, pair * 128 + 128)
        fed_pair, grad_pair = fed[:, lanes], grad[0, :, lanes]
        none = jnp.zeros_like(fed_pair)
        apart = jnp.concatenate(
            (jnp.where(across < HEADDIM, fed_pair, none), jnp.where(across < HEADDIM, none, fed_pair)),
            axis=0,
        )
        grad_mixing = mm(apart, grad_pair, (1, 1))
        mixing = []
        for which in range(2):
            head = LANE + 2 * pair + which
            gap = turned[head : head + 1] - jnp.broadcast_to(sums[:, head : head + 1], (CHUNK, CHUNK))
            decays = jnp.exp(gap + bias)
            mixing.append((scores * decays).astype(BF16))
            grad_scores = grad_scores + grad_mixing[which * CHUNK : which * CHUNK + CHUNK] * decays
        both = mm(jnp.concatenate(mixing, axis=0), grad_pair)
        fed_out[0, :, lanes] = jnp.where(across < HEADDIM, both[:CHUNK], both[CHUNK:])
    grad_scores = grad_scores.astype(BF16)
    b_out[0] = mm(grad_scores, c_in)
    c_out[0] = mm(grad_scores, b_in, (0, 0))


def outer_back_kernel(
    fed_in, b_in, c_in, x, bc, raw, seg, par, spread, before, reach, start, after, beyond, grad_end,
    end, total_reach, grad, y, rows,
    x_out, bc_out, raw_out, sums_out, skip_out, carry,
):
    @pl.when(pl.program_id(1) == 0)
    def _():
        sums_out[...] = jnp.zeros_like(sums_out)
        skip_out[...] = jnp.zeros_like(skip_out)
        last_state = end[0] + total_reach[0, 0:1] * start[0]
        meet = jnp.sum((grad_end[0] * last_state).reshape(STATE // 8, 8, INNER_Q), axis=0)
        meet = jnp.sum(spread_mm(meet, spread[...], (1, 1)), axis=0, keepdims=True)
        carry[...] = jnp.broadcast_to(meet, carry.shape)

    step, sums, total = step_terms(raw, par)
    lines, _, ahead, last = seg_terms(seg)
    ones = spread[...]
    state = (before[0, 0] + reach[0, 0, 0:1] * start[0]).astype(BF16)
    grad_state = after[0, 0] + beyond[0, 0, 0:1] * grad_end[0]
    values = x[0].astype(F32)
    grad_y = grad[0].astype(F32)
    wide_step = spread_mm(step, ones)
    leaving = spread_mm(jnp.where(lines == last, jnp.exp(total - sums), 0.0), ones)
    entering = spread_mm(jnp.where(lines == ahead, jnp.exp(sums), 0.0), ones)
    fed = (values * wide_step).astype(BF16).astype(F32)
    grad_fed = fed_in[0] + leaving * mm_wide(bc[0, :, :STATE], grad_state)
    x_out[0] = wide_step * grad_fed + rows[0:1] * grad_y
    bc_out[0, :, :STATE] = b_in[0] + mm((leaving * fed).astype(BF16), grad_state.astype(BF16), (1, 1))
    bc_out[0, :, STATE:] = c_in[0] + mm((entering * grad_y).astype(BF16), state, (1, 1))
    skip_out[0] += jnp.sum((grad_y * values).reshape(CHUNK // 8, 8, INNER_Q), axis=0)

    by_step = spread_mm(values * grad_fed, ones, (1, 1))
    flow = spread_mm(grad_y * y[0] - fed * grad_fed, ones, (1, 1))
    down, across = grids((CHUNK, CHUNK))
    upper = (across >= down).astype(F32).astype(BF16)
    grad_log = mm_exact(upper, flow) + carry[0:1]
    carry[...] = jnp.broadcast_to(grad_log[0:1], carry.shape)
    rate = par[1:2]
    grad_raw = (by_step - rate * grad_log) * sigmoid(raw[0] + par[0:1])
    raw_out[0] = grad_raw
    fold = lambda v: jnp.sum(v.reshape(CHUNK // 8, 8, CHUNK), axis=0)
    sums_out[0, 0:8] += fold(-rate * step * grad_log)
    sums_out[0, 8:16] += fold(grad_raw)


def chunk_spec(width, back=0, column_block=0):
    turn = (lambda c: back - 1 - c) if back else (lambda c: c)
    return pl.BlockSpec((1, CHUNK, width), lambda s, c: (s, turn(c), column_block))


def per_chunk(lines, width, back=0):
    turn = (lambda c: back - 1 - c) if back else (lambda c: c)
    return pl.BlockSpec((1, 1, lines, width), lambda s, c: (s, turn(c), 0, 0))


def per_sequence(lines, width):
    return pl.BlockSpec((1, lines, width), lambda s, c: (s, 0, 0))


def fixed(lines, width):
    return pl.BlockSpec((lines, width), lambda s, c: (0, 0))


def shaped(shape, dtype=F32):
    return jax.ShapeDtypeStruct(shape, dtype)


def call(kernel, name, chunks, ins, outs, operands, scratch=(), flops=0, after=()):
    in_specs = [spec for spec, _ in zip(ins, operands, strict=True)]
    moved = sum(v.size * v.dtype.itemsize for v in operands)
    moved += sum(v.size * v.dtype.itemsize for _, v in outs)
    count, skipped = len(in_specs), len(after)
    in_specs = in_specs + [pl.BlockSpec(memory_space=pl.ANY)] * skipped
    operands = tuple(operands) + tuple(after)
    return pl.pallas_call(
        lambda *refs: kernel(*refs[:count], *refs[count + skipped :]),
        name=name,
        grid=(2, chunks),
        in_specs=in_specs,
        out_specs=[spec for spec, _ in outs],
        out_shape=[shape for _, shape in outs],
        scratch_shapes=list(scratch),
        cost_estimate=pl.CostEstimate(flops=flops, bytes_accessed=moved, transcendentals=0),
        compiler_params=pltpu.CompilerParams(
            dimension_semantics=("arbitrary", "arbitrary"), vmem_limit_bytes=STEP_BYTES
        ),
    )(*operands)


STATE_SCRATCH = (pltpu.VMEM((STATE, INNER_Q), F32), pltpu.VMEM((8, INNER_Q), F32))


def scan_states(x, bc, raw, seg, par, spread, after=()):
    span = x.shape[1]
    n = span // CHUNK
    return call(
        state_kernel, "chunk_states", n,
        [chunk_spec(INNER_Q), chunk_spec(2 * STATE), chunk_spec(128, 0, TILE), per_chunk(8, 128), fixed(8, 128),
         fixed(128, INNER_Q)],
        [(per_chunk(STATE, INNER_Q), shaped((2, n, STATE, INNER_Q))), (per_chunk(8, INNER_Q), shaped((2, n, 8, INNER_Q))),
         (per_sequence(STATE, INNER_Q), shaped((2, STATE, INNER_Q))), (per_sequence(8, INNER_Q), shaped((2, 8, INNER_Q))),
         (per_sequence(16, INNER_Q), shaped((2, 16, INNER_Q), BF16))],
        (x, bc, raw, seg, par, spread), STATE_SCRATCH, 2 * 2 * span * STATE * INNER_Q, after=after,
    )


def scan_inside(x, bc, raw, seg, par, spread, after=()):
    span = x.shape[1]
    n = span // CHUNK
    return call(
        inside_kernel, "inside_chunks", n,
        [chunk_spec(INNER_Q), chunk_spec(2 * STATE), chunk_spec(128, 0, TILE), per_chunk(8, 128), fixed(8, 128),
         fixed(128, INNER_Q)],
        [(chunk_spec(INNER_Q), shaped(x.shape))],
        (x, bc, raw, seg, par, spread), (), 8 * 2 * span * CHUNK * INNER_Q, after=after,
    )[0]


def scan_outer(y, x, bc, raw, seg, par, spread, before, reach, start, gate, rows, after=()):
    span = x.shape[1]
    n = span // CHUNK
    return call(
        outer_kernel, "scan_and_gate", n,
        [chunk_spec(INNER_Q), chunk_spec(INNER_Q), chunk_spec(2 * STATE), chunk_spec(128, 0, TILE), per_chunk(8, 128), fixed(8, 128),
         fixed(128, INNER_Q), per_chunk(STATE, INNER_Q), per_chunk(8, INNER_Q), per_sequence(STATE, INNER_Q),
         chunk_spec(INNER_Q), fixed(8, INNER_Q)],
        [(chunk_spec(INNER_Q), shaped(x.shape)), (chunk_spec(INNER_Q), shaped(x.shape)),
         (per_chunk(1, 128), shaped((2, n, 1, 128)))],
        (y, x, bc, raw, seg, par, spread, before, reach, start, gate, rows), (), 8 * span * STATE * INNER_Q, after=after,
    )


def gate_along(grad, gated, rows, scale, after=()):
    span = gated.shape[1]
    n = span // CHUNK
    return call(
        along_kernel, "gate_along", n,
        [chunk_spec(INNER_Q), chunk_spec(INNER_Q), fixed(8, INNER_Q), per_chunk(1, 128)],
        [(per_chunk(1, 128), shaped((2, n, 1, 128))), (per_sequence(8, INNER_Q), shaped((2, 8, INNER_Q)))],
        (grad, gated, rows, scale), (), 10 * span * INNER_Q, after=after,
    )


def gate_back(grad, gated, y, x, gate, bc, raw, seg, par, spread, rows, scale, along, after=()):
    span = x.shape[1]
    n = span // CHUNK
    return call(
        gate_back_kernel, "gate_back_and_states", n,
        [chunk_spec(INNER_Q, n)] * 5 + [chunk_spec(2 * STATE, n), chunk_spec(128, n, TILE), per_chunk(8, 128, n), fixed(8, 128),
         fixed(128, INNER_Q), fixed(8, INNER_Q), per_chunk(1, 128, n), per_chunk(1, 128, n)],
        [(chunk_spec(INNER_Q, n), shaped(x.shape, BF16)), (chunk_spec(INNER_Q, n), shaped(x.shape, BF16)),
         (per_chunk(STATE, INNER_Q, n), shaped((2, n, STATE, INNER_Q))), (per_chunk(8, INNER_Q, n), shaped((2, n, 8, INNER_Q))),
         (per_sequence(STATE, INNER_Q), shaped((2, STATE, INNER_Q)))],
        (grad, gated, y, x, gate, bc, raw, seg, par, spread, rows, scale, along), STATE_SCRATCH,
        8 * span * STATE * INNER_Q, after=after,
    )


def scan_inside_back(x, bc, raw, seg, par, spread, grad, after=()):
    span = x.shape[1]
    n = span // CHUNK
    return call(
        inside_back_kernel, "inside_chunks_back", n,
        [chunk_spec(INNER_Q), chunk_spec(2 * STATE), chunk_spec(128, 0, TILE), per_chunk(8, 128), fixed(8, 128),
         fixed(128, INNER_Q), chunk_spec(INNER_Q)],
        [(chunk_spec(INNER_Q), shaped(x.shape)), (chunk_spec(STATE), shaped((2, span, STATE))),
         (chunk_spec(STATE), shaped((2, span, STATE)))],
        (x, bc, raw, seg, par, spread, grad), (), 24 * 2 * span * CHUNK * INNER_Q, after=after,
    )


def scan_outer_back(
    fed, b, c, x, bc, raw, seg, par, spread, before, reach, start, later, beyond, grad_end, end, total, grad, y, rows, after=()
):
    span = x.shape[1]
    n = span // CHUNK
    return call(
        outer_back_kernel, "scan_back", n,
        [chunk_spec(INNER_Q, n), chunk_spec(STATE, n), chunk_spec(STATE, n), chunk_spec(INNER_Q, n), chunk_spec(2 * STATE, n),
         chunk_spec(128, n, TILE), per_chunk(8, 128, n), fixed(8, 128), fixed(128, INNER_Q), per_chunk(STATE, INNER_Q, n),
         per_chunk(8, INNER_Q, n), per_sequence(STATE, INNER_Q), per_chunk(STATE, INNER_Q, n), per_chunk(8, INNER_Q, n),
         per_sequence(STATE, INNER_Q), per_sequence(STATE, INNER_Q), per_sequence(8, INNER_Q), chunk_spec(INNER_Q, n),
         chunk_spec(INNER_Q, n), fixed(8, INNER_Q)],
        [(chunk_spec(INNER_Q, n), shaped(x.shape)), (chunk_spec(2 * STATE, n), shaped((2, span, 2 * STATE))),
         (chunk_spec(128, n), shaped((2, span, 128))), (per_sequence(16, 128), shaped((2, 16, 128))),
         (per_sequence(8, INNER_Q), shaped((2, 8, INNER_Q)))],
        (fed, b, c, x, bc, raw, seg, par, spread, before, reach, start, later, beyond, grad_end, end, total, grad, y, rows),
        (pltpu.VMEM((8, 128), F32),), 24 * span * STATE * INNER_Q, after=after,
    )


def seg_table(seg_now, seg_before):
    span = seg_now.shape[1]
    rows = seg_now.reshape(2, span // CHUNK, 1, CHUNK)
    last = rows[..., -1:]
    before = jnp.concatenate((seg_before.reshape(2, 1, 1, 1), last[:, :-1]), axis=1)
    spread = lambda v: jnp.broadcast_to(v, rows.shape)
    return jnp.concatenate((rows, spread(before), spread(last)) + (rows,) * 5, axis=2)


def conv_terms(wide_ref, halo_ref, taps_ref, mask_ref, tail):
    own = wide_ref[0].astype(BF16).astype(F32)
    longer = jnp.concatenate((tail, own), axis=0)
    rows = [own]
    total = taps_ref[CONV : CONV + 1] + taps_ref[CONV - 1 : CONV] * own
    for back in range(1, CONV):
        same = jnp.concatenate([column(mask_ref[0, 0, back : back + 1])] * (own.shape[1] // 128), axis=1)
        earlier = longer[8 - back : 8 - back + CHUNK] * same
        rows.append(earlier)
        total = total + taps_ref[CONV - 1 - back : CONV - back] * earlier
    return own, rows, total


def conv_kernel(wide, halo, taps, mask, out, tail):
    @pl.when(pl.program_id(1) == 0)
    def _():
        tail[...] = halo[0].astype(F32)

    own, _, total = conv_terms(wide, halo, taps, mask, tail[...])
    tail[...] = own[CHUNK - 8 :]
    out[0] = (total * sigmoid(total)).astype(BF16)


def conv_back_kernel(wide, before, halo, taps, mask, grad, returned, out, sums_out, ahead):
    chunk = pl.num_programs(1) - 1 - pl.program_id(1)

    @pl.when(pl.program_id(1) == 0)
    def _():
        sums_out[...] = jnp.zeros_like(sums_out)
        ahead[...] = jnp.zeros_like(ahead)

    tail = jnp.where(chunk == 0, halo[0].astype(F32), before[0].astype(BF16).astype(F32))
    _, rows, total = conv_terms(wide, halo, taps, mask, tail)
    sig = sigmoid(total)
    pull = grad[0] * (sig * (1.0 + total * (1.0 - sig)))
    result = taps[CONV - 1 : CONV] * pull
    fold = lambda v: jnp.sum(v.reshape(CHUNK // 8, 8, v.shape[1]), axis=0)
    for back in range(1, CONV):
        same = jnp.concatenate([column(mask[0, 0, back : back + 1])] * (pull.shape[1] // 128), axis=1)
        masked = pull * same
        longer = jnp.concatenate((masked, ahead[8 * back - 8 : 8 * back]), axis=0)
        result = result + taps[CONV - 1 - back : CONV - back] * longer[back : back + CHUNK]
        ahead[8 * back - 8 : 8 * back] = masked[:8]
    for back in range(CONV):
        place = CONV - 1 - back
        sums_out[0, 8 * place : 8 * place + 8] += fold(pull * rows[back])
    sums_out[0, 8 * CONV : 8 * CONV + 8] += fold(pull)
    late = (pl.program_id(1) == 0).astype(F32) * returned[0].astype(F32)
    late = jnp.concatenate((jnp.zeros((CHUNK - 8, late.shape[1]), F32), late), axis=0)
    out[0] = (result + late).astype(BF16)


def conv_forward(wide, halo, taps, mask, width, at, after=()):
    n = wide.shape[1] // CHUNK
    lines = lambda rows: pl.BlockSpec((1, rows, width), lambda s, c: (s, 0, at))
    return call(
        conv_kernel, "conv", n,
        [chunk_spec(width, 0, at), lines(8), pl.BlockSpec((8, width), lambda s, c: (0, at)), per_chunk(8, 128)],
        [(chunk_spec(width), shaped(wide.shape[:2] + (width,), BF16))],
        (wide, halo, taps, mask), (pltpu.VMEM((8, width), F32),), 30 * wide.shape[1] * width, after=after,
    )[0]


def conv_backward(wide, halo, taps, mask, grad, returned, width, at, after=()):
    n = wide.shape[1] // CHUNK
    lines = lambda rows: pl.BlockSpec((1, rows, width), lambda s, c: (s, 0, at))
    steps = CHUNK // 8
    early = pl.BlockSpec(
        (1, 8, width), lambda s, c: (s, jnp.maximum((n - 1 - c) * steps - 1, 0), at)
    )
    return call(
        conv_back_kernel, "conv_back", n,
        [chunk_spec(width, n, at), early, lines(8), pl.BlockSpec((8, width), lambda s, c: (0, at)),
         per_chunk(8, 128, n), chunk_spec(width, n), lines(8)],
        [(chunk_spec(width, n), shaped(wide.shape[:2] + (width,), BF16)), (per_sequence(8 * CONV + 8, width), shaped((2, 8 * CONV + 8, width)))],
        (wide, wide, halo, taps, mask, grad, returned), (pltpu.VMEM((8 * CONV, width), F32),), 60 * wide.shape[1] * width, after=after,
    )


def mask_table(seg_ext, edge_rows):
    span = seg_ext.shape[1] - edge_rows
    here = seg_ext[:, edge_rows:]
    rows = [here == seg_ext[:, edge_rows - back : edge_rows - back + span] for back in range(CONV)]
    table = jnp.stack(rows + rows, axis=1).astype(F32)
    return jnp.moveaxis(table.reshape(2, 2 * CONV, span // CHUNK, CHUNK), 2, 1)


def tile_picks(owner, rows):
    down, across = grids((2 * STATE, 128))
    bc = (down - BC_Q * owner == across) & (across < BC_Q)
    down, across = grids((HEADS, 128))
    head = across - LANE
    dt = (down - HEADS_Q * owner == head) & (head >= 0) & (head < HEADS_Q)
    return bc.astype(F32), dt.astype(F32)


def cut_weights_kernel(q_ref, weight, *outs):
    for layer in range(weight.shape[0]):
        for k in range(TEAM):
            owner = q_ref[0] ^ k
            start = pl.multiple_of(owner * INNER_Q, 128)
            part = outs[layer * TEAM + k]
            part[:, :INNER_Q] = weight[layer, :, pl.ds(start, INNER_Q)]
            part[:, INNER_Q : 2 * INNER_Q] = weight[layer, :, pl.ds(INNER + start, INNER_Q)]
            bc, dt = tile_picks(owner, None)
            tile = mm(weight[layer, :, 2 * INNER : 2 * INNER + 2 * STATE], bc.astype(BF16))
            tile = tile + mm(weight[layer, :, INNER + CONVDIM :], dt.astype(BF16))
            part[:, 2 * INNER_Q :] = tile.astype(BF16)


def whole_spec(shape):
    return pl.BlockSpec(shape, lambda *_: (0,) * len(shape))


def whole_call(kernel, name, index, operands, outs, after=()):
    count, skipped = 1 + len(operands), len(after)
    return pl.pallas_call(
        lambda *refs: kernel(*refs[:count], *refs[count + skipped :]),
        name=name,
        grid_spec=pltpu.PrefetchScalarGridSpec(
            num_scalar_prefetch=1,
            grid=(1,),
            in_specs=[whole_spec(v.shape) for v in operands]
            + [pl.BlockSpec(memory_space=pl.ANY)] * skipped,
            out_specs=[whole_spec(s.shape) for s in outs],
        ),
        out_shape=list(outs),
        compiler_params=pltpu.CompilerParams(vmem_limit_bytes=VMEM_BYTES),
    )(index, *operands, *after)


def tie(value, *after):
    anywhere = pl.BlockSpec(memory_space=pl.ANY)
    return pl.pallas_call(
        lambda *refs: None,
        name="tie",
        in_specs=[anywhere] * (1 + len(after)),
        out_specs=anywhere,
        out_shape=shaped(value.shape, value.dtype),
        input_output_aliases={0: 0},
    )(value, *after)


def norm_kernel(x_ref, stream, gain, out):
    values = stream[...].astype(F32)
    mean = jnp.mean(values * values, axis=-1, keepdims=True)
    normed = (values * lax.rsqrt(mean + EPS) * gain[...]).astype(BF16)
    width = normed.shape[1] // 2
    x = x_ref[0]
    out[:, pl.ds(pl.multiple_of(x * width, 128), width)] = normed[:, :width]
    out[:, pl.ds(pl.multiple_of((1 - x) * width, 128), width)] = normed[:, width:]


def norm_rows(x, stream, gain, after=()):
    return whole_call(norm_kernel, "norm", x, (stream, gain), [shaped(stream.shape, BF16)], after)[0]


def scale_kernel(gated, scale, rows, out):
    lines = jnp.concatenate([column(scale[0, 0])] * (INNER_Q // 128), axis=1)
    out[0] = (gated[0] * lines * rows[1:2]).astype(BF16)


def scale_rows(gated, scale, rows, after=()):
    n = gated.shape[1] // CHUNK
    return call(
        scale_kernel, "scale_rows", n,
        [chunk_spec(INNER_Q), per_chunk(1, 128), fixed(8, INNER_Q)],
        [(chunk_spec(INNER_Q), shaped(gated.shape, BF16))],
        (gated, scale, rows), (), 4 * gated.size, after=after,
    )[0]


def cut_weights(q, weight):
    layers, rows = weight.shape[:2]
    outs = [shaped((rows, INNER_Q + WIDE), BF16)] * (TEAM * layers)
    outs = whole_call(cut_weights_kernel, "cut_weights", q, (weight,), outs)
    return [outs[TEAM * layer : TEAM * layer + TEAM] for layer in range(layers)]


def place_of(owner):
    return (owner % 2) * 2 + owner // 2


def wide_piece_kernel(q_ref, *refs):
    out = refs[-1]
    for k in range(TEAM):
        out[place_of(q_ref[0] ^ k)] = refs[k][:, INNER_Q:]


def gate_piece_kernel(q_ref, *refs):
    rows, out = refs[TEAM], refs[-1]
    for k in range(TEAM):
        out[place_of(q_ref[0] ^ k)] = refs[k][:, :INNER_Q]
    for block in range(TEAM):
        half = block % 2 * INNER_Q
        out[TEAM + block] = rows[block // 2, :, half : half + INNER_Q]


def all_piece_kernel(q_ref, *refs):
    out = refs[-1]
    for k in range(TEAM):
        out[place_of(q_ref[0] ^ k)] = refs[k][...]


def all_piece(q, parts, after=()):
    shape = (TEAM,) + parts[0].shape
    return whole_call(all_piece_kernel, "all_piece", q, parts, [shaped(shape, BF16)], after)[0]


def arrange_kernel(_, gathered, gate, wide):
    for x in range(2):
        for z in range(gate.shape[2]):
            for block in range(TEAM):
                rows = gathered[x, z, block]
                gate[x, block // 2, z, block % 2] = rows[:, :INNER_Q]
                wide[x, block // 2, z, block % 2] = rows[:, INNER_Q:]


def arrange(index, gathered):
    size, rows = gathered.shape[1], gathered.shape[3]
    outs = [shaped((2, 2, size, 2, rows, width), BF16) for width in (INNER_Q, WIDE)]
    gate, wide = whole_call(arrange_kernel, "arrange", index, (gathered,), outs)
    return wide.reshape(-1, WIDE), gate.reshape(-1, INNER_Q)


def by_owner_kernel(x_ref, grad, out):
    for side in range(2):
        x = x_ref[0] if side == 0 else 1 - x_ref[0]
        for z in range(out.shape[1]):
            for block in range(TEAM):
                out[x, z, block] = grad[side, block // 2, z, block % 2].astype(BF16)


def both_by_owner_kernel(x_ref, gate, out_grad, out):
    for side in range(2):
        x = x_ref[0] if side == 0 else 1 - x_ref[0]
        for z in range(out.shape[1]):
            for block in range(TEAM):
                upper, lower = block // 2, block % 2
                half = slice(lower * INNER_Q, lower * INNER_Q + INNER_Q)
                out[x, z, block] = gate[side, upper, z, lower].astype(BF16)
                out[side, z, TEAM + block] = out_grad[z, side, upper, :, half].astype(BF16)


def both_by_owner(x_first_of, gate, out_grad, size, rows):
    operands = (
        gate.reshape(2, 2, size, 2, rows, INNER_Q),
        out_grad.reshape(size, 2, 2, rows, 2 * INNER_Q),
    )
    outs = [shaped((2, size, 2 * TEAM, rows, INNER_Q), BF16)]
    return whole_call(both_by_owner_kernel, "both_by_owner", x_first_of, operands, outs)[0]


def by_owner(x_first_of, grad, size, rows):
    width = grad.shape[-1]
    operands = (grad.reshape(2, 2, size, 2, rows, width),)
    outs = [shaped((2, size, TEAM, rows, width), BF16)]
    return whole_call(by_owner_kernel, "by_owner", x_first_of, operands, outs)[0]


def wide_piece(q, parts, after=()):
    shape = (TEAM, parts[0].shape[0], WIDE)
    return whole_call(wide_piece_kernel, "wide_piece", q, parts, [shaped(shape, BF16)], after)[0]


def gate_piece(q, parts, rows, after=()):
    count = parts[0].shape[0]
    operands = tuple(parts) + (rows.reshape(2, count, -1),)
    outs = [shaped((2 * TEAM, count, INNER_Q), BF16)]
    return whole_call(gate_piece_kernel, "gate_piece", q, operands, outs, after)[0]


def arrange_both_kernel(x_ref, gathered, gate, out):
    for side in range(2):
        x = x_ref[0] if side == 0 else 1 - x_ref[0]
        for z in range(gate.shape[2]):
            for block in range(TEAM):
                upper, lower = block // 2, block % 2
                gate[side, upper, z, lower] = gathered[x, z, block]
                half = slice(lower * INNER_Q, lower * INNER_Q + INNER_Q)
                out[z, side, upper, :, half] = gathered[side, z, TEAM + block]


def arrange_both(x_first_of, gathered):
    size, rows = gathered.shape[1], gathered.shape[3]
    outs = [
        shaped((2, 2, size, 2, rows, INNER_Q), BF16),
        shaped((size, 2, 2, rows, 2 * INNER_Q), BF16),
    ]
    gate, out = whole_call(arrange_both_kernel, "arrange_both", x_first_of, (gathered,), outs)
    return gate.reshape(-1, INNER_Q), out.reshape(-1, 2 * INNER_Q)


def whole_wide_kernel(place, *refs):
    out = refs[-1]
    size = out.shape[2]
    for side in range(2):
        for hop in range(size):
            source = lax.rem(place[0] - hop + size, size)
            for block in range(TEAM):
                out[side, block // 2, source, block % 2] = refs[side * size + hop][block]


def whole_columns(place, pieces, after=()):
    size = len(pieces) // 2
    rows, width = pieces[0].shape[1:]
    outs = [shaped((2, 2, size, 2, rows, width), BF16)]
    whole = whole_call(whole_wide_kernel, "whole_columns", place, pieces, outs, after)[0]
    return whole.reshape(-1, width)


def grad_parts_kernel(q_ref, gate, wide, *outs):
    for k in range(TEAM):
        block = place_of(q_ref[0] ^ k)
        outs[k][:, :INNER_Q] = gate[block]
        outs[k][:, INNER_Q:] = wide[block]


def grad_parts(q, gate, wide):
    outs = [shaped((wide.shape[1], INNER_Q + WIDE), BF16)] * TEAM
    return whole_call(grad_parts_kernel, "grad_parts", q, (gate, wide), outs)


def cut_params_kernel(q_ref, conv_weight, conv_bias, dt_bias, a_log, skip, out_gain, spread, taps, par, rows):
    owner = q_ref[0]
    start = pl.multiple_of(owner * INNER_Q, 128)
    bc, dt = tile_picks(owner, None)
    bc, dt = bc.astype(BF16), dt.astype(BF16)
    mine = pl.ds(start, INNER_Q)
    for layer in range(conv_weight.shape[0]):
        one = slice(layer, layer + 1)
        taps[layer, :CONV, :INNER_Q] = conv_weight[layer, :, mine]
        taps[layer, :CONV, INNER_Q:] = exact_mm(conv_weight[layer, :, INNER:], bc)
        taps[layer, CONV : CONV + 1, :INNER_Q] = conv_bias[one, mine]
        taps[layer, CONV : CONV + 1, INNER_Q:] = exact_mm(conv_bias[one, INNER:], bc)
        taps[layer, CONV + 1 :] = jnp.zeros((7 - CONV, WIDE), F32)
        par[layer, 0:1] = exact_mm(dt_bias[one], dt)
        par[layer, 1:2] = exact_mm(jnp.exp(a_log[one]), dt)
        par[layer, 2:] = jnp.zeros((6, 128), F32)
        rows[layer, 0:1] = exact_mm(exact_mm(skip[one], dt), spread[...])
        rows[layer, 1:2] = out_gain[one, mine]
        rows[layer, 2:] = jnp.zeros((6, INNER_Q), F32)


def cut_params(q, params, after):
    layers = params[0].shape[0]
    shapes = [(layers, 8, WIDE), (layers, 8, 128), (layers, 8, INNER_Q)]
    return whole_call(cut_params_kernel, "cut_params", q, params, [shaped(s) for s in shapes], after)


def join_kernel(q_ref, *refs):
    out = refs[-1]
    for layer in range(out.shape[0]):
        shared = 0.0
        for k in range(TEAM):
            owner = q_ref[0] ^ k
            start = pl.multiple_of(owner * INNER_Q, 128)
            part = refs[layer * TEAM + k]
            out[layer, :, pl.ds(start, INNER_Q)] = part[:, :INNER_Q].astype(F32)
            out[layer, :, pl.ds(INNER + start, INNER_Q)] = part[:, INNER_Q : 2 * INNER_Q].astype(F32)
            bc, dt = tile_picks(owner, None)
            both = jnp.concatenate((bc, dt), axis=0).astype(BF16)
            shared = shared + mm(part[:, 2 * INNER_Q :], both, (1, 1))
        out[layer, :, 2 * INNER :] = shared


def join_weights(q, parts):
    flat = [v for layer in parts for v in layer]
    shape = (len(parts), flat[0].shape[0], 2 * INNER + 2 * STATE + HEADS)
    return whole_call(join_kernel, "join_weights", q, flat, [shaped(shape)])[0]


SMALL = (16, WIDE)


def pack_small_kernel(conv_x, conv_tile, heads, skip, gain, norm, spread, out):
    fold = lambda v, rows: jnp.sum(v[:, rows], axis=(0, 1), keepdims=True)[0]
    for line in range(CONV + 1):
        rows = slice(8 * line, 8 * line + 8)
        out[line : line + 1, :INNER_Q] = fold(conv_x[...], rows)
        out[line : line + 1, INNER_Q:] = fold(conv_tile[...], rows)
    line = CONV + 1
    out[line:] = jnp.zeros((SMALL[0] - line, WIDE), F32)
    every = slice(0, 8)
    out[line + 1 : line + 2, :INNER_Q] = fold(gain[...], every)
    out[line + 2 : line + 3, :128] = fold(heads[...], slice(8, 16))
    out[line + 3 : line + 4, :128] = fold(heads[...], every)
    by_head = exact_mm(skip[0] + skip[1], spread[...], (1, 1))
    out[line + 4 : line + 5, :128] = jnp.sum(by_head, axis=0, keepdims=True)
    width = norm.shape[1] // 2
    out[line + 5 : line + 6, :width] = norm[:, :width]
    out[line + 6 : line + 7, :width] = norm[:, width:]


def pack_small(*parts):
    return pl.pallas_call(pack_small_kernel, name="pack_small", out_shape=shaped(SMALL))(*parts)


def lanes_of(values):
    return lax.broadcasted_iota(jnp.int32, values.shape, 1)


def open_small_kernel(q_ref, *refs):
    norm, conv_weight, conv_bias, dt_bias, a_log, skip, gain = refs[-7:]
    layers = norm.shape[0]
    line = CONV + 1
    for layer in range(layers):
        one = slice(layer, layer + 1)
        packs = [ref[layer] for ref in refs[:TEAM]]
        shared, heads = [], 0.0
        for k in range(TEAM):
            owner = q_ref[0] ^ k
            start = pl.multiple_of(owner * INNER_Q, 128)
            mine = pl.ds(start, INNER_Q)
            pack = packs[k]
            conv_weight[layer, :, mine] = pack[:CONV, :INNER_Q]
            conv_bias[one, mine] = pack[CONV:line, :INNER_Q]
            tile = pack[:8, INNER_Q:]
            tile = jnp.where(lanes_of(tile) < BC_Q, tile, 0.0)
            tile = jnp.where(owner % 2 == 0, tile, pltpu.roll(tile, BC_Q, 1))
            shared.append([jnp.where(owner // 2 == side, tile, 0.0) for side in range(2)])
            rows = pack[line + 2 : line + 5, :128]
            in_head = (lanes_of(rows) >= LANE) & (lanes_of(rows) < LANE + HEADS_Q)
            rows = jnp.where(in_head, rows, 0.0)
            placed = 0.0
            for which in range(TEAM):
                turned = pltpu.roll(rows, (HEADS_Q * which - LANE) % 128, 1)
                placed = placed + jnp.where(owner == which, turned, 0.0)
            heads = heads + placed[:, :HEADS]
            gain[one, mine] = pack[line + 1 : line + 2, :INNER_Q]
        shared = jnp.concatenate([sum([s[side] for s in shared]) for side in range(2)], axis=1)
        conv_weight[layer, :, INNER:] = shared[:CONV]
        conv_bias[one, INNER:] = shared[CONV:line]
        dt_bias[one], a_log[one], skip[one] = heads[0:1], heads[1:2], heads[2:3]
        width = norm.shape[1] // 2
        halves_of = lambda n: packs[n][line + 5 : line + 7, :width]
        total = (halves_of(0) + halves_of(1)) + (halves_of(2) + halves_of(3))
        norm[one, :width] = total[0:1]
        norm[one, width:] = total[1:2]


def open_small(q, packs, features):
    layers = packs[0].shape[0]
    flat = list(packs)
    shapes = [
        (layers, features), (layers, CONV, CONVDIM), (layers, CONVDIM), (layers, HEADS), (layers, HEADS),
        (layers, HEADS), (layers, INNER),
    ]
    return pl.pallas_call(
        open_small_kernel,
        name="open_small",
        grid_spec=pltpu.PrefetchScalarGridSpec(
            num_scalar_prefetch=1,
            grid=(1,),
            in_specs=[whole_spec(v.shape) for v in flat],
            out_specs=[whole_spec(s) for s in shapes],
        ),
        out_shape=[shaped(s) for s in shapes],
    )(q, *flat)


def spread_matrix():
    head = jnp.arange(128)[:, None] - LANE
    return (jnp.arange(INNER_Q)[None, :] // HEADDIM == head).astype(BF16)


def gap_decays(spans):
    rows = []
    for start in range(len(spans)):
        row = []
        running = jnp.ones_like(spans[0])
        for stop, span in enumerate(spans):
            if stop <= start:
                row.append(jnp.zeros_like(running))
                continue
            row.append(running)
            running = running * span
        rows.append(jnp.stack(row))
    return jnp.stack(rows)


def mix_states(states, bits=None, weights=None):
    size = lax.axis_size("z")
    z = lax.axis_index("z")
    width = states.shape[1] // size
    decay = lambda rows: jnp.sum(rows[:, :3].astype(F32), axis=1)
    if size > NEAR:
        if weights is None:
            weights = gap_decays([decay(v) for v in lax.all_gather(bits, "z")])
        cuts = jnp.moveaxis(states.reshape(2, size, width, -1), 1, 0).astype(BF16)
        parts = lax.all_to_all(cuts, "z", 0, 0, tiled=True).astype(F32)
        sums = jnp.sum(weights[:, :, :, None] * parts[:, None], axis=0)
        back = lax.all_to_all(sums.astype(BF16), "z", 0, 0, tiled=True).astype(F32)
        return jnp.moveaxis(back, 0, 1).reshape(states.shape), weights
    ring = lambda k: lax.rem(z + k + size, size)

    def cut(k):
        part = lax.dynamic_slice_in_dim(states, k * width, width, 1).astype(BF16)
        return part if weights is not None else jnp.concatenate((part, bits), axis=1)

    parts = [cut(z)] + [shift(cut(ring(hop)), "z", hop) for hop in range(1, size)]
    if weights is None:
        everyone = jnp.stack([decay(p[:, width:]) for p in parts])
        spans = [
            lax.dynamic_index_in_dim(everyone, lax.rem(z - k + size, size), 0, False)
            for k in range(size)
        ]
        weights = gap_decays(spans)
        parts = [p[:, :width] for p in parts]
    results = []
    for away in range(size):
        to = lax.dynamic_index_in_dim(weights, ring(away), 1, False)
        total = 0.0
        for hop in range(size):
            weight = lax.dynamic_index_in_dim(to, ring(-hop), 0, False)
            total = total + weight[:, None] * parts[hop].astype(F32)
        results.append(total)
    back = [results[0]] + [
        shift(results[hop].astype(BF16), "z", hop).astype(F32) for hop in range(1, size)
    ]
    whole = jnp.zeros(states.shape, F32)
    for hop in range(size):
        whole = lax.dynamic_update_slice_in_dim(whole, back[hop], ring(-hop) * width, 1)
    return whole, weights


def local(
    tokens,
    segments,
    out_grad,
    norm_gain,
    in_weight,
    conv_weight,
    conv_bias,
    dt_bias,
    a_log,
    skip,
    out_gain,
    out_weight,
):
    _, length, features = tokens.shape
    edge = CONV - 1
    layer_count, in_rows = in_weight.shape[:2]
    out_rows = out_weight.shape[1]
    layers = range(layer_count)
    q = member()
    owner = q.reshape(1)
    span = 2 * length
    row_count = 2 * span

    near = lax.axis_size("z") <= NEAR
    x_place = lax.axis_index("x").reshape(1)
    cuts = cut_weights(owner, in_weight)
    size = lax.axis_size("z")
    place = jnp.stack((lax.axis_index("z"), lax.axis_index("x")))
    exchanged = [around_team(parts) for parts in cuts]
    moved = [lax.ppermute(out_weight[k], ("x", "y"), TURN) for k in layers]
    nowhere = jnp.zeros((1,), jnp.int32)

    def fetch_rows(rows):
        return lax.all_gather(rows, ("z", "x"), axis=0, tiled=True)

    def fetch_columns(layer_id, after):
        gathered = lax.all_gather(all_piece(owner, exchanged[layer_id], after), ("x", "z"))
        return arrange(nowhere, gathered.reshape((2, size) + gathered.shape[1:]))

    if near:
        wide_line, wide_all = fetch(wide_piece(owner, exchanged[0]))

    seg_now = team_gather(segments.astype(F32).reshape(length))
    prev_seg = step_line(seg_now[:, span - edge :], "z", 1)
    seg_ext = jnp.concatenate((prev_seg, seg_now), axis=1)
    seg = seg_table(seg_now, seg_ext[:, edge - 1])
    mask = mask_table(seg_ext, edge)
    spread = spread_matrix()
    all_taps, all_par, all_rows = cut_params(
        owner, (conv_weight, conv_bias, dt_bias, a_log, skip, out_gain, spread), exchanged[0][1:]
    )

    stream = tokens.astype(F32).reshape(length, features)
    saved, full = [], []
    for layer_id in layers:
        taps, par, rows = all_taps[layer_id], all_par[layer_id], all_rows[layer_id]
        first, final = layer_id == 0, layer_id == layer_count - 1
        fast = near and first
        x_order = x_place if fast else nowhere
        normed = norm_rows(
            x_order,
            tokens.reshape(length, features) if first else stream,
            norm_gain[layer_id : layer_id + 1],
            wide_all[1:] if fast else [],
        )
        normed = team_gather(normed)
        earlier = step_line(normed[:, span - 16 :], "z", 1).reshape(32, features)
        normed = normed.reshape(row_count, features)
        if first:
            last_grad = team_gather(out_grad.reshape(length, features))
        dot = partial(jnp.dot, preferred_element_type=F32)
        if fast:
            piece = gate_piece(
                owner, exchanged[0], moved[0], wide_all[1:] + [seg, mask, all_taps]
            )
            gathered = lax.all_gather(piece, ("x", "z")).reshape((2, size) + piece.shape)
            full_gate, full_out = arrange_both(x_place, gathered)
            full_wide = whole_columns(place, wide_all)
        elif first:
            full_wide, full_gate = fetch_columns(0, [])
        else:
            full_wide, full_gate = next_columns
        wide = dot(normed, full_wide).reshape(2, span, WIDE)
        if not fast:
            full_out = fetch_rows(moved[0]) if first else next_rows
        gate_raw = dot(normed, full_gate).reshape(2, span, INNER_Q)
        full.append((full_wide, full_gate, full_out))
        halo = dot(earlier, full_wide).reshape(2, 16, WIDE)[:, 8:].astype(BF16).astype(F32)
        bc_own = conv_forward(
            wide, halo, taps, mask, 128, TILE, [v for e in exchanged[1:] for v in e[1:]] if first else []
        )[..., :BC_Q]
        bc_same = y_swap(bc_own)
        bc = jnp.concatenate(
            in_order((bc_own, core_swap(bc_own)[::-1], bc_same, core_swap(bc_same)[::-1])), axis=-1
        )
        heads_x = conv_forward(wide, halo, taps, mask, INNER_Q, 0)
        scan_in = (heads_x, bc, wide, seg, par, spread)
        before, reach, end, total_reach, bits = scan_states(
            *scan_in
        )
        start, weights = mix_states(end, bits)
        inside = scan_inside(*scan_in, after=[] if first else [full_out])
        if not final:
            next_columns = fetch_columns(layer_id + 1, [start, inside])
            next_rows = fetch_rows(tie(moved[layer_id + 1], start))
        scan_y, gated, square = scan_outer(
            inside, *scan_in, before, reach, start, gate_raw, rows,
            [last_grad] if first else [],
        )
        scale = lax.rsqrt(team_sum(square) / INNER + EPS)
        normed_y = scale_rows(gated, scale, rows)
        normed_y = normed_y.reshape(row_count, INNER_Q)
        sequence = lambda v, k: lax.slice_in_dim(v, k * span, (k + 1) * span, axis=0)
        branch_far = dot(sequence(normed_y, 1), full_out)
        branch = dot(sequence(normed_y, 0), full_out)
        saved.append(
            (
                stream,
                normed,
                gate_raw,
                halo,
                scan_in,
                (before, reach, start),
                (end, total_reach),
                weights,
                scan_y,
                gated,
                scale,
                normed_y,
                taps,
                rows,
            )
        )
        stream = stream + team_scatter(branch, branch_far)
    grad_stream = out_grad.astype(F32).reshape(length, features)
    in_parts = [None] * layer_count
    out_shards = [None] * layer_count
    small = [None] * layer_count
    for layer_id in reversed(layers):
        (
            stream_in,
            normed,
            gate_raw,
            halo,
            scan_in,
            states_before,
            states_end,
            weights,
            scan_y,
            gated,
            scale,
            normed_y,
            taps,
            rows,
        ) = saved[layer_id]
        heads_x, scan_rest = scan_in[0], scan_in[1:]
        wide = scan_in[2]
        full_wide, full_gate, full_out = full[layer_id]
        last = layer_id == 0
        grad_branch = team_gather(grad_stream.astype(BF16)) if last_grad is None else last_grad
        last_grad = None
        grad_branch = grad_branch.reshape(row_count, features)
        out_full_grad = jnp.einsum("ri,rd->id", normed_y, grad_branch, preferred_element_type=F32)
        back = partial(jnp.einsum, "rp,dp->rd", preferred_element_type=F32)
        grad_normed_y = back(grad_branch, full_out).reshape(2, span, INNER_Q)
        along, grad_gain = gate_along(grad_normed_y, gated, rows, scale)
        along = team_sum(along)
        grad_ssd, grad_gate, after, beyond, grad_start = gate_back(
            grad_normed_y, gated, scan_y, heads_x, gate_raw, *scan_rest, rows, scale, along,
            [out_full_grad],
        )
        turn = partial(jnp.einsum, "rd,rp->dp", preferred_element_type=F32)
        grad_gate = grad_gate.reshape(row_count, INNER_Q)
        gate_grad = turn(normed, grad_gate)
        fast = near and last
        x_order = x_place if fast else nowhere
        both = both_by_owner(x_order, gate_grad, out_full_grad, size, in_rows)
        both_total = sum_to_owner(both)
        gate_total = both_total[:TEAM]
        out_total = both_total[TEAM:].reshape(2, 2, in_rows, INNER_Q).swapaxes(1, 2)
        out_total = out_total.reshape(out_rows, features)
        out_shards[layer_id] = lax.ppermute(out_total, ("x", "y"), TURN).astype(F32)
        grad_end, _ = mix_states(grad_start, None, weights.swapaxes(0, 1))
        grad_inside = scan_inside_back(*scan_in, grad_ssd, after=[both])
        grad_x, grad_bc, grad_raw, head_sums, skip_sums = scan_outer_back(
            *grad_inside,
            *scan_in,
            *states_before,
            after,
            beyond,
            grad_end,
            *states_end,
            grad_ssd,
            scan_y,
            rows,
        )
        blocks = [grad_bc[..., BC_Q * k : BC_Q * k + BC_Q].astype(BF16) for k in range(TEAM)]
        turned = lambda k: lax.select_n(q ^ k, *blocks)
        half = lambda k: turned(k).astype(F32) + core_swap(turned(k ^ 1)).astype(F32)[::-1]
        grad_bc_own = half(0) + y_swap(half(2).astype(BF16)).astype(F32)
        grad_tile = jnp.pad(grad_bc_own, ((0, 0), (0, 0), (0, 128 - BC_Q)))

        edge_in = jnp.concatenate(
            (halo[:, 8 - edge :], wide[:, :edge].astype(BF16).astype(F32)), axis=1
        )
        edge_conv = lambda v: conv_piece(seg_ext[:, : 2 * edge], v, taps[:CONV], taps[CONV])
        edge_grad = jnp.concatenate((grad_x[:, :edge], grad_tile[:, :edge]), axis=-1)
        edge_grad = jax.vjp(edge_conv, edge_in)[1](edge_grad)[0][:, :edge].astype(BF16)
        returned = step_line(edge_grad, "z", -1).astype(F32)
        returned = jnp.pad(returned, ((0, 0), (8 - edge, 0), (0, 0)))
        grad_conv_x, conv_sums = conv_backward(
            wide, halo, taps, mask, grad_x, returned, INNER_Q, 0
        )
        grad_conv_tile, tile_sums = conv_backward(
            wide, halo, taps, mask, grad_tile, returned, 128, TILE
        )
        grad_wide = jnp.concatenate(
            (grad_conv_x, grad_conv_tile[..., :BC_Q], grad_raw[..., BC_Q:].astype(BF16)), axis=-1
        ).reshape(row_count, WIDE)
        in_grad = turn(normed, grad_wide)
        total = sum_to_owner(by_owner(x_order, in_grad, size, in_rows))
        in_parts[layer_id] = around_team(grad_parts(owner, gate_total, total))
        full_wide, full_gate, _ = full[layer_id]
        sequence = lambda v, k: lax.slice_in_dim(v, k * span, (k + 1) * span, axis=0)
        both_back = lambda k: back(sequence(grad_wide, k), full_wide) + back(
            sequence(grad_gate, k), full_gate
        )
        grad_far, grad_normed = both_back(1), both_back(0)
        norm_grad = jnp.sum(in_grad * full_wide.astype(F32), axis=1)
        norm_grad = norm_grad + jnp.sum(gate_grad * full_gate.astype(F32), axis=1)
        if fast:
            norm_grad = x_first(norm_grad)
        norm_grad = norm_grad / norm_gain[layer_id]
        grad_normed = team_scatter(grad_normed, grad_far)
        if fast:
            grad_normed = x_first(grad_normed)
        else:
            grad_normed = tie(grad_normed, both_total)
        _, pull_norm = jax.vjp(lambda v: norm_piece(v, norm_gain[layer_id]), stream_in)
        (grad_inner,) = pull_norm(grad_normed)
        grad_stream = grad_stream + grad_inner
        small[layer_id] = pack_small(
            conv_sums, tile_sums, head_sums, skip_sums, grad_gain, norm_grad.reshape(1, features),
            spread,
        )
    mixed = stream.reshape(1, length, features).astype(BF16)
    pack = xor_sum(xor_sum(jnp.stack(small), "x"), "z")
    across = y_swap(pack)
    packs = (pack, core_swap(pack), across, core_swap(across))
    norm_sum, taps_sum, bias_sum, dt_sum, decay_sum, skip_sum, gain_sum = open_small(
        owner, packs, features
    )
    return (
        mixed,
        grad_stream.reshape(1, length, features),
        norm_sum,
        join_weights(owner, in_parts),
        taps_sum,
        bias_sum,
        dt_sum,
        decay_sum,
        skip_sum,
        gain_sum,
        jnp.stack(out_shards),
    )


def solution(mesh):
    rows, spans = mesh.devices.shape
    split = Mesh(mesh.devices.reshape(rows // 2, 2, spans // 2, 2), ("x", "core", "z", "y"))
    tokens = P(("x", "core"), ("z", "y"), None)
    weight = P(None, ("x", "core", "z", "y"), None)
    return jax.shard_map(
        local,
        mesh=split,
        in_specs=(
            tokens,
            P(("x", "core"), ("z", "y")),
            tokens,
            P(),
            weight,
            P(),
            P(),
            P(),
            P(),
            P(),
            P(),
            weight,
        ),
        out_specs=(tokens, tokens, P(), weight, P(), P(), P(), P(), P(), P(), weight),
        check_vma=False,
    )
```

```python
from functools import partial

import jax
import jax.numpy as jnp
from jax import lax
from jax.experimental import pallas as pl
from jax.experimental.pallas import tpu as pltpu
from jax.sharding import Mesh
from jax.sharding import PartitionSpec as P

HEADS = 48
HEADDIM = 64
STATE = 128
CONV = 4
INNER = 3072
CONVDIM = 3328

TEAM = 4
HEADS_Q = HEADS // TEAM
INNER_Q = INNER // TEAM
BC_Q = 2 * STATE // TEAM
CONV_Q = INNER_Q + BC_Q
WIDE = 896

EPS = 1e-05
VMEM_BYTES = 32 * 1024 * 1024
STEP_BYTES = 14 * 1024 * 1024
NEAR = 4
SWAP = [(0, 1), (1, 0)]
BF16 = jnp.bfloat16
F32 = jnp.float32


def shift(block, axis, distance):
    size = lax.axis_size(axis)
    return lax.ppermute(block, axis, [(i, (i + distance) % size) for i in range(size)])


def step_line(block, axis, distance):
    devices = range(lax.axis_size(axis))
    return lax.ppermute(block, axis, [(i, i + distance) for i in devices if i + distance in devices])


def core_swap(block):
    return lax.ppermute(block, "core", SWAP)


def y_swap(block):
    return lax.ppermute(block, "y", SWAP)


def diagonal_swap(block):
    return lax.ppermute(block, ("core", "y"), [(0, 3), (1, 2), (2, 1), (3, 0)])


def xor_sum(values, axis):
    size = lax.axis_size(axis)
    bit = 1
    while bit < size:
        values = tie(values + lax.ppermute(values, axis, [(i, i ^ bit) for i in range(size)]))
        bit *= 2
    return values


def member():
    return lax.axis_index("y") * 2 + lax.axis_index("core")


def in_order(parts):
    q = member()
    return [lax.select_n(q ^ j, *parts) for j in range(TEAM)]


def around_team(blocks):
    return blocks[0], core_swap(blocks[1]), y_swap(blocks[2]), diagonal_swap(blocks[3])


def by_y(own, other):
    first = lax.axis_index("y") == 0
    return jnp.where(first, jnp.concatenate((own, other), 1), jnp.concatenate((other, own), 1))


def team_gather(block):
    pair = jnp.stack((block, core_swap(block)))
    crossed = y_swap(block)
    other = jnp.stack((crossed, core_swap(crossed)))
    return by_y(pair, other)


def team_scatter(own, other):
    total = own + core_swap(other.astype(BF16)).astype(F32)
    half = total.shape[0] // 2
    y = lax.axis_index("y")
    mine = lax.dynamic_slice_in_dim(total, y * half, half, 0)
    theirs = lax.dynamic_slice_in_dim(total, (1 - y) * half, half, 0)
    return mine + y_swap(theirs.astype(BF16)).astype(F32)


def team_sum(values):
    across = core_swap(values) + diagonal_swap(values)
    return (values + y_swap(values)) + across[::-1]


def x_swap(block):
    return lax.ppermute(block, "x", SWAP)


def line_pieces(piece):
    return [piece] + [shift(piece, "z", hop) for hop in range(1, lax.axis_size("z"))]


def fetch(piece):
    line = line_pieces(piece)
    return line, line + [x_swap(p) for p in line]


def sum_to_owner(blocks):
    flat = blocks.reshape((-1,) + blocks.shape[2:])
    return lax.psum_scatter(flat, ("x", "z"), scatter_dimension=0)


TURN = [(0, 0), (1, 2), (2, 1), (3, 3)]


def x_first(values):
    low, high = jnp.split(values, 2, axis=-1)
    first = lax.axis_index("x") == 0
    return jnp.where(first, jnp.concatenate((low, high), -1), jnp.concatenate((high, low), -1))


def rms_scale(values):
    return values * lax.rsqrt(jnp.mean(values * values, axis=-1, keepdims=True) + EPS)


def norm_piece(stream, norm_scale):
    return rms_scale(stream) * norm_scale


def conv_piece(seg_ext, extended, conv_taps, conv_shift):
    length = extended.shape[-2] - CONV + 1
    seg_here = seg_ext[..., CONV - 1 :]
    summed = conv_shift
    for offset in range(CONV):
        same_doc = (seg_ext[..., offset : offset + length] == seg_here)[..., None]
        summed = summed + conv_taps[offset] * extended[..., offset : offset + length, :] * same_doc
    return jax.nn.silu(summed)


CHUNK = 128
LANE = 64
NEVER = -1e30
TILE = INNER_Q // 128


def split_parts(values):
    high = values.astype(BF16)
    rest = values - high.astype(F32)
    middle = rest.astype(BF16)
    return high, middle, (rest - middle.astype(F32)).astype(BF16)


def mm(a, b, over=(1, 0)):
    return lax.dot_general(
        a, b, (((over[0],), (over[1],)), ((), ())), preferred_element_type=F32
    )


def exact_mm(values, ones, over=(1, 0)):
    high, middle, low = split_parts(values)
    return (mm(low, ones, over) + mm(middle, ones, over)) + mm(high, ones, over)


def spread_mm(values, ones, over=(1, 0)):
    high, low = halves(values)
    return mm(low, ones, over) + mm(high, ones, over)


def mm_exact(ones, values):
    high, middle, low = split_parts(values)
    return (mm(ones, low) + mm(ones, middle)) + mm(ones, high)


def halves(values):
    high = values.astype(BF16)
    return high, (values - high.astype(F32)).astype(BF16)


def mm_wide(narrow, values, over=(1, 0)):
    high, low = halves(values)
    return mm(narrow, low, over) + mm(narrow, high, over)


def softplus(values):
    tail = jnp.exp(-jnp.abs(values))
    series = tail * (1.0 - tail * (0.5 - tail * (1.0 / 3.0)))
    return jnp.maximum(values, 0.0) + jnp.where(tail < 0.01, series, jnp.log(1.0 + tail))


def sigmoid(values):
    return 1.0 / (1.0 + jnp.exp(-values))


def grids(shape):
    return lax.broadcasted_iota(jnp.int32, shape, 0), lax.broadcasted_iota(jnp.int32, shape, 1)


def column(row):
    return jnp.broadcast_to(row, (CHUNK, CHUNK)).T


def step_terms(raw_ref, par_ref):
    down, across = grids((CHUNK, CHUNK))
    lower = (down >= across).astype(F32).astype(BF16)
    step = softplus(raw_ref[0] + par_ref[0:1])
    sums = mm_exact(lower, -par_ref[1:2] * step)
    return step, sums, sums[CHUNK - 1 :]


def seg_terms(seg_ref):
    return column(seg_ref[0, 0, 0:1]), seg_ref[0, 0, 0:1], seg_ref[0, 0, 1:2], seg_ref[0, 0, 2:3]


def chunk_decay(total, before, last, spread):
    kept = jnp.exp(total) * (before == last).astype(F32)
    return exact_mm(jnp.broadcast_to(kept, (8, CHUNK)), spread)


def state_kernel(x, bc, raw, seg, par, spread, before_out, reach_out, end_out, total_out, bits_out, state, reach):
    @pl.when(pl.program_id(1) == 0)
    def _():
        state[...] = jnp.zeros_like(state)
        reach[...] = jnp.ones_like(reach)

    step, sums, total = step_terms(raw, par)
    lines, _, before, last = seg_terms(seg)
    before_out[0, 0] = state[...]
    reach_out[0, 0] = reach[...]
    leaving = jnp.where(lines == last, jnp.exp(total - sums), 0.0)
    fed = (x[0].astype(F32) * spread_mm(step, spread[...])).astype(BF16).astype(F32)
    fed = fed * spread_mm(leaving, spread[...])
    decay = chunk_decay(total, before, last, spread[...])
    state[...] = state[...] * decay[0:1] + mm_wide(bc[0, :, :STATE], fed, (0, 0))
    reach[...] = reach[...] * decay
    end_out[0] = state[...]
    total_out[0] = reach[...]
    lines = [v[0:1] for v in split_parts(reach[...])]
    bits_out[0] = jnp.concatenate(lines + [jnp.zeros((13, INNER_Q), BF16)], axis=0)


def inside_kernel(x, bc, raw, seg, par, spread, y_out):
    step, sums, _ = step_terms(raw, par)
    lines, row, _, _ = seg_terms(seg)
    down, across = grids((CHUNK, CHUNK))
    bias = jnp.where((lines == row) & (down >= across), 0.0, NEVER)
    scores = mm(bc[0, :, STATE:], bc[0, :, :STATE], (1, 1))
    turned = sums.T
    fed = (x[0].astype(F32) * spread_mm(step, spread[...])).astype(BF16)
    for pair in range(HEADS_Q // 2):
        lanes = slice(pair * 128, pair * 128 + 128)
        mixing = []
        for head in (LANE + 2 * pair, LANE + 2 * pair + 1):
            gap = jnp.broadcast_to(sums[:, head : head + 1], (CHUNK, CHUNK)) - turned[head : head + 1]
            mixing.append((scores * jnp.exp(gap + bias)).astype(BF16))
        both = mm(jnp.concatenate(mixing, axis=0), fed[:, lanes])
        y_out[0, :, lanes] = jnp.where(across < HEADDIM, both[:CHUNK], both[CHUNK:])


def outer_kernel(
    y_in, x, bc, raw, seg, par, spread, before, reach, start, gate, rows, y_out, gated_out, square_out
):
    _, sums, _ = step_terms(raw, par)
    lines, _, ahead, _ = seg_terms(seg)
    entering = spread_mm(jnp.where(lines == ahead, jnp.exp(sums), 0.0), spread[...])
    state = before[0, 0] + reach[0, 0, 0:1] * start[0]
    y = y_in[0] + entering * mm_wide(bc[0, :, STATE:], state)
    y_out[0] = y
    raw_gate = gate[0]
    gated = (y + rows[0:1] * x[0].astype(F32)) * (raw_gate * sigmoid(raw_gate))
    gated_out[0] = gated
    square = gated * gated
    folded = square[:, :128]
    for tile in range(1, INNER_Q // 128):
        folded = folded + square[:, tile * 128 : tile * 128 + 128]
    square_out[0, 0] = jnp.sum(folded.T, axis=0, keepdims=True)


def along_kernel(grad, gated, rows, scale, along_out, gain_out):
    @pl.when(pl.program_id(1) == 0)
    def _():
        gain_out[...] = jnp.zeros_like(gain_out)

    product = grad[0] * gated[0]
    weighed = product * rows[1:2]
    folded = weighed[:, :128]
    for tile in range(1, INNER_Q // 128):
        folded = folded + weighed[:, tile * 128 : tile * 128 + 128]
    along_out[0, 0] = jnp.sum(folded.T, axis=0, keepdims=True)
    lines = jnp.concatenate([column(scale[0, 0])] * (INNER_Q // 128), axis=1)
    gain_out[0] += jnp.sum((product * lines).reshape(CHUNK // 8, 8, INNER_Q), axis=0)


def gate_back_kernel(
    grad, gated, y, x, gate, bc, raw, seg, par, spread, rows, scale, along,
    grad_out, gate_out, after_out, beyond_out, start_out, state, reach,
):
    @pl.when(pl.program_id(1) == 0)
    def _():
        state[...] = jnp.zeros_like(state)
        reach[...] = jnp.ones_like(reach)

    wide = lambda row: jnp.concatenate([column(row)] * (INNER_Q // 128), axis=1)
    factor = scale[0, 0]
    pull = factor * factor * factor * along[0, 0] * (1.0 / INNER)
    grad_gated = grad[0] * rows[1:2] * wide(factor) - gated[0] * wide(pull)
    raw_gate = gate[0]
    sig = sigmoid(raw_gate)
    grad_y = (grad_gated * (raw_gate * sig)).astype(BF16)
    ssd_y = y[0] + rows[0:1] * x[0].astype(F32)
    gate_out[0] = (grad_gated * ssd_y * (sig * (1.0 + raw_gate * (1.0 - sig)))).astype(BF16)
    grad_out[0] = grad_y

    _, sums, total = step_terms(raw, par)
    lines, _, before, last = seg_terms(seg)
    after_out[0, 0] = state[...]
    beyond_out[0, 0] = reach[...]
    entering = spread_mm(jnp.where(lines == before, jnp.exp(sums), 0.0), spread[...])
    decay = chunk_decay(total, before, last, spread[...])
    fed = grad_y.astype(F32) * entering
    state[...] = state[...] * decay[0:1] + mm_wide(bc[0, :, STATE:], fed, (0, 0))
    reach[...] = reach[...] * decay
    start_out[0] = state[...]


def inside_back_kernel(x, bc, raw, seg, par, spread, grad, fed_out, b_out, c_out):
    step, sums, _ = step_terms(raw, par)
    lines, row, _, _ = seg_terms(seg)
    down, across = grids((CHUNK, CHUNK))
    bias = jnp.where((lines == row) & (across >= down), 0.0, NEVER)
    b_in, c_in = bc[0, :, :STATE], bc[0, :, STATE:]
    scores = mm(b_in, c_in, (1, 1))
    turned = sums.T
    fed = (x[0].astype(F32) * spread_mm(step, spread[...])).astype(BF16)
    grad_scores = jnp.zeros((CHUNK, CHUNK), F32)
    for pair in range(HEADS_Q // 2):
        lanes = slice(pair * 128, pair * 128 + 128)
        fed_pair, grad_pair = fed[:, lanes], grad[0, :, lanes]
        none = jnp.zeros_like(fed_pair)
        apart = jnp.concatenate(
            (jnp.where(across < HEADDIM, fed_pair, none), jnp.where(across < HEADDIM, none, fed_pair)),
            axis=0,
        )
        grad_mixing = mm(apart, grad_pair, (1, 1))
        mixing = []
        for which in range(2):
            head = LANE + 2 * pair + which
            gap = turned[head : head + 1] - jnp.broadcast_to(sums[:, head : head + 1], (CHUNK, CHUNK))
            decays = jnp.exp(gap + bias)
            mixing.append((scores * decays).astype(BF16))
            grad_scores = grad_scores + grad_mixing[which * CHUNK : which * CHUNK + CHUNK] * decays
        both = mm(jnp.concatenate(mixing, axis=0), grad_pair)
        fed_out[0, :, lanes] = jnp.where(across < HEADDIM, both[:CHUNK], both[CHUNK:])
    grad_scores = grad_scores.astype(BF16)
    b_out[0] = mm(grad_scores, c_in)
    c_out[0] = mm(grad_scores, b_in, (0, 0))


def outer_back_kernel(
    fed_in, b_in, c_in, x, bc, raw, seg, par, spread, before, reach, start, after, beyond, grad_end,
    end, total_reach, grad, y, rows,
    x_out, bc_out, raw_out, sums_out, skip_out, carry,
):
    @pl.when(pl.program_id(1) == 0)
    def _():
        sums_out[...] = jnp.zeros_like(sums_out)
        skip_out[...] = jnp.zeros_like(skip_out)
        last_state = end[0] + total_reach[0, 0:1] * start[0]
        meet = jnp.sum((grad_end[0] * last_state).reshape(STATE // 8, 8, INNER_Q), axis=0)
        meet = jnp.sum(spread_mm(meet, spread[...], (1, 1)), axis=0, keepdims=True)
        carry[...] = jnp.broadcast_to(meet, carry.shape)

    step, sums, total = step_terms(raw, par)
    lines, _, ahead, last = seg_terms(seg)
    ones = spread[...]
    state = (before[0, 0] + reach[0, 0, 0:1] * start[0]).astype(BF16)
    grad_state = after[0, 0] + beyond[0, 0, 0:1] * grad_end[0]
    values = x[0].astype(F32)
    grad_y = grad[0].astype(F32)
    wide_step = spread_mm(step, ones)
    leaving = spread_mm(jnp.where(lines == last, jnp.exp(total - sums), 0.0), ones)
    entering = spread_mm(jnp.where(lines == ahead, jnp.exp(sums), 0.0), ones)
    fed = (values * wide_step).astype(BF16).astype(F32)
    grad_fed = fed_in[0] + leaving * mm_wide(bc[0, :, :STATE], grad_state)
    x_out[0] = wide_step * grad_fed + rows[0:1] * grad_y
    bc_out[0, :, :STATE] = b_in[0] + mm((leaving * fed).astype(BF16), grad_state.astype(BF16), (1, 1))
    bc_out[0, :, STATE:] = c_in[0] + mm((entering * grad_y).astype(BF16), state, (1, 1))
    skip_out[0] += jnp.sum((grad_y * values).reshape(CHUNK // 8, 8, INNER_Q), axis=0)

    by_step = spread_mm(values * grad_fed, ones, (1, 1))
    flow = spread_mm(grad_y * y[0] - fed * grad_fed, ones, (1, 1))
    down, across = grids((CHUNK, CHUNK))
    upper = (across >= down).astype(F32).astype(BF16)
    grad_log = mm_exact(upper, flow) + carry[0:1]
    carry[...] = jnp.broadcast_to(grad_log[0:1], carry.shape)
    rate = par[1:2]
    grad_raw = (by_step - rate * grad_log) * sigmoid(raw[0] + par[0:1])
    raw_out[0] = grad_raw
    fold = lambda v: jnp.sum(v.reshape(CHUNK // 8, 8, CHUNK), axis=0)
    sums_out[0, 0:8] += fold(-rate * step * grad_log)
    sums_out[0, 8:16] += fold(grad_raw)


def chunk_spec(width, back=0, column_block=0):
    turn = (lambda c: back - 1 - c) if back else (lambda c: c)
    return pl.BlockSpec((1, CHUNK, width), lambda s, c: (s, turn(c), column_block))


def per_chunk(lines, width, back=0):
    turn = (lambda c: back - 1 - c) if back else (lambda c: c)
    return pl.BlockSpec((1, 1, lines, width), lambda s, c: (s, turn(c), 0, 0))


def per_sequence(lines, width):
    return pl.BlockSpec((1, lines, width), lambda s, c: (s, 0, 0))


def fixed(lines, width):
    return pl.BlockSpec((lines, width), lambda s, c: (0, 0))


def shaped(shape, dtype=F32):
    return jax.ShapeDtypeStruct(shape, dtype)


def call(kernel, name, chunks, ins, outs, operands, scratch=(), flops=0, after=()):
    in_specs = [spec for spec, _ in zip(ins, operands, strict=True)]
    moved = sum(v.size * v.dtype.itemsize for v in operands)
    moved += sum(v.size * v.dtype.itemsize for _, v in outs)
    count, skipped = len(in_specs), len(after)
    in_specs = in_specs + [pl.BlockSpec(memory_space=pl.ANY)] * skipped
    operands = tuple(operands) + tuple(after)
    return pl.pallas_call(
        lambda *refs: kernel(*refs[:count], *refs[count + skipped :]),
        name=name,
        grid=(2, chunks),
        in_specs=in_specs,
        out_specs=[spec for spec, _ in outs],
        out_shape=[shape for _, shape in outs],
        scratch_shapes=list(scratch),
        cost_estimate=pl.CostEstimate(flops=flops, bytes_accessed=moved, transcendentals=0),
        compiler_params=pltpu.CompilerParams(
            dimension_semantics=("arbitrary", "arbitrary"), vmem_limit_bytes=STEP_BYTES
        ),
    )(*operands)


STATE_SCRATCH = (pltpu.VMEM((STATE, INNER_Q), F32), pltpu.VMEM((8, INNER_Q), F32))


def scan_states(x, bc, raw, seg, par, spread, after=()):
    span = x.shape[1]
    n = span // CHUNK
    return call(
        state_kernel, "chunk_states", n,
        [chunk_spec(INNER_Q), chunk_spec(2 * STATE), chunk_spec(128, 0, TILE), per_chunk(8, 128), fixed(8, 128),
         fixed(128, INNER_Q)],
        [(per_chunk(STATE, INNER_Q), shaped((2, n, STATE, INNER_Q))), (per_chunk(8, INNER_Q), shaped((2, n, 8, INNER_Q))),
         (per_sequence(STATE, INNER_Q), shaped((2, STATE, INNER_Q))), (per_sequence(8, INNER_Q), shaped((2, 8, INNER_Q))),
         (per_sequence(16, INNER_Q), shaped((2, 16, INNER_Q), BF16))],
        (x, bc, raw, seg, par, spread), STATE_SCRATCH, 2 * 2 * span * STATE * INNER_Q, after=after,
    )


def scan_inside(x, bc, raw, seg, par, spread, after=()):
    span = x.shape[1]
    n = span // CHUNK
    return call(
        inside_kernel, "inside_chunks", n,
        [chunk_spec(INNER_Q), chunk_spec(2 * STATE), chunk_spec(128, 0, TILE), per_chunk(8, 128), fixed(8, 128),
         fixed(128, INNER_Q)],
        [(chunk_spec(INNER_Q), shaped(x.shape))],
        (x, bc, raw, seg, par, spread), (), 8 * 2 * span * CHUNK * INNER_Q, after=after,
    )[0]


def scan_outer(y, x, bc, raw, seg, par, spread, before, reach, start, gate, rows, after=()):
    span = x.shape[1]
    n = span // CHUNK
    return call(
        outer_kernel, "scan_and_gate", n,
        [chunk_spec(INNER_Q), chunk_spec(INNER_Q), chunk_spec(2 * STATE), chunk_spec(128, 0, TILE), per_chunk(8, 128), fixed(8, 128),
         fixed(128, INNER_Q), per_chunk(STATE, INNER_Q), per_chunk(8, INNER_Q), per_sequence(STATE, INNER_Q),
         chunk_spec(INNER_Q), fixed(8, INNER_Q)],
        [(chunk_spec(INNER_Q), shaped(x.shape)), (chunk_spec(INNER_Q), shaped(x.shape)),
         (per_chunk(1, 128), shaped((2, n, 1, 128)))],
        (y, x, bc, raw, seg, par, spread, before, reach, start, gate, rows), (), 8 * span * STATE * INNER_Q, after=after,
    )


def gate_along(grad, gated, rows, scale, after=()):
    span = gated.shape[1]
    n = span // CHUNK
    return call(
        along_kernel, "gate_along", n,
        [chunk_spec(INNER_Q), chunk_spec(INNER_Q), fixed(8, INNER_Q), per_chunk(1, 128)],
        [(per_chunk(1, 128), shaped((2, n, 1, 128))), (per_sequence(8, INNER_Q), shaped((2, 8, INNER_Q)))],
        (grad, gated, rows, scale), (), 10 * span * INNER_Q, after=after,
    )


def gate_back(grad, gated, y, x, gate, bc, raw, seg, par, spread, rows, scale, along, after=()):
    span = x.shape[1]
    n = span // CHUNK
    return call(
        gate_back_kernel, "gate_back_and_states", n,
        [chunk_spec(INNER_Q, n)] * 5 + [chunk_spec(2 * STATE, n), chunk_spec(128, n, TILE), per_chunk(8, 128, n), fixed(8, 128),
         fixed(128, INNER_Q), fixed(8, INNER_Q), per_chunk(1, 128, n), per_chunk(1, 128, n)],
        [(chunk_spec(INNER_Q, n), shaped(x.shape, BF16)), (chunk_spec(INNER_Q, n), shaped(x.shape, BF16)),
         (per_chunk(STATE, INNER_Q, n), shaped((2, n, STATE, INNER_Q))), (per_chunk(8, INNER_Q, n), shaped((2, n, 8, INNER_Q))),
         (per_sequence(STATE, INNER_Q), shaped((2, STATE, INNER_Q)))],
        (grad, gated, y, x, gate, bc, raw, seg, par, spread, rows, scale, along), STATE_SCRATCH,
        8 * span * STATE * INNER_Q, after=after,
    )


def scan_inside_back(x, bc, raw, seg, par, spread, grad, after=()):
    span = x.shape[1]
    n = span // CHUNK
    return call(
        inside_back_kernel, "inside_chunks_back", n,
        [chunk_spec(INNER_Q), chunk_spec(2 * STATE), chunk_spec(128, 0, TILE), per_chunk(8, 128), fixed(8, 128),
         fixed(128, INNER_Q), chunk_spec(INNER_Q)],
        [(chunk_spec(INNER_Q), shaped(x.shape)), (chunk_spec(STATE), shaped((2, span, STATE))),
         (chunk_spec(STATE), shaped((2, span, STATE)))],
        (x, bc, raw, seg, par, spread, grad), (), 24 * 2 * span * CHUNK * INNER_Q, after=after,
    )


def scan_outer_back(
    fed, b, c, x, bc, raw, seg, par, spread, before, reach, start, later, beyond, grad_end, end, total, grad, y, rows, after=()
):
    span = x.shape[1]
    n = span // CHUNK
    return call(
        outer_back_kernel, "scan_back", n,
        [chunk_spec(INNER_Q, n), chunk_spec(STATE, n), chunk_spec(STATE, n), chunk_spec(INNER_Q, n), chunk_spec(2 * STATE, n),
         chunk_spec(128, n, TILE), per_chunk(8, 128, n), fixed(8, 128), fixed(128, INNER_Q), per_chunk(STATE, INNER_Q, n),
         per_chunk(8, INNER_Q, n), per_sequence(STATE, INNER_Q), per_chunk(STATE, INNER_Q, n), per_chunk(8, INNER_Q, n),
         per_sequence(STATE, INNER_Q), per_sequence(STATE, INNER_Q), per_sequence(8, INNER_Q), chunk_spec(INNER_Q, n),
         chunk_spec(INNER_Q, n), fixed(8, INNER_Q)],
        [(chunk_spec(INNER_Q, n), shaped(x.shape)), (chunk_spec(2 * STATE, n), shaped((2, span, 2 * STATE))),
         (chunk_spec(128, n), shaped((2, span, 128))), (per_sequence(16, 128), shaped((2, 16, 128))),
         (per_sequence(8, INNER_Q), shaped((2, 8, INNER_Q)))],
        (fed, b, c, x, bc, raw, seg, par, spread, before, reach, start, later, beyond, grad_end, end, total, grad, y, rows),
        (pltpu.VMEM((8, 128), F32),), 24 * span * STATE * INNER_Q, after=after,
    )


def seg_table(seg_now, seg_before):
    span = seg_now.shape[1]
    rows = seg_now.reshape(2, span // CHUNK, 1, CHUNK)
    last = rows[..., -1:]
    before = jnp.concatenate((seg_before.reshape(2, 1, 1, 1), last[:, :-1]), axis=1)
    spread = lambda v: jnp.broadcast_to(v, rows.shape)
    return jnp.concatenate((rows, spread(before), spread(last)) + (rows,) * 5, axis=2)


def conv_terms(wide_ref, halo_ref, taps_ref, mask_ref, tail):
    own = wide_ref[0].astype(BF16).astype(F32)
    longer = jnp.concatenate((tail, own), axis=0)
    rows = [own]
    total = taps_ref[CONV : CONV + 1] + taps_ref[CONV - 1 : CONV] * own
    for back in range(1, CONV):
        same = jnp.concatenate([column(mask_ref[0, 0, back : back + 1])] * (own.shape[1] // 128), axis=1)
        earlier = longer[8 - back : 8 - back + CHUNK] * same
        rows.append(earlier)
        total = total + taps_ref[CONV - 1 - back : CONV - back] * earlier
    return own, rows, total


def conv_kernel(wide, halo, taps, mask, out, tail):
    @pl.when(pl.program_id(1) == 0)
    def _():
        tail[...] = halo[0].astype(F32)

    own, _, total = conv_terms(wide, halo, taps, mask, tail[...])
    tail[...] = own[CHUNK - 8 :]
    out[0] = (total * sigmoid(total)).astype(BF16)


def conv_back_kernel(wide, before, halo, taps, mask, grad, returned, out, sums_out, ahead):
    chunk = pl.num_programs(1) - 1 - pl.program_id(1)

    @pl.when(pl.program_id(1) == 0)
    def _():
        sums_out[...] = jnp.zeros_like(sums_out)
        ahead[...] = jnp.zeros_like(ahead)

    tail = jnp.where(chunk == 0, halo[0].astype(F32), before[0].astype(BF16).astype(F32))
    _, rows, total = conv_terms(wide, halo, taps, mask, tail)
    sig = sigmoid(total)
    pull = grad[0] * (sig * (1.0 + total * (1.0 - sig)))
    result = taps[CONV - 1 : CONV] * pull
    fold = lambda v: jnp.sum(v.reshape(CHUNK // 8, 8, v.shape[1]), axis=0)
    for back in range(1, CONV):
        same = jnp.concatenate([column(mask[0, 0, back : back + 1])] * (pull.shape[1] // 128), axis=1)
        masked = pull * same
        longer = jnp.concatenate((masked, ahead[8 * back - 8 : 8 * back]), axis=0)
        result = result + taps[CONV - 1 - back : CONV - back] * longer[back : back + CHUNK]
        ahead[8 * back - 8 : 8 * back] = masked[:8]
    for back in range(CONV):
        place = CONV - 1 - back
        sums_out[0, 8 * place : 8 * place + 8] += fold(pull * rows[back])
    sums_out[0, 8 * CONV : 8 * CONV + 8] += fold(pull)
    late = (pl.program_id(1) == 0).astype(F32) * returned[0].astype(F32)
    late = jnp.concatenate((jnp.zeros((CHUNK - 8, late.shape[1]), F32), late), axis=0)
    out[0] = (result + late).astype(BF16)


def conv_forward(wide, halo, taps, mask, width, at, after=()):
    n = wide.shape[1] // CHUNK
    lines = lambda rows: pl.BlockSpec((1, rows, width), lambda s, c: (s, 0, at))
    return call(
        conv_kernel, "conv", n,
        [chunk_spec(width, 0, at), lines(8), pl.BlockSpec((8, width), lambda s, c: (0, at)), per_chunk(8, 128)],
        [(chunk_spec(width), shaped(wide.shape[:2] + (width,), BF16))],
        (wide, halo, taps, mask), (pltpu.VMEM((8, width), F32),), 30 * wide.shape[1] * width, after=after,
    )[0]


def conv_backward(wide, halo, taps, mask, grad, returned, width, at, after=()):
    n = wide.shape[1] // CHUNK
    lines = lambda rows: pl.BlockSpec((1, rows, width), lambda s, c: (s, 0, at))
    steps = CHUNK // 8
    early = pl.BlockSpec(
        (1, 8, width), lambda s, c: (s, jnp.maximum((n - 1 - c) * steps - 1, 0), at)
    )
    return call(
        conv_back_kernel, "conv_back", n,
        [chunk_spec(width, n, at), early, lines(8), pl.BlockSpec((8, width), lambda s, c: (0, at)),
         per_chunk(8, 128, n), chunk_spec(width, n), lines(8)],
        [(chunk_spec(width, n), shaped(wide.shape[:2] + (width,), BF16)), (per_sequence(8 * CONV + 8, width), shaped((2, 8 * CONV + 8, width)))],
        (wide, wide, halo, taps, mask, grad, returned), (pltpu.VMEM((8 * CONV, width), F32),), 60 * wide.shape[1] * width, after=after,
    )


def mask_table(seg_ext, edge_rows):
    span = seg_ext.shape[1] - edge_rows
    here = seg_ext[:, edge_rows:]
    rows = [here == seg_ext[:, edge_rows - back : edge_rows - back + span] for back in range(CONV)]
    table = jnp.stack(rows + rows, axis=1).astype(F32)
    return jnp.moveaxis(table.reshape(2, 2 * CONV, span // CHUNK, CHUNK), 2, 1)


def tile_picks(owner, rows):
    down, across = grids((2 * STATE, 128))
    bc = (down - BC_Q * owner == across) & (across < BC_Q)
    down, across = grids((HEADS, 128))
    head = across - LANE
    dt = (down - HEADS_Q * owner == head) & (head >= 0) & (head < HEADS_Q)
    return bc.astype(F32), dt.astype(F32)


def cut_weights_kernel(q_ref, weight, *outs):
    for layer in range(weight.shape[0]):
        for k in range(TEAM):
            owner = q_ref[0] ^ k
            start = pl.multiple_of(owner * INNER_Q, 128)
            part = outs[layer * TEAM + k]
            part[:, :INNER_Q] = weight[layer, :, pl.ds(start, INNER_Q)]
            part[:, INNER_Q : 2 * INNER_Q] = weight[layer, :, pl.ds(INNER + start, INNER_Q)]
            bc, dt = tile_picks(owner, None)
            tile = mm(weight[layer, :, 2 * INNER : 2 * INNER + 2 * STATE], bc.astype(BF16))
            tile = tile + mm(weight[layer, :, INNER + CONVDIM :], dt.astype(BF16))
            part[:, 2 * INNER_Q :] = tile.astype(BF16)


def whole_spec(shape):
    return pl.BlockSpec(shape, lambda *_: (0,) * len(shape))


def whole_call(kernel, name, index, operands, outs, after=()):
    count, skipped = 1 + len(operands), len(after)
    return pl.pallas_call(
        lambda *refs: kernel(*refs[:count], *refs[count + skipped :]),
        name=name,
        grid_spec=pltpu.PrefetchScalarGridSpec(
            num_scalar_prefetch=1,
            grid=(1,),
            in_specs=[whole_spec(v.shape) for v in operands]
            + [pl.BlockSpec(memory_space=pl.ANY)] * skipped,
            out_specs=[whole_spec(s.shape) for s in outs],
        ),
        out_shape=list(outs),
        compiler_params=pltpu.CompilerParams(vmem_limit_bytes=VMEM_BYTES),
    )(index, *operands, *after)


def tie(value, *after):
    anywhere = pl.BlockSpec(memory_space=pl.ANY)
    return pl.pallas_call(
        lambda *refs: None,
        name="tie",
        in_specs=[anywhere] * (1 + len(after)),
        out_specs=anywhere,
        out_shape=shaped(value.shape, value.dtype),
        input_output_aliases={0: 0},
    )(value, *after)


def norm_kernel(x_ref, stream, gain, out):
    values = stream[...].astype(F32)
    mean = jnp.mean(values * values, axis=-1, keepdims=True)
    normed = (values * lax.rsqrt(mean + EPS) * gain[...]).astype(BF16)
    width = normed.shape[1] // 2
    x = x_ref[0]
    out[:, pl.ds(pl.multiple_of(x * width, 128), width)] = normed[:, :width]
    out[:, pl.ds(pl.multiple_of((1 - x) * width, 128), width)] = normed[:, width:]


def norm_rows(x, stream, gain, after=()):
    return whole_call(norm_kernel, "norm", x, (stream, gain), [shaped(stream.shape, BF16)], after)[0]


def scale_kernel(gated, scale, rows, out):
    lines = jnp.concatenate([column(scale[0, 0])] * (INNER_Q // 128), axis=1)
    out[0] = (gated[0] * lines * rows[1:2]).astype(BF16)


def scale_rows(gated, scale, rows, after=()):
    n = gated.shape[1] // CHUNK
    return call(
        scale_kernel, "scale_rows", n,
        [chunk_spec(INNER_Q), per_chunk(1, 128), fixed(8, INNER_Q)],
        [(chunk_spec(INNER_Q), shaped(gated.shape, BF16))],
        (gated, scale, rows), (), 4 * gated.size, after=after,
    )[0]


def cut_weights(q, weight):
    layers, rows = weight.shape[:2]
    outs = [shaped((rows, INNER_Q + WIDE), BF16)] * (TEAM * layers)
    outs = whole_call(cut_weights_kernel, "cut_weights", q, (weight,), outs)
    return [outs[TEAM * layer : TEAM * layer + TEAM] for layer in range(layers)]


def place_of(owner):
    return (owner % 2) * 2 + owner // 2


def wide_piece_kernel(q_ref, *refs):
    out = refs[-1]
    for k in range(TEAM):
        out[place_of(q_ref[0] ^ k)] = refs[k][:, INNER_Q:]


def gate_piece_kernel(q_ref, *refs):
    rows, out = refs[TEAM], refs[-1]
    for k in range(TEAM):
        out[place_of(q_ref[0] ^ k)] = refs[k][:, :INNER_Q]
    for block in range(TEAM):
        half = block % 2 * INNER_Q
        out[TEAM + block] = rows[block // 2, :, half : half + INNER_Q]


def all_piece_kernel(q_ref, *refs):
    out = refs[-1]
    for k in range(TEAM):
        out[place_of(q_ref[0] ^ k)] = refs[k][...]


def all_piece(q, parts, after=()):
    shape = (TEAM,) + parts[0].shape
    return whole_call(all_piece_kernel, "all_piece", q, parts, [shaped(shape, BF16)], after)[0]


def arrange_kernel(_, gathered, gate, wide):
    for x in range(2):
        for z in range(gate.shape[2]):
            for block in range(TEAM):
                rows = gathered[x, z, block]
                gate[x, block // 2, z, block % 2] = rows[:, :INNER_Q]
                wide[x, block // 2, z, block % 2] = rows[:, INNER_Q:]


def arrange(index, gathered):
    size, rows = gathered.shape[1], gathered.shape[3]
    outs = [shaped((2, 2, size, 2, rows, width), BF16) for width in (INNER_Q, WIDE)]
    gate, wide = whole_call(arrange_kernel, "arrange", index, (gathered,), outs)
    return wide.reshape(-1, WIDE), gate.reshape(-1, INNER_Q)


def by_owner_kernel(x_ref, grad, out):
    for side in range(2):
        x = x_ref[0] if side == 0 else 1 - x_ref[0]
        for z in range(out.shape[1]):
            for block in range(TEAM):
                out[x, z, block] = grad[side, block // 2, z, block % 2].astype(BF16)


def both_by_owner_kernel(x_ref, gate, out_grad, out):
    for side in range(2):
        x = x_ref[0] if side == 0 else 1 - x_ref[0]
        for z in range(out.shape[1]):
            for block in range(TEAM):
                upper, lower = block // 2, block % 2
                half = slice(lower * INNER_Q, lower * INNER_Q + INNER_Q)
                out[x, z, block] = gate[side, upper, z, lower].astype(BF16)
                out[side, z, TEAM + block] = out_grad[z, side, upper, :, half].astype(BF16)


def both_by_owner(x_first_of, gate, out_grad, size, rows):
    operands = (
        gate.reshape(2, 2, size, 2, rows, INNER_Q),
        out_grad.reshape(size, 2, 2, rows, 2 * INNER_Q),
    )
    outs = [shaped((2, size, 2 * TEAM, rows, INNER_Q), BF16)]
    return whole_call(both_by_owner_kernel, "both_by_owner", x_first_of, operands, outs)[0]


def by_owner(x_first_of, grad, size, rows):
    width = grad.shape[-1]
    operands = (grad.reshape(2, 2, size, 2, rows, width),)
    outs = [shaped((2, size, TEAM, rows, width), BF16)]
    return whole_call(by_owner_kernel, "by_owner", x_first_of, operands, outs)[0]


def wide_piece(q, parts, after=()):
    shape = (TEAM, parts[0].shape[0], WIDE)
    return whole_call(wide_piece_kernel, "wide_piece", q, parts, [shaped(shape, BF16)], after)[0]


def gate_piece(q, parts, rows, after=()):
    count = parts[0].shape[0]
    operands = tuple(parts) + (rows.reshape(2, count, -1),)
    outs = [shaped((2 * TEAM, count, INNER_Q), BF16)]
    return whole_call(gate_piece_kernel, "gate_piece", q, operands, outs, after)[0]


def arrange_both_kernel(x_ref, gathered, gate, out):
    for side in range(2):
        x = x_ref[0] if side == 0 else 1 - x_ref[0]
        for z in range(gate.shape[2]):
            for block in range(TEAM):
                upper, lower = block // 2, block % 2
                gate[side, upper, z, lower] = gathered[x, z, block]
                half = slice(lower * INNER_Q, lower * INNER_Q + INNER_Q)
                out[z, side, upper, :, half] = gathered[side, z, TEAM + block]


def arrange_both(x_first_of, gathered):
    size, rows = gathered.shape[1], gathered.shape[3]
    outs = [
        shaped((2, 2, size, 2, rows, INNER_Q), BF16),
        shaped((size, 2, 2, rows, 2 * INNER_Q), BF16),
    ]
    gate, out = whole_call(arrange_both_kernel, "arrange_both", x_first_of, (gathered,), outs)
    return gate.reshape(-1, INNER_Q), out.reshape(-1, 2 * INNER_Q)


def whole_wide_kernel(place, *refs):
    out = refs[-1]
    size = out.shape[2]
    for side in range(2):
        for hop in range(size):
            source = lax.rem(place[0] - hop + size, size)
            for block in range(TEAM):
                out[side, block // 2, source, block % 2] = refs[side * size + hop][block]


def whole_columns(place, pieces, after=()):
    size = len(pieces) // 2
    rows, width = pieces[0].shape[1:]
    outs = [shaped((2, 2, size, 2, rows, width), BF16)]
    whole = whole_call(whole_wide_kernel, "whole_columns", place, pieces, outs, after)[0]
    return whole.reshape(-1, width)


def grad_parts_kernel(q_ref, gate, wide, *outs):
    for k in range(TEAM):
        block = place_of(q_ref[0] ^ k)
        outs[k][:, :INNER_Q] = gate[block]
        outs[k][:, INNER_Q:] = wide[block]


def grad_parts(q, gate, wide):
    outs = [shaped((wide.shape[1], INNER_Q + WIDE), BF16)] * TEAM
    return whole_call(grad_parts_kernel, "grad_parts", q, (gate, wide), outs)


def cut_params_kernel(q_ref, conv_weight, conv_bias, dt_bias, a_log, skip, out_gain, spread, taps, par, rows):
    owner = q_ref[0]
    start = pl.multiple_of(owner * INNER_Q, 128)
    bc, dt = tile_picks(owner, None)
    bc, dt = bc.astype(BF16), dt.astype(BF16)
    mine = pl.ds(start, INNER_Q)
    for layer in range(conv_weight.shape[0]):
        one = slice(layer, layer + 1)
        taps[layer, :CONV, :INNER_Q] = conv_weight[layer, :, mine]
        taps[layer, :CONV, INNER_Q:] = exact_mm(conv_weight[layer, :, INNER:], bc)
        taps[layer, CONV : CONV + 1, :INNER_Q] = conv_bias[one, mine]
        taps[layer, CONV : CONV + 1, INNER_Q:] = exact_mm(conv_bias[one, INNER:], bc)
        taps[layer, CONV + 1 :] = jnp.zeros((7 - CONV, WIDE), F32)
        par[layer, 0:1] = exact_mm(dt_bias[one], dt)
        par[layer, 1:2] = exact_mm(jnp.exp(a_log[one]), dt)
        par[layer, 2:] = jnp.zeros((6, 128), F32)
        rows[layer, 0:1] = exact_mm(exact_mm(skip[one], dt), spread[...])
        rows[layer, 1:2] = out_gain[one, mine]
        rows[layer, 2:] = jnp.zeros((6, INNER_Q), F32)


def cut_params(q, params, after):
    layers = params[0].shape[0]
    shapes = [(layers, 8, WIDE), (layers, 8, 128), (layers, 8, INNER_Q)]
    return whole_call(cut_params_kernel, "cut_params", q, params, [shaped(s) for s in shapes], after)


def join_kernel(q_ref, *refs):
    out = refs[-1]
    for layer in range(out.shape[0]):
        shared = 0.0
        for k in range(TEAM):
            owner = q_ref[0] ^ k
            start = pl.multiple_of(owner * INNER_Q, 128)
            part = refs[layer * TEAM + k]
            out[layer, :, pl.ds(start, INNER_Q)] = part[:, :INNER_Q].astype(F32)
            out[layer, :, pl.ds(INNER + start, INNER_Q)] = part[:, INNER_Q : 2 * INNER_Q].astype(F32)
            bc, dt = tile_picks(owner, None)
            both = jnp.concatenate((bc, dt), axis=0).astype(BF16)
            shared = shared + mm(part[:, 2 * INNER_Q :], both, (1, 1))
        out[layer, :, 2 * INNER :] = shared


def join_weights(q, parts):
    flat = [v for layer in parts for v in layer]
    shape = (len(parts), flat[0].shape[0], 2 * INNER + 2 * STATE + HEADS)
    return whole_call(join_kernel, "join_weights", q, flat, [shaped(shape)])[0]


SMALL = (16, WIDE)


def pack_small_kernel(conv_x, conv_tile, heads, skip, gain, norm, spread, out):
    fold = lambda v, rows: jnp.sum(v[:, rows], axis=(0, 1), keepdims=True)[0]
    for line in range(CONV + 1):
        rows = slice(8 * line, 8 * line + 8)
        out[line : line + 1, :INNER_Q] = fold(conv_x[...], rows)
        out[line : line + 1, INNER_Q:] = fold(conv_tile[...], rows)
    line = CONV + 1
    out[line:] = jnp.zeros((SMALL[0] - line, WIDE), F32)
    every = slice(0, 8)
    out[line + 1 : line + 2, :INNER_Q] = fold(gain[...], every)
    out[line + 2 : line + 3, :128] = fold(heads[...], slice(8, 16))
    out[line + 3 : line + 4, :128] = fold(heads[...], every)
    by_head = exact_mm(skip[0] + skip[1], spread[...], (1, 1))
    out[line + 4 : line + 5, :128] = jnp.sum(by_head, axis=0, keepdims=True)
    width = norm.shape[1] // 2
    out[line + 5 : line + 6, :width] = norm[:, :width]
    out[line + 6 : line + 7, :width] = norm[:, width:]


def pack_small(*parts):
    return pl.pallas_call(pack_small_kernel, name="pack_small", out_shape=shaped(SMALL))(*parts)


def lanes_of(values):
    return lax.broadcasted_iota(jnp.int32, values.shape, 1)


def open_small_kernel(q_ref, *refs):
    norm, conv_weight, conv_bias, dt_bias, a_log, skip, gain = refs[-7:]
    layers = norm.shape[0]
    line = CONV + 1
    for layer in range(layers):
        one = slice(layer, layer + 1)
        packs = [ref[layer] for ref in refs[:TEAM]]
        shared, heads = [], 0.0
        for k in range(TEAM):
            owner = q_ref[0] ^ k
            start = pl.multiple_of(owner * INNER_Q, 128)
            mine = pl.ds(start, INNER_Q)
            pack = packs[k]
            conv_weight[layer, :, mine] = pack[:CONV, :INNER_Q]
            conv_bias[one, mine] = pack[CONV:line, :INNER_Q]
            tile = pack[:8, INNER_Q:]
            tile = jnp.where(lanes_of(tile) < BC_Q, tile, 0.0)
            tile = jnp.where(owner % 2 == 0, tile, pltpu.roll(tile, BC_Q, 1))
            shared.append([jnp.where(owner // 2 == side, tile, 0.0) for side in range(2)])
            rows = pack[line + 2 : line + 5, :128]
            in_head = (lanes_of(rows) >= LANE) & (lanes_of(rows) < LANE + HEADS_Q)
            rows = jnp.where(in_head, rows, 0.0)
            placed = 0.0
            for which in range(TEAM):
                turned = pltpu.roll(rows, (HEADS_Q * which - LANE) % 128, 1)
                placed = placed + jnp.where(owner == which, turned, 0.0)
            heads = heads + placed[:, :HEADS]
            gain[one, mine] = pack[line + 1 : line + 2, :INNER_Q]
        shared = jnp.concatenate([sum([s[side] for s in shared]) for side in range(2)], axis=1)
        conv_weight[layer, :, INNER:] = shared[:CONV]
        conv_bias[one, INNER:] = shared[CONV:line]
        dt_bias[one], a_log[one], skip[one] = heads[0:1], heads[1:2], heads[2:3]
        width = norm.shape[1] // 2
        halves_of = lambda n: packs[n][line + 5 : line + 7, :width]
        total = (halves_of(0) + halves_of(1)) + (halves_of(2) + halves_of(3))
        norm[one, :width] = total[0:1]
        norm[one, width:] = total[1:2]


def open_small(q, packs, features):
    layers = packs[0].shape[0]
    flat = list(packs)
    shapes = [
        (layers, features), (layers, CONV, CONVDIM), (layers, CONVDIM), (layers, HEADS), (layers, HEADS),
        (layers, HEADS), (layers, INNER),
    ]
    return pl.pallas_call(
        open_small_kernel,
        name="open_small",
        grid_spec=pltpu.PrefetchScalarGridSpec(
            num_scalar_prefetch=1,
            grid=(1,),
            in_specs=[whole_spec(v.shape) for v in flat],
            out_specs=[whole_spec(s) for s in shapes],
        ),
        out_shape=[shaped(s) for s in shapes],
    )(q, *flat)


def spread_matrix():
    head = jnp.arange(128)[:, None] - LANE
    return (jnp.arange(INNER_Q)[None, :] // HEADDIM == head).astype(BF16)


def gap_decays(spans):
    rows = []
    for start in range(len(spans)):
        row = []
        running = jnp.ones_like(spans[0])
        for stop, span in enumerate(spans):
            if stop <= start:
                row.append(jnp.zeros_like(running))
                continue
            row.append(running)
            running = running * span
        rows.append(jnp.stack(row))
    return jnp.stack(rows)


def mix_states(states, bits=None, weights=None):
    size = lax.axis_size("z")
    z = lax.axis_index("z")
    width = states.shape[1] // size
    decay = lambda rows: jnp.sum(rows[:, :3].astype(F32), axis=1)
    if size > NEAR:
        if weights is None:
            weights = gap_decays([decay(v) for v in lax.all_gather(bits, "z")])
        cuts = jnp.moveaxis(states.reshape(2, size, width, -1), 1, 0).astype(BF16)
        parts = lax.all_to_all(cuts, "z", 0, 0, tiled=True).astype(F32)
        sums = jnp.sum(weights[:, :, :, None] * parts[:, None], axis=0)
        back = lax.all_to_all(sums.astype(BF16), "z", 0, 0, tiled=True).astype(F32)
        return jnp.moveaxis(back, 0, 1).reshape(states.shape), weights
    ring = lambda k: lax.rem(z + k + size, size)

    def cut(k):
        part = lax.dynamic_slice_in_dim(states, k * width, width, 1).astype(BF16)
        return part if weights is not None else jnp.concatenate((part, bits), axis=1)

    parts = [cut(z)] + [shift(cut(ring(hop)), "z", hop) for hop in range(1, size)]
    if weights is None:
        everyone = jnp.stack([decay(p[:, width:]) for p in parts])
        spans = [
            lax.dynamic_index_in_dim(everyone, lax.rem(z - k + size, size), 0, False)
            for k in range(size)
        ]
        weights = gap_decays(spans)
        parts = [p[:, :width] for p in parts]
    results = []
    for away in range(size):
        to = lax.dynamic_index_in_dim(weights, ring(away), 1, False)
        total = 0.0
        for hop in range(size):
            weight = lax.dynamic_index_in_dim(to, ring(-hop), 0, False)
            total = total + weight[:, None] * parts[hop].astype(F32)
        results.append(total)
    back = [results[0]] + [
        shift(results[hop].astype(BF16), "z", hop).astype(F32) for hop in range(1, size)
    ]
    whole = jnp.zeros(states.shape, F32)
    for hop in range(size):
        whole = lax.dynamic_update_slice_in_dim(whole, back[hop], ring(-hop) * width, 1)
    return whole, weights


def local(
    tokens,
    segments,
    out_grad,
    norm_gain,
    in_weight,
    conv_weight,
    conv_bias,
    dt_bias,
    a_log,
    skip,
    out_gain,
    out_weight,
):
    _, length, features = tokens.shape
    edge = CONV - 1
    layer_count, in_rows = in_weight.shape[:2]
    out_rows = out_weight.shape[1]
    layers = range(layer_count)
    q = member()
    owner = q.reshape(1)
    span = 2 * length
    row_count = 2 * span

    near = lax.axis_size("z") <= NEAR
    x_place = lax.axis_index("x").reshape(1)
    cuts = cut_weights(owner, in_weight)
    size = lax.axis_size("z")
    place = jnp.stack((lax.axis_index("z"), lax.axis_index("x")))
    exchanged = [around_team(parts) for parts in cuts]
    moved = [lax.ppermute(out_weight[k], ("x", "y"), TURN) for k in layers]
    nowhere = jnp.zeros((1,), jnp.int32)

    def fetch_rows(rows):
        return lax.all_gather(rows, ("z", "x"), axis=0, tiled=True)

    def fetch_columns(layer_id, after):
        gathered = lax.all_gather(all_piece(owner, exchanged[layer_id], after), ("x", "z"))
        return arrange(nowhere, gathered.reshape((2, size) + gathered.shape[1:]))

    if near:
        wide_line, wide_all = fetch(wide_piece(owner, exchanged[0]))

    seg_now = team_gather(segments.astype(F32).reshape(length))
    prev_seg = step_line(seg_now[:, span - edge :], "z", 1)
    seg_ext = jnp.concatenate((prev_seg, seg_now), axis=1)
    seg = seg_table(seg_now, seg_ext[:, edge - 1])
    mask = mask_table(seg_ext, edge)
    spread = spread_matrix()
    all_taps, all_par, all_rows = cut_params(
        owner, (conv_weight, conv_bias, dt_bias, a_log, skip, out_gain, spread), exchanged[0][1:]
    )

    stream = tokens.astype(F32).reshape(length, features)
    saved, full = [], []
    for layer_id in layers:
        taps, par, rows = all_taps[layer_id], all_par[layer_id], all_rows[layer_id]
        first, final = layer_id == 0, layer_id == layer_count - 1
        fast = near and first
        x_order = x_place if fast else nowhere
        normed = norm_rows(
            x_order,
            tokens.reshape(length, features) if first else stream,
            norm_gain[layer_id : layer_id + 1],
            wide_line[1:2] if fast else [],
        )
        normed = team_gather(normed)
        earlier = step_line(normed[:, span - 16 :], "z", 1).reshape(32, features)
        normed = normed.reshape(row_count, features)
        if first:
            last_grad = team_gather(tie(out_grad.reshape(length, features), normed))
        dot = partial(jnp.dot, preferred_element_type=F32)
        if fast:
            piece = gate_piece(
                owner, exchanged[0], moved[0], wide_line[1:] + [normed, seg, mask, all_taps]
            )
            gathered = lax.all_gather(piece, ("x", "z")).reshape((2, size) + piece.shape)
            full_gate, full_out = arrange_both(x_place, gathered)
            full_wide = whole_columns(place, wide_all, [earlier])
        elif first:
            full_wide, full_gate = fetch_columns(0, [])
        else:
            full_wide, full_gate = next_columns
        wide = dot(normed, full_wide).reshape(2, span, WIDE)
        if not fast:
            full_out = fetch_rows(moved[0]) if first else next_rows
        gate_raw = dot(normed, full_gate).reshape(2, span, INNER_Q)
        full.append((full_wide, full_gate, full_out))
        halo = dot(earlier, full_wide).reshape(2, 16, WIDE)[:, 8:].astype(BF16).astype(F32)
        bc_own = conv_forward(
            wide, halo, taps, mask, 128, TILE, [v for e in exchanged[1:] for v in e[1:]] if first else []
        )[..., :BC_Q]
        bc_same = y_swap(bc_own)
        bc = jnp.concatenate(
            in_order((bc_own, core_swap(bc_own)[::-1], bc_same, core_swap(bc_same)[::-1])), axis=-1
        )
        heads_x = conv_forward(wide, halo, taps, mask, INNER_Q, 0)
        scan_in = (heads_x, bc, wide, seg, par, spread)
        before, reach, end, total_reach, bits = scan_states(
            *scan_in, after=[last_grad] if first else []
        )
        start, weights = mix_states(end, bits)
        inside = scan_inside(*scan_in, after=[] if first else [full_out])
        if not final:
            next_columns = fetch_columns(layer_id + 1, [start, inside])
            next_rows = fetch_rows(tie(moved[layer_id + 1], start))
        scan_y, gated, square = scan_outer(
            inside, *scan_in, before, reach, start, gate_raw, rows,
        )
        scale = lax.rsqrt(team_sum(square) / INNER + EPS)
        normed_y = scale_rows(gated, scale, rows)
        normed_y = normed_y.reshape(row_count, INNER_Q)
        sequence = lambda v, k: lax.slice_in_dim(v, k * span, (k + 1) * span, axis=0)
        branch_far = dot(sequence(normed_y, 1), full_out)
        branch = dot(sequence(normed_y, 0), full_out)
        saved.append(
            (
                stream,
                normed,
                gate_raw,
                halo,
                scan_in,
                (before, reach, start),
                (end, total_reach),
                weights,
                scan_y,
                gated,
                scale,
                normed_y,
                taps,
                rows,
            )
        )
        stream = stream + team_scatter(branch, branch_far)
    grad_stream = out_grad.astype(F32).reshape(length, features)
    in_parts = [None] * layer_count
    out_shards = [None] * layer_count
    small = [None] * layer_count
    for layer_id in reversed(layers):
        (
            stream_in,
            normed,
            gate_raw,
            halo,
            scan_in,
            states_before,
            states_end,
            weights,
            scan_y,
            gated,
            scale,
            normed_y,
            taps,
            rows,
        ) = saved[layer_id]
        heads_x, scan_rest = scan_in[0], scan_in[1:]
        wide = scan_in[2]
        full_wide, full_gate, full_out = full[layer_id]
        last = layer_id == 0
        grad_branch = team_gather(grad_stream.astype(BF16)) if last_grad is None else last_grad
        last_grad = None
        grad_branch = grad_branch.reshape(row_count, features)
        out_full_grad = jnp.einsum("ri,rd->id", normed_y, grad_branch, preferred_element_type=F32)
        back = partial(jnp.einsum, "rp,dp->rd", preferred_element_type=F32)
        grad_normed_y = back(grad_branch, full_out).reshape(2, span, INNER_Q)
        along, grad_gain = gate_along(grad_normed_y, gated, rows, scale)
        along = team_sum(along)
        grad_ssd, grad_gate, after, beyond, grad_start = gate_back(
            grad_normed_y, gated, scan_y, heads_x, gate_raw, *scan_rest, rows, scale, along,
            [out_full_grad],
        )
        turn = partial(jnp.einsum, "rd,rp->dp", preferred_element_type=F32)
        grad_gate = grad_gate.reshape(row_count, INNER_Q)
        gate_grad = turn(normed, grad_gate)
        fast = near and last
        x_order = x_place if fast else nowhere
        both = both_by_owner(x_order, gate_grad, out_full_grad, size, in_rows)
        both_total = sum_to_owner(both)
        gate_total = both_total[:TEAM]
        out_total = both_total[TEAM:].reshape(2, 2, in_rows, INNER_Q).swapaxes(1, 2)
        out_total = out_total.reshape(out_rows, features)
        out_shards[layer_id] = lax.ppermute(out_total, ("x", "y"), TURN).astype(F32)
        grad_end, _ = mix_states(grad_start, None, weights.swapaxes(0, 1))
        grad_inside = scan_inside_back(*scan_in, grad_ssd, after=[both])
        grad_x, grad_bc, grad_raw, head_sums, skip_sums = scan_outer_back(
            *grad_inside,
            *scan_in,
            *states_before,
            after,
            beyond,
            grad_end,
            *states_end,
            grad_ssd,
            scan_y,
            rows,
        )
        blocks = [grad_bc[..., BC_Q * k : BC_Q * k + BC_Q].astype(BF16) for k in range(TEAM)]
        turned = lambda k: lax.select_n(q ^ k, *blocks)
        half = lambda k: turned(k).astype(F32) + core_swap(turned(k ^ 1)).astype(F32)[::-1]
        grad_bc_own = half(0) + y_swap(half(2).astype(BF16)).astype(F32)
        grad_tile = jnp.pad(grad_bc_own, ((0, 0), (0, 0), (0, 128 - BC_Q)))

        edge_in = jnp.concatenate(
            (halo[:, 8 - edge :], wide[:, :edge].astype(BF16).astype(F32)), axis=1
        )
        edge_conv = lambda v: conv_piece(seg_ext[:, : 2 * edge], v, taps[:CONV], taps[CONV])
        edge_grad = jnp.concatenate((grad_x[:, :edge], grad_tile[:, :edge]), axis=-1)
        edge_grad = jax.vjp(edge_conv, edge_in)[1](edge_grad)[0][:, :edge].astype(BF16)
        returned = step_line(edge_grad, "z", -1).astype(F32)
        returned = jnp.pad(returned, ((0, 0), (8 - edge, 0), (0, 0)))
        grad_conv_x, conv_sums = conv_backward(
            wide, halo, taps, mask, grad_x, returned, INNER_Q, 0
        )
        grad_conv_tile, tile_sums = conv_backward(
            wide, halo, taps, mask, grad_tile, returned, 128, TILE
        )
        grad_wide = jnp.concatenate(
            (grad_conv_x, grad_conv_tile[..., :BC_Q], grad_raw[..., BC_Q:].astype(BF16)), axis=-1
        ).reshape(row_count, WIDE)
        in_grad = turn(normed, grad_wide)
        total = sum_to_owner(by_owner(x_order, in_grad, size, in_rows))
        in_parts[layer_id] = around_team(grad_parts(owner, gate_total, total))
        full_wide, full_gate, _ = full[layer_id]
        sequence = lambda v, k: lax.slice_in_dim(v, k * span, (k + 1) * span, axis=0)
        both_back = lambda k: back(sequence(grad_wide, k), full_wide) + back(
            sequence(grad_gate, k), full_gate
        )
        grad_far, grad_normed = both_back(1), both_back(0)
        norm_grad = jnp.sum(in_grad * full_wide.astype(F32), axis=1)
        norm_grad = norm_grad + jnp.sum(gate_grad * full_gate.astype(F32), axis=1)
        if fast:
            norm_grad = x_first(norm_grad)
        norm_grad = norm_grad / norm_gain[layer_id]
        grad_normed = team_scatter(grad_normed, grad_far)
        if fast:
            grad_normed = x_first(grad_normed)
        else:
            grad_normed = tie(grad_normed, both_total)
        _, pull_norm = jax.vjp(lambda v: norm_piece(v, norm_gain[layer_id]), stream_in)
        (grad_inner,) = pull_norm(grad_normed)
        grad_stream = grad_stream + grad_inner
        small[layer_id] = pack_small(
            conv_sums, tile_sums, head_sums, skip_sums, grad_gain, norm_grad.reshape(1, features),
            spread,
        )
    mixed = stream.reshape(1, length, features).astype(BF16)
    pack = xor_sum(xor_sum(jnp.stack(small), "x"), "z")
    across = y_swap(pack)
    packs = (pack, core_swap(pack), across, core_swap(across))
    norm_sum, taps_sum, bias_sum, dt_sum, decay_sum, skip_sum, gain_sum = open_small(
        owner, packs, features
    )
    return (
        mixed,
        grad_stream.reshape(1, length, features),
        norm_sum,
        join_weights(owner, in_parts),
        taps_sum,
        bias_sum,
        dt_sum,
        decay_sum,
        skip_sum,
        gain_sum,
        jnp.stack(out_shards),
    )


def solution(mesh):
    rows, spans = mesh.devices.shape
    split = Mesh(mesh.devices.reshape(rows // 2, 2, spans // 2, 2), ("x", "core", "z", "y"))
    tokens = P(("x", "core"), ("z", "y"), None)
    weight = P(None, ("x", "core", "z", "y"), None)
    return jax.shard_map(
        local,
        mesh=split,
        in_specs=(
            tokens,
            P(("x", "core"), ("z", "y")),
            tokens,
            P(),
            weight,
            P(),
            P(),
            P(),
            P(),
            P(),
            P(),
            weight,
        ),
        out_specs=(tokens, tokens, P(), weight, P(), P(), P(), P(), P(), P(), weight),
        check_vma=False,
    )
```
